32 devices in a mesh: seq: 4 (over y, core), tensor: 8 (over z, x).
Axes of the slice: x: 2, y: 2, z: 4, core: 2. Of those that a mesh axis runs over, the one named last changes fastest.
Arguments:
- tokens: bfloat16 [2048, 3584], P('seq', 'tensor'), may hold values from -6 to 6
- w_zx: bfloat16 [2, 3584, 1024], P(None, None, 'tensor'), may hold values from -0.09375 to 0.09375
- w_bc: bfloat16 [3584, 128], replicated, may hold values from -0.09375 to 0.09375
- w_dt: bfloat16 [3584, 16], P(None, 'tensor'), may hold values from -0.09375 to 0.09375
- dt_bias: float32 [16], P('tensor'), may hold values from -2 to 0.5
- a_rate: float32 [16], P('tensor'), may hold values from 0.00024414062 to 0.05
- d_skip: float32 [16], P('tensor'), may hold values from 0.3 to 1.5
- conv_x: float32 [4, 1024], P(None, 'tensor'), may hold values from -3 to 3
- conv_bc: float32 [4, 128], replicated, may hold values from -3 to 3
- norm_gain: float32 [1024], P('tensor'), may hold values from 0.25 to 1.75
- w_out: bfloat16 [1024, 3584], P('tensor'), may hold values from -0.1875 to 0.1875
- segments: int32 [2048], P('seq'), may hold values from 0 to 5, never falling along the last dimension, each value on 1 to 1024 neighbouring positions
Outputs:
- mixed: bfloat16 [2048, 3584], P(('seq', 'tensor'))
The draws below stay inside these ranges and needn't reach their ends.
Inputs may be any that keep to these rules, and one draw needn't show every extreme that they name: `segments`: prompt ids never fall along the tokens, so each prompt's tokens are contiguous.
All inputs are finite; a program needn't handle non-finite values.
Results may differ from the reference program's by a relative error of at most 0.02.
Values may be sent and summed in bfloat16 or wider, within the bound.
No kernel may reach another device: no remote copies, remote signals or barrier semaphores. Data moves between devices by JAX's collectives and lax.ppermute only.
A program may use at most 64 MiB of HBM per device.

```python
import math
import jax
import jax.numpy as jnp
import numpy as np
from jax import lax

D = 3584
P_SIZE = 64
N = 64
KCONV = 4
BLOCK = 256
HEAD_DEV = 2
SEGS = 6
HEADS = 16
TOKENS = 2048


def level_of(key, extent, shards, least, top_value):
    gain, own = 1.0, jax.random.fold_in(key, 6)
    for axis_at, shards_of in shards:
        draws = jnp.exp(jax.random.uniform(jax.random.fold_in(own, axis_at), (shards_of,), jnp.float32, least / len(shards), top_value / len(shards)))
        gain = gain * jnp.repeat(draws, extent[axis_at] // shards_of).reshape([-1 if axis == axis_at else 1 for axis in range(len(extent))])
    return gain


def length_profile(amount, total, reach, slope):
    weights = [(1 << 20) // math.isqrt(rank ** slope) + 1 for rank in range(2, amount + 1)]
    surplus, holding = total - reach - (amount - 1), [1] * (amount - 1)
    while surplus > 0:
        movable = [i for i in range(amount - 1) if holding[i] < reach]
        pool, budget = sum([weights[i] for i in movable]), surplus
        for i in movable:
            addition = min(reach - holding[i], max(1, budget * weights[i] // pool), surplus)
            holding[i] = holding[i] + addition
            surplus = surplus - addition
    return np.array([reach] + holding)


def uneven(own_key, count, total, limit, slope):
    if count == 2:
        one = jax.random.randint(own_key, (), max(1, total - limit), min(limit, total - 1) + 1)
        return jnp.stack([one, total - one])
    lengths = jnp.asarray(length_profile(count, total, limit, slope), jnp.int32)
    couples = (count - 1) // 2
    donor, receiver = lengths[1:1 + 2 * couples:2], lengths[2:2 + 2 * couples:2]
    margin = jnp.minimum(donor - 1, limit - receiver)
    passed = jax.random.randint(jax.random.fold_in(own_key, 1), (couples,), 0, 1 << 20) % (margin + 1)
    lengths = lengths.at[1:1 + 2 * couples:2].set(donor - passed).at[2:2 + 2 * couples:2].set(receiver + passed)
    return lengths[jax.random.permutation(jax.random.fold_in(own_key, 2), count)]


def scatter_about(own_key, dims, spread, limit, cuts=(), kind=jnp.bfloat16):
    result = spread * jax.random.normal(own_key, dims, jnp.float32)
    if cuts:
        result = result * level_of(own_key, dims, cuts, -0.22, 0.18)
    return jnp.clip(result, -limit, limit).astype(kind)


def setup_inputs(seed: int = 0) -> dict:
    streams_of = jax.random.split(jax.random.key(seed), 13)
    tokens = scatter_about(streams_of[0], (TOKENS, D), 1.0, 6.0, ((0, 4), (1, 8)))
    w_zx = scatter_about(streams_of[1], (2, D, HEADS * P_SIZE), D ** -0.5, 0.09375, ((2, 8),))
    w_bc = scatter_about(streams_of[2], (D, 2 * N), D ** -0.5, 0.09375)
    w_dt = scatter_about(streams_of[3], (D, HEADS), D ** -0.5, 0.09375, ((1, 8),))
    dt_bias = jnp.clip(-2.0 + 2.5 * jax.random.uniform(streams_of[4], (HEADS,), jnp.float32) ** level_of(streams_of[4], (HEADS,), ((0, 8),), -0.2, 0.2), -2.0, 0.5)
    a_rate = jnp.clip(jnp.exp(math.log(0.05) - 5.322034 * jax.random.uniform(streams_of[5], (HEADS,), jnp.float32) ** level_of(streams_of[5], (HEADS,), ((0, 8),), -0.2, 0.2)), 0.00024414062, 0.05)
    d_skip = jnp.clip(0.3 + 1.2 * jax.random.uniform(streams_of[6], (HEADS,), jnp.float32) ** level_of(streams_of[6], (HEADS,), ((0, 8),), -0.2, 0.2), 0.3, 1.5)
    conv_x = scatter_about(streams_of[7], (KCONV, HEADS * P_SIZE), 0.5, 3.0, ((1, 8),), jnp.float32)
    conv_bc = scatter_about(streams_of[8], (KCONV, 2 * N), 0.5, 3.0, (), jnp.float32)
    norm_gain = jnp.clip(1.0 + 0.15 * jax.random.normal(streams_of[9], (HEADS * P_SIZE,), jnp.float32), 0.25, 1.75)
    w_out = scatter_about(streams_of[10], (HEADS * P_SIZE, D), (HEADS * P_SIZE) ** -0.5, 0.1875, ((0, 8),))
    segments = jnp.searchsorted(jnp.cumsum(uneven(streams_of[11], SEGS, TOKENS, TOKENS // 2, 2)), jnp.arange(TOKENS), side="right").astype(jnp.int32)
    return {"tokens": tokens, "w_zx": w_zx, "w_bc": w_bc, "w_dt": w_dt, "dt_bias": dt_bias, "a_rate": a_rate, "d_skip": d_skip, "conv_x": conv_x, "conv_bc": conv_bc, "norm_gain": norm_gain, "w_out": w_out, "segments": segments}


HIGHEST_PREC = lax.Precision.HIGHEST
NORM_EPS = 1e-05

def conv_tail(extended, seg_ext, taps, tok_rows):
    conv_len = taps.shape[0]
    seg_now = seg_ext[conv_len - 1:]
    conv_sum = taps[conv_len - 1] * extended[conv_len - 1:]
    for offset in range(1, conv_len):
        earlier = extended[conv_len - 1 - offset:conv_len - 1 - offset + tok_rows]
        seg_then = seg_ext[conv_len - 1 - offset:conv_len - 1 - offset + tok_rows]
        conv_sum = conv_sum + taps[conv_len - 1 - offset] * jnp.where((seg_then == seg_now)[:, None], earlier, 0.0)
    return jax.nn.silu(conv_sum)

def ssd_block(carry, block):
    state, last_seg = carry
    inner_x, step_size, logdec, bmat, cmat, seg_ids = block
    cum_decay = jnp.cumsum(logdec, axis=0)
    position = jnp.arange(seg_ids.shape[0])
    visible = (seg_ids[:, None] == seg_ids[None, :]) & (position[:, None] >= position[None, :])
    gap_decay = jnp.where(visible[:, :, None], cum_decay[:, None, :] - cum_decay[None, :, :], -jnp.inf)
    scores = jnp.dot(cmat, bmat.T, precision=HIGHEST_PREC)
    weights = jnp.exp(gap_decay) * scores[:, :, None] * step_size[None, :, :]
    block_out = jnp.einsum('tsh,shp->thp', weights, inner_x, precision=HIGHEST_PREC)
    enter = jnp.where((seg_ids == last_seg)[:, None], jnp.exp(cum_decay), 0.0)
    block_out = block_out + enter[:, :, None] * jnp.einsum('tn,hpn->thp', cmat, state, precision=HIGHEST_PREC)
    tail_weight = jnp.where((seg_ids == seg_ids[-1])[:, None], jnp.exp(cum_decay[-1][None, :] - cum_decay), 0.0) * step_size
    carry_keep = jnp.where(seg_ids[-1] == last_seg, jnp.exp(cum_decay[-1]), 0.0)
    new_state = carry_keep[:, None, None] * state + jnp.einsum('sh,shp,sn->hpn', tail_weight, inner_x, bmat, precision=HIGHEST_PREC)
    return ((new_state, seg_ids[-1]), block_out)

def add_partial(total, group):
    normed_part, weight_part = group
    partial_value = jnp.dot(normed_part, weight_part, preferred_element_type=jnp.float32).astype(jnp.bfloat16)
    partial_value = lax.optimization_barrier(partial_value)
    return (total + partial_value.astype(jnp.float32), None)

def reference(tokens, w_zx, w_bc, w_dt, dt_bias, a_rate, d_skip, conv_x, conv_bc, norm_gain, w_out, segments):
    gate_proj = jnp.dot(tokens, w_zx[0], preferred_element_type=jnp.float32).astype(jnp.bfloat16)
    inner_proj = jnp.dot(tokens, w_zx[1], preferred_element_type=jnp.float32).astype(jnp.bfloat16)
    bc_proj = jnp.dot(tokens, w_bc, preferred_element_type=jnp.float32).astype(jnp.bfloat16)
    dt_raw = jnp.dot(tokens, w_dt, preferred_element_type=jnp.float32)
    rim_len = KCONV - 1
    seg_ext = jnp.concatenate([jnp.full((rim_len,), -1, jnp.int32), segments.astype(jnp.int32)], 0)
    conv_inner = conv_tail(jnp.concatenate([jnp.zeros((rim_len, HEADS * P_SIZE), jnp.float32), inner_proj.astype(jnp.float32)], 0), seg_ext, conv_x, TOKENS)
    conv_state = conv_tail(jnp.concatenate([jnp.zeros((rim_len, 2 * N), jnp.float32), bc_proj.astype(jnp.float32)], 0), seg_ext, conv_bc, TOKENS)
    bmat = conv_state[:, :N]
    cmat = conv_state[:, N:]
    step_size = jax.nn.softplus(dt_raw + dt_bias)
    logdec = -a_rate * step_size
    inner_heads = conv_inner.reshape(TOKENS, HEADS, P_SIZE)
    nblocks = TOKENS // BLOCK
    blocks = (inner_heads.reshape(nblocks, BLOCK, HEADS, P_SIZE), step_size.reshape(nblocks, BLOCK, HEADS), logdec.reshape(nblocks, BLOCK, HEADS), bmat.reshape(nblocks, BLOCK, N), cmat.reshape(nblocks, BLOCK, N), segments.astype(jnp.int32).reshape(nblocks, BLOCK))
    start = (jnp.zeros((HEADS, P_SIZE, N), jnp.float32), jnp.array(-1, jnp.int32))
    _, block_outs = lax.scan(ssd_block, start, blocks)
    ssd_out = block_outs.reshape(TOKENS, HEADS, P_SIZE) + d_skip[None, :, None] * inner_heads
    gated = ssd_out.reshape(TOKENS, HEADS * P_SIZE) * jax.nn.silu(gate_proj.astype(jnp.float32))
    scale = lax.rsqrt(lax.optimization_barrier(jnp.mean(gated * gated, axis=1)) + NORM_EPS)
    normed = (gated * scale[:, None] * norm_gain).astype(jnp.bfloat16)
    groups = HEADS // HEAD_DEV
    group_w = HEAD_DEV * P_SIZE
    normed_groups = jnp.transpose(normed.reshape(TOKENS, groups, group_w), (1, 0, 2))
    weight_groups = w_out.reshape(groups, group_w, D)
    total, _ = lax.scan(add_partial, jnp.zeros((TOKENS, D), jnp.float32), (normed_groups, weight_groups))
    return total.astype(jnp.bfloat16)
```

```python
import functools

import jax
import jax.numpy as jnp
import numpy as np
from jax import lax
from jax.experimental import pallas as pl
from jax.experimental.pallas import tpu as pltpu
from jax.sharding import PartitionSpec as P

NORM_EPS = 1e-05
F32 = jnp.float32
BF16 = jnp.bfloat16
VMEM = pl.BlockSpec(memory_space=pltpu.VMEM)
SMEM = pl.BlockSpec(memory_space=pltpu.SMEM)
ANY = pl.BlockSpec(memory_space=pl.ANY)
HALO = 8


def ring_order(n):
    width = 1
    while 2 * width * (2 * width) * 2 <= 2 * n and width * width * 2 < n:
        width *= 2
    depth = n // width
    if width == 1:
        return list(range(n))
    order = [z * width for z in range(depth)]
    for back, z in enumerate(reversed(range(depth))):
        row = [z * width + x for x in range(1, width)]
        order += row if back % 2 == 0 else row[::-1]
    return order


def ring_shift(block, order, step):
    n = len(order)
    return lax.ppermute(block, "tensor", [(order[i], order[(i + step) % n]) for i in range(n)])


def ring_gather(block, order):
    n = len(order)
    forth = back = block
    for step in range(1, n // 2):
        forth, back = ring_shift(forth, order, 1), ring_shift(back, order, -1)
        yield [(-step, forth), (step, back)]
    half = block.shape[0] // 2
    yield [(n // 2, (ring_shift(forth[:half], order, 1), ring_shift(back[half:], order, -1)))]


def pack(rows):
    count, width = rows.shape
    groups = 1
    while (groups * width) % 128:
        groups *= 2
    return jnp.concatenate(jnp.split(rows, groups, 0), 1)


def unpack(packed, width):
    return jnp.concatenate(jnp.split(packed, packed.shape[1] // width, 1), 0)


def silu(v):
    return v / (1.0 + jnp.exp(-v))


def dot(a, b, dims=((1,), (0,))):
    return lax.dot_general(a.astype(BF16), b.astype(BF16), (dims, ((), ())), preferred_element_type=F32)


def conv(ext, seg_ext, taps, rows):
    size = taps.shape[0]
    seg_now = seg_ext[HALO : HALO + rows]
    total = taps[size - 1 : size] * ext[HALO : HALO + rows]
    for offset in range(1, size):
        same = seg_ext[HALO - offset : HALO - offset + rows] == seg_now
        total = total + taps[size - 1 - offset : size - offset] * jnp.where(
            same, ext[HALO - offset : HALO - offset + rows], 0.0
        )
    return silu(total)


def prefix_sum(values):
    rows = values.shape[0]
    lower = lax.broadcasted_iota(jnp.int32, (rows, rows), 0) >= lax.broadcasted_iota(jnp.int32, (rows, rows), 1)
    lower = jnp.where(lower, 1.0, 0.0).astype(BF16)
    total = jnp.zeros(values.shape, F32)
    rest = values
    parts = []
    for _ in range(3):
        part = rest.astype(BF16)
        parts.append(part)
        rest = rest - part.astype(F32)
    for part in reversed(parts):
        total = total + jnp.dot(lower, part, preferred_element_type=F32)
    return total


def block_front(ext_x, ext_bc, seg_ext, dt_raw, taps_x, taps_bc, bias, rate, rows, seg_enter, seg_leave):
    conv_x = conv(ext_x, seg_ext, taps_x, rows)
    conv_bc = conv(ext_bc, seg_ext, taps_bc, rows)
    seg = seg_ext[HALO : HALO + rows]
    shifted = dt_raw + bias
    step_size = jnp.maximum(shifted, 0.0) + jnp.log1p(jnp.exp(-jnp.abs(shifted)))
    cum = prefix_sum(-rate * step_size)
    scaled = conv_x * step_size
    last = cum[rows - 1 : rows]
    tail = jnp.where(seg == seg_leave, jnp.exp(last - cum), 0.0)
    state_w = conv_bc.shape[1] // 2
    state = dot(conv_bc, tail * scaled, ((0,), (0,)))[:state_w]
    enter = jnp.where(seg == seg_enter, jnp.exp(cum), 0.0)
    return conv_x, conv_bc, cum, scaled, state, enter, last


def block_inner(conv_bc, cum, scaled, seg_col, seg_row, heads):
    rows, width = scaled.shape
    state_w = conv_bc.shape[1] // 2
    head_w = width // heads
    scores = dot(conv_bc[:, state_w:], conv_bc[:, :state_w], ((1,), (1,)))
    later = lax.broadcasted_iota(jnp.int32, (rows, rows), 0) >= lax.broadcasted_iota(jnp.int32, (rows, rows), 1)
    visible = (seg_col == seg_row) & later
    cum_rows = cum.T
    lane = lax.broadcasted_iota(jnp.int32, (rows, width), 1)
    result = jnp.zeros((rows, width), F32)
    scaled = scaled.astype(BF16)
    for head in range(heads):
        at = head * head_w
        gap = jnp.where(visible, cum[:, at : at + 1] - cum_rows[at : at + 1, :], -jnp.inf)
        part = dot(jnp.exp(gap) * scores, scaled)
        result = jnp.where((lane >= at) & (lane < at + head_w), part, result)
    return result


def later_block(heads, width, rows, lead, proj, seg_ext, seg_row, taps_x, taps_bc, bias, rate, skip,
                out, bc_out, enter_out, state_out, gate_out, ext_x, ext_bc):
    start = lead - HALO
    rounded = proj[start:, : 3 * width].astype(BF16).astype(F32)
    gate_out[...] = silu(rounded[HALO:, :width])
    ext_x[...] = rounded[:, width : 2 * width]
    ext_bc[...] = rounded[:, 2 * width : 3 * width]
    seg_enter = seg_ext[HALO - 1 : HALO]
    seg_leave = seg_ext[HALO + rows - 1 : HALO + rows]
    conv_x, conv_bc, cum, scaled, state, enter, last = block_front(
        ext_x, ext_bc, seg_ext, proj[lead:, 3 * width :], taps_x, taps_bc[...], bias[...], rate[...], rows, seg_enter, seg_leave
    )
    out[...] = block_inner(conv_bc, cum, scaled, seg_ext[HALO:], seg_row[...], heads) + skip[...] * conv_x
    bc_out[...] = conv_bc
    enter_out[...] = enter
    keep = jnp.where(seg_enter == seg_leave, jnp.exp(last), 0.0)
    state_w = state.shape[0]
    state_out[:state_w] = state
    state_out[state_w : state_w + 1] = keep
    state_out[state_w + 1 : state_w + 2] = last
    state_out[state_w + 2 :] = jnp.zeros((state_out.shape[0] - state_w - 2, width), F32)


def first_front(width, rows, proj_a, proj_b, halo, seg_ext, seg_last, state_b, taps_x, taps_bc, bias, rate,
                conv_out, bc_out, cum_out, scaled_out, enter_out, state_out, message, ext_x, ext_bc, dt):
    own = proj_a.shape[0]
    ext_x[:HALO] = halo[:, :width].astype(F32)
    ext_bc[:HALO] = halo[:, width:].astype(F32)
    ext_x[HALO : HALO + own] = proj_a[:, width : 2 * width].astype(BF16).astype(F32)
    ext_bc[HALO : HALO + own] = proj_a[:, 2 * width : 3 * width].astype(BF16).astype(F32)
    ext_x[HALO + own :] = proj_b[: rows - own, width : 2 * width].astype(BF16).astype(F32)
    ext_bc[HALO + own :] = proj_b[: rows - own, 2 * width : 3 * width].astype(BF16).astype(F32)
    dt[:own] = proj_a[:, 3 * width :]
    dt[own:] = proj_b[: rows - own, 3 * width :]
    seg_enter = seg_ext[HALO : HALO + 1]
    seg_leave = seg_ext[HALO + rows - 1 : HALO + rows]
    conv_x, conv_bc, cum, scaled, state, enter, last = block_front(
        ext_x, ext_bc, seg_ext, dt[...], taps_x, taps_bc[...], bias[...], rate[...], rows, seg_enter, seg_leave
    )
    conv_out[...] = conv_x
    bc_out[...] = conv_bc
    cum_out[...] = cum
    scaled_out[...] = scaled
    enter_out[...] = enter
    keep = jnp.where(seg_enter == seg_leave, jnp.exp(last), 0.0)
    state_w = state.shape[0]
    state_out[:state_w] = state
    state_out[state_w : state_w + 1] = keep
    state_out[state_w + 1 :] = jnp.zeros((state_out.shape[0] - state_w - 1, width), F32)
    message[:state_w] = state_b[state_w : state_w + 1] * state + state_b[:state_w]
    message[state_w : state_w + 1] = last + state_b[state_w + 1 : state_w + 2]
    message[state_w + 1 : state_w + 2] = jnp.broadcast_to(seg_last[...].astype(F32), (1, width))
    message[state_w + 2 :] = jnp.zeros((message.shape[0] - state_w - 2, width), F32)


def first_inner(heads, width, rows, conv_x, conv_bc, cum, scaled, proj_a, proj_b, seg_col, seg_row, skip, out, gate_out):
    own = proj_a.shape[0]
    gate_out[:own] = silu(proj_a[:, :width].astype(BF16).astype(F32))
    gate_out[own:] = silu(proj_b[: rows - own, :width].astype(BF16).astype(F32))
    out[...] = (
        block_inner(conv_bc[...], cum[...], scaled[...], seg_col[HALO:], seg_row[...], heads) + skip[...] * conv_x[...]
    )


def finish(count, rows, seg_first, out_a, gate_a, bc_a, enter_a, state_a, out_b, gate_b, bc_b, enter_b, *rest):
    messages, gated = rest[:count], rest[count]
    state_w = bc_a.shape[1] // 2
    entering = jnp.zeros((state_w, out_a.shape[1]), F32)
    decay = jnp.zeros((1, out_a.shape[1]), F32)
    first = seg_first[...].astype(F32)
    for message in messages:
        passes = jnp.where(message[state_w + 1 : state_w + 2] == first, jnp.exp(decay), 0.0)
        entering = entering + passes * message[:state_w]
        decay = decay + message[state_w : state_w + 1]
    second = state_a[state_w : state_w + 1] * entering + state_a[:state_w]
    gated[:rows] = ((out_a[...] + enter_a[...] * dot(bc_a[:, state_w:], entering)) * gate_a[...]).astype(BF16)
    gated[rows:] = ((out_b[...] + enter_b[...] * dot(bc_b[:, state_w:], second)) * gate_b[...]).astype(BF16)


def project_out(parts, where, place, core, gated, *rest):
    pieces, (out, held, sems) = rest[:parts], rest[parts:]
    copies = []
    for k, (side, block, row) in enumerate(where):
        size = pieces[k].shape[0]
        copies.append(pltpu.make_async_copy(pieces[k], held.at[side, block, pl.ds(row, size)], sems.at[k]))
        copies[-1].start()
    blocks, rows, width = gated.shape
    squares = jnp.zeros((rows, width), F32)
    for block in range(blocks):
        value = gated[block].astype(F32)
        squares = squares + value * value
    scale = lax.rsqrt(jnp.sum(squares, axis=1, keepdims=True) / (blocks * width) + NORM_EPS)
    columns = held.shape[3]
    sums = [jnp.zeros((rows, columns), F32)] * 2
    for block in range(blocks):
        for k, (side, at, _) in enumerate(where):
            if at == block:
                copies[k].wait()
        value = gated[place[block]]
        for side in range(2):
            sums[side] = sums[side] + jnp.dot(value, held[side, block], preferred_element_type=F32)
    sums = [(s * scale).astype(BF16) for s in sums]
    is_first = core[0] == 0
    out[:, :columns] = jnp.where(is_first, sums[0], sums[1])
    out[:, columns:] = jnp.where(is_first, sums[1], sums[0])


def call(body, outs, scratch=(), vmem=48, flops=10**7, **kw):
    return pl.pallas_call(
        body,
        out_shape=outs,
        scratch_shapes=list(scratch),
        compiler_params=pltpu.CompilerParams(vmem_limit_bytes=vmem << 20),
        cost_estimate=pl.CostEstimate(flops=flops, bytes_accessed=1 << 21, transcendentals=1 << 17),
        **kw,
    )


def local(
    tokens, w_zx, w_bc, w_dt, dt_bias, a_rate, d_skip, conv_x, conv_bc, norm_gain, w_out, segments
):
    tok_rows, feat = tokens.shape
    width = w_zx.shape[2]
    heads = dt_bias.shape[0]
    head_w = width // heads
    state_w = w_bc.shape[1] // 2
    model = w_zx.shape[1]
    n_seq, n_tensor = lax.axis_size("seq"), lax.axis_size("tensor")
    seq_at, tensor_at = lax.axis_index("seq"), lax.axis_index("tensor")
    rows = tok_rows // 2
    lead = 32
    shape = lambda *s, kind=F32: jax.ShapeDtypeStruct(s, kind)

    order = ring_order(n_tensor)
    sources = np.zeros((n_tensor, n_tensor), np.int32)
    for i, device in enumerate(order):
        for distance in range(n_tensor):
            sources[device, distance] = order[(i + distance) % n_tensor]
    source = lax.dynamic_index_in_dim(jnp.asarray(sources), tensor_at, 0, False)

    spread = lambda v: jnp.repeat(v, head_w, axis=-1)
    weights = jnp.concatenate([w_zx[0], w_zx[1], w_bc, spread(w_dt)], 1).reshape(n_tensor, feat, 4 * width)

    def weight_of(distance):
        return lax.dynamic_index_in_dim(weights, source[distance % n_tensor], 0, False)

    def project(chunk):
        packed = pack(chunk)
        total = jnp.dot(chunk, weight_of(0), preferred_element_type=F32)
        rests = []
        for arrived in ring_gather(packed, order):
            for distance, part in arrived:
                if isinstance(part, tuple):
                    part = jnp.concatenate(part, 0)
                total = total + jnp.dot(unpack(part, feat), weight_of(distance), preferred_element_type=F32)
            rests.append(arrived)
        return total, rests

    split = rows - lead
    proj_b, steps_b = project(tokens[split:])
    first_chunk, _ = lax.optimization_barrier((tokens[:split], steps_b[-2][0][1]))
    proj_a, steps_a = project(first_chunk)

    ahead = [(i, i + 1) for i in range(n_seq - 1)]
    seg_halo = lax.ppermute(segments[tok_rows - HALO :], "seq", ahead)
    seg_all = jnp.concatenate([seg_halo, segments])[:, None]
    seg_ext_a, seg_ext_b = seg_all[: HALO + rows], seg_all[rows:]
    seg_row_a, seg_row_b = segments[None, :rows], segments[None, rows:]
    seg_first, seg_last = segments[None, :1], segments[None, tok_rows - 1 :]
    halo = lax.ppermute(proj_b[lead + rows - HALO :, width : 3 * width].astype(BF16), "seq", ahead)
    bias, rate, skip = spread(dt_bias)[None], spread(a_rate)[None], spread(d_skip)[None]

    msg_rows = state_w + 8
    block = shape(rows, width)
    ext = pltpu.VMEM((HALO + rows, width), F32)
    out_b, bc_b, enter_b, state_b, gate_b = call(
        functools.partial(later_block, heads, width, rows, lead),
        [block, block, block, shape(msg_rows, width), block],
        [ext, ext],
    )(proj_b, seg_ext_b, seg_row_b, conv_x, conv_bc, bias, rate, skip)
    cx_a, bc_a, cum_a, scaled_a, enter_a, state_a, message = call(
        functools.partial(first_front, width, rows),
        [block] * 5 + [shape(msg_rows, width)] * 2,
        [ext, ext, pltpu.VMEM((rows, width), F32)],
    )(proj_a, proj_b, halo, seg_ext_a, seg_last, state_b, conv_x, conv_bc, bias, rate)
    messages = [
        lax.ppermute(message, "seq", [(i, i + far) for i in range(n_seq - far)]) for far in range(1, n_seq)
    ]
    out_a, gate_a = call(functools.partial(first_inner, heads, width, rows), [block, block])(
        cx_a, bc_a, cum_a, scaled_a, proj_a, proj_b, seg_ext_a, seg_row_a, skip
    )
    gated = call(
        functools.partial(finish, len(messages), rows), shape(tok_rows, width, kind=BF16)
    )(seg_first, out_a, gate_a, bc_a, enter_a, state_a, out_b, gate_b, bc_b, enter_b, *messages)

    core = seq_at % 2
    scaled_out = (w_out.astype(F32) * norm_gain[:, None]).astype(BF16)
    columns = model // 2
    own_half = lax.dynamic_slice_in_dim(scaled_out, core * columns, columns, 1)
    other_half = lax.dynamic_slice_in_dim(scaled_out, (1 - core) * columns, columns, 1)
    own_first, _ = lax.optimization_barrier((own_half, steps_a[-2][0][1]))
    swap = [(i, i ^ 1) for i in range(n_seq)]
    pieces, where = [own_half, other_half], [(0, 0, 0), (1, 0, 0)]
    for arrived in ring_gather(own_first, order):
        for distance, part in arrived:
            row = 0
            for part in part if isinstance(part, tuple) else (part,):
                pieces += [part, lax.ppermute(part, "seq", swap)]
                where += [(side, distance % n_tensor, row) for side in range(2)]
                row += part.shape[0]

    mine = lax.all_to_all(gated.reshape(n_tensor, tok_rows // n_tensor, width), "tensor", 0, 0)
    return call(
        functools.partial(project_out, len(pieces), tuple(where)),
        shape(tok_rows // n_tensor, model, kind=BF16),
        [pltpu.VMEM((2, n_tensor, width, columns), BF16), pltpu.SemaphoreType.DMA((len(pieces),))],
        in_specs=[SMEM, SMEM, VMEM] + [ANY] * len(pieces),
        flops=10**9,
    )(source, core[None], mine, *pieces)


def solution(mesh):
    in_specs = (
        P("seq", "tensor"),
        P(None, None, "tensor"),
        P(),
        P(None, "tensor"),
        P("tensor"),
        P("tensor"),
        P("tensor"),
        P(None, "tensor"),
        P(),
        P("tensor"),
        P("tensor", None),
        P("seq"),
    )
    out_specs = P(("seq", "tensor"), None)
    return jax.shard_map(local, mesh=mesh, in_specs=in_specs, out_specs=out_specs, check_vma=False)
```

```python
import functools

import jax
import jax.numpy as jnp
import numpy as np
from jax import lax
from jax.experimental import pallas as pl
from jax.experimental.pallas import tpu as pltpu
from jax.sharding import PartitionSpec as P

NORM_EPS = 1e-05
F32 = jnp.float32
BF16 = jnp.bfloat16
VMEM = pl.BlockSpec(memory_space=pltpu.VMEM)
ANY = pl.BlockSpec(memory_space=pl.ANY)
HALO = 8


def ring_place(index, n):
    return jnp.where(index % 2 == 0, index // 2, (2 * n - 1 - index) // 2)


def ring_index(place, n):
    return jnp.where(place < n // 2, 2 * place, 2 * n - 1 - 2 * place)


def ring_shift(block, step):
    n = lax.axis_size("tensor")
    order = [2 * i if i < n // 2 else 2 * n - 1 - 2 * i for i in range(n)]
    return lax.ppermute(block, "tensor", [(order[i], order[(i + step) % n]) for i in range(n)])


def ring_gather(block):
    n = lax.axis_size("tensor")
    forth = back = block
    steps = []
    for _ in range(1, n // 2):
        forth, back = ring_shift(forth, 1), ring_shift(back, -1)
        steps.append((forth, back))
    half = block.shape[0] // 32 * 16
    steps.append((ring_shift(forth[:half], 1), ring_shift(back[half:], -1)))
    return steps


def silu(v):
    return v / (1.0 + jnp.exp(-v))


def dot(a, b, dims=((1,), (0,))):
    return lax.dot_general(a.astype(BF16), b.astype(BF16), (dims, ((), ())), preferred_element_type=F32)


def source_of(distance):
    n = lax.axis_size("tensor")
    return ring_index((ring_place(lax.axis_index("tensor"), n) + distance + n) % n, n)


def project(distances, first, *refs):
    count = len(distances)
    blocks, (w_zx, w_bc, w_dt), refs = refs[:count], refs[count : count + 3], refs[count + 3 :]
    total, (out, held, sems) = (None, refs) if first else (refs[0], refs[1:])
    feat = w_bc.shape[0] // lax.axis_size("tensor")
    width = w_bc.shape[1]
    sources = [w_zx.at[0], w_zx.at[1], w_bc, w_dt]
    copies = []
    for k, (distance, size, skip) in enumerate(distances):
        rows = pl.ds(pl.multiple_of(source_of(distance) * feat + skip, 16), size)
        for j, source in enumerate(sources):
            copies.append(
                pltpu.make_async_copy(
                    source.at[rows], held.at[k, pl.ds(0, size), pl.ds(j * width, width)], sems.at[k, j]
                )
            )
            copies[-1].start()
    result = 0.0 if first else total[...]
    for k, (_, size, _) in enumerate(distances):
        for j in range(len(sources)):
            copies[k * len(sources) + j].wait()
        result = result + dot(blocks[k][...], held[k, :size], ((0,), (0,)))
    out[...] = result


def conv(ext, seg_ext, taps, rows):
    size = taps.shape[0]
    seg_now = seg_ext[HALO : HALO + rows]
    total = taps[size - 1 : size] * ext[HALO : HALO + rows]
    for offset in range(1, size):
        same = seg_ext[HALO - offset : HALO - offset + rows] == seg_now
        total = total + taps[size - 1 - offset : size - offset] * jnp.where(
            same, ext[HALO - offset : HALO - offset + rows], 0.0
        )
    return silu(total)


def prefix_sum(values):
    rows = values.shape[0]
    lower = lax.broadcasted_iota(jnp.int32, (rows, rows), 0) >= lax.broadcasted_iota(jnp.int32, (rows, rows), 1)
    lower = jnp.where(lower, 1.0, 0.0).astype(BF16)
    total = jnp.zeros(values.shape, F32)
    rest = values
    parts = []
    for _ in range(3):
        part = rest.astype(BF16)
        parts.append(part)
        rest = rest - part.astype(F32)
    for part in reversed(parts):
        total = total + jnp.dot(lower, part, preferred_element_type=F32)
    return total


def block_front(ext_x, ext_bc, seg_ext, dt_raw, taps_x, taps_bc, bias, rate, rows, seg_enter, seg_leave):
    conv_x = conv(ext_x, seg_ext, taps_x, rows)
    conv_bc = conv(ext_bc, seg_ext, taps_bc, rows)
    seg = seg_ext[HALO : HALO + rows]
    shifted = dt_raw + bias
    step_size = jnp.maximum(shifted, 0.0) + jnp.log1p(jnp.exp(-jnp.abs(shifted)))
    cum = prefix_sum(-rate * step_size)
    scaled = conv_x * step_size
    last = cum[rows - 1 : rows]
    tail = jnp.where(seg == seg_leave, jnp.exp(last - cum), 0.0)
    state_w = conv_bc.shape[1] // 2
    state = dot(conv_bc, tail * scaled, ((0,), (0,)))[:state_w]
    enter = jnp.where(seg == seg_enter, jnp.exp(cum), 0.0)
    return conv_x, conv_bc, cum, scaled, state, enter, last


def block_inner(conv_bc, cum, scaled, seg_col, seg_row, heads):
    rows, width = scaled.shape
    state_w = conv_bc.shape[1] // 2
    head_w = width // heads
    scores = dot(conv_bc[:, state_w:], conv_bc[:, :state_w], ((1,), (1,)))
    later = lax.broadcasted_iota(jnp.int32, (rows, rows), 0) >= lax.broadcasted_iota(jnp.int32, (rows, rows), 1)
    visible = (seg_col == seg_row) & later
    cum_rows = cum.T
    lane = lax.broadcasted_iota(jnp.int32, (rows, width), 1)
    result = jnp.zeros((rows, width), F32)
    scaled = scaled.astype(BF16)
    for head in range(heads):
        at = head * head_w
        gap = jnp.where(visible, cum[:, at : at + 1] - cum_rows[at : at + 1, :], -jnp.inf)
        part = dot(jnp.exp(gap) * scores, scaled)
        result = jnp.where((lane >= at) & (lane < at + head_w), part, result)
    return result


def later_block(heads, width, rows, proj, seg_ext, seg_row, taps_x, taps_bc, bias, rate, skip,
                out, bc_out, enter_out, state_out, gate_out, ext_x, ext_bc):
    rounded = proj[rows - HALO :, : 3 * width].astype(BF16).astype(F32)
    gate_out[...] = silu(rounded[HALO:, :width])
    ext_x[...] = rounded[:, width : 2 * width]
    ext_bc[...] = rounded[:, 2 * width : 3 * width]
    seg_enter = seg_ext[HALO - 1 : HALO]
    seg_leave = seg_ext[HALO + rows - 1 : HALO + rows]
    conv_x, conv_bc, cum, scaled, state, enter, last = block_front(
        ext_x, ext_bc, seg_ext, proj[rows:, 3 * width :], taps_x, taps_bc[...], bias[...], rate[...], rows, seg_enter, seg_leave
    )
    out[...] = block_inner(conv_bc, cum, scaled, seg_ext[HALO:], seg_row[...], heads) + skip[...] * conv_x
    bc_out[...] = conv_bc
    enter_out[...] = enter
    keep = jnp.where(seg_enter == seg_leave, jnp.exp(last), 0.0)
    state_w = state.shape[0]
    state_out[:state_w] = state
    state_out[state_w : state_w + 1] = keep
    state_out[state_w + 1 : state_w + 2] = last
    state_out[state_w + 2 :] = jnp.zeros((state_out.shape[0] - state_w - 2, width), F32)


def first_front(width, rows, proj, halo, seg_ext, seg_last, state_b, taps_x, taps_bc, bias, rate,
                conv_out, bc_out, cum_out, scaled_out, enter_out, state_out, message, ext_x, ext_bc):
    ext_x[:HALO] = halo[:, :width].astype(F32)
    ext_bc[:HALO] = halo[:, width:].astype(F32)
    ext_x[HALO:] = proj[:rows, width : 2 * width].astype(BF16).astype(F32)
    ext_bc[HALO:] = proj[:rows, 2 * width : 3 * width].astype(BF16).astype(F32)
    seg_enter = seg_ext[HALO : HALO + 1]
    seg_leave = seg_ext[HALO + rows - 1 : HALO + rows]
    conv_x, conv_bc, cum, scaled, state, enter, last = block_front(
        ext_x, ext_bc, seg_ext, proj[:rows, 3 * width :], taps_x, taps_bc[...], bias[...], rate[...], rows, seg_enter, seg_leave
    )
    conv_out[...] = conv_x
    bc_out[...] = conv_bc
    cum_out[...] = cum
    scaled_out[...] = scaled
    enter_out[...] = enter
    keep = jnp.where(seg_enter == seg_leave, jnp.exp(last), 0.0)
    state_w = state.shape[0]
    state_out[:state_w] = state
    state_out[state_w : state_w + 1] = keep
    state_out[state_w + 1 :] = jnp.zeros((state_out.shape[0] - state_w - 1, width), F32)
    message[:state_w] = state_b[state_w : state_w + 1] * state + state_b[:state_w]
    message[state_w : state_w + 1] = last + state_b[state_w + 1 : state_w + 2]
    message[state_w + 1 : state_w + 2] = jnp.broadcast_to(seg_last[...].astype(F32), (1, width))
    message[state_w + 2 :] = jnp.zeros((message.shape[0] - state_w - 2, width), F32)


def first_inner(heads, width, rows, conv_x, conv_bc, cum, scaled, proj, seg_col, seg_row, skip, out, gate_out):
    gate_out[...] = silu(proj[:rows, :width].astype(BF16).astype(F32))
    out[...] = (
        block_inner(conv_bc[...], cum[...], scaled[...], seg_col[HALO:], seg_row[...], heads) + skip[...] * conv_x[...]
    )


def finish(count, rows, seg_first, out_a, gate_a, bc_a, enter_a, state_a, out_b, gate_b, bc_b, enter_b, *rest):
    messages, gated = rest[:count], rest[count]
    state_w = bc_a.shape[1] // 2
    entering = jnp.zeros((state_w, out_a.shape[1]), F32)
    decay = jnp.zeros((1, out_a.shape[1]), F32)
    first = seg_first[...].astype(F32)
    for message in messages:
        passes = jnp.where(message[state_w + 1 : state_w + 2] == first, jnp.exp(decay), 0.0)
        entering = entering + passes * message[:state_w]
        decay = decay + message[state_w : state_w + 1]
    second = state_a[state_w : state_w + 1] * entering + state_a[:state_w]
    gated[:rows] = ((out_a[...] + enter_a[...] * dot(bc_a[:, state_w:], entering)) * gate_a[...]).astype(BF16)
    gated[rows:] = ((out_b[...] + enter_b[...] * dot(bc_b[:, state_w:], second)) * gate_b[...]).astype(BF16)


def product(gated, where, pieces, held, sems):
    copies = []
    for k, (slot, _, row) in enumerate(where):
        copies.append(
            pltpu.make_async_copy(pieces[k], held.at[slot, pl.ds(row, pieces[k].shape[0])], sems.at[k])
        )
        copies[-1].start()
    sums = [0.0] * len(gated)
    waited = set()
    for k, (slot, distance, _) in enumerate(where):
        if slot in waited:
            continue
        waited.add(slot)
        for j, (other, _, _) in enumerate(where):
            if other == slot:
                copies[j].wait()
        source = source_of(distance)
        for i, rows in enumerate(gated):
            sums[i] = sums[i] + jnp.dot(rows[source], held[slot], preferred_element_type=F32)
    return sums


def product_early(where, mine, other, *rest):
    pieces, (out, held, sems) = rest[: len(where)], rest[len(where) :]
    sums = product((mine, other), where, pieces, held, sems)
    rows = mine.shape[1]
    out[:rows] = sums[0]
    out[rows:] = sums[1]


def product_last(where, mine, other, total, *rest):
    pieces, (mine_out, other_out, held, sems) = rest[: len(where)], rest[len(where) :]
    sums = product((mine, other), where, pieces, held, sems)
    blocks, rows, width = mine.shape
    for i, (gated, out) in enumerate(((mine, mine_out), (other, other_out))):
        squares = jnp.zeros((rows, width), F32)
        for block in range(blocks):
            value = gated[block].astype(F32)
            squares = squares + value * value
        scale = lax.rsqrt(jnp.sum(squares, axis=1, keepdims=True) / (blocks * width) + NORM_EPS)
        out[...] = ((sums[i] + total[i * rows : (i + 1) * rows]) * scale).astype(BF16)


def call(body, outs, scratch=(), vmem=48, flops=10**7, **kw):
    return pl.pallas_call(
        body,
        out_shape=outs,
        scratch_shapes=list(scratch),
        compiler_params=pltpu.CompilerParams(vmem_limit_bytes=vmem << 20),
        cost_estimate=pl.CostEstimate(flops=flops, bytes_accessed=1 << 21, transcendentals=1 << 17),
        **kw,
    )


def local(
    tokens, w_zx, w_bc, w_dt, dt_bias, a_rate, d_skip, conv_x, conv_bc, norm_gain, w_out, segments
):
    tok_rows, feat = tokens.shape
    width = w_zx.shape[2]
    heads = dt_bias.shape[0]
    head_w = width // heads
    state_w = w_bc.shape[1] // 2
    model = w_zx.shape[1]
    n_seq, n_tensor = lax.axis_size("seq"), lax.axis_size("tensor")
    seq_at = lax.axis_index("seq")
    rows = tok_rows // 2
    shape = lambda *s, kind=F32: jax.ShapeDtypeStruct(s, kind)

    spread = lambda v: jnp.repeat(v, head_w, axis=-1)
    expand = np.repeat(np.eye(heads, dtype=np.float32), head_w, axis=1)
    w_step = jnp.dot(w_dt, expand.astype(BF16))
    block = tokens.T
    steps = ring_gather(block)
    last = n_tensor // 2
    arrivals = [[(0, block, 0)]]
    arrivals += [[(-i - 1, forth, 0), (i + 1, back, 0)] for i, (forth, back) in enumerate(steps[:-1])]
    arrivals += [[(last, steps[-1][0], 0), (last, steps[-1][1], steps[-1][0].shape[0])]]
    proj = ()
    for arrived in arrivals:
        proj = (
            call(
                functools.partial(project, [(d, part.shape[0], skip) for d, part, skip in arrived], not proj),
                shape(tok_rows, 4 * width),
                [
                    pltpu.VMEM((len(arrived), max(part.shape[0] for _, part, _ in arrived), 4 * width), BF16),
                    pltpu.SemaphoreType.DMA((len(arrived), 4)),
                ],
                in_specs=[VMEM] * len(arrived) + [ANY] * 3 + [VMEM] * len(proj),
                flops=10**9,
            )(*[part for _, part, _ in arrived], w_zx, w_bc, w_step, *proj),
        )
    (proj,) = proj

    ahead = [(i, i + 1) for i in range(n_seq - 1)]
    seg_halo = lax.ppermute(segments[tok_rows - HALO :], "seq", ahead)
    seg_all = jnp.concatenate([seg_halo, segments])[:, None]
    seg_ext_a, seg_ext_b = seg_all[: HALO + rows], seg_all[rows:]
    seg_row_a, seg_row_b = segments[None, :rows], segments[None, rows:]
    seg_first, seg_last = segments[None, :1], segments[None, tok_rows - 1 :]
    halo = lax.ppermute(proj[tok_rows - HALO :, width : 3 * width].astype(BF16), "seq", ahead)
    bias, rate, skip = spread(dt_bias)[None], spread(a_rate)[None], spread(d_skip)[None]

    msg_rows = state_w + 8
    plane = shape(rows, width)
    ext = pltpu.VMEM((HALO + rows, width), F32)
    out_b, bc_b, enter_b, state_b, gate_b = call(
        functools.partial(later_block, heads, width, rows),
        [plane, plane, plane, shape(msg_rows, width), plane],
        [ext, ext],
    )(proj, seg_ext_b, seg_row_b, conv_x, conv_bc, bias, rate, skip)
    cx_a, bc_a, cum_a, scaled_a, enter_a, state_a, message = call(
        functools.partial(first_front, width, rows),
        [plane] * 5 + [shape(msg_rows, width)] * 2,
        [ext, ext],
    )(proj, halo, seg_ext_a, seg_last, state_b, conv_x, conv_bc, bias, rate)
    messages = [
        lax.ppermute(message, "seq", [(i, i + far) for i in range(n_seq - far)]) for far in range(1, n_seq)
    ]
    out_a, gate_a = call(functools.partial(first_inner, heads, width, rows), [plane, plane])(
        cx_a, bc_a, cum_a, scaled_a, proj, seg_ext_a, seg_row_a, skip
    )
    gated = call(
        functools.partial(finish, len(messages), rows), shape(tok_rows, width, kind=BF16)
    )(seg_first, out_a, gate_a, bc_a, enter_a, state_a, out_b, gate_b, bc_b, enter_b, *messages)

    core = seq_at % 2
    columns = model // 2
    own = (lax.dynamic_slice_in_dim(w_out, core * columns, columns, 1).astype(F32) * norm_gain[:, None]).astype(BF16)
    own_first, _ = lax.optimization_barrier((own, steps[-1]))
    w_steps = ring_gather(own_first)
    swap = [(i, i ^ 1) for i in range(n_seq)]
    tok_own = tok_rows // n_tensor
    mine = lax.all_to_all(gated.reshape(n_tensor, tok_own, width), "tensor", 0, 0)
    other = lax.ppermute(mine, "seq", swap)
    pieces, where = [own], [(0, 0, 0)]
    for i, pair in enumerate(w_steps[:-1]):
        pieces += pair
        where += [(2 * i + 1, -i - 1, 0), (2 * i + 2, i + 1, 0)]
    total = call(
        functools.partial(product_early, where),
        shape(2 * tok_own, columns),
        [pltpu.VMEM((len(where), width, columns), BF16), pltpu.SemaphoreType.DMA((len(where),))],
        in_specs=[VMEM, VMEM] + [ANY] * len(pieces),
        flops=10**9,
    )(mine, other, *pieces)
    where = [(0, last, 0), (0, last, w_steps[-1][0].shape[0])]
    half = shape(tok_own, columns, kind=BF16)
    out_own, out_other = call(
        functools.partial(product_last, where),
        [half, half],
        [pltpu.VMEM((1, width, columns), BF16), pltpu.SemaphoreType.DMA((2,))],
        in_specs=[VMEM, VMEM, VMEM] + [ANY] * 2,
        flops=10**8,
    )(mine, other, total, *w_steps[-1])
    arrived = lax.ppermute(out_other, "seq", swap)
    is_first = core == 0
    return jnp.concatenate([jnp.where(is_first, out_own, arrived), jnp.where(is_first, arrived, out_own)], 1)


def solution(mesh):
    in_specs = (
        P("seq", "tensor"),
        P(None, None, "tensor"),
        P(),
        P(None, "tensor"),
        P("tensor"),
        P("tensor"),
        P("tensor"),
        P(None, "tensor"),
        P(),
        P("tensor"),
        P("tensor", None),
        P("seq"),
    )
    out_specs = P(("seq", "tensor"), None)
    return jax.shard_map(local, mesh=mesh, in_specs=in_specs, out_specs=out_specs, check_vma=False)
```

```python
import functools

import jax
import jax.numpy as jnp
import numpy as np
from jax import lax
from jax.experimental import pallas as pl
from jax.experimental.pallas import tpu as pltpu
from jax.sharding import PartitionSpec as P

NORM_EPS = 1e-05
F32 = jnp.float32
BF16 = jnp.bfloat16
VMEM = pl.BlockSpec(memory_space=pltpu.VMEM)
ANY = pl.BlockSpec(memory_space=pl.ANY)
HALO = 8


def ring_place(index, n):
    return jnp.where(index % 2 == 0, index // 2, (2 * n - 1 - index) // 2)


def ring_index(place, n):
    return jnp.where(place < n // 2, 2 * place, 2 * n - 1 - 2 * place)


def ring_shift(block, step):
    n = lax.axis_size("tensor")
    order = [2 * i if i < n // 2 else 2 * n - 1 - 2 * i for i in range(n)]
    return lax.ppermute(block, "tensor", [(order[i], order[(i + step) % n]) for i in range(n)])


def after(values, *earlier):
    return lax.optimization_barrier((values, earlier))[0]


def ring_step(forth, back, step):
    if step < lax.axis_size("tensor") // 2:
        return ring_shift(forth, 1), ring_shift(back, -1)
    half = forth.shape[0] // 32 * 16
    return ring_shift(forth[:half], 1), ring_shift(back[half:], -1)


def silu(v):
    return v / (1.0 + jnp.exp(-v))


def dot(a, b, dims=((1,), (0,))):
    return lax.dot_general(a.astype(BF16), b.astype(BF16), (dims, ((), ())), preferred_element_type=F32)


def source_of(distance):
    n = lax.axis_size("tensor")
    return ring_index((ring_place(lax.axis_index("tensor"), n) + distance + n) % n, n)


def project(distances, first, *refs):
    count = len(distances)
    blocks, (w_zx, w_bc, w_dt), refs = refs[:count], refs[count : count + 3], refs[count + 3 :]
    total, (out, held, sems) = (None, refs) if first else (refs[0], refs[1:])
    feat = w_bc.shape[0] // lax.axis_size("tensor")
    width = w_bc.shape[1]
    sources = [w_zx.at[0], w_zx.at[1], w_bc, w_dt]
    copies = []
    for k, (distance, size, skip) in enumerate(distances):
        rows = pl.ds(pl.multiple_of(source_of(distance) * feat + skip, 16), size)
        for j, source in enumerate(sources):
            copies.append(
                pltpu.make_async_copy(
                    source.at[rows], held.at[k, pl.ds(0, size), pl.ds(j * width, width)], sems.at[k, j]
                )
            )
            copies[-1].start()
    result = 0.0 if first else total[...]
    for k, (_, size, _) in enumerate(distances):
        for j in range(len(sources)):
            copies[k * len(sources) + j].wait()
        result = result + dot(blocks[k][...], held[k, :size], ((0,), (0,)))
    out[...] = result


def conv(ext, seg_ext, taps, rows):
    size = taps.shape[0]
    seg_now = seg_ext[HALO : HALO + rows]
    total = taps[size - 1 : size] * ext[HALO : HALO + rows]
    for offset in range(1, size):
        same = seg_ext[HALO - offset : HALO - offset + rows] == seg_now
        total = total + taps[size - 1 - offset : size - offset] * jnp.where(
            same, ext[HALO - offset : HALO - offset + rows], 0.0
        )
    return silu(total)


def prefix_sum(values):
    rows = values.shape[0]
    lower = lax.broadcasted_iota(jnp.int32, (rows, rows), 0) >= lax.broadcasted_iota(jnp.int32, (rows, rows), 1)
    lower = jnp.where(lower, 1.0, 0.0).astype(BF16)
    total = jnp.zeros(values.shape, F32)
    rest = values
    parts = []
    for _ in range(3):
        part = rest.astype(BF16)
        parts.append(part)
        rest = rest - part.astype(F32)
    for part in reversed(parts):
        total = total + jnp.dot(lower, part, preferred_element_type=F32)
    return total


def block_front(ext_x, ext_bc, seg_ext, dt_raw, taps_x, taps_bc, bias, rate, rows, seg_enter, seg_leave):
    conv_x = conv(ext_x, seg_ext, taps_x, rows)
    conv_bc = conv(ext_bc, seg_ext, taps_bc, rows)
    seg = seg_ext[HALO : HALO + rows]
    shifted = dt_raw + bias
    step_size = jnp.maximum(shifted, 0.0) + jnp.log1p(jnp.exp(-jnp.abs(shifted)))
    cum = prefix_sum(-rate * step_size)
    scaled = conv_x * step_size
    last = cum[rows - 1 : rows]
    tail = jnp.where(seg == seg_leave, jnp.exp(last - cum), 0.0)
    state_w = conv_bc.shape[1] // 2
    state = dot(conv_bc, tail * scaled, ((0,), (0,)))[:state_w]
    enter = jnp.where(seg == seg_enter, jnp.exp(cum), 0.0)
    return conv_x, conv_bc, cum, scaled, state, enter, last


def block_inner(conv_bc, cum, scaled, seg_col, seg_row, heads):
    rows, width = scaled.shape
    state_w = conv_bc.shape[1] // 2
    head_w = width // heads
    scores = dot(conv_bc[:, state_w:], conv_bc[:, :state_w], ((1,), (1,)))
    later = lax.broadcasted_iota(jnp.int32, (rows, rows), 0) >= lax.broadcasted_iota(jnp.int32, (rows, rows), 1)
    visible = (seg_col == seg_row) & later
    cum_rows = cum.T
    lane = lax.broadcasted_iota(jnp.int32, (rows, width), 1)
    result = jnp.zeros((rows, width), F32)
    scaled = scaled.astype(BF16)
    for head in range(heads):
        at = head * head_w
        gap = jnp.where(visible, cum[:, at : at + 1] - cum_rows[at : at + 1, :], -jnp.inf)
        part = dot(jnp.exp(gap) * scores, scaled)
        result = jnp.where((lane >= at) & (lane < at + head_w), part, result)
    return result


def later_block(heads, width, rows, proj, seg_ext, seg_row, taps_x, taps_bc, bias, rate, skip,
                out, bc_out, enter_out, state_out, gate_out, ext_x, ext_bc):
    rounded = proj[rows - HALO :, : 3 * width].astype(BF16).astype(F32)
    gate_out[...] = silu(rounded[HALO:, :width])
    ext_x[...] = rounded[:, width : 2 * width]
    ext_bc[...] = rounded[:, 2 * width : 3 * width]
    seg_enter = seg_ext[HALO - 1 : HALO]
    seg_leave = seg_ext[HALO + rows - 1 : HALO + rows]
    conv_x, conv_bc, cum, scaled, state, enter, last = block_front(
        ext_x, ext_bc, seg_ext, proj[rows:, 3 * width :], taps_x, taps_bc[...], bias[...], rate[...], rows, seg_enter, seg_leave
    )
    out[...] = block_inner(conv_bc, cum, scaled, seg_ext[HALO:], seg_row[...], heads) + skip[...] * conv_x
    bc_out[...] = conv_bc
    enter_out[...] = enter
    keep = jnp.where(seg_enter == seg_leave, jnp.exp(last), 0.0)
    state_w = state.shape[0]
    state_out[:state_w] = state
    state_out[state_w : state_w + 1] = keep
    state_out[state_w + 1 : state_w + 2] = last
    state_out[state_w + 2 :] = jnp.zeros((state_out.shape[0] - state_w - 2, width), F32)


def first_front(width, rows, proj, halo, seg_ext, seg_last, state_b, taps_x, taps_bc, bias, rate,
                conv_out, bc_out, cum_out, scaled_out, enter_out, state_out, message, ext_x, ext_bc):
    ext_x[:HALO] = halo[:, :width].astype(F32)
    ext_bc[:HALO] = halo[:, width:].astype(F32)
    ext_x[HALO:] = proj[:rows, width : 2 * width].astype(BF16).astype(F32)
    ext_bc[HALO:] = proj[:rows, 2 * width : 3 * width].astype(BF16).astype(F32)
    seg_enter = seg_ext[HALO : HALO + 1]
    seg_leave = seg_ext[HALO + rows - 1 : HALO + rows]
    conv_x, conv_bc, cum, scaled, state, enter, last = block_front(
        ext_x, ext_bc, seg_ext, proj[:rows, 3 * width :], taps_x, taps_bc[...], bias[...], rate[...], rows, seg_enter, seg_leave
    )
    conv_out[...] = conv_x
    bc_out[...] = conv_bc
    cum_out[...] = cum
    scaled_out[...] = scaled
    enter_out[...] = enter
    keep = jnp.where(seg_enter == seg_leave, jnp.exp(last), 0.0)
    state_w = state.shape[0]
    state_out[:state_w] = state
    state_out[state_w : state_w + 1] = keep
    state_out[state_w + 1 :] = jnp.zeros((state_out.shape[0] - state_w - 1, width), F32)
    message[:state_w] = state_b[state_w : state_w + 1] * state + state_b[:state_w]
    message[state_w : state_w + 1] = last + state_b[state_w + 1 : state_w + 2]
    message[state_w + 1 : state_w + 2] = jnp.broadcast_to(seg_last[...].astype(F32), (1, width))
    message[state_w + 2 :] = jnp.zeros((message.shape[0] - state_w - 2, width), F32)


def first_inner(heads, width, rows, conv_x, conv_bc, cum, scaled, proj, seg_col, seg_row, skip, out, gate_out):
    gate_out[...] = silu(proj[:rows, :width].astype(BF16).astype(F32))
    out[...] = (
        block_inner(conv_bc[...], cum[...], scaled[...], seg_col[HALO:], seg_row[...], heads) + skip[...] * conv_x[...]
    )


def finish(count, rows, seg_first, out_a, gate_a, bc_a, enter_a, state_a, out_b, gate_b, bc_b, enter_b, *rest):
    messages, gated = rest[:count], rest[count]
    state_w = bc_a.shape[1] // 2
    entering = jnp.zeros((state_w, out_a.shape[1]), F32)
    decay = jnp.zeros((1, out_a.shape[1]), F32)
    first = seg_first[...].astype(F32)
    for message in messages:
        passes = jnp.where(message[state_w + 1 : state_w + 2] == first, jnp.exp(decay), 0.0)
        entering = entering + passes * message[:state_w]
        decay = decay + message[state_w : state_w + 1]
    second = state_a[state_w : state_w + 1] * entering + state_a[:state_w]
    gated[:rows] = ((out_a[...] + enter_a[...] * dot(bc_a[:, state_w:], entering)) * gate_a[...]).astype(BF16)
    gated[rows:] = ((out_b[...] + enter_b[...] * dot(bc_b[:, state_w:], second)) * gate_b[...]).astype(BF16)


def product(gated, where, pieces, held, sems):
    copies = []
    for k, (slot, _, row) in enumerate(where):
        copies.append(
            pltpu.make_async_copy(pieces[k], held.at[slot, pl.ds(row, pieces[k].shape[0])], sems.at[k])
        )
        copies[-1].start()
    sums = [0.0] * len(gated)
    waited = set()
    for k, (slot, distance, _) in enumerate(where):
        if slot in waited:
            continue
        waited.add(slot)
        for j, (other, _, _) in enumerate(where):
            if other == slot:
                copies[j].wait()
        source = source_of(distance)
        for i, rows in enumerate(gated):
            sums[i] = sums[i] + jnp.dot(rows[source], held[slot], preferred_element_type=F32)
    return sums


def product_early(where, mine, other, *rest):
    pieces, (out, held, sems) = rest[: len(where)], rest[len(where) :]
    sums = product((mine, other), where, pieces, held, sems)
    rows = mine.shape[1]
    out[:rows] = sums[0]
    out[rows:] = sums[1]


def product_last(where, mine, other, total, *rest):
    pieces, (mine_out, other_out, held, sems) = rest[: len(where)], rest[len(where) :]
    sums = product((mine, other), where, pieces, held, sems)
    blocks, rows, width = mine.shape
    for i, (gated, out) in enumerate(((mine, mine_out), (other, other_out))):
        squares = jnp.zeros((rows, width), F32)
        for block in range(blocks):
            value = gated[block].astype(F32)
            squares = squares + value * value
        scale = lax.rsqrt(jnp.sum(squares, axis=1, keepdims=True) / (blocks * width) + NORM_EPS)
        out[...] = ((sums[i] + total[i * rows : (i + 1) * rows]) * scale).astype(BF16)


def call(body, outs, scratch=(), vmem=48, flops=10**7, **kw):
    return pl.pallas_call(
        body,
        out_shape=outs,
        scratch_shapes=list(scratch),
        compiler_params=pltpu.CompilerParams(vmem_limit_bytes=vmem << 20),
        cost_estimate=pl.CostEstimate(flops=flops, bytes_accessed=1 << 21, transcendentals=1 << 17),
        **kw,
    )


def local(
    tokens, w_zx, w_bc, w_dt, dt_bias, a_rate, d_skip, conv_x, conv_bc, norm_gain, w_out, segments
):
    tok_rows, feat = tokens.shape
    width = w_zx.shape[2]
    heads = dt_bias.shape[0]
    head_w = width // heads
    state_w = w_bc.shape[1] // 2
    model = w_zx.shape[1]
    n_seq, n_tensor = lax.axis_size("seq"), lax.axis_size("tensor")
    seq_at = lax.axis_index("seq")
    rows = tok_rows // 2
    shape = lambda *s, kind=F32: jax.ShapeDtypeStruct(s, kind)

    spread = lambda v: jnp.repeat(v, head_w, axis=-1)
    expand = np.repeat(np.eye(heads, dtype=np.float32), head_w, axis=1)
    w_step = jnp.dot(w_dt, expand.astype(BF16))
    block = tokens.T
    last = n_tensor // 2
    forth = back = block
    arrived, projs = [(0, block, 0)], []
    for step in range(1, last + 2):
        if step <= last:
            if step > 1:
                forth, back = after((forth, back), projs[step - 2])
            forth, back = ring_step(forth, back, step)
        sizes = [(distance, part.shape[0], skip) for distance, part, skip in arrived]
        total = projs[-1:]
        projs.append(
            call(
                functools.partial(project, sizes, not total),
                shape(tok_rows, 4 * width),
                [
                    pltpu.VMEM((len(sizes), max(size for _, size, _ in sizes), 4 * width), BF16),
                    pltpu.SemaphoreType.DMA((len(sizes), 4)),
                ],
                in_specs=[VMEM] * len(sizes) + [ANY] * 3 + [VMEM] * len(total),
                flops=10**9,
            )(*[part for _, part, _ in arrived], w_zx, w_bc, w_step, *total)
        )
        arrived = [(-step, forth, 0), (step, back, 0)]
        if step == last:
            arrived = [(last, forth, 0), (last, back, forth.shape[0])]
    proj = projs[-1]
    tokens_there = (forth, back, projs[-2])

    ahead = [(i, i + 1) for i in range(n_seq - 1)]
    seg_halo = lax.ppermute(segments[tok_rows - HALO :], "seq", ahead)
    seg_all = jnp.concatenate([seg_halo, segments])[:, None]
    seg_ext_a, seg_ext_b = seg_all[: HALO + rows], seg_all[rows:]
    seg_row_a, seg_row_b = segments[None, :rows], segments[None, rows:]
    seg_first, seg_last = segments[None, :1], segments[None, tok_rows - 1 :]
    halo = lax.ppermute(proj[tok_rows - HALO :, width : 3 * width].astype(BF16), "seq", ahead)
    bias, rate, skip = spread(dt_bias)[None], spread(a_rate)[None], spread(d_skip)[None]

    msg_rows = state_w + 8
    plane = shape(rows, width)
    ext = pltpu.VMEM((HALO + rows, width), F32)
    out_b, bc_b, enter_b, state_b, gate_b = call(
        functools.partial(later_block, heads, width, rows),
        [plane, plane, plane, shape(msg_rows, width), plane],
        [ext, ext],
    )(proj, seg_ext_b, seg_row_b, conv_x, conv_bc, bias, rate, skip)
    cx_a, bc_a, cum_a, scaled_a, enter_a, state_a, message = call(
        functools.partial(first_front, width, rows),
        [plane] * 5 + [shape(msg_rows, width)] * 2,
        [ext, ext],
    )(proj, halo, seg_ext_a, seg_last, state_b, conv_x, conv_bc, bias, rate)
    messages = [
        lax.ppermute(message, "seq", [(i, i + far) for i in range(n_seq - far)]) for far in range(1, n_seq)
    ]
    out_a, gate_a = call(functools.partial(first_inner, heads, width, rows), [plane, plane])(
        cx_a, bc_a, cum_a, scaled_a, proj, seg_ext_a, seg_row_a, skip
    )
    gated = call(
        functools.partial(finish, len(messages), rows), shape(tok_rows, width, kind=BF16)
    )(seg_first, out_a, gate_a, bc_a, enter_a, state_a, out_b, gate_b, bc_b, enter_b, *messages)

    tok_own = tok_rows // n_tensor
    mine = lax.all_to_all(gated.reshape(n_tensor, tok_own, width), "tensor", 0, 0)

    core = seq_at % 2
    columns = model // 2
    own = (lax.dynamic_slice_in_dim(w_out, core * columns, columns, 1).astype(F32) * norm_gain[:, None]).astype(BF16)
    orders = [tokens_there, messages, mine]
    forth = back = own
    w_steps = []
    for step in range(1, last + 1):
        if step <= len(orders):
            forth, back = after((forth, back), orders[step - 1])
        forth, back = ring_step(forth, back, step)
        w_steps.append((forth, back))
    swap = [(i, i ^ 1) for i in range(n_seq)]
    other = lax.ppermute(mine, "seq", swap)
    pieces, where = [own], [(0, 0, 0)]
    for i, pair in enumerate(w_steps[:-1]):
        pieces += pair
        where += [(2 * i + 1, -i - 1, 0), (2 * i + 2, i + 1, 0)]
    total = call(
        functools.partial(product_early, where),
        shape(2 * tok_own, columns),
        [pltpu.VMEM((len(where), width, columns), BF16), pltpu.SemaphoreType.DMA((len(where),))],
        in_specs=[VMEM, VMEM] + [ANY] * len(pieces),
        flops=10**9,
    )(mine, other, *pieces)
    where = [(0, last, 0), (0, last, w_steps[-1][0].shape[0])]
    half = shape(tok_own, columns, kind=BF16)
    out_own, out_other = call(
        functools.partial(product_last, where),
        [half, half],
        [pltpu.VMEM((1, width, columns), BF16), pltpu.SemaphoreType.DMA((2,))],
        in_specs=[VMEM, VMEM, VMEM] + [ANY] * 2,
        flops=10**8,
    )(mine, other, total, *w_steps[-1])
    arrived = lax.ppermute(out_other, "seq", swap)
    is_first = core == 0
    return jnp.concatenate([jnp.where(is_first, out_own, arrived), jnp.where(is_first, arrived, out_own)], 1)


def solution(mesh):
    in_specs = (
        P("seq", "tensor"),
        P(None, None, "tensor"),
        P(),
        P(None, "tensor"),
        P("tensor"),
        P("tensor"),
        P("tensor"),
        P(None, "tensor"),
        P(),
        P("tensor"),
        P("tensor", None),
        P("seq"),
    )
    out_specs = P(("seq", "tensor"), None)
    return jax.shard_map(local, mesh=mesh, in_specs=in_specs, out_specs=out_specs, check_vma=False)
```

```python
import functools

import jax
import jax.numpy as jnp
import numpy as np
from jax import lax
from jax.experimental import pallas as pl
from jax.experimental.pallas import tpu as pltpu
from jax.sharding import PartitionSpec as P

NORM_EPS = 1e-05
F32 = jnp.float32
BF16 = jnp.bfloat16
VMEM = pl.BlockSpec(memory_space=pltpu.VMEM)
ANY = pl.BlockSpec(memory_space=pl.ANY)
HALO = 8


def ring_place(index, n):
    return jnp.where(index % 2 == 0, index // 2, (2 * n - 1 - index) // 2)


def ring_index(place, n):
    return jnp.where(place < n // 2, 2 * place, 2 * n - 1 - 2 * place)


def ring_shift(block, step):
    n = lax.axis_size("tensor")
    order = [2 * i if i < n // 2 else 2 * n - 1 - 2 * i for i in range(n)]
    return lax.ppermute(block, "tensor", [(order[i], order[(i + step) % n]) for i in range(n)])


def after(values, *earlier):
    return lax.optimization_barrier((values, earlier))[0]


def halves(forth, back, top, bottom):
    size = top.shape[0]
    top[...] = forth[:size]
    bottom[...] = back[size:]


def silu(v):
    return v / (1.0 + jnp.exp(-v))


def dot(a, b, dims=((1,), (0,))):
    return lax.dot_general(a.astype(BF16), b.astype(BF16), (dims, ((), ())), preferred_element_type=F32)


def source_of(distance):
    n = lax.axis_size("tensor")
    return ring_index((ring_place(lax.axis_index("tensor"), n) + distance + n) % n, n)


def project(distances, first, *refs):
    count = len(distances)
    blocks, (w_zx, w_bc, w_dt), refs = refs[:count], refs[count : count + 3], refs[count + 3 :]
    total, (out, held, sems) = (None, refs) if first else (refs[0], refs[1:])
    feat = w_bc.shape[0] // lax.axis_size("tensor")
    width = w_bc.shape[1]
    sources = [w_zx.at[0], w_zx.at[1], w_bc, w_dt]
    copies = []
    for k, (distance, size, skip) in enumerate(distances):
        rows = pl.ds(pl.multiple_of(source_of(distance) * feat + skip, 16), size)
        for j, source in enumerate(sources):
            copies.append(
                pltpu.make_async_copy(
                    source.at[rows], held.at[k, pl.ds(0, size), pl.ds(j * width, width)], sems.at[k, j]
                )
            )
            copies[-1].start()
    result = 0.0 if first else total[...]
    for k, (_, size, _) in enumerate(distances):
        for j in range(len(sources)):
            copies[k * len(sources) + j].wait()
        result = result + dot(blocks[k][...], held[k, :size], ((0,), (0,)))
    out[...] = result


def conv(ext, seg_ext, taps, rows):
    size = taps.shape[0]
    seg_now = seg_ext[HALO : HALO + rows]
    total = taps[size - 1 : size] * ext[HALO : HALO + rows]
    for offset in range(1, size):
        same = seg_ext[HALO - offset : HALO - offset + rows] == seg_now
        total = total + taps[size - 1 - offset : size - offset] * jnp.where(
            same, ext[HALO - offset : HALO - offset + rows], 0.0
        )
    return silu(total)


def prefix_sum(values):
    rows = values.shape[0]
    lower = lax.broadcasted_iota(jnp.int32, (rows, rows), 0) >= lax.broadcasted_iota(jnp.int32, (rows, rows), 1)
    lower = jnp.where(lower, 1.0, 0.0).astype(BF16)
    total = jnp.zeros(values.shape, F32)
    rest = values
    parts = []
    for _ in range(3):
        part = rest.astype(BF16)
        parts.append(part)
        rest = rest - part.astype(F32)
    for part in reversed(parts):
        total = total + jnp.dot(lower, part, preferred_element_type=F32)
    return total


def block_front(ext_x, ext_bc, seg_ext, dt_raw, taps_x, taps_bc, bias, rate, rows, seg_enter, seg_leave):
    conv_x = conv(ext_x, seg_ext, taps_x, rows)
    conv_bc = conv(ext_bc, seg_ext, taps_bc, rows)
    seg = seg_ext[HALO : HALO + rows]
    shifted = dt_raw + bias
    step_size = jnp.maximum(shifted, 0.0) + jnp.log1p(jnp.exp(-jnp.abs(shifted)))
    cum = prefix_sum(-rate * step_size)
    scaled = conv_x * step_size
    last = cum[rows - 1 : rows]
    tail = jnp.where(seg == seg_leave, jnp.exp(last - cum), 0.0)
    state_w = conv_bc.shape[1] // 2
    state = dot(conv_bc, tail * scaled, ((0,), (0,)))[:state_w]
    enter = jnp.where(seg == seg_enter, jnp.exp(cum), 0.0)
    return conv_x, conv_bc, cum, scaled, state, enter, last


def block_inner(conv_bc, cum, scaled, seg_col, seg_row, heads):
    rows, width = scaled.shape
    state_w = conv_bc.shape[1] // 2
    head_w = width // heads
    scores = dot(conv_bc[:, state_w:], conv_bc[:, :state_w], ((1,), (1,)))
    later = lax.broadcasted_iota(jnp.int32, (rows, rows), 0) >= lax.broadcasted_iota(jnp.int32, (rows, rows), 1)
    visible = (seg_col == seg_row) & later
    cum_rows = cum.T
    lane = lax.broadcasted_iota(jnp.int32, (rows, width), 1)
    result = jnp.zeros((rows, width), F32)
    scaled = scaled.astype(BF16)
    for head in range(heads):
        at = head * head_w
        gap = jnp.where(visible, cum[:, at : at + 1] - cum_rows[at : at + 1, :], -jnp.inf)
        part = dot(jnp.exp(gap) * scores, scaled)
        result = jnp.where((lane >= at) & (lane < at + head_w), part, result)
    return result


def later_block(heads, width, rows, proj, seg_ext, seg_row, taps_x, taps_bc, bias, rate, skip,
                out, bc_out, enter_out, state_out, gate_out, ext_x, ext_bc):
    rounded = proj[rows - HALO :, : 3 * width].astype(BF16).astype(F32)
    gate_out[...] = silu(rounded[HALO:, :width])
    ext_x[...] = rounded[:, width : 2 * width]
    ext_bc[...] = rounded[:, 2 * width : 3 * width]
    seg_enter = seg_ext[HALO - 1 : HALO]
    seg_leave = seg_ext[HALO + rows - 1 : HALO + rows]
    conv_x, conv_bc, cum, scaled, state, enter, last = block_front(
        ext_x, ext_bc, seg_ext, proj[rows:, 3 * width :], taps_x, taps_bc[...], bias[...], rate[...], rows, seg_enter, seg_leave
    )
    out[...] = block_inner(conv_bc, cum, scaled, seg_ext[HALO:], seg_row[...], heads) + skip[...] * conv_x
    bc_out[...] = conv_bc
    enter_out[...] = enter
    keep = jnp.where(seg_enter == seg_leave, jnp.exp(last), 0.0)
    state_w = state.shape[0]
    state_out[:state_w] = state
    state_out[state_w : state_w + 1] = keep
    state_out[state_w + 1 : state_w + 2] = last
    state_out[state_w + 2 :] = jnp.zeros((state_out.shape[0] - state_w - 2, width), F32)


def first_front(width, rows, proj, halo, seg_ext, seg_last, state_b, taps_x, taps_bc, bias, rate,
                conv_out, bc_out, cum_out, scaled_out, enter_out, state_out, message, ext_x, ext_bc):
    ext_x[:HALO] = halo[:, :width].astype(F32)
    ext_bc[:HALO] = halo[:, width:].astype(F32)
    ext_x[HALO:] = proj[:rows, width : 2 * width].astype(BF16).astype(F32)
    ext_bc[HALO:] = proj[:rows, 2 * width : 3 * width].astype(BF16).astype(F32)
    seg_enter = seg_ext[HALO : HALO + 1]
    seg_leave = seg_ext[HALO + rows - 1 : HALO + rows]
    conv_x, conv_bc, cum, scaled, state, enter, last = block_front(
        ext_x, ext_bc, seg_ext, proj[:rows, 3 * width :], taps_x, taps_bc[...], bias[...], rate[...], rows, seg_enter, seg_leave
    )
    conv_out[...] = conv_x
    bc_out[...] = conv_bc
    cum_out[...] = cum
    scaled_out[...] = scaled
    enter_out[...] = enter
    keep = jnp.where(seg_enter == seg_leave, jnp.exp(last), 0.0)
    state_w = state.shape[0]
    state_out[:state_w] = state
    state_out[state_w : state_w + 1] = keep
    state_out[state_w + 1 :] = jnp.zeros((state_out.shape[0] - state_w - 1, width), F32)
    message[:state_w] = state_b[state_w : state_w + 1] * state + state_b[:state_w]
    message[state_w : state_w + 1] = last + state_b[state_w + 1 : state_w + 2]
    message[state_w + 1 : state_w + 2] = jnp.broadcast_to(seg_last[...].astype(F32), (1, width))
    message[state_w + 2 :] = jnp.zeros((message.shape[0] - state_w - 2, width), F32)


def first_inner(heads, width, rows, conv_x, conv_bc, cum, scaled, proj, seg_col, seg_row, skip, out, gate_out):
    gate_out[...] = silu(proj[:rows, :width].astype(BF16).astype(F32))
    out[...] = (
        block_inner(conv_bc[...], cum[...], scaled[...], seg_col[HALO:], seg_row[...], heads) + skip[...] * conv_x[...]
    )


def finish(rows, seg_first, messages, out_a, gate_a, bc_a, enter_a, state_a, out_b, gate_b, bc_b, enter_b, gated):
    state_w = bc_a.shape[1] // 2
    entering = jnp.zeros((state_w, out_a.shape[1]), F32)
    decay = jnp.zeros((1, out_a.shape[1]), F32)
    first = seg_first[...].astype(F32)
    place = lax.axis_index("seq")
    for device in reversed(range(messages.shape[0] - 1)):
        earlier = device < place
        passes = earlier & (messages[device, state_w + 1 : state_w + 2] == first)
        passes = jnp.where(passes, jnp.exp(decay), 0.0)
        entering = entering + passes * messages[device, :state_w]
        decay = decay + jnp.where(earlier, messages[device, state_w : state_w + 1], 0.0)
    second = state_a[state_w : state_w + 1] * entering + state_a[:state_w]
    gated[:rows] = ((out_a[...] + enter_a[...] * dot(bc_a[:, state_w:], entering)) * gate_a[...]).astype(BF16)
    gated[rows:] = ((out_b[...] + enter_b[...] * dot(bc_b[:, state_w:], second)) * gate_b[...]).astype(BF16)


def product(gated, where, pieces, held, sems):
    copies = []
    for k, (slot, _, row) in enumerate(where):
        copies.append(
            pltpu.make_async_copy(pieces[k], held.at[slot, pl.ds(row, pieces[k].shape[0])], sems.at[k])
        )
        copies[-1].start()
    total = 0.0
    waited = set()
    for k, (slot, distance, _) in enumerate(where):
        if slot in waited:
            continue
        waited.add(slot)
        for j, (other, _, _) in enumerate(where):
            if other == slot:
                copies[j].wait()
        source = source_of(distance)
        rows = jnp.concatenate([part[source] for part in gated], 0)
        total = total + jnp.dot(rows, held[slot], preferred_element_type=F32)
    return total


def product_early(where, mine, other, *rest):
    pieces, (out, held, sems) = rest[: len(where)], rest[len(where) :]
    out[...] = product((mine, other), where, pieces, held, sems)


def product_last(where, mine, other, total, *rest):
    pieces, (mine_out, other_out, held, sems) = rest[: len(where)], rest[len(where) :]
    result = product((mine, other), where, pieces, held, sems) + total[...]
    blocks, rows, width = mine.shape
    for i, (gated, out) in enumerate(((mine, mine_out), (other, other_out))):
        squares = jnp.zeros((rows, width), F32)
        for block in range(blocks):
            value = gated[block].astype(F32)
            squares = squares + value * value
        scale = lax.rsqrt(jnp.sum(squares, axis=1, keepdims=True) / (blocks * width) + NORM_EPS)
        out[...] = (result[i * rows : (i + 1) * rows] * scale).astype(BF16)


def call(body, outs, scratch=(), vmem=48, flops=10**7, **kw):
    return pl.pallas_call(
        body,
        out_shape=outs,
        scratch_shapes=list(scratch),
        compiler_params=pltpu.CompilerParams(vmem_limit_bytes=vmem << 20),
        cost_estimate=pl.CostEstimate(flops=flops, bytes_accessed=1 << 21, transcendentals=1 << 17),
        **kw,
    )


def local(
    tokens, w_zx, w_bc, w_dt, dt_bias, a_rate, d_skip, conv_x, conv_bc, norm_gain, w_out, segments
):
    tok_rows, feat = tokens.shape
    width = w_zx.shape[2]
    heads = dt_bias.shape[0]
    head_w = width // heads
    state_w = w_bc.shape[1] // 2
    model = w_zx.shape[1]
    n_seq, n_tensor = lax.axis_size("seq"), lax.axis_size("tensor")
    seq_at = lax.axis_index("seq")
    rows = tok_rows // 2
    shape = lambda *s, kind=F32: jax.ShapeDtypeStruct(s, kind)

    spread = lambda v: jnp.repeat(v, head_w, axis=-1)
    expand = np.repeat(np.eye(heads, dtype=np.float32), head_w, axis=1)
    w_step = jnp.dot(w_dt, expand.astype(BF16))
    block = tokens.T
    core = seq_at % 2
    columns = model // 2
    own = (lax.dynamic_slice_in_dim(w_out, core * columns, columns, 1).astype(F32) * norm_gain[:, None]).astype(BF16)
    last = n_tensor // 2
    w_half = width // 2
    w_forth = w_back = (own[:w_half], own[w_half:])
    w_steps = []

    cut = feat // 32 * 16
    far = source_of(last) * feat
    w_far = jnp.concatenate(
        [lax.dynamic_slice_in_dim(w, far, feat, 0) for w in (w_zx[0], w_zx[1], w_bc, w_step)], 1
    )
    forth = back = block
    arrived, projs = [(0, block), None], []
    for step in range(1, last + 1):
        if step > 1:
            forth, back = after((forth, back), projs[step - 2])
        if step == last:
            forth, back = call(halves, [shape(cut, tok_rows, kind=BF16), shape(feat - cut, tok_rows, kind=BF16)])(
                forth, back
            )
        if step == 2:
            tops = after((w_forth[0], w_back[0]), forth, back)
        if step == 3:
            bottoms = after((w_forth[1], w_back[1]), forth, back)
        forth, back = ring_shift(forth, 1), ring_shift(back, -1)
        if step == 2:
            tops = ring_shift(tops[0], 1), ring_shift(tops[1], -1)
        if step == 3:
            bottoms = ring_shift(bottoms[0], 1), ring_shift(bottoms[1], -1)
        blocks = [item for item in arrived if item]
        total = projs[-1:]
        projs.append(
            call(
                functools.partial(project, [(distance, feat, 0) for distance, _ in blocks], not total),
                shape(tok_rows, 4 * width),
                [pltpu.VMEM((len(blocks), feat, 4 * width), BF16), pltpu.SemaphoreType.DMA((len(blocks), 4))],
                in_specs=[VMEM] * len(blocks) + [ANY] * 3 + [VMEM] * len(total),
                flops=10**9,
            )(*[part for _, part in blocks], w_zx, w_bc, w_step, *total)
        )
        arrived = [(-step, forth), (step, back)]
    w_far = after(w_far, projs[0])
    tokens_there = (forth, back, projs[-1], w_far)
    proj = projs[-1]
    for part, rows_of in ((forth, w_far[:cut]), (back, w_far[cut:])):
        proj = proj + lax.dot_general(part, rows_of, (((0,), (0,)), ((), ())), preferred_element_type=F32)

    ahead = [(i, i + 1) for i in range(n_seq - 1)]
    seg_halo = lax.ppermute(segments[tok_rows - HALO :], "seq", ahead)
    seg_all = jnp.concatenate([seg_halo, segments])[:, None]
    seg_ext_a, seg_ext_b = seg_all[: HALO + rows], seg_all[rows:]
    seg_row_a, seg_row_b = segments[None, :rows], segments[None, rows:]
    seg_first, seg_last = segments[None, :1], segments[None, tok_rows - 1 :]
    halo = lax.ppermute(proj[tok_rows - HALO :, width : 3 * width].astype(BF16), "seq", ahead)
    bias, rate, skip = spread(dt_bias)[None], spread(a_rate)[None], spread(d_skip)[None]

    msg_rows = state_w + 8
    plane = shape(rows, width)
    ext = pltpu.VMEM((HALO + rows, width), F32)
    out_b, bc_b, enter_b, state_b, gate_b = call(
        functools.partial(later_block, heads, width, rows),
        [plane, plane, plane, shape(msg_rows, width), plane],
        [ext, ext],
    )(proj, seg_ext_b, seg_row_b, conv_x, conv_bc, bias, rate, skip)
    cx_a, bc_a, cum_a, scaled_a, enter_a, state_a, message = call(
        functools.partial(first_front, width, rows),
        [plane] * 5 + [shape(msg_rows, width)] * 2,
        [ext, ext],
    )(proj, halo, seg_ext_a, seg_last, state_b, conv_x, conv_bc, bias, rate)
    messages = lax.all_gather(message, "seq")
    out_a, gate_a = call(functools.partial(first_inner, heads, width, rows), [plane, plane])(
        cx_a, bc_a, cum_a, scaled_a, proj, seg_ext_a, seg_row_a, skip
    )
    gated = call(functools.partial(finish, rows), shape(tok_rows, width, kind=BF16))(
        seg_first, messages, out_a, gate_a, bc_a, enter_a, state_a, out_b, gate_b, bc_b, enter_b
    )

    tok_own = tok_rows // n_tensor
    mine = lax.all_to_all(gated.reshape(n_tensor, tok_own, width), "tensor", 0, 0)

    w_forth, w_back = (tops[0], bottoms[0]), (tops[1], bottoms[1])
    w_steps = [(w_forth, w_back)]
    orders = [tokens_there, messages, mine]
    for step in range(2, last + 1):
        if step - 2 < len(orders):
            w_forth, w_back = after((w_forth, w_back), orders[step - 2])
        if step < last:
            w_forth = tuple(ring_shift(part, 1) for part in w_forth)
            w_back = tuple(ring_shift(part, -1) for part in w_back)
            w_steps.append((w_forth, w_back))
        else:
            w_far_parts = ring_shift(w_forth[0], 1), ring_shift(w_back[1], -1)
    swap = [(i, i ^ 1) for i in range(n_seq)]
    other = lax.ppermute(mine, "seq", swap)
    pieces, where = [own], [(0, 0, 0)]
    for i, pair in enumerate(w_steps):
        for side, parts in enumerate(pair):
            distance = i + 1 if side else -i - 1
            pieces += parts
            where += [(2 * i + 1 + side, distance, 0), (2 * i + 1 + side, distance, w_half)]
    total = call(
        functools.partial(product_early, where),
        shape(2 * tok_own, columns),
        [pltpu.VMEM((n_tensor - 1, width, columns), BF16), pltpu.SemaphoreType.DMA((len(where),))],
        in_specs=[VMEM, VMEM] + [ANY] * len(pieces),
        flops=10**9,
    )(mine, other, *pieces)
    where = [(0, last, 0), (0, last, w_half)]
    half = shape(tok_own, columns, kind=BF16)
    out_own, out_other = call(
        functools.partial(product_last, where),
        [half, half],
        [pltpu.VMEM((1, width, columns), BF16), pltpu.SemaphoreType.DMA((2,))],
        in_specs=[VMEM, VMEM, VMEM] + [ANY] * 2,
        flops=10**8,
    )(mine, other, total, *w_far_parts)
    arrived = lax.ppermute(out_other, "seq", swap)
    is_first = core == 0
    return jnp.concatenate([jnp.where(is_first, out_own, arrived), jnp.where(is_first, arrived, out_own)], 1)


def solution(mesh):
    in_specs = (
        P("seq", "tensor"),
        P(None, None, "tensor"),
        P(),
        P(None, "tensor"),
        P("tensor"),
        P("tensor"),
        P("tensor"),
        P(None, "tensor"),
        P(),
        P("tensor"),
        P("tensor", None),
        P("seq"),
    )
    out_specs = P(("seq", "tensor"), None)
    return jax.shard_map(local, mesh=mesh, in_specs=in_specs, out_specs=out_specs, check_vma=False)
```

```python
import functools

import jax
import jax.numpy as jnp
import numpy as np
from jax import lax
from jax.experimental import pallas as pl
from jax.experimental.pallas import tpu as pltpu
from jax.sharding import PartitionSpec as P

NORM_EPS = 1e-05
F32 = jnp.float32
BF16 = jnp.bfloat16
VMEM = pl.BlockSpec(memory_space=pltpu.VMEM)
ANY = pl.BlockSpec(memory_space=pl.ANY)
HALO = 8
W_FIRST = 3


def ring_place(index, n):
    return jnp.where(index % 2 == 0, index // 2, (2 * n - 1 - index) // 2)


def ring_index(place, n):
    return jnp.where(place < n // 2, 2 * place, 2 * n - 1 - 2 * place)


def ring_shift(block, step):
    n = lax.axis_size("tensor")
    order = [2 * i if i < n // 2 else 2 * n - 1 - 2 * i for i in range(n)]
    return lax.ppermute(block, "tensor", [(order[i], order[(i + step) % n]) for i in range(n)])


def after(values, *earlier):
    return lax.optimization_barrier((values, earlier))[0]


def halves(forth, back, top, bottom):
    size = top.shape[0]
    top[...] = forth[:size]
    bottom[...] = back[size:]


def silu(v):
    return v / (1.0 + jnp.exp(-v))


def dot(a, b, dims=((1,), (0,))):
    return lax.dot_general(a.astype(BF16), b.astype(BF16), (dims, ((), ())), preferred_element_type=F32)


def source_of(distance):
    n = lax.axis_size("tensor")
    return ring_index((ring_place(lax.axis_index("tensor"), n) + distance + n) % n, n)


def project(distances, first, *refs):
    count = len(distances)
    blocks, (w_zx, w_bc, w_dt), refs = refs[:count], refs[count : count + 3], refs[count + 3 :]
    total, (out, held, sems) = (None, refs) if first else (refs[0], refs[1:])
    feat = w_bc.shape[0] // lax.axis_size("tensor")
    width = w_bc.shape[1]
    sources = [w_zx.at[0], w_zx.at[1], w_bc, w_dt]
    copies = []
    for k, (distance, size, skip) in enumerate(distances):
        rows = pl.ds(pl.multiple_of(source_of(distance) * feat + skip, 16), size)
        for j, source in enumerate(sources):
            copies.append(
                pltpu.make_async_copy(
                    source.at[rows], held.at[k, pl.ds(0, size), pl.ds(j * width, width)], sems.at[k, j]
                )
            )
            copies[-1].start()
    result = 0.0 if first else total[...]
    for k, (_, size, _) in enumerate(distances):
        for j in range(len(sources)):
            copies[k * len(sources) + j].wait()
        result = result + dot(blocks[k][...], held[k, :size], ((0,), (0,)))
    out[...] = result


def conv(ext, seg_ext, taps, rows):
    size = taps.shape[0]
    seg_now = seg_ext[HALO : HALO + rows]
    total = taps[size - 1 : size] * ext[HALO : HALO + rows]
    for offset in range(1, size):
        same = seg_ext[HALO - offset : HALO - offset + rows] == seg_now
        total = total + taps[size - 1 - offset : size - offset] * jnp.where(
            same, ext[HALO - offset : HALO - offset + rows], 0.0
        )
    return silu(total)


def prefix_sum(values):
    rows = values.shape[0]
    lower = lax.broadcasted_iota(jnp.int32, (rows, rows), 0) >= lax.broadcasted_iota(jnp.int32, (rows, rows), 1)
    lower = jnp.where(lower, 1.0, 0.0).astype(BF16)
    total = jnp.zeros(values.shape, F32)
    rest = values
    parts = []
    for _ in range(3):
        part = rest.astype(BF16)
        parts.append(part)
        rest = rest - part.astype(F32)
    for part in reversed(parts):
        total = total + jnp.dot(lower, part, preferred_element_type=F32)
    return total


def block_front(ext_x, ext_bc, seg_ext, dt_raw, taps_x, taps_bc, bias, rate, rows, seg_enter, seg_leave):
    conv_x = conv(ext_x, seg_ext, taps_x, rows)
    conv_bc = conv(ext_bc, seg_ext, taps_bc, rows)
    seg = seg_ext[HALO : HALO + rows]
    shifted = dt_raw + bias
    step_size = jnp.maximum(shifted, 0.0) + jnp.log1p(jnp.exp(-jnp.abs(shifted)))
    cum = prefix_sum(-rate * step_size)
    scaled = conv_x * step_size
    last = cum[rows - 1 : rows]
    tail = jnp.where(seg == seg_leave, jnp.exp(last - cum), 0.0)
    state_w = conv_bc.shape[1] // 2
    state = dot(conv_bc, tail * scaled, ((0,), (0,)))[:state_w]
    enter = jnp.where(seg == seg_enter, jnp.exp(cum), 0.0)
    return conv_x, conv_bc, cum, scaled, state, enter, last


def block_inner(conv_bc, cum, scaled, seg_col, seg_row, heads):
    rows, width = scaled.shape
    state_w = conv_bc.shape[1] // 2
    head_w = width // heads
    scores = dot(conv_bc[:, state_w:], conv_bc[:, :state_w], ((1,), (1,)))
    later = lax.broadcasted_iota(jnp.int32, (rows, rows), 0) >= lax.broadcasted_iota(jnp.int32, (rows, rows), 1)
    visible = (seg_col == seg_row) & later
    cum_rows = cum.T
    lane = lax.broadcasted_iota(jnp.int32, (rows, width), 1)
    result = jnp.zeros((rows, width), F32)
    scaled = scaled.astype(BF16)
    for head in range(heads):
        at = head * head_w
        gap = jnp.where(visible, cum[:, at : at + 1] - cum_rows[at : at + 1, :], -jnp.inf)
        part = dot(jnp.exp(gap) * scores, scaled)
        result = jnp.where((lane >= at) & (lane < at + head_w), part, result)
    return result


def later_block(heads, width, rows, proj, seg_ext, seg_row, taps_x, taps_bc, bias, rate, skip,
                out, bc_out, enter_out, state_out, gate_out, ext_x, ext_bc):
    rounded = proj[rows - HALO :, : 3 * width].astype(BF16).astype(F32)
    gate_out[...] = silu(rounded[HALO:, :width])
    ext_x[...] = rounded[:, width : 2 * width]
    ext_bc[...] = rounded[:, 2 * width : 3 * width]
    seg_enter = seg_ext[HALO - 1 : HALO]
    seg_leave = seg_ext[HALO + rows - 1 : HALO + rows]
    conv_x, conv_bc, cum, scaled, state, enter, last = block_front(
        ext_x, ext_bc, seg_ext, proj[rows:, 3 * width :], taps_x, taps_bc[...], bias[...], rate[...], rows, seg_enter, seg_leave
    )
    out[...] = block_inner(conv_bc, cum, scaled, seg_ext[HALO:], seg_row[...], heads) + skip[...] * conv_x
    bc_out[...] = conv_bc
    enter_out[...] = enter
    keep = jnp.where(seg_enter == seg_leave, jnp.exp(last), 0.0)
    state_w = state.shape[0]
    state_out[:state_w] = state
    state_out[state_w : state_w + 1] = keep
    state_out[state_w + 1 : state_w + 2] = last
    state_out[state_w + 2 :] = jnp.zeros((state_out.shape[0] - state_w - 2, width), F32)


def first_front(width, rows, proj, halo, seg_ext, seg_last, state_b, taps_x, taps_bc, bias, rate,
                conv_out, bc_out, cum_out, scaled_out, enter_out, state_out, message, ext_x, ext_bc):
    ext_x[:HALO] = halo[:, :width].astype(F32)
    ext_bc[:HALO] = halo[:, width:].astype(F32)
    ext_x[HALO:] = proj[:rows, width : 2 * width].astype(BF16).astype(F32)
    ext_bc[HALO:] = proj[:rows, 2 * width : 3 * width].astype(BF16).astype(F32)
    seg_enter = seg_ext[HALO : HALO + 1]
    seg_leave = seg_ext[HALO + rows - 1 : HALO + rows]
    conv_x, conv_bc, cum, scaled, state, enter, last = block_front(
        ext_x, ext_bc, seg_ext, proj[:rows, 3 * width :], taps_x, taps_bc[...], bias[...], rate[...], rows, seg_enter, seg_leave
    )
    conv_out[...] = conv_x
    bc_out[...] = conv_bc
    cum_out[...] = cum
    scaled_out[...] = scaled
    enter_out[...] = enter
    keep = jnp.where(seg_enter == seg_leave, jnp.exp(last), 0.0)
    state_w = state.shape[0]
    state_out[:state_w] = state
    state_out[state_w : state_w + 1] = keep
    state_out[state_w + 1 :] = jnp.zeros((state_out.shape[0] - state_w - 1, width), F32)
    message[:state_w] = state_b[state_w : state_w + 1] * state + state_b[:state_w]
    message[state_w : state_w + 1] = last + state_b[state_w + 1 : state_w + 2]
    message[state_w + 1 : state_w + 2] = jnp.broadcast_to(seg_last[...].astype(F32), (1, width))
    message[state_w + 2 :] = jnp.zeros((message.shape[0] - state_w - 2, width), F32)


def first_inner(heads, width, rows, conv_x, conv_bc, cum, scaled, proj, seg_col, seg_row, skip, out, gate_out):
    gate_out[...] = silu(proj[:rows, :width].astype(BF16).astype(F32))
    out[...] = (
        block_inner(conv_bc[...], cum[...], scaled[...], seg_col[HALO:], seg_row[...], heads) + skip[...] * conv_x[...]
    )


def finish(rows, seg_first, messages, out_a, gate_a, bc_a, enter_a, state_a, out_b, gate_b, bc_b, enter_b, gated):
    state_w = bc_a.shape[1] // 2
    entering = jnp.zeros((state_w, out_a.shape[1]), F32)
    decay = jnp.zeros((1, out_a.shape[1]), F32)
    first = seg_first[...].astype(F32)
    place = lax.axis_index("seq")
    for device in reversed(range(messages.shape[0] - 1)):
        earlier = device < place
        passes = earlier & (messages[device, state_w + 1 : state_w + 2] == first)
        passes = jnp.where(passes, jnp.exp(decay), 0.0)
        entering = entering + passes * messages[device, :state_w]
        decay = decay + jnp.where(earlier, messages[device, state_w : state_w + 1], 0.0)
    second = state_a[state_w : state_w + 1] * entering + state_a[:state_w]
    gated[:rows] = ((out_a[...] + enter_a[...] * dot(bc_a[:, state_w:], entering)) * gate_a[...]).astype(BF16)
    gated[rows:] = ((out_b[...] + enter_b[...] * dot(bc_b[:, state_w:], second)) * gate_b[...]).astype(BF16)


def product(gated, distances, pieces):
    total = 0.0
    for distance, piece in zip(distances, pieces):
        source = source_of(distance)
        rows = jnp.concatenate([part[source] for part in gated], 0)
        total = total + jnp.dot(rows, piece[...], preferred_element_type=F32)
    return total


def product_early(distances, mine, other, *rest):
    rest[-1][...] = product((mine, other), distances, rest[:-1])


def product_last(distance, mine, other, total, top, bottom, mine_out, other_out, held):
    held[: top.shape[0]] = top[...]
    held[top.shape[0] :] = bottom[...]
    result = product((mine, other), [distance], [held]) + total[...]
    blocks, rows, width = mine.shape
    for i, (gated, out) in enumerate(((mine, mine_out), (other, other_out))):
        squares = jnp.zeros((rows, width), F32)
        for block in range(blocks):
            value = gated[block].astype(F32)
            squares = squares + value * value
        scale = lax.rsqrt(jnp.sum(squares, axis=1, keepdims=True) / (blocks * width) + NORM_EPS)
        out[...] = (result[i * rows : (i + 1) * rows] * scale).astype(BF16)


def call(body, outs, scratch=(), vmem=48, flops=10**7, **kw):
    return pl.pallas_call(
        body,
        out_shape=outs,
        scratch_shapes=list(scratch),
        compiler_params=pltpu.CompilerParams(vmem_limit_bytes=vmem << 20),
        cost_estimate=pl.CostEstimate(flops=flops, bytes_accessed=1 << 21, transcendentals=1 << 17),
        **kw,
    )


def local(
    tokens, w_zx, w_bc, w_dt, dt_bias, a_rate, d_skip, conv_x, conv_bc, norm_gain, w_out, segments
):
    tok_rows, feat = tokens.shape
    width = w_zx.shape[2]
    heads = dt_bias.shape[0]
    head_w = width // heads
    state_w = w_bc.shape[1] // 2
    model = w_zx.shape[1]
    n_seq, n_tensor = lax.axis_size("seq"), lax.axis_size("tensor")
    seq_at = lax.axis_index("seq")
    rows = tok_rows // 2
    shape = lambda *s, kind=F32: jax.ShapeDtypeStruct(s, kind)

    spread = lambda v: jnp.repeat(v, head_w, axis=-1)
    expand = np.repeat(np.eye(heads, dtype=np.float32), head_w, axis=1)
    w_step = jnp.dot(w_dt, expand.astype(BF16))
    block = tokens.T
    core = seq_at % 2
    columns = model // 2
    own = (lax.dynamic_slice_in_dim(w_out, core * columns, columns, 1).astype(F32) * norm_gain[:, None]).astype(BF16)
    last = n_tensor // 2
    w_half = width // 2
    w_forth = w_back = own

    cut = feat // 32 * 16
    forth = back = block
    arrived, projs = [(0, block, 0)], []
    for step in range(1, last + 2):
        if step <= last:
            if step > 1:
                forth, back = after(forth, projs[step - 2]), after(back, projs[step - 2])
            if step == last:
                forth, back = call(
                    halves, [shape(cut, tok_rows, kind=BF16), shape(feat - cut, tok_rows, kind=BF16)]
                )(forth, back)
            if step == W_FIRST:
                w_forth, w_back = after((w_forth, w_back), forth, back)
            forth, back = ring_shift(forth, 1), ring_shift(back, -1)
            if step == W_FIRST:
                w_forth, w_back = ring_shift(w_forth, 1), ring_shift(w_back, -1)
        sizes = [(distance, part.shape[0], skip) for distance, part, skip in arrived]
        total = projs[-1:]
        projs.append(
            call(
                functools.partial(project, sizes, not total),
                shape(tok_rows, 4 * width),
                [
                    pltpu.VMEM((len(sizes), max(size for _, size, _ in sizes), 4 * width), BF16),
                    pltpu.SemaphoreType.DMA((len(sizes), 4)),
                ],
                in_specs=[VMEM] * len(sizes) + [ANY] * 3 + [VMEM] * len(total),
                flops=10**9,
            )(*[part for _, part, _ in arrived], w_zx, w_bc, w_step, *total)
        )
        arrived = [(-step, forth, 0), (step, back, 0)]
        if step == last:
            arrived = [(last, forth, 0), (last, back, cut)]
    proj = projs[-1]

    ahead = [(i, i + 1) for i in range(n_seq - 1)]
    seg_halo = lax.ppermute(segments[tok_rows - HALO :], "seq", ahead)
    seg_all = jnp.concatenate([seg_halo, segments])[:, None]
    seg_ext_a, seg_ext_b = seg_all[: HALO + rows], seg_all[rows:]
    seg_row_a, seg_row_b = segments[None, :rows], segments[None, rows:]
    seg_first, seg_last = segments[None, :1], segments[None, tok_rows - 1 :]
    halo = lax.ppermute(proj[tok_rows - HALO :, width : 3 * width].astype(BF16), "seq", ahead)
    bias, rate, skip = spread(dt_bias)[None], spread(a_rate)[None], spread(d_skip)[None]

    msg_rows = state_w + 8
    plane = shape(rows, width)
    ext = pltpu.VMEM((HALO + rows, width), F32)
    out_b, bc_b, enter_b, state_b, gate_b = call(
        functools.partial(later_block, heads, width, rows),
        [plane, plane, plane, shape(msg_rows, width), plane],
        [ext, ext],
    )(proj, seg_ext_b, seg_row_b, conv_x, conv_bc, bias, rate, skip)
    cx_a, bc_a, cum_a, scaled_a, enter_a, state_a, message = call(
        functools.partial(first_front, width, rows),
        [plane] * 5 + [shape(msg_rows, width)] * 2,
        [ext, ext],
    )(proj, halo, seg_ext_a, seg_last, state_b, conv_x, conv_bc, bias, rate)
    messages = lax.all_gather(message, "seq")
    out_a, gate_a = call(functools.partial(first_inner, heads, width, rows), [plane, plane])(
        cx_a, bc_a, cum_a, scaled_a, proj, seg_ext_a, seg_row_a, skip
    )
    gated = call(functools.partial(finish, rows), shape(tok_rows, width, kind=BF16))(
        seg_first, messages, out_a, gate_a, bc_a, enter_a, state_a, out_b, gate_b, bc_b, enter_b
    )

    tok_own = tok_rows // n_tensor

    w_steps = [(w_forth, w_back)]
    orders = [proj, messages]
    for step in range(2, last + 1):
        if step - 2 < len(orders):
            w_forth, w_back = after((w_forth, w_back), orders[step - 2])
        if step == 4:
            w_forth, w_back = after((w_forth, w_back), mine)
        if step == last:
            half = shape(w_half, columns, kind=BF16)
            w_forth, w_back = call(halves, [half, half])(w_forth, w_back)
        w_forth, w_back = ring_shift(w_forth, 1), ring_shift(w_back, -1)
        w_steps.append((w_forth, w_back))
        if step == 2:
            blocks = after(gated, w_forth, w_back).reshape(n_tensor, tok_own, width)
            mine = lax.all_to_all(blocks, "tensor", 0, 0)
    swap = [(i, i ^ 1) for i in range(n_seq)]
    other = lax.ppermute(mine, "seq", swap)
    pieces, distances = [own], [0]
    for i, pair in enumerate(w_steps[:-1]):
        pieces += pair
        distances += [-i - 1, i + 1]
    total = call(functools.partial(product_early, distances), shape(2 * tok_own, columns), flops=10**9)(
        mine, other, *pieces
    )
    half = shape(tok_own, columns, kind=BF16)
    out_own, out_other = call(
        functools.partial(product_last, last), [half, half], [pltpu.VMEM((width, columns), BF16)], flops=10**8
    )(mine, other, total, *w_steps[-1])
    arrived = lax.ppermute(out_other, "seq", swap)
    is_first = core == 0
    return jnp.concatenate([jnp.where(is_first, out_own, arrived), jnp.where(is_first, arrived, out_own)], 1)


def solution(mesh):
    in_specs = (
        P("seq", "tensor"),
        P(None, None, "tensor"),
        P(),
        P(None, "tensor"),
        P("tensor"),
        P("tensor"),
        P("tensor"),
        P(None, "tensor"),
        P(),
        P("tensor"),
        P("tensor", None),
        P("seq"),
    )
    out_specs = P(("seq", "tensor"), None)
    return jax.shard_map(local, mesh=mesh, in_specs=in_specs, out_specs=out_specs, check_vma=False)
```

```python
import functools

import jax
import jax.numpy as jnp
import numpy as np
from jax import lax
from jax.experimental import pallas as pl
from jax.experimental.pallas import tpu as pltpu
from jax.sharding import PartitionSpec as P

NORM_EPS = 1e-05
F32 = jnp.float32
BF16 = jnp.bfloat16
VMEM = pl.BlockSpec(memory_space=pltpu.VMEM)
ANY = pl.BlockSpec(memory_space=pl.ANY)
HALO = 8


def ring_place(index, n):
    return jnp.where(index % 2 == 0, index // 2, (2 * n - 1 - index) // 2)


def ring_index(place, n):
    return jnp.where(place < n // 2, 2 * place, 2 * n - 1 - 2 * place)


def ring_shift(block, step):
    n = lax.axis_size("tensor")
    order = [2 * i if i < n // 2 else 2 * n - 1 - 2 * i for i in range(n)]
    return lax.ppermute(block, "tensor", [(order[i], order[(i + step) % n]) for i in range(n)])


def after(values, *earlier):
    return lax.optimization_barrier((values, earlier))[0]


def far_shift(forth, back):
    n_seq, n = lax.axis_size("seq"), lax.axis_size("tensor")
    order = [2 * i if i < n // 2 else 2 * n - 1 - 2 * i for i in range(n)]
    moves = []
    for place in range(n_seq):
        step = 1 - 2 * (place % 2)
        moves += [(place * n + order[i], place * n + order[(i + step) % n]) for i in range(n)]
    chosen = call(choose, jax.ShapeDtypeStruct(forth.shape, forth.dtype))(forth, back)
    return lax.ppermute(chosen, ("seq", "tensor"), moves)


def choose(forth, back, out):
    first = lax.axis_index("seq") % 2 == 0

    @pl.when(first)
    def _():
        out[...] = forth[...]

    @pl.when(jnp.logical_not(first))
    def _():
        out[...] = back[...]


def join(*refs):
    count = len(refs) // 3
    odd = lax.axis_index("seq") // 2 % 2
    for own, other, out in zip(refs[:count], refs[count : 2 * count], refs[2 * count :]):
        size = own.shape[0]
        out[pl.ds(pl.multiple_of(odd * size, size), size)] = own[...]
        out[pl.ds(pl.multiple_of((1 - odd) * size, size), size)] = other[...]


def silu(v):
    return v / (1.0 + jnp.exp(-v))


def dot(a, b, dims=((1,), (0,))):
    return lax.dot_general(a.astype(BF16), b.astype(BF16), (dims, ((), ())), preferred_element_type=F32)


def source_of(distance):
    n = lax.axis_size("tensor")
    return ring_index((ring_place(lax.axis_index("tensor"), n) + distance + n) % n, n)


def project(distances, ahead, first, *refs):
    count, fetched = len(distances), len(distances) + bool(ahead)
    blocks, (w_zx, w_bc, w_dt), refs = refs[:count], refs[count : count + 3], refs[count + 3 :]
    total, refs = (None, refs) if first else (refs[0], refs[1:])
    out, far_out, held, sems = refs if ahead else (refs[0], None, *refs[1:])
    feat, width = held.shape[1], w_bc.shape[1]
    sources = [w_zx.at[0], w_zx.at[1], w_bc, w_dt]
    copies = []
    for k, distance in enumerate([*distances, ahead][:fetched]):
        rows = pl.ds(pl.multiple_of(source_of(distance) * feat, 16), feat)
        for j, source in enumerate(sources):
            target = held.at[k] if k < count else far_out
            copies.append(
                pltpu.make_async_copy(source.at[rows], target.at[:, pl.ds(j * width, width)], sems.at[k, j])
            )
            copies[-1].start()
    result = 0.0 if first else total[...]
    for k in range(count):
        for j in range(len(sources)):
            copies[k * len(sources) + j].wait()
        result = result + dot(blocks[k][...], held[k], ((0,), (0,)))
    out[...] = result
    for copy in copies[count * len(sources) :]:
        copy.wait()


def project_far(block, weights, total, out):
    out[...] = total[...] + dot(block[...], weights[...], ((0,), (0,)))


def conv(ext, seg_ext, taps, rows):
    size = taps.shape[0]
    seg_now = seg_ext[HALO : HALO + rows]
    total = taps[size - 1 : size] * ext[HALO : HALO + rows]
    for offset in range(1, size):
        same = seg_ext[HALO - offset : HALO - offset + rows] == seg_now
        total = total + taps[size - 1 - offset : size - offset] * jnp.where(
            same, ext[HALO - offset : HALO - offset + rows], 0.0
        )
    return silu(total)


def prefix_sum(values):
    rows = values.shape[0]
    lower = lax.broadcasted_iota(jnp.int32, (rows, rows), 0) >= lax.broadcasted_iota(jnp.int32, (rows, rows), 1)
    lower = jnp.where(lower, 1.0, 0.0).astype(BF16)
    total = jnp.zeros(values.shape, F32)
    rest = values
    parts = []
    for _ in range(3):
        part = rest.astype(BF16)
        parts.append(part)
        rest = rest - part.astype(F32)
    for part in reversed(parts):
        total = total + jnp.dot(lower, part, preferred_element_type=F32)
    return total


def block_front(ext_x, ext_bc, seg_ext, dt_raw, taps_x, taps_bc, bias, rate, rows, seg_enter, seg_leave):
    conv_x = conv(ext_x, seg_ext, taps_x, rows)
    conv_bc = conv(ext_bc, seg_ext, taps_bc, rows)
    seg = seg_ext[HALO : HALO + rows]
    shifted = dt_raw + bias
    step_size = jnp.maximum(shifted, 0.0) + jnp.log1p(jnp.exp(-jnp.abs(shifted)))
    cum = prefix_sum(-rate * step_size)
    scaled = conv_x * step_size
    last = cum[rows - 1 : rows]
    tail = jnp.where(seg == seg_leave, jnp.exp(last - cum), 0.0)
    state_w = conv_bc.shape[1] // 2
    state = dot(conv_bc, tail * scaled, ((0,), (0,)))[:state_w]
    enter = jnp.where(seg == seg_enter, jnp.exp(cum), 0.0)
    return conv_x, conv_bc, cum, scaled, state, enter, last


def block_inner(conv_bc, cum, scaled, seg_col, seg_row, heads):
    rows, width = scaled.shape
    state_w = conv_bc.shape[1] // 2
    head_w = width // heads
    scores = dot(conv_bc[:, state_w:], conv_bc[:, :state_w], ((1,), (1,)))
    later = lax.broadcasted_iota(jnp.int32, (rows, rows), 0) >= lax.broadcasted_iota(jnp.int32, (rows, rows), 1)
    visible = (seg_col == seg_row) & later
    cum_rows = cum.T
    lane = lax.broadcasted_iota(jnp.int32, (rows, width), 1)
    result = jnp.zeros((rows, width), F32)
    scaled = scaled.astype(BF16)
    for head in range(heads):
        at = head * head_w
        gap = jnp.where(visible, cum[:, at : at + 1] - cum_rows[at : at + 1, :], -jnp.inf)
        part = dot(jnp.exp(gap) * scores, scaled)
        result = jnp.where((lane >= at) & (lane < at + head_w), part, result)
    return result


def later_block(heads, width, rows, proj, seg_ext, seg_row, taps_x, taps_bc, bias, rate, skip,
                out, bc_out, enter_out, state_out, gate_out, ext_x, ext_bc):
    rounded = proj[rows - HALO :, : 3 * width].astype(BF16).astype(F32)
    gate_out[...] = silu(rounded[HALO:, :width])
    ext_x[...] = rounded[:, width : 2 * width]
    ext_bc[...] = rounded[:, 2 * width : 3 * width]
    seg_enter = seg_ext[HALO - 1 : HALO]
    seg_leave = seg_ext[HALO + rows - 1 : HALO + rows]
    conv_x, conv_bc, cum, scaled, state, enter, last = block_front(
        ext_x, ext_bc, seg_ext, proj[rows:, 3 * width :], taps_x, taps_bc[...], bias[...], rate[...], rows, seg_enter, seg_leave
    )
    out[...] = block_inner(conv_bc, cum, scaled, seg_ext[HALO:], seg_row[...], heads) + skip[...] * conv_x
    bc_out[...] = conv_bc
    enter_out[...] = enter
    keep = jnp.where(seg_enter == seg_leave, jnp.exp(last), 0.0)
    state_w = state.shape[0]
    state_out[:state_w] = state
    state_out[state_w : state_w + 1] = keep
    state_out[state_w + 1 : state_w + 2] = last
    state_out[state_w + 2 :] = jnp.zeros((state_out.shape[0] - state_w - 2, width), F32)


def first_front(width, rows, proj, halo, seg_ext, seg_last, state_b, taps_x, taps_bc, bias, rate,
                conv_out, bc_out, cum_out, scaled_out, enter_out, state_out, message, ext_x, ext_bc):
    ext_x[:HALO] = halo[:, :width].astype(F32)
    ext_bc[:HALO] = halo[:, width:].astype(F32)
    ext_x[HALO:] = proj[:rows, width : 2 * width].astype(BF16).astype(F32)
    ext_bc[HALO:] = proj[:rows, 2 * width : 3 * width].astype(BF16).astype(F32)
    seg_enter = seg_ext[HALO : HALO + 1]
    seg_leave = seg_ext[HALO + rows - 1 : HALO + rows]
    conv_x, conv_bc, cum, scaled, state, enter, last = block_front(
        ext_x, ext_bc, seg_ext, proj[:rows, 3 * width :], taps_x, taps_bc[...], bias[...], rate[...], rows, seg_enter, seg_leave
    )
    conv_out[...] = conv_x
    bc_out[...] = conv_bc
    cum_out[...] = cum
    scaled_out[...] = scaled
    enter_out[...] = enter
    keep = jnp.where(seg_enter == seg_leave, jnp.exp(last), 0.0)
    state_w = state.shape[0]
    state_out[:state_w] = state
    state_out[state_w : state_w + 1] = keep
    state_out[state_w + 1 :] = jnp.zeros((state_out.shape[0] - state_w - 1, width), F32)
    message[:state_w] = state_b[state_w : state_w + 1] * state + state_b[:state_w]
    message[state_w : state_w + 1] = last + state_b[state_w + 1 : state_w + 2]
    message[state_w + 1 : state_w + 2] = jnp.broadcast_to(seg_last[...].astype(F32), (1, width))
    message[state_w + 2 :] = jnp.zeros((message.shape[0] - state_w - 2, width), F32)


def first_inner(heads, width, rows, conv_x, conv_bc, cum, scaled, proj, seg_col, seg_row, skip, out, gate_out):
    gate_out[...] = silu(proj[:rows, :width].astype(BF16).astype(F32))
    out[...] = (
        block_inner(conv_bc[...], cum[...], scaled[...], seg_col[HALO:], seg_row[...], heads) + skip[...] * conv_x[...]
    )


def finish(rows, seg_first, messages, out_a, gate_a, bc_a, enter_a, state_a, out_b, gate_b, bc_b, enter_b, gated):
    state_w = bc_a.shape[1] // 2
    entering = jnp.zeros((state_w, out_a.shape[1]), F32)
    decay = jnp.zeros((1, out_a.shape[1]), F32)
    first = seg_first[...].astype(F32)
    place = lax.axis_index("seq")
    for device in reversed(range(messages.shape[0] - 1)):
        earlier = device < place
        passes = earlier & (messages[device, state_w + 1 : state_w + 2] == first)
        passes = jnp.where(passes, jnp.exp(decay), 0.0)
        entering = entering + passes * messages[device, :state_w]
        decay = decay + jnp.where(earlier, messages[device, state_w : state_w + 1], 0.0)
    second = state_a[state_w : state_w + 1] * entering + state_a[:state_w]
    gated[:rows] = ((out_a[...] + enter_a[...] * dot(bc_a[:, state_w:], entering)) * gate_a[...]).astype(BF16)
    gated[rows:] = ((out_b[...] + enter_b[...] * dot(bc_b[:, state_w:], second)) * gate_b[...]).astype(BF16)


def product(gated, distances, pieces):
    total = 0.0
    for distance, piece in zip(distances, pieces):
        source = source_of(distance)
        rows = jnp.concatenate([part[source] for part in gated], 0)
        total = total + jnp.dot(rows, piece[...], preferred_element_type=F32)
    return total


def product_early(distances, mine, other, *rest):
    rest[-1][...] = product((mine, other), distances, rest[:-1])


def product_last(distance, mine, other, total, piece, mine_out, other_out):
    result = product((mine, other), [distance], [piece]) + total[...]
    blocks, rows, width = mine.shape
    for i, (gated, out) in enumerate(((mine, mine_out), (other, other_out))):
        squares = jnp.zeros((rows, width), F32)
        for block in range(blocks):
            value = gated[block].astype(F32)
            squares = squares + value * value
        scale = lax.rsqrt(jnp.sum(squares, axis=1, keepdims=True) / (blocks * width) + NORM_EPS)
        out[...] = (result[i * rows : (i + 1) * rows] * scale).astype(BF16)


def call(body, outs, scratch=(), vmem=48, flops=10**7, **kw):
    return pl.pallas_call(
        body,
        out_shape=outs,
        scratch_shapes=list(scratch),
        compiler_params=pltpu.CompilerParams(vmem_limit_bytes=vmem << 20),
        cost_estimate=pl.CostEstimate(flops=flops, bytes_accessed=1 << 21, transcendentals=1 << 17),
        **kw,
    )


def local(
    tokens, w_zx, w_bc, w_dt, dt_bias, a_rate, d_skip, conv_x, conv_bc, norm_gain, w_out, segments
):
    tok_rows, feat = tokens.shape
    width = w_zx.shape[2]
    heads = dt_bias.shape[0]
    head_w = width // heads
    state_w = w_bc.shape[1] // 2
    model = w_zx.shape[1]
    n_seq, n_tensor = lax.axis_size("seq"), lax.axis_size("tensor")
    seq_at = lax.axis_index("seq")
    rows = tok_rows // 2
    shape = lambda *s, kind=F32: jax.ShapeDtypeStruct(s, kind)

    spread = lambda v: jnp.repeat(v, head_w, axis=-1)
    expand = np.repeat(np.eye(heads, dtype=np.float32), head_w, axis=1)
    w_step = jnp.dot(w_dt, expand.astype(BF16))
    block = tokens.T
    core = seq_at % 2
    columns = model // 2
    own = (lax.dynamic_slice_in_dim(w_out, core * columns, columns, 1).astype(F32) * norm_gain[:, None]).astype(BF16)
    last = n_tensor // 2
    w_half = width // 2
    own_rows = lax.dynamic_slice_in_dim(own, seq_at // 2 % 2 * w_half, w_half, 0)
    other_y = [(i, i ^ 2) for i in range(n_seq)]
    shift_rows = [(i, i + 1) for i in range(n_seq - 1)]

    seg_halo = lax.ppermute(segments[tok_rows - HALO :], "seq", shift_rows)
    seg_all = jnp.concatenate([seg_halo, segments])[:, None]
    small = (
        (seg_all[: HALO + rows], seg_all[rows:]),
        (segments[None, :rows], segments[None, rows:]),
        (segments[None, :1], segments[None, tok_rows - 1 :]),
        (spread(dt_bias)[None], spread(a_rate)[None], spread(d_skip)[None]),
    )

    forth = back = block
    arrived, projs = [(0, block)], []
    for step in range(1, last + 1):
        if step == 3:
            w_arrived, small, forth, back = after((w_arrived, small, forth, back), projs[1])
        elif step > 1:
            forth, back = after(forth, projs[step - 2]), after(back, projs[step - 2])
        if step == 4:
            w_swapped, forth, back = after((w_swapped, forth, back))
        if step == 2:
            w_sent = after(own_rows, forth, back)
        if step < last:
            forth, back = ring_shift(forth, 1), ring_shift(back, -1)
        else:
            far = far_shift(forth, back)
        if step == 2:
            w_arrived = ring_shift(w_sent, 1), ring_shift(w_sent, -1)
        if step == 3:
            w_swapped = [lax.ppermute(part, "seq", other_y) for part in w_arrived]
        ahead = last if step == last else 0
        total = projs[-1:]
        fetched = len(arrived) + bool(ahead)
        outs = [shape(tok_rows, 4 * width)] + [shape(feat, 4 * width, kind=BF16)] * bool(ahead)
        results = call(
            functools.partial(project, [distance for distance, _ in arrived], ahead, not total),
            outs,
            [pltpu.VMEM((len(arrived), feat, 4 * width), BF16), pltpu.SemaphoreType.DMA((fetched, 4))],
            in_specs=[VMEM] * len(arrived) + [ANY] * 3 + [VMEM] * len(total),
            flops=10**9,
        )(*[part for _, part in arrived], w_zx, w_bc, w_step, *total)
        projs.append(results[0])
        arrived = [(-step, forth), (step, back)]
    whole = shape(width, columns, kind=BF16)
    w_forth, w_back = call(join, [whole, whole])(*w_arrived, *w_swapped)
    proj = call(project_far, shape(tok_rows, 4 * width), flops=10**9)(
        far, results[1], after(projs[-1], w_forth, w_back)
    )

    (seg_ext_a, seg_ext_b), (seg_row_a, seg_row_b), (seg_first, seg_last), (bias, rate, skip) = small
    halo = lax.ppermute(proj[tok_rows - HALO :, width : 3 * width].astype(BF16), "seq", shift_rows)

    msg_rows = state_w + 8
    plane = shape(rows, width)
    ext = pltpu.VMEM((HALO + rows, width), F32)
    out_b, bc_b, enter_b, state_b, gate_b = call(
        functools.partial(later_block, heads, width, rows),
        [plane, plane, plane, shape(msg_rows, width), plane],
        [ext, ext],
    )(proj, seg_ext_b, seg_row_b, conv_x, conv_bc, bias, rate, skip)
    cx_a, bc_a, cum_a, scaled_a, enter_a, state_a, message = call(
        functools.partial(first_front, width, rows),
        [plane] * 5 + [shape(msg_rows, width)] * 2,
        [ext, ext],
    )(proj, halo, seg_ext_a, seg_last, state_b, conv_x, conv_bc, bias, rate)
    messages = lax.all_gather(message, "seq")
    out_a, gate_a = call(functools.partial(first_inner, heads, width, rows), [plane, plane])(
        cx_a, bc_a, cum_a, scaled_a, proj, seg_ext_a, seg_row_a, skip
    )
    gated = call(functools.partial(finish, rows), shape(tok_rows, width, kind=BF16))(
        seg_first, messages, out_a, gate_a, bc_a, enter_a, state_a, out_b, gate_b, bc_b, enter_b
    )

    tok_own = tok_rows // n_tensor

    w_steps = [(w_forth, w_back)]
    orders = [proj, messages]
    for step in range(2, last + 1):
        if step - 2 < len(orders):
            w_forth, w_back = after((w_forth, w_back), orders[step - 2])
        if step == 4:
            w_forth, w_back = after((w_forth, w_back), mine)
        if step == last:
            w_far = far_shift(w_forth, w_back)
            break
        w_forth, w_back = ring_shift(w_forth, 1), ring_shift(w_back, -1)
        w_steps.append((w_forth, w_back))
        if step == 2:
            blocks = after(gated, w_forth, w_back).reshape(n_tensor, tok_own, width)
            mine = lax.all_to_all(blocks, "tensor", 0, 0)
    swap = [(i, i ^ 1) for i in range(n_seq)]
    other = lax.ppermute(mine, "seq", swap)
    pieces, distances = [own], [0]
    for i, pair in enumerate(w_steps):
        pieces += pair
        distances += [-i - 1, i + 1]
    total = call(functools.partial(product_early, distances), shape(2 * tok_own, columns), flops=10**9)(
        mine, other, *pieces
    )
    half = shape(tok_own, columns, kind=BF16)
    out_own, out_other = call(
        functools.partial(product_last, last), [half, half], flops=10**8
    )(mine, other, total, w_far)
    arrived = lax.ppermute(out_other, "seq", swap)
    is_first = core == 0
    return jnp.concatenate([jnp.where(is_first, out_own, arrived), jnp.where(is_first, arrived, out_own)], 1)


def solution(mesh):
    in_specs = (
        P("seq", "tensor"),
        P(None, None, "tensor"),
        P(),
        P(None, "tensor"),
        P("tensor"),
        P("tensor"),
        P("tensor"),
        P(None, "tensor"),
        P(),
        P("tensor"),
        P("tensor", None),
        P("seq"),
    )
    out_specs = P(("seq", "tensor"), None)
    return jax.shard_map(local, mesh=mesh, in_specs=in_specs, out_specs=out_specs, check_vma=False)
```

```python
import functools

import jax
import jax.numpy as jnp
import numpy as np
from jax import lax
from jax.experimental import pallas as pl
from jax.experimental.pallas import tpu as pltpu
from jax.sharding import PartitionSpec as P

NORM_EPS = 1e-05
F32 = jnp.float32
BF16 = jnp.bfloat16
VMEM = pl.BlockSpec(memory_space=pltpu.VMEM)
ANY = pl.BlockSpec(memory_space=pl.ANY)
HALO = 8


def ring_place(index, n):
    return jnp.where(index % 2 == 0, index // 2, (2 * n - 1 - index) // 2)


def ring_index(place, n):
    return jnp.where(place < n // 2, 2 * place, 2 * n - 1 - 2 * place)


def ring_shift(block, step):
    n = lax.axis_size("tensor")
    order = [2 * i if i < n // 2 else 2 * n - 1 - 2 * i for i in range(n)]
    return lax.ppermute(block, "tensor", [(order[i], order[(i + step) % n]) for i in range(n)])


def after(values, *earlier):
    return lax.optimization_barrier((values, earlier))[0]


def far_shift(forth, back):
    cut = forth.shape[0] // 32 * 16
    parts = [jax.ShapeDtypeStruct((size, forth.shape[1]), forth.dtype) for size in (cut, forth.shape[0] - cut)]
    top, bottom = call(halves, parts)(forth, back)
    return ring_shift(top, 1), ring_shift(bottom, -1)


def halves(forth, back, top, bottom):
    size = top.shape[0]
    top[...] = forth[:size]
    bottom[...] = back[size:]


def join(*refs):
    count = len(refs) // 3
    odd = lax.axis_index("seq") // 2 % 2
    for own, other, out in zip(refs[:count], refs[count : 2 * count], refs[2 * count :]):
        size = own.shape[0]
        out[pl.ds(pl.multiple_of(odd * size, size), size)] = own[...]
        out[pl.ds(pl.multiple_of((1 - odd) * size, size), size)] = other[...]


def silu(v):
    return v / (1.0 + jnp.exp(-v))


def dot(a, b, dims=((1,), (0,))):
    return lax.dot_general(a.astype(BF16), b.astype(BF16), (dims, ((), ())), preferred_element_type=F32)


def source_of(distance):
    n = lax.axis_size("tensor")
    return ring_index((ring_place(lax.axis_index("tensor"), n) + distance + n) % n, n)


def project(distances, ahead, first, *refs):
    count, fetched = len(distances), len(distances) + bool(ahead)
    blocks, (w_zx, w_bc, w_dt), refs = refs[:count], refs[count : count + 3], refs[count + 3 :]
    total, refs = (None, refs) if first else (refs[0], refs[1:])
    out, far_out, held, sems = refs if ahead else (refs[0], None, *refs[1:])
    feat, width = held.shape[1], w_bc.shape[1]
    sources = [w_zx.at[0], w_zx.at[1], w_bc, w_dt]
    copies = []
    for k, distance in enumerate([*distances, ahead][:fetched]):
        rows = pl.ds(pl.multiple_of(source_of(distance) * feat, 16), feat)
        for j, source in enumerate(sources):
            target = held.at[k] if k < count else far_out
            copies.append(
                pltpu.make_async_copy(source.at[rows], target.at[:, pl.ds(j * width, width)], sems.at[k, j])
            )
            copies[-1].start()
    result = 0.0 if first else total[...]
    for k in range(count):
        for j in range(len(sources)):
            copies[k * len(sources) + j].wait()
        result = result + dot(blocks[k][...], held[k], ((0,), (0,)))
    out[...] = result
    for copy in copies[count * len(sources) :]:
        copy.wait()


def project_far(top, bottom, weights, total, out):
    cut = top.shape[0]
    out[...] = (
        total[...] + dot(top[...], weights[:cut], ((0,), (0,))) + dot(bottom[...], weights[cut:], ((0,), (0,)))
    )


def conv(ext, seg_ext, taps, rows):
    size = taps.shape[0]
    seg_now = seg_ext[HALO : HALO + rows]
    total = taps[size - 1 : size] * ext[HALO : HALO + rows]
    for offset in range(1, size):
        same = seg_ext[HALO - offset : HALO - offset + rows] == seg_now
        total = total + taps[size - 1 - offset : size - offset] * jnp.where(
            same, ext[HALO - offset : HALO - offset + rows], 0.0
        )
    return silu(total)


def prefix_sum(values):
    rows = values.shape[0]
    lower = lax.broadcasted_iota(jnp.int32, (rows, rows), 0) >= lax.broadcasted_iota(jnp.int32, (rows, rows), 1)
    lower = jnp.where(lower, 1.0, 0.0).astype(BF16)
    total = jnp.zeros(values.shape, F32)
    rest = values
    parts = []
    for _ in range(3):
        part = rest.astype(BF16)
        parts.append(part)
        rest = rest - part.astype(F32)
    for part in reversed(parts):
        total = total + jnp.dot(lower, part, preferred_element_type=F32)
    return total


def block_front(ext_x, ext_bc, seg_ext, dt_raw, taps_x, taps_bc, bias, rate, rows, seg_enter, seg_leave):
    conv_x = conv(ext_x, seg_ext, taps_x, rows)
    conv_bc = conv(ext_bc, seg_ext, taps_bc, rows)
    seg = seg_ext[HALO : HALO + rows]
    shifted = dt_raw + bias
    step_size = jnp.maximum(shifted, 0.0) + jnp.log1p(jnp.exp(-jnp.abs(shifted)))
    cum = prefix_sum(-rate * step_size)
    scaled = conv_x * step_size
    last = cum[rows - 1 : rows]
    tail = jnp.where(seg == seg_leave, jnp.exp(last - cum), 0.0)
    state_w = conv_bc.shape[1] // 2
    state = dot(conv_bc, tail * scaled, ((0,), (0,)))[:state_w]
    enter = jnp.where(seg == seg_enter, jnp.exp(cum), 0.0)
    return conv_x, conv_bc, cum, scaled, state, enter, last


def block_inner(conv_bc, cum, scaled, seg_col, seg_row, heads):
    rows, width = scaled.shape
    state_w = conv_bc.shape[1] // 2
    head_w = width // heads
    scores = dot(conv_bc[:, state_w:], conv_bc[:, :state_w], ((1,), (1,)))
    later = lax.broadcasted_iota(jnp.int32, (rows, rows), 0) >= lax.broadcasted_iota(jnp.int32, (rows, rows), 1)
    visible = (seg_col == seg_row) & later
    cum_rows = cum.T
    lane = lax.broadcasted_iota(jnp.int32, (rows, width), 1)
    result = jnp.zeros((rows, width), F32)
    scaled = scaled.astype(BF16)
    for head in range(heads):
        at = head * head_w
        gap = jnp.where(visible, cum[:, at : at + 1] - cum_rows[at : at + 1, :], -jnp.inf)
        part = dot(jnp.exp(gap) * scores, scaled)
        result = jnp.where((lane >= at) & (lane < at + head_w), part, result)
    return result


def later_block(heads, width, rows, proj, seg_ext, seg_row, taps_x, taps_bc, bias, rate, skip,
                out, bc_out, enter_out, state_out, gate_out, ext_x, ext_bc):
    rounded = proj[rows - HALO :, : 3 * width].astype(BF16).astype(F32)
    gate_out[...] = silu(rounded[HALO:, :width])
    ext_x[...] = rounded[:, width : 2 * width]
    ext_bc[...] = rounded[:, 2 * width : 3 * width]
    seg_enter = seg_ext[HALO - 1 : HALO]
    seg_leave = seg_ext[HALO + rows - 1 : HALO + rows]
    conv_x, conv_bc, cum, scaled, state, enter, last = block_front(
        ext_x, ext_bc, seg_ext, proj[rows:, 3 * width :], taps_x, taps_bc[...], bias[...], rate[...], rows, seg_enter, seg_leave
    )
    out[...] = block_inner(conv_bc, cum, scaled, seg_ext[HALO:], seg_row[...], heads) + skip[...] * conv_x
    bc_out[...] = conv_bc
    enter_out[...] = enter
    keep = jnp.where(seg_enter == seg_leave, jnp.exp(last), 0.0)
    state_w = state.shape[0]
    state_out[:state_w] = state
    state_out[state_w : state_w + 1] = keep
    state_out[state_w + 1 : state_w + 2] = last
    state_out[state_w + 2 :] = jnp.zeros((state_out.shape[0] - state_w - 2, width), F32)


def first_front(width, rows, proj, halo, seg_ext, seg_last, state_b, taps_x, taps_bc, bias, rate,
                conv_out, bc_out, cum_out, scaled_out, enter_out, state_out, message, ext_x, ext_bc):
    ext_x[:HALO] = halo[:, :width].astype(F32)
    ext_bc[:HALO] = halo[:, width:].astype(F32)
    ext_x[HALO:] = proj[:rows, width : 2 * width].astype(BF16).astype(F32)
    ext_bc[HALO:] = proj[:rows, 2 * width : 3 * width].astype(BF16).astype(F32)
    seg_enter = seg_ext[HALO : HALO + 1]
    seg_leave = seg_ext[HALO + rows - 1 : HALO + rows]
    conv_x, conv_bc, cum, scaled, state, enter, last = block_front(
        ext_x, ext_bc, seg_ext, proj[:rows, 3 * width :], taps_x, taps_bc[...], bias[...], rate[...], rows, seg_enter, seg_leave
    )
    conv_out[...] = conv_x
    bc_out[...] = conv_bc
    cum_out[...] = cum
    scaled_out[...] = scaled
    enter_out[...] = enter
    keep = jnp.where(seg_enter == seg_leave, jnp.exp(last), 0.0)
    state_w = state.shape[0]
    state_out[:state_w] = state
    state_out[state_w : state_w + 1] = keep
    state_out[state_w + 1 :] = jnp.zeros((state_out.shape[0] - state_w - 1, width), F32)
    message[:state_w] = state_b[state_w : state_w + 1] * state + state_b[:state_w]
    message[state_w : state_w + 1] = last + state_b[state_w + 1 : state_w + 2]
    message[state_w + 1 : state_w + 2] = jnp.broadcast_to(seg_last[...].astype(F32), (1, width))
    message[state_w + 2 :] = jnp.zeros((message.shape[0] - state_w - 2, width), F32)


def first_inner(heads, width, rows, conv_x, conv_bc, cum, scaled, proj, seg_col, seg_row, skip, out, gate_out):
    gate_out[...] = silu(proj[:rows, :width].astype(BF16).astype(F32))
    out[...] = (
        block_inner(conv_bc[...], cum[...], scaled[...], seg_col[HALO:], seg_row[...], heads) + skip[...] * conv_x[...]
    )


def finish(rows, seg_first, messages, out_a, gate_a, bc_a, enter_a, state_a, out_b, gate_b, bc_b, enter_b, gated):
    state_w = bc_a.shape[1] // 2
    entering = jnp.zeros((state_w, out_a.shape[1]), F32)
    decay = jnp.zeros((1, out_a.shape[1]), F32)
    first = seg_first[...].astype(F32)
    place = lax.axis_index("seq")
    for device in reversed(range(messages.shape[0] - 1)):
        earlier = device < place
        passes = earlier & (messages[device, state_w + 1 : state_w + 2] == first)
        passes = jnp.where(passes, jnp.exp(decay), 0.0)
        entering = entering + passes * messages[device, :state_w]
        decay = decay + jnp.where(earlier, messages[device, state_w : state_w + 1], 0.0)
    second = state_a[state_w : state_w + 1] * entering + state_a[:state_w]
    gated[:rows] = ((out_a[...] + enter_a[...] * dot(bc_a[:, state_w:], entering)) * gate_a[...]).astype(BF16)
    gated[rows:] = ((out_b[...] + enter_b[...] * dot(bc_b[:, state_w:], second)) * gate_b[...]).astype(BF16)


def product(gated, distances, pieces):
    total = 0.0
    for distance, piece in zip(distances, pieces):
        source = source_of(distance)
        rows = jnp.concatenate([part[source] for part in gated], 0)
        total = total + jnp.dot(rows, piece[...], preferred_element_type=F32)
    return total


def product_early(distances, mine, other, *rest):
    rest[-1][...] = product((mine, other), distances, rest[:-1])


def product_last(distance, mine, other, total, top, bottom, mine_out, other_out, held):
    held[: top.shape[0]] = top[...]
    held[top.shape[0] :] = bottom[...]
    result = product((mine, other), [distance], [held]) + total[...]
    blocks, rows, width = mine.shape
    for i, (gated, out) in enumerate(((mine, mine_out), (other, other_out))):
        squares = jnp.zeros((rows, width), F32)
        for block in range(blocks):
            value = gated[block].astype(F32)
            squares = squares + value * value
        scale = lax.rsqrt(jnp.sum(squares, axis=1, keepdims=True) / (blocks * width) + NORM_EPS)
        out[...] = (result[i * rows : (i + 1) * rows] * scale).astype(BF16)


def call(body, outs, scratch=(), vmem=48, flops=10**7, **kw):
    return pl.pallas_call(
        body,
        out_shape=outs,
        scratch_shapes=list(scratch),
        compiler_params=pltpu.CompilerParams(vmem_limit_bytes=vmem << 20),
        cost_estimate=pl.CostEstimate(flops=flops, bytes_accessed=1 << 21, transcendentals=1 << 17),
        **kw,
    )


def local(
    tokens, w_zx, w_bc, w_dt, dt_bias, a_rate, d_skip, conv_x, conv_bc, norm_gain, w_out, segments
):
    tok_rows, feat = tokens.shape
    width = w_zx.shape[2]
    heads = dt_bias.shape[0]
    head_w = width // heads
    state_w = w_bc.shape[1] // 2
    model = w_zx.shape[1]
    n_seq, n_tensor = lax.axis_size("seq"), lax.axis_size("tensor")
    seq_at = lax.axis_index("seq")
    rows = tok_rows // 2
    shape = lambda *s, kind=F32: jax.ShapeDtypeStruct(s, kind)

    spread = lambda v: jnp.repeat(v, head_w, axis=-1)
    expand = np.repeat(np.eye(heads, dtype=np.float32), head_w, axis=1)
    w_step = jnp.dot(w_dt, expand.astype(BF16))
    block = tokens.T
    core = seq_at % 2
    columns = model // 2
    own = (lax.dynamic_slice_in_dim(w_out, core * columns, columns, 1).astype(F32) * norm_gain[:, None]).astype(BF16)
    last = n_tensor // 2
    w_half = width // 2
    own_rows = lax.dynamic_slice_in_dim(own, seq_at // 2 % 2 * w_half, w_half, 0)
    other_y = [(i, i ^ 2) for i in range(n_seq)]
    shift_rows = [(i, i + 1) for i in range(n_seq - 1)]

    seg_halo = lax.ppermute(segments[tok_rows - HALO :], "seq", shift_rows)
    seg_all = jnp.concatenate([seg_halo, segments])[:, None]
    small = (
        (seg_all[: HALO + rows], seg_all[rows:]),
        (segments[None, :rows], segments[None, rows:]),
        (segments[None, :1], segments[None, tok_rows - 1 :]),
        (spread(dt_bias)[None], spread(a_rate)[None], spread(d_skip)[None]),
    )

    forth = back = block
    arrived, projs = [(0, block)], []
    for step in range(1, last + 1):
        if step == 3:
            forth, back = after(forth, projs[1], small), after(back, projs[1], small)
            w_arrived = after(w_arrived, forth, back)
        elif step > 1:
            forth, back = after(forth, projs[step - 2]), after(back, projs[step - 2])
        if step == 4:
            w_swapped, forth, back = after((w_swapped, forth, back))
        if step == 2:
            w_sent = after(own_rows, forth, back)
        if step < last:
            forth, back = ring_shift(forth, 1), ring_shift(back, -1)
        else:
            far = far_shift(forth, back)
        if step == 2:
            w_arrived = ring_shift(w_sent, 1), ring_shift(w_sent, -1)
        if step == 3:
            w_swapped = [lax.ppermute(part, "seq", other_y) for part in w_arrived]
        ahead = last if step == last else 0
        total = projs[-1:]
        fetched = len(arrived) + bool(ahead)
        outs = [shape(tok_rows, 4 * width)] + [shape(feat, 4 * width, kind=BF16)] * bool(ahead)
        results = call(
            functools.partial(project, [distance for distance, _ in arrived], ahead, not total),
            outs,
            [pltpu.VMEM((len(arrived), feat, 4 * width), BF16), pltpu.SemaphoreType.DMA((fetched, 4))],
            in_specs=[VMEM] * len(arrived) + [ANY] * 3 + [VMEM] * len(total),
            flops=10**9,
        )(*[part for _, part in arrived], w_zx, w_bc, w_step, *total)
        projs.append(results[0])
        arrived = [(-step, forth), (step, back)]
    whole = shape(width, columns, kind=BF16)
    w_forth, w_back = call(join, [whole, whole])(*w_arrived, *w_swapped)
    proj = call(project_far, shape(tok_rows, 4 * width), flops=10**9)(
        *far, results[1], after(projs[-1], w_forth, w_back)
    )

    (seg_ext_a, seg_ext_b), (seg_row_a, seg_row_b), (seg_first, seg_last), (bias, rate, skip) = small
    halo = lax.ppermute(proj[tok_rows - HALO :, width : 3 * width].astype(BF16), "seq", shift_rows)

    msg_rows = state_w + 8
    plane = shape(rows, width)
    ext = pltpu.VMEM((HALO + rows, width), F32)
    out_b, bc_b, enter_b, state_b, gate_b = call(
        functools.partial(later_block, heads, width, rows),
        [plane, plane, plane, shape(msg_rows, width), plane],
        [ext, ext],
    )(proj, seg_ext_b, seg_row_b, conv_x, conv_bc, bias, rate, skip)
    cx_a, bc_a, cum_a, scaled_a, enter_a, state_a, message = call(
        functools.partial(first_front, width, rows),
        [plane] * 5 + [shape(msg_rows, width)] * 2,
        [ext, ext],
    )(proj, halo, seg_ext_a, seg_last, state_b, conv_x, conv_bc, bias, rate)
    messages = lax.all_gather(message, "seq")
    out_a, gate_a = call(functools.partial(first_inner, heads, width, rows), [plane, plane])(
        cx_a, bc_a, cum_a, scaled_a, proj, seg_ext_a, seg_row_a, skip
    )
    gated = call(functools.partial(finish, rows), shape(tok_rows, width, kind=BF16))(
        seg_first, messages, out_a, gate_a, bc_a, enter_a, state_a, out_b, gate_b, bc_b, enter_b
    )

    tok_own = tok_rows // n_tensor

    w_steps = [(w_forth, w_back)]
    orders = [(proj, halo), messages]
    for step in range(2, last + 1):
        if step - 2 < len(orders):
            w_forth, w_back = after((w_forth, w_back), orders[step - 2])
        if step == 4:
            w_forth, w_back = after((w_forth, w_back), mine)
        if step == last:
            w_far = far_shift(w_forth, w_back)
            break
        w_forth, w_back = ring_shift(w_forth, 1), ring_shift(w_back, -1)
        w_steps.append((w_forth, w_back))
        if step == 2:
            blocks = after(gated, w_forth, w_back).reshape(n_tensor, tok_own, width)
            mine = lax.all_to_all(blocks, "tensor", 0, 0)
    swap = [(i, i ^ 1) for i in range(n_seq)]
    other = lax.ppermute(mine, "seq", swap)
    pieces, distances = [own], [0]
    for i, pair in enumerate(w_steps):
        pieces += pair
        distances += [-i - 1, i + 1]
    total = call(functools.partial(product_early, distances), shape(2 * tok_own, columns), flops=10**9)(
        mine, other, *pieces
    )
    half = shape(tok_own, columns, kind=BF16)
    out_own, out_other = call(
        functools.partial(product_last, last), [half, half], [pltpu.VMEM((width, columns), BF16)], flops=10**8
    )(mine, other, total, *w_far)
    arrived = lax.ppermute(out_other, "seq", swap)
    is_first = core == 0
    return jnp.concatenate([jnp.where(is_first, out_own, arrived), jnp.where(is_first, arrived, out_own)], 1)


def solution(mesh):
    in_specs = (
        P("seq", "tensor"),
        P(None, None, "tensor"),
        P(),
        P(None, "tensor"),
        P("tensor"),
        P("tensor"),
        P("tensor"),
        P(None, "tensor"),
        P(),
        P("tensor"),
        P("tensor", None),
        P("seq"),
    )
    out_specs = P(("seq", "tensor"), None)
    return jax.shard_map(local, mesh=mesh, in_specs=in_specs, out_specs=out_specs, check_vma=False)
```

```python
import functools

import jax
import jax.numpy as jnp
import numpy as np
from jax import lax
from jax.experimental import pallas as pl
from jax.experimental.pallas import tpu as pltpu
from jax.sharding import PartitionSpec as P

NORM_EPS = 1e-05
F32 = jnp.float32
BF16 = jnp.bfloat16
VMEM = pl.BlockSpec(memory_space=pltpu.VMEM)
ANY = pl.BlockSpec(memory_space=pl.ANY)
HALO = 8


def ring_place(index, n):
    return jnp.where(index % 2 == 0, index // 2, (2 * n - 1 - index) // 2)


def ring_index(place, n):
    return jnp.where(place < n // 2, 2 * place, 2 * n - 1 - 2 * place)


def ring_shift(block, step):
    n = lax.axis_size("tensor")
    order = [2 * i if i < n // 2 else 2 * n - 1 - 2 * i for i in range(n)]
    return lax.ppermute(block, "tensor", [(order[i], order[(i + step) % n]) for i in range(n)])


def after(values, *earlier):
    return lax.optimization_barrier((values, earlier))[0]


def far_shift(forth, back):
    cut = forth.shape[0] // 32 * 16
    parts = [jax.ShapeDtypeStruct((size, forth.shape[1]), forth.dtype) for size in (cut, forth.shape[0] - cut)]
    top, bottom = call(halves, parts)(forth, back)
    return ring_shift(top, 1), ring_shift(bottom, -1)


def halves(forth, back, top, bottom):
    size = top.shape[0]
    top[...] = forth[:size]
    bottom[...] = back[size:]


def silu(v):
    return v / (1.0 + jnp.exp(-v))


def dot(a, b, dims=((1,), (0,))):
    return lax.dot_general(a.astype(BF16), b.astype(BF16), (dims, ((), ())), preferred_element_type=F32)


def source_of(distance):
    n = lax.axis_size("tensor")
    return ring_index((ring_place(lax.axis_index("tensor"), n) + distance + n) % n, n)


def project(distances, ahead, first, *refs):
    count, fetched = len(distances), len(distances) + bool(ahead)
    blocks, (w_zx, w_bc, w_dt), refs = refs[:count], refs[count : count + 3], refs[count + 3 :]
    total, refs = (None, refs) if first else (refs[0], refs[1:])
    out, far_out, held, sems = refs if ahead else (refs[0], None, *refs[1:])
    feat, width = held.shape[1], w_bc.shape[1]
    sources = [w_zx.at[0], w_zx.at[1], w_bc, w_dt]
    copies = []
    for k, distance in enumerate([*distances, ahead][:fetched]):
        rows = pl.ds(pl.multiple_of(source_of(distance) * feat, 16), feat)
        for j, source in enumerate(sources):
            target = held.at[k] if k < count else far_out
            copies.append(
                pltpu.make_async_copy(source.at[rows], target.at[:, pl.ds(j * width, width)], sems.at[k, j])
            )
            copies[-1].start()
    result = 0.0 if first else total[...]
    for k in range(count):
        for j in range(len(sources)):
            copies[k * len(sources) + j].wait()
        result = result + dot(blocks[k][...], held[k], ((0,), (0,)))
    out[...] = result
    for copy in copies[count * len(sources) :]:
        copy.wait()


def project_far(top, bottom, weights, total, out):
    cut = top.shape[0]
    out[...] = (
        total[...] + dot(top[...], weights[:cut], ((0,), (0,))) + dot(bottom[...], weights[cut:], ((0,), (0,)))
    )


def conv(ext, seg_ext, taps, rows):
    size = taps.shape[0]
    seg_now = seg_ext[HALO : HALO + rows]
    total = taps[size - 1 : size] * ext[HALO : HALO + rows]
    for offset in range(1, size):
        same = seg_ext[HALO - offset : HALO - offset + rows] == seg_now
        total = total + taps[size - 1 - offset : size - offset] * jnp.where(
            same, ext[HALO - offset : HALO - offset + rows], 0.0
        )
    return silu(total)


def prefix_sum(values):
    rows = values.shape[0]
    lower = lax.broadcasted_iota(jnp.int32, (rows, rows), 0) >= lax.broadcasted_iota(jnp.int32, (rows, rows), 1)
    lower = jnp.where(lower, 1.0, 0.0).astype(BF16)
    total = jnp.zeros(values.shape, F32)
    rest = values
    parts = []
    for _ in range(3):
        part = rest.astype(BF16)
        parts.append(part)
        rest = rest - part.astype(F32)
    for part in reversed(parts):
        total = total + jnp.dot(lower, part, preferred_element_type=F32)
    return total


def block_front(ext_x, ext_bc, seg_ext, dt_raw, taps_x, taps_bc, bias, rate, rows, seg_enter, seg_leave):
    conv_x = conv(ext_x, seg_ext, taps_x, rows)
    conv_bc = conv(ext_bc, seg_ext, taps_bc, rows)
    seg = seg_ext[HALO : HALO + rows]
    shifted = dt_raw + bias
    step_size = jnp.maximum(shifted, 0.0) + jnp.log1p(jnp.exp(-jnp.abs(shifted)))
    cum = prefix_sum(-rate * step_size)
    scaled = conv_x * step_size
    last = cum[rows - 1 : rows]
    tail = jnp.where(seg == seg_leave, jnp.exp(last - cum), 0.0)
    state_w = conv_bc.shape[1] // 2
    state = dot(conv_bc, tail * scaled, ((0,), (0,)))[:state_w]
    enter = jnp.where(seg == seg_enter, jnp.exp(cum), 0.0)
    return conv_x, conv_bc, cum, scaled, state, enter, last


def block_inner(conv_bc, cum, scaled, seg_col, seg_row, heads):
    rows, width = scaled.shape
    state_w = conv_bc.shape[1] // 2
    head_w = width // heads
    scores = dot(conv_bc[:, state_w:], conv_bc[:, :state_w], ((1,), (1,)))
    later = lax.broadcasted_iota(jnp.int32, (rows, rows), 0) >= lax.broadcasted_iota(jnp.int32, (rows, rows), 1)
    visible = (seg_col == seg_row) & later
    cum_rows = cum.T
    lane = lax.broadcasted_iota(jnp.int32, (rows, width), 1)
    result = jnp.zeros((rows, width), F32)
    scaled = scaled.astype(BF16)
    for head in range(heads):
        at = head * head_w
        gap = jnp.where(visible, cum[:, at : at + 1] - cum_rows[at : at + 1, :], -jnp.inf)
        part = dot(jnp.exp(gap) * scores, scaled)
        result = jnp.where((lane >= at) & (lane < at + head_w), part, result)
    return result


def later_block(heads, width, rows, proj, seg_ext, seg_row, taps_x, taps_bc, bias, rate, skip,
                out, bc_out, enter_out, state_out, gate_out, ext_x, ext_bc):
    rounded = proj[rows - HALO :, : 3 * width].astype(BF16).astype(F32)
    gate_out[...] = silu(rounded[HALO:, :width])
    ext_x[...] = rounded[:, width : 2 * width]
    ext_bc[...] = rounded[:, 2 * width : 3 * width]
    seg_enter = seg_ext[HALO - 1 : HALO]
    seg_leave = seg_ext[HALO + rows - 1 : HALO + rows]
    conv_x, conv_bc, cum, scaled, state, enter, last = block_front(
        ext_x, ext_bc, seg_ext, proj[rows:, 3 * width :], taps_x, taps_bc[...], bias[...], rate[...], rows, seg_enter, seg_leave
    )
    out[...] = block_inner(conv_bc, cum, scaled, seg_ext[HALO:], seg_row[...], heads) + skip[...] * conv_x
    bc_out[...] = conv_bc
    enter_out[...] = enter
    keep = jnp.where(seg_enter == seg_leave, jnp.exp(last), 0.0)
    state_w = state.shape[0]
    state_out[:state_w] = state
    state_out[state_w : state_w + 1] = keep
    state_out[state_w + 1 : state_w + 2] = last
    state_out[state_w + 2 :] = jnp.zeros((state_out.shape[0] - state_w - 2, width), F32)


def first_front(width, rows, proj, halo, seg_ext, seg_last, state_b, taps_x, taps_bc, bias, rate,
                conv_out, bc_out, cum_out, scaled_out, enter_out, state_out, message, ext_x, ext_bc):
    ext_x[:HALO] = halo[:, :width].astype(F32)
    ext_bc[:HALO] = halo[:, width:].astype(F32)
    ext_x[HALO:] = proj[:rows, width : 2 * width].astype(BF16).astype(F32)
    ext_bc[HALO:] = proj[:rows, 2 * width : 3 * width].astype(BF16).astype(F32)
    seg_enter = seg_ext[HALO : HALO + 1]
    seg_leave = seg_ext[HALO + rows - 1 : HALO + rows]
    conv_x, conv_bc, cum, scaled, state, enter, last = block_front(
        ext_x, ext_bc, seg_ext, proj[:rows, 3 * width :], taps_x, taps_bc[...], bias[...], rate[...], rows, seg_enter, seg_leave
    )
    conv_out[...] = conv_x
    bc_out[...] = conv_bc
    cum_out[...] = cum
    scaled_out[...] = scaled
    enter_out[...] = enter
    keep = jnp.where(seg_enter == seg_leave, jnp.exp(last), 0.0)
    state_w = state.shape[0]
    state_out[:state_w] = state
    state_out[state_w : state_w + 1] = keep
    state_out[state_w + 1 :] = jnp.zeros((state_out.shape[0] - state_w - 1, width), F32)
    message[:state_w] = state_b[state_w : state_w + 1] * state + state_b[:state_w]
    message[state_w : state_w + 1] = last + state_b[state_w + 1 : state_w + 2]
    message[state_w + 1 : state_w + 2] = jnp.broadcast_to(seg_last[...].astype(F32), (1, width))
    message[state_w + 2 :] = jnp.zeros((message.shape[0] - state_w - 2, width), F32)


def first_inner(heads, width, rows, conv_x, conv_bc, cum, scaled, proj, seg_col, seg_row, skip, out, gate_out):
    gate_out[...] = silu(proj[:rows, :width].astype(BF16).astype(F32))
    out[...] = (
        block_inner(conv_bc[...], cum[...], scaled[...], seg_col[HALO:], seg_row[...], heads) + skip[...] * conv_x[...]
    )


def finish(rows, seg_first, messages, out_a, gate_a, bc_a, enter_a, state_a, out_b, gate_b, bc_b, enter_b, gated):
    state_w = bc_a.shape[1] // 2
    entering = jnp.zeros((state_w, out_a.shape[1]), F32)
    decay = jnp.zeros((1, out_a.shape[1]), F32)
    first = seg_first[...].astype(F32)
    place = lax.axis_index("seq")
    for device in reversed(range(messages.shape[0] - 1)):
        earlier = device < place
        passes = earlier & (messages[device, state_w + 1 : state_w + 2] == first)
        passes = jnp.where(passes, jnp.exp(decay), 0.0)
        entering = entering + passes * messages[device, :state_w]
        decay = decay + jnp.where(earlier, messages[device, state_w : state_w + 1], 0.0)
    second = state_a[state_w : state_w + 1] * entering + state_a[:state_w]
    gated[:rows] = ((out_a[...] + enter_a[...] * dot(bc_a[:, state_w:], entering)) * gate_a[...]).astype(BF16)
    gated[rows:] = ((out_b[...] + enter_b[...] * dot(bc_b[:, state_w:], second)) * gate_b[...]).astype(BF16)


def product(gated, distances, pieces):
    total = 0.0
    odd = lax.axis_index("seq") // 2 % 2 == 1
    for distance, (near, other) in zip(distances, pieces):
        source = source_of(distance)
        rows = jnp.concatenate([part[source] for part in gated], 0)
        half = rows.shape[1] // 2
        swapped = jnp.concatenate([rows[:, half:], rows[:, :half]], 1)
        rows = jnp.where(odd, swapped, rows)
        total = total + jnp.dot(rows, jnp.concatenate([near[...], other[...]], 0), preferred_element_type=F32)
    return total


def product_early(distances, mine, other, *rest):
    pieces, out = rest[:-1], rest[-1]
    out[...] = product((mine, other), distances, list(zip(pieces[::2], pieces[1::2])))


def product_last(distance, mine, other, total, near, far, mine_out, other_out):
    result = product((mine, other), [distance], [(near, far)]) + total[...]
    blocks, rows, width = mine.shape
    for i, (gated, out) in enumerate(((mine, mine_out), (other, other_out))):
        squares = jnp.zeros((rows, width), F32)
        for block in range(blocks):
            value = gated[block].astype(F32)
            squares = squares + value * value
        scale = lax.rsqrt(jnp.sum(squares, axis=1, keepdims=True) / (blocks * width) + NORM_EPS)
        out[...] = (result[i * rows : (i + 1) * rows] * scale).astype(BF16)


def call(body, outs, scratch=(), vmem=48, flops=10**7, **kw):
    return pl.pallas_call(
        body,
        out_shape=outs,
        scratch_shapes=list(scratch),
        compiler_params=pltpu.CompilerParams(vmem_limit_bytes=vmem << 20),
        cost_estimate=pl.CostEstimate(flops=flops, bytes_accessed=1 << 21, transcendentals=1 << 17),
        **kw,
    )


def local(
    tokens, w_zx, w_bc, w_dt, dt_bias, a_rate, d_skip, conv_x, conv_bc, norm_gain, w_out, segments
):
    tok_rows, feat = tokens.shape
    width = w_zx.shape[2]
    heads = dt_bias.shape[0]
    head_w = width // heads
    state_w = w_bc.shape[1] // 2
    model = w_zx.shape[1]
    n_seq, n_tensor = lax.axis_size("seq"), lax.axis_size("tensor")
    seq_at = lax.axis_index("seq")
    rows = tok_rows // 2
    shape = lambda *s, kind=F32: jax.ShapeDtypeStruct(s, kind)

    spread = lambda v: jnp.repeat(v, head_w, axis=-1)
    expand = np.repeat(np.eye(heads, dtype=np.float32), head_w, axis=1)
    w_delta = jnp.dot(w_dt, expand.astype(BF16))
    block = tokens.T
    core = seq_at % 2
    columns = model // 2
    own = (lax.dynamic_slice_in_dim(w_out, core * columns, columns, 1).astype(F32) * norm_gain[:, None]).astype(BF16)
    last = n_tensor // 2
    w_half = width // 2
    odd = seq_at // 2 % 2
    own_halves = [lax.dynamic_slice_in_dim(own, place * w_half, w_half, 0) for place in (odd, 1 - odd)]
    other_y = [(i, i ^ 2) for i in range(n_seq)]
    w_near, w_other = {0: own_halves[0]}, {0: own_halves[1]}

    def w_step(k, *earlier):
        before = after((w_near[1 - k], w_near[k - 1]), *earlier)
        w_near[-k], w_near[k] = ring_shift(before[0], 1), ring_shift(before[1], -1)
        return w_near[-k], w_near[k]

    def w_swap(k, *earlier):
        sides = (-k, k) if k < last else (k,)
        for side in sides:
            w_other[side] = lax.ppermute(after(w_near[side], *earlier), "seq", other_y)
        return tuple(w_other[side] for side in sides)

    shift_rows = [(i, i + 1) for i in range(n_seq - 1)]

    seg_halo = lax.ppermute(segments[tok_rows - HALO :], "seq", shift_rows)
    seg_all = jnp.concatenate([seg_halo, segments])[:, None]
    small = (
        (seg_all[: HALO + rows], seg_all[rows:]),
        (segments[None, :rows], segments[None, rows:]),
        (segments[None, :1], segments[None, tok_rows - 1 :]),
        (spread(dt_bias)[None], spread(a_rate)[None], spread(d_skip)[None]),
    )

    forth = back = block
    arrived, projs = [(0, block)], []
    moved = ()
    for step in range(1, last + 1):
        if step > 1:
            ready = (projs[step - 2], moved, small) if step == 3 else (projs[step - 2], moved)
            forth, back = after(forth, ready), after(back, ready)
        arrivals = (forth, back)
        if step < last:
            forth, back = ring_shift(forth, 1), ring_shift(back, -1)
        else:
            far = far_shift(forth, back)
        moved = ()
        if step > 2:
            moved += w_swap(step - 2, arrivals)
        if 1 < step < last:
            moved += w_step(step - 1, arrivals)
        ahead = last if step == last else 0
        total = projs[-1:]
        fetched = len(arrived) + bool(ahead)
        outs = [shape(tok_rows, 4 * width)] + [shape(feat, 4 * width, kind=BF16)] * bool(ahead)
        results = call(
            functools.partial(project, [distance for distance, _ in arrived], ahead, not total),
            outs,
            [pltpu.VMEM((len(arrived), feat, 4 * width), BF16), pltpu.SemaphoreType.DMA((fetched, 4))],
            in_specs=[VMEM] * len(arrived) + [ANY] * 3 + [VMEM] * len(total),
            flops=10**9,
        )(*[part for _, part in arrived], w_zx, w_bc, w_delta, *total)
        projs.append(results[0])
        arrived = [(-step, forth), (step, back)]
    proj = call(project_far, shape(tok_rows, 4 * width), flops=10**9)(*far, results[1], projs[-1])
    w_late = w_step(last - 1, far)

    (seg_ext_a, seg_ext_b), (seg_row_a, seg_row_b), (seg_first, seg_last), (bias, rate, skip) = small
    halo = lax.ppermute(proj[tok_rows - HALO :, width : 3 * width].astype(BF16), "seq", shift_rows)
    halo = after(halo, moved)

    msg_rows = state_w + 8
    plane = shape(rows, width)
    ext = pltpu.VMEM((HALO + rows, width), F32)
    out_b, bc_b, enter_b, state_b, gate_b = call(
        functools.partial(later_block, heads, width, rows),
        [plane, plane, plane, shape(msg_rows, width), plane],
        [ext, ext],
    )(proj, seg_ext_b, seg_row_b, conv_x, conv_bc, bias, rate, skip)
    cx_a, bc_a, cum_a, scaled_a, enter_a, state_a, message = call(
        functools.partial(first_front, width, rows),
        [plane] * 5 + [shape(msg_rows, width)] * 2,
        [ext, ext],
    )(proj, halo, seg_ext_a, seg_last, state_b, conv_x, conv_bc, bias, rate)
    messages = after(lax.all_gather(message, "seq"), w_late)
    out_a, gate_a = call(functools.partial(first_inner, heads, width, rows), [plane, plane])(
        cx_a, bc_a, cum_a, scaled_a, proj, seg_ext_a, seg_row_a, skip
    )
    gated = call(functools.partial(finish, rows), shape(tok_rows, width, kind=BF16))(
        seg_first, messages, out_a, gate_a, bc_a, enter_a, state_a, out_b, gate_b, bc_b, enter_b
    )

    tok_own = tok_rows // n_tensor

    w_near[last] = ring_shift(after(w_near[1 - last], messages), 1)
    w_swap(last - 1, messages)
    mine = lax.all_to_all(gated.reshape(n_tensor, tok_own, width), "tensor", 0, 0)
    mine = after(mine, w_near[last], w_other[1 - last], w_other[last - 1])
    w_swap(last, mine)
    swap = [(i, i ^ 1) for i in range(n_seq)]
    other = lax.ppermute(mine, "seq", swap)
    distances = [0] + [side * k for k in range(1, last) for side in (-1, 1)]
    pieces = [held[distance] for distance in distances for held in (w_near, w_other)]
    total = call(functools.partial(product_early, distances), shape(2 * tok_own, columns), flops=10**9)(
        mine, other, *pieces
    )
    half = shape(tok_own, columns, kind=BF16)
    out_own, out_other = call(
        functools.partial(product_last, last), [half, half], flops=10**8
    )(mine, other, total, w_near[last], w_other[last])
    arrived = lax.ppermute(out_other, "seq", swap)
    is_first = core == 0
    return jnp.concatenate([jnp.where(is_first, out_own, arrived), jnp.where(is_first, arrived, out_own)], 1)


def solution(mesh):
    in_specs = (
        P("seq", "tensor"),
        P(None, None, "tensor"),
        P(),
        P(None, "tensor"),
        P("tensor"),
        P("tensor"),
        P("tensor"),
        P(None, "tensor"),
        P(),
        P("tensor"),
        P("tensor", None),
        P("seq"),
    )
    out_specs = P(("seq", "tensor"), None)
    return jax.shard_map(local, mesh=mesh, in_specs=in_specs, out_specs=out_specs, check_vma=False)
```

```python
import functools

import jax
import jax.numpy as jnp
import numpy as np
from jax import lax
from jax.experimental import pallas as pl
from jax.experimental.pallas import tpu as pltpu
from jax.sharding import PartitionSpec as P

NORM_EPS = 1e-05
F32 = jnp.float32
BF16 = jnp.bfloat16
VMEM = pl.BlockSpec(memory_space=pltpu.VMEM)
ANY = pl.BlockSpec(memory_space=pl.ANY)
HALO = 8


def ring_place(index, n):
    return jnp.where(index % 2 == 0, index // 2, (2 * n - 1 - index) // 2)


def ring_index(place, n):
    return jnp.where(place < n // 2, 2 * place, 2 * n - 1 - 2 * place)


def ring_shift(block, step):
    n = lax.axis_size("tensor")
    order = [2 * i if i < n // 2 else 2 * n - 1 - 2 * i for i in range(n)]
    return lax.ppermute(block, "tensor", [(order[i], order[(i + step) % n]) for i in range(n)])


def after(values, *earlier):
    return lax.optimization_barrier((values, earlier))[0]


def far_shift(forth, back):
    cut = forth.shape[0] // 32 * 16
    parts = [jax.ShapeDtypeStruct((size, forth.shape[1]), forth.dtype) for size in (cut, forth.shape[0] - cut)]
    top, bottom = call(halves, parts)(forth, back)
    return ring_shift(top, 1), ring_shift(bottom, -1)


def halves(forth, back, top, bottom):
    size = top.shape[0]
    top[...] = forth[:size]
    bottom[...] = back[size:]


def silu(v):
    return v / (1.0 + jnp.exp(-v))


def dot(a, b, dims=((1,), (0,))):
    return lax.dot_general(a.astype(BF16), b.astype(BF16), (dims, ((), ())), preferred_element_type=F32)


def source_of(distance):
    n = lax.axis_size("tensor")
    return ring_index((ring_place(lax.axis_index("tensor"), n) + distance + n) % n, n)


def project(distances, ahead, first, *refs):
    count, fetched = len(distances), len(distances) + bool(ahead)
    blocks, (w_zx, w_bc, w_dt), refs = refs[:count], refs[count : count + 3], refs[count + 3 :]
    total, refs = (None, refs) if first else (refs[0], refs[1:])
    out, far_out, held, sems = refs if ahead else (refs[0], None, *refs[1:])
    feat, width = held.shape[1], w_bc.shape[1]
    sources = [w_zx.at[0], w_zx.at[1], w_bc, w_dt]
    copies = []
    for k, distance in enumerate([*distances, ahead][:fetched]):
        rows = pl.ds(pl.multiple_of(source_of(distance) * feat, 16), feat)
        for j, source in enumerate(sources):
            target = held.at[k] if k < count else far_out
            copies.append(
                pltpu.make_async_copy(source.at[rows], target.at[:, pl.ds(j * width, width)], sems.at[k, j])
            )
            copies[-1].start()
    result = 0.0 if first else total[...]
    for k in range(count):
        for j in range(len(sources)):
            copies[k * len(sources) + j].wait()
        result = result + dot(blocks[k][...], held[k], ((0,), (0,)))
    out[...] = result
    for copy in copies[count * len(sources) :]:
        copy.wait()


def conv(ext, seg_ext, taps, rows):
    size = taps.shape[0]
    seg_now = seg_ext[HALO : HALO + rows]
    total = taps[size - 1 : size] * ext[HALO : HALO + rows]
    for offset in range(1, size):
        same = seg_ext[HALO - offset : HALO - offset + rows] == seg_now
        total = total + taps[size - 1 - offset : size - offset] * jnp.where(
            same, ext[HALO - offset : HALO - offset + rows], 0.0
        )
    return silu(total)


def prefix_sum(values):
    rows = values.shape[0]
    lower = lax.broadcasted_iota(jnp.int32, (rows, rows), 0) >= lax.broadcasted_iota(jnp.int32, (rows, rows), 1)
    lower = jnp.where(lower, 1.0, 0.0).astype(BF16)
    total = jnp.zeros(values.shape, F32)
    rest = values
    parts = []
    for _ in range(3):
        part = rest.astype(BF16)
        parts.append(part)
        rest = rest - part.astype(F32)
    for part in reversed(parts):
        total = total + jnp.dot(lower, part, preferred_element_type=F32)
    return total


def block_front(ext_x, ext_bc, seg_ext, dt_raw, taps_x, taps_bc, bias, rate, rows, seg_enter, seg_leave):
    conv_x = conv(ext_x, seg_ext, taps_x, rows)
    conv_bc = conv(ext_bc, seg_ext, taps_bc, rows)
    seg = seg_ext[HALO : HALO + rows]
    shifted = dt_raw + bias
    step_size = jnp.maximum(shifted, 0.0) + jnp.log1p(jnp.exp(-jnp.abs(shifted)))
    cum = prefix_sum(-rate * step_size)
    scaled = conv_x * step_size
    last = cum[rows - 1 : rows]
    tail = jnp.where(seg == seg_leave, jnp.exp(last - cum), 0.0)
    state_w = conv_bc.shape[1] // 2
    state = dot(conv_bc, tail * scaled, ((0,), (0,)))[:state_w]
    enter = jnp.where(seg == seg_enter, jnp.exp(cum), 0.0)
    return conv_x, conv_bc, cum, scaled, state, enter, last


def block_inner(conv_bc, cum, scaled, seg_col, seg_row, heads):
    rows, width = scaled.shape
    state_w = conv_bc.shape[1] // 2
    head_w = width // heads
    scores = dot(conv_bc[:, state_w:], conv_bc[:, :state_w], ((1,), (1,)))
    later = lax.broadcasted_iota(jnp.int32, (rows, rows), 0) >= lax.broadcasted_iota(jnp.int32, (rows, rows), 1)
    visible = (seg_col == seg_row) & later
    cum_rows = cum.T
    lane = lax.broadcasted_iota(jnp.int32, (rows, width), 1)
    result = jnp.zeros((rows, width), F32)
    scaled = scaled.astype(BF16)
    for head in range(heads):
        at = head * head_w
        gap = jnp.where(visible, cum[:, at : at + 1] - cum_rows[at : at + 1, :], -jnp.inf)
        part = dot(jnp.exp(gap) * scores, scaled)
        result = jnp.where((lane >= at) & (lane < at + head_w), part, result)
    return result


def later_block(heads, width, rows, proj, seg_ext, seg_row, taps_x, taps_bc, bias, rate, skip,
                out, bc_out, enter_out, state_out, gate_out, ext_x, ext_bc):
    rounded = proj[rows - HALO :, : 3 * width].astype(BF16).astype(F32)
    gate_out[...] = silu(rounded[HALO:, :width])
    ext_x[...] = rounded[:, width : 2 * width]
    ext_bc[...] = rounded[:, 2 * width : 3 * width]
    seg_enter = seg_ext[HALO - 1 : HALO]
    seg_leave = seg_ext[HALO + rows - 1 : HALO + rows]
    conv_x, conv_bc, cum, scaled, state, enter, last = block_front(
        ext_x, ext_bc, seg_ext, proj[rows:, 3 * width :], taps_x, taps_bc[...], bias[...], rate[...], rows, seg_enter, seg_leave
    )
    out[...] = block_inner(conv_bc, cum, scaled, seg_ext[HALO:], seg_row[...], heads) + skip[...] * conv_x
    bc_out[...] = conv_bc
    enter_out[...] = enter
    keep = jnp.where(seg_enter == seg_leave, jnp.exp(last), 0.0)
    state_w = state.shape[0]
    state_out[:state_w] = state
    state_out[state_w : state_w + 1] = keep
    state_out[state_w + 1 : state_w + 2] = last
    state_out[state_w + 2 :] = jnp.zeros((state_out.shape[0] - state_w - 2, width), F32)


def first_front(width, rows, proj, halo, seg_ext, seg_last, state_b, taps_x, taps_bc, bias, rate,
                conv_out, bc_out, cum_out, scaled_out, enter_out, state_out, message, ext_x, ext_bc):
    ext_x[:HALO] = halo[:, :width].astype(F32)
    ext_bc[:HALO] = halo[:, width:].astype(F32)
    ext_x[HALO:] = proj[:rows, width : 2 * width].astype(BF16).astype(F32)
    ext_bc[HALO:] = proj[:rows, 2 * width : 3 * width].astype(BF16).astype(F32)
    seg_enter = seg_ext[HALO : HALO + 1]
    seg_leave = seg_ext[HALO + rows - 1 : HALO + rows]
    conv_x, conv_bc, cum, scaled, state, enter, last = block_front(
        ext_x, ext_bc, seg_ext, proj[:rows, 3 * width :], taps_x, taps_bc[...], bias[...], rate[...], rows, seg_enter, seg_leave
    )
    conv_out[...] = conv_x
    bc_out[...] = conv_bc
    cum_out[...] = cum
    scaled_out[...] = scaled
    enter_out[...] = enter
    keep = jnp.where(seg_enter == seg_leave, jnp.exp(last), 0.0)
    state_w = state.shape[0]
    state_out[:state_w] = state
    state_out[state_w : state_w + 1] = keep
    state_out[state_w + 1 :] = jnp.zeros((state_out.shape[0] - state_w - 1, width), F32)
    message[:state_w] = state_b[state_w : state_w + 1] * state + state_b[:state_w]
    message[state_w : state_w + 1] = last + state_b[state_w + 1 : state_w + 2]
    message[state_w + 1 : state_w + 2] = jnp.broadcast_to(seg_last[...].astype(F32), (1, width))
    message[state_w + 2 :] = jnp.zeros((message.shape[0] - state_w - 2, width), F32)


def front(heads, width, rows, top, bottom, weights, total, halo_part, halo_far, seg_ext_a, seg_ext_b, seg_row_b,
          seg_last, taps_x, taps_bc, bias, rate, skip, out_b, bc_b, enter_b, gate_b, conv_a, bc_a, cum_a, scaled_a,
          enter_a, gate_a, state_a, message, proj, state_b, ext_x, ext_bc):
    cut = top.shape[0]
    proj[...] = (
        total[...] + dot(top[...], weights[:cut], ((0,), (0,))) + dot(bottom[...], weights[cut:], ((0,), (0,)))
    )
    halo = (halo_part[...] + dot(halo_far[...], weights[:, width : 3 * width])).astype(BF16)
    later_block(heads, width, rows, proj, seg_ext_b, seg_row_b, taps_x, taps_bc, bias, rate, skip,
                out_b, bc_b, enter_b, state_b, gate_b, ext_x, ext_bc)
    gate_a[...] = silu(proj[:rows, :width].astype(BF16).astype(F32))
    first_front(width, rows, proj, halo, seg_ext_a, seg_last, state_b, taps_x, taps_bc, bias, rate,
                conv_a, bc_a, cum_a, scaled_a, enter_a, state_a, message, ext_x, ext_bc)


def finish(heads, rows, seg_first, messages, seg_ext_a, seg_row_a, skip, conv_a, bc_a, cum_a, scaled_a, enter_a,
           gate_a, state_a, out_b, bc_b, enter_b, gate_b, gated):
    state_w = bc_a.shape[1] // 2
    entering = jnp.zeros((state_w, out_b.shape[1]), F32)
    decay = jnp.zeros((1, out_b.shape[1]), F32)
    first = seg_first[...].astype(F32)
    place = lax.axis_index("seq")
    for device in reversed(range(messages.shape[0] - 1)):
        earlier = device < place
        passes = earlier & (messages[device, state_w + 1 : state_w + 2] == first)
        passes = jnp.where(passes, jnp.exp(decay), 0.0)
        entering = entering + passes * messages[device, :state_w]
        decay = decay + jnp.where(earlier, messages[device, state_w : state_w + 1], 0.0)
    second = state_a[state_w : state_w + 1] * entering + state_a[:state_w]
    out_a = block_inner(bc_a[...], cum_a[...], scaled_a[...], seg_ext_a[HALO:], seg_row_a[...], heads)
    out_a = out_a + skip[...] * conv_a[...]
    gated[:rows] = ((out_a + enter_a[...] * dot(bc_a[:, state_w:], entering)) * gate_a[...]).astype(BF16)
    gated[rows:] = ((out_b[...] + enter_b[...] * dot(bc_b[:, state_w:], second)) * gate_b[...]).astype(BF16)


def product(gated, distances, pieces):
    total = 0.0
    for distance, piece in zip(distances, pieces):
        source = source_of(distance)
        rows = jnp.concatenate([part[source] for part in gated], 0)
        total = total + jnp.dot(rows, piece[...], preferred_element_type=F32)
    return total


def product_early(distances, mine, other, *rest):
    rest[-1][...] = product((mine, other), distances, rest[:-1])


def product_last(distance, mine, other, total, top, bottom, mine_out, other_out, held):
    held[: top.shape[0]] = top[...]
    held[top.shape[0] :] = bottom[...]
    result = product((mine, other), [distance], [held]) + total[...]
    blocks, rows, width = mine.shape
    for i, (gated, out) in enumerate(((mine, mine_out), (other, other_out))):
        squares = jnp.zeros((rows, width), F32)
        for block in range(blocks):
            value = gated[block].astype(F32)
            squares = squares + value * value
        scale = lax.rsqrt(jnp.sum(squares, axis=1, keepdims=True) / (blocks * width) + NORM_EPS)
        out[...] = (result[i * rows : (i + 1) * rows] * scale).astype(BF16)


def call(body, outs, scratch=(), vmem=48, flops=10**7, **kw):
    return pl.pallas_call(
        body,
        out_shape=outs,
        scratch_shapes=list(scratch),
        compiler_params=pltpu.CompilerParams(vmem_limit_bytes=vmem << 20),
        cost_estimate=pl.CostEstimate(flops=flops, bytes_accessed=1 << 21, transcendentals=1 << 17),
        **kw,
    )


def local(
    tokens, w_zx, w_bc, w_dt, dt_bias, a_rate, d_skip, conv_x, conv_bc, norm_gain, w_out, segments
):
    tok_rows, feat = tokens.shape
    width = w_zx.shape[2]
    heads = dt_bias.shape[0]
    head_w = width // heads
    state_w = w_bc.shape[1] // 2
    model = w_zx.shape[1]
    n_seq, n_tensor = lax.axis_size("seq"), lax.axis_size("tensor")
    seq_at = lax.axis_index("seq")
    rows = tok_rows // 2
    shape = lambda *s, kind=F32: jax.ShapeDtypeStruct(s, kind)

    spread = lambda v: jnp.repeat(v, head_w, axis=-1)
    expand = np.repeat(np.eye(heads, dtype=np.float32), head_w, axis=1)
    w_step = jnp.dot(w_dt, expand.astype(BF16))
    block = tokens.T
    core = seq_at % 2
    columns = model // 2
    own = (lax.dynamic_slice_in_dim(w_out, core * columns, columns, 1).astype(F32) * norm_gain[:, None]).astype(BF16)
    last = n_tensor // 2
    w_half = width // 2
    shift_rows = [(i, i + 1) for i in range(n_seq - 1)]

    seg_halo = lax.ppermute(segments[tok_rows - HALO :], "seq", shift_rows)
    seg_all = jnp.concatenate([seg_halo, segments])[:, None]
    order = [2 * i if i < last else 2 * n_tensor - 1 - 2 * i for i in range(n_tensor)]
    halo_far = lax.ppermute(
        tokens[tok_rows - HALO :],
        ("seq", "tensor"),
        [
            (place * n_tensor + order[(i + last) % n_tensor], (place + 1) * n_tensor + order[i])
            for place in range(n_seq - 1)
            for i in range(n_tensor)
        ],
    )
    small = (
        halo_far,
        (seg_all[: HALO + rows], seg_all[rows:]),
        (segments[None, :rows], segments[None, rows:]),
        (segments[None, :1], segments[None, tok_rows - 1 :]),
        (spread(dt_bias)[None], spread(a_rate)[None], spread(d_skip)[None]),
    )

    forth = back = block
    w_steps = []
    arrived, projs = [(0, block)], []
    for step in range(1, last + 1):
        if step > 1:
            ready = (projs[step - 2], small) if step == 3 else projs[step - 2]
            forth, back = after(forth, ready), after(back, ready)
        arrivals = (forth, back)
        if step < last:
            forth, back = ring_shift(forth, 1), ring_shift(back, -1)
        else:
            far = far_shift(forth, back)
        if step == 2:
            w_forth, w_back = after((own, own), arrivals)
            w_steps.append((ring_shift(w_forth, 1), ring_shift(w_back, -1)))
        ahead = last if step == last else 0
        total = projs[-1:]
        fetched = len(arrived) + bool(ahead)
        outs = [shape(tok_rows, 4 * width)] + [shape(feat, 4 * width, kind=BF16)] * bool(ahead)
        results = call(
            functools.partial(project, [distance for distance, _ in arrived], ahead, not total),
            outs,
            [pltpu.VMEM((len(arrived), feat, 4 * width), BF16), pltpu.SemaphoreType.DMA((fetched, 4))],
            in_specs=[VMEM] * len(arrived) + [ANY] * 3 + [VMEM] * len(total),
            flops=10**9,
        )(*[part for _, part in arrived], w_zx, w_bc, w_step, *total)
        projs.append(results[0])
        arrived = [(-step, forth), (step, back)]
    w_forth, w_back = after(w_steps[-1], projs[-1])
    w_steps.append((ring_shift(w_forth, 1), ring_shift(w_back, -1)))
    halo_part = lax.ppermute(projs[-1][tok_rows - HALO :, width : 3 * width], "seq", shift_rows)

    halo_far, (seg_ext_a, seg_ext_b), (seg_row_a, seg_row_b), (seg_first, seg_last), (bias, rate, skip) = small
    msg_rows = state_w + 8
    plane = shape(rows, width)
    state = shape(msg_rows, width)
    ext = pltpu.VMEM((HALO + rows, width), F32)
    *kept, message = call(
        functools.partial(front, heads, width, rows),
        [plane] * 10 + [state] * 2,
        [pltpu.VMEM((tok_rows, 4 * width), F32), pltpu.VMEM((msg_rows, width), F32), ext, ext],
        flops=10**8,
    )(*far, results[1], projs[-1], halo_part, halo_far, seg_ext_a, seg_ext_b, seg_row_b, seg_last,
      conv_x, conv_bc, bias, rate, skip)
    later, first = kept[:4], kept[4:]
    messages = lax.all_gather(message, "seq")
    gated = call(functools.partial(finish, heads, rows), shape(tok_rows, width, kind=BF16))(
        seg_first, messages, seg_ext_a, seg_row_a, skip, *first, *later
    )
    tok_own = tok_rows // n_tensor

    mine = lax.all_to_all(gated.reshape(n_tensor, tok_own, width), "tensor", 0, 0)
    for step in range(3, last):
        w_forth, w_back = after(w_steps[-1], messages)
        w_steps.append((ring_shift(w_forth, 1), ring_shift(w_back, -1)))
    w_far = far_shift(*after(w_steps[-1], mine))
    swap = [(i, i ^ 1) for i in range(n_seq)]
    other = lax.ppermute(mine, "seq", swap)
    pieces, distances = [own], [0]
    for i, pair in enumerate(w_steps):
        pieces += pair
        distances += [-i - 1, i + 1]
    total = call(functools.partial(product_early, distances), shape(2 * tok_own, columns), flops=10**9)(
        mine, other, *pieces
    )
    half = shape(tok_own, columns, kind=BF16)
    out_own, out_other = call(
        functools.partial(product_last, last), [half, half], [pltpu.VMEM((width, columns), BF16)], flops=10**8
    )(mine, other, total, *w_far)
    arrived = lax.ppermute(out_other, "seq", swap)
    is_first = core == 0
    return jnp.concatenate([jnp.where(is_first, out_own, arrived), jnp.where(is_first, arrived, out_own)], 1)


def solution(mesh):
    in_specs = (
        P("seq", "tensor"),
        P(None, None, "tensor"),
        P(),
        P(None, "tensor"),
        P("tensor"),
        P("tensor"),
        P("tensor"),
        P(None, "tensor"),
        P(),
        P("tensor"),
        P("tensor", None),
        P("seq"),
    )
    out_specs = P(("seq", "tensor"), None)
    return jax.shard_map(local, mesh=mesh, in_specs=in_specs, out_specs=out_specs, check_vma=False)
```

```python
import functools

import jax
import jax.numpy as jnp
import numpy as np
from jax import lax
from jax.experimental import pallas as pl
from jax.experimental.pallas import tpu as pltpu
from jax.sharding import PartitionSpec as P

NORM_EPS = 1e-05
F32 = jnp.float32
BF16 = jnp.bfloat16
VMEM = pl.BlockSpec(memory_space=pltpu.VMEM)
ANY = pl.BlockSpec(memory_space=pl.ANY)
HALO = 8


def ring_place(index, n):
    return jnp.where(index % 2 == 0, index // 2, (2 * n - 1 - index) // 2)


def ring_index(place, n):
    return jnp.where(place < n // 2, 2 * place, 2 * n - 1 - 2 * place)


def ring_shift(block, step):
    n = lax.axis_size("tensor")
    order = [2 * i if i < n // 2 else 2 * n - 1 - 2 * i for i in range(n)]
    return lax.ppermute(block, "tensor", [(order[i], order[(i + step) % n]) for i in range(n)])


def after(values, *earlier):
    return lax.optimization_barrier((values, earlier))[0]


def far_shift(forth, back):
    cut = forth.shape[0] // 32 * 16
    parts = [jax.ShapeDtypeStruct((size, forth.shape[1]), forth.dtype) for size in (cut, forth.shape[0] - cut)]
    top, bottom = call(halves, parts)(forth, back)
    return ring_shift(top, 1), ring_shift(bottom, -1)


def halves(forth, back, top, bottom):
    size = top.shape[0]
    top[...] = forth[:size]
    bottom[...] = back[size:]


def silu(v):
    return v / (1.0 + jnp.exp(-v))


def dot(a, b, dims=((1,), (0,))):
    return lax.dot_general(a.astype(BF16), b.astype(BF16), (dims, ((), ())), preferred_element_type=F32)


def source_of(distance):
    n = lax.axis_size("tensor")
    return ring_index((ring_place(lax.axis_index("tensor"), n) + distance + n) % n, n)


def project(distances, ahead, first, *refs):
    count, fetched = len(distances), len(distances) + bool(ahead)
    blocks, (w_zx, w_bc, w_dt), refs = refs[:count], refs[count : count + 3], refs[count + 3 :]
    total, refs = (None, refs) if first else (refs[0], refs[1:])
    out, far_out, held, sems = refs if ahead else (refs[0], None, *refs[1:])
    feat, width = held.shape[1], w_bc.shape[1]
    sources = [w_zx.at[0], w_zx.at[1], w_bc, w_dt]
    copies = []
    for k, distance in enumerate([*distances, ahead][:fetched]):
        rows = pl.ds(pl.multiple_of(source_of(distance) * feat, 16), feat)
        for j, source in enumerate(sources):
            target = held.at[k] if k < count else far_out
            copies.append(
                pltpu.make_async_copy(source.at[rows], target.at[:, pl.ds(j * width, width)], sems.at[k, j])
            )
            copies[-1].start()
    result = 0.0 if first else total[...]
    for k in range(count):
        for j in range(len(sources)):
            copies[k * len(sources) + j].wait()
        result = result + dot(blocks[k][...], held[k], ((0,), (0,)))
    out[...] = result
    for copy in copies[count * len(sources) :]:
        copy.wait()


def conv(ext, seg_ext, taps, rows):
    size = taps.shape[0]
    seg_now = seg_ext[HALO : HALO + rows]
    total = taps[size - 1 : size] * ext[HALO : HALO + rows]
    for offset in range(1, size):
        same = seg_ext[HALO - offset : HALO - offset + rows] == seg_now
        total = total + taps[size - 1 - offset : size - offset] * jnp.where(
            same, ext[HALO - offset : HALO - offset + rows], 0.0
        )
    return silu(total)


def prefix_sum(values):
    rows = values.shape[0]
    lower = lax.broadcasted_iota(jnp.int32, (rows, rows), 0) >= lax.broadcasted_iota(jnp.int32, (rows, rows), 1)
    lower = jnp.where(lower, 1.0, 0.0).astype(BF16)
    total = jnp.zeros(values.shape, F32)
    rest = values
    parts = []
    for _ in range(3):
        part = rest.astype(BF16)
        parts.append(part)
        rest = rest - part.astype(F32)
    for part in reversed(parts):
        total = total + jnp.dot(lower, part, preferred_element_type=F32)
    return total


def block_front(ext_x, ext_bc, seg_ext, dt_raw, taps_x, taps_bc, bias, rate, rows, seg_enter, seg_leave):
    conv_x = conv(ext_x, seg_ext, taps_x, rows)
    conv_bc = conv(ext_bc, seg_ext, taps_bc, rows)
    seg = seg_ext[HALO : HALO + rows]
    shifted = dt_raw + bias
    step_size = jnp.maximum(shifted, 0.0) + jnp.log1p(jnp.exp(-jnp.abs(shifted)))
    cum = prefix_sum(-rate * step_size)
    scaled = conv_x * step_size
    last = cum[rows - 1 : rows]
    tail = jnp.where(seg == seg_leave, jnp.exp(last - cum), 0.0)
    state_w = conv_bc.shape[1] // 2
    state = dot(conv_bc, tail * scaled, ((0,), (0,)))[:state_w]
    enter = jnp.where(seg == seg_enter, jnp.exp(cum), 0.0)
    return conv_x, conv_bc, cum, scaled, state, enter, last


def block_inner(conv_bc, cum, scaled, seg_col, seg_row, heads):
    rows, width = scaled.shape
    state_w = conv_bc.shape[1] // 2
    head_w = width // heads
    scores = dot(conv_bc[:, state_w:], conv_bc[:, :state_w], ((1,), (1,)))
    later = lax.broadcasted_iota(jnp.int32, (rows, rows), 0) >= lax.broadcasted_iota(jnp.int32, (rows, rows), 1)
    visible = (seg_col == seg_row) & later
    cum_rows = cum.T
    lane = lax.broadcasted_iota(jnp.int32, (rows, width), 1)
    result = jnp.zeros((rows, width), F32)
    scaled = scaled.astype(BF16)
    for head in range(heads):
        at = head * head_w
        gap = jnp.where(visible, cum[:, at : at + 1] - cum_rows[at : at + 1, :], -jnp.inf)
        part = dot(jnp.exp(gap) * scores, scaled)
        result = jnp.where((lane >= at) & (lane < at + head_w), part, result)
    return result


def later_block(heads, width, rows, proj, seg_ext, seg_row, taps_x, taps_bc, bias, rate, skip,
                out, bc_out, enter_out, state_out, gate_out, ext_x, ext_bc):
    rounded = proj[rows - HALO :, : 3 * width].astype(BF16).astype(F32)
    gate_out[...] = silu(rounded[HALO:, :width])
    ext_x[...] = rounded[:, width : 2 * width]
    ext_bc[...] = rounded[:, 2 * width : 3 * width]
    seg_enter = seg_ext[HALO - 1 : HALO]
    seg_leave = seg_ext[HALO + rows - 1 : HALO + rows]
    conv_x, conv_bc, cum, scaled, state, enter, last = block_front(
        ext_x, ext_bc, seg_ext, proj[rows:, 3 * width :], taps_x, taps_bc[...], bias[...], rate[...], rows, seg_enter, seg_leave
    )
    out[...] = block_inner(conv_bc, cum, scaled, seg_ext[HALO:], seg_row[...], heads) + skip[...] * conv_x
    bc_out[...] = conv_bc
    enter_out[...] = enter
    keep = jnp.where(seg_enter == seg_leave, jnp.exp(last), 0.0)
    state_w = state.shape[0]
    state_out[:state_w] = state
    state_out[state_w : state_w + 1] = keep
    state_out[state_w + 1 : state_w + 2] = last
    state_out[state_w + 2 :] = jnp.zeros((state_out.shape[0] - state_w - 2, width), F32)


def first_front(width, rows, proj, halo, seg_ext, seg_last, state_b, taps_x, taps_bc, bias, rate,
                conv_out, bc_out, cum_out, scaled_out, enter_out, state_out, message, ext_x, ext_bc):
    ext_x[:HALO] = halo[:, :width].astype(F32)
    ext_bc[:HALO] = halo[:, width:].astype(F32)
    ext_x[HALO:] = proj[:rows, width : 2 * width].astype(BF16).astype(F32)
    ext_bc[HALO:] = proj[:rows, 2 * width : 3 * width].astype(BF16).astype(F32)
    seg_enter = seg_ext[HALO : HALO + 1]
    seg_leave = seg_ext[HALO + rows - 1 : HALO + rows]
    conv_x, conv_bc, cum, scaled, state, enter, last = block_front(
        ext_x, ext_bc, seg_ext, proj[:rows, 3 * width :], taps_x, taps_bc[...], bias[...], rate[...], rows, seg_enter, seg_leave
    )
    conv_out[...] = conv_x
    bc_out[...] = conv_bc
    cum_out[...] = cum
    scaled_out[...] = scaled
    enter_out[...] = enter
    keep = jnp.where(seg_enter == seg_leave, jnp.exp(last), 0.0)
    state_w = state.shape[0]
    state_out[:state_w] = state
    state_out[state_w : state_w + 1] = keep
    state_out[state_w + 1 :] = jnp.zeros((state_out.shape[0] - state_w - 1, width), F32)
    message[:state_w] = state_b[state_w : state_w + 1] * state + state_b[:state_w]
    message[state_w : state_w + 1] = last + state_b[state_w + 1 : state_w + 2]
    message[state_w + 1 : state_w + 2] = jnp.broadcast_to(seg_last[...].astype(F32), (1, width))
    message[state_w + 2 :] = jnp.zeros((message.shape[0] - state_w - 2, width), F32)


def front(heads, width, rows, top, bottom, weights, total, halo_part, halo_far, seg_ext_a, seg_ext_b, seg_row_b,
          seg_last, taps_x, taps_bc, bias, rate, skip, out_b, bc_b, enter_b, gate_b, conv_a, bc_a, cum_a, scaled_a,
          enter_a, gate_a, state_a, message, proj, state_b, ext_x, ext_bc):
    cut = top.shape[0]
    proj[...] = (
        total[...] + dot(top[...], weights[:cut], ((0,), (0,))) + dot(bottom[...], weights[cut:], ((0,), (0,)))
    )
    halo = (halo_part[...] + dot(halo_far[...], weights[:, width : 3 * width])).astype(BF16)
    later_block(heads, width, rows, proj, seg_ext_b, seg_row_b, taps_x, taps_bc, bias, rate, skip,
                out_b, bc_b, enter_b, state_b, gate_b, ext_x, ext_bc)
    gate_a[...] = silu(proj[:rows, :width].astype(BF16).astype(F32))
    first_front(width, rows, proj, halo, seg_ext_a, seg_last, state_b, taps_x, taps_bc, bias, rate,
                conv_a, bc_a, cum_a, scaled_a, enter_a, state_a, message, ext_x, ext_bc)


def finish(heads, rows, seg_first, messages, seg_ext_a, seg_row_a, skip, conv_a, bc_a, cum_a, scaled_a, enter_a,
           gate_a, state_a, out_b, bc_b, enter_b, gate_b, gated):
    state_w = bc_a.shape[1] // 2
    entering = jnp.zeros((state_w, out_b.shape[1]), F32)
    decay = jnp.zeros((1, out_b.shape[1]), F32)
    first = seg_first[...].astype(F32)
    place = lax.axis_index("seq")
    for device in reversed(range(messages.shape[0] - 1)):
        earlier = device < place
        passes = earlier & (messages[device, state_w + 1 : state_w + 2] == first)
        passes = jnp.where(passes, jnp.exp(decay), 0.0)
        entering = entering + passes * messages[device, :state_w]
        decay = decay + jnp.where(earlier, messages[device, state_w : state_w + 1], 0.0)
    second = state_a[state_w : state_w + 1] * entering + state_a[:state_w]
    out_a = block_inner(bc_a[...], cum_a[...], scaled_a[...], seg_ext_a[HALO:], seg_row_a[...], heads)
    out_a = out_a + skip[...] * conv_a[...]
    gated[:rows] = ((out_a + enter_a[...] * dot(bc_a[:, state_w:], entering)) * gate_a[...]).astype(BF16)
    gated[rows:] = ((out_b[...] + enter_b[...] * dot(bc_b[:, state_w:], second)) * gate_b[...]).astype(BF16)


def product(gated, distances, pieces):
    total = 0.0
    for distance, piece in zip(distances, pieces):
        source = source_of(distance)
        rows = jnp.concatenate([part[source] for part in gated], 0)
        total = total + jnp.dot(rows, piece[...], preferred_element_type=F32)
    return total


def product_early(distances, mine, other, *rest):
    rest[-1][...] = product((mine, other), distances, rest[:-1])


def product_last(distance, mine, other, total, top, bottom, mine_out, other_out, held):
    held[: top.shape[0]] = top[...]
    held[top.shape[0] :] = bottom[...]
    result = product((mine, other), [distance], [held]) + total[...]
    blocks, rows, width = mine.shape
    for i, (gated, out) in enumerate(((mine, mine_out), (other, other_out))):
        squares = jnp.zeros((rows, width), F32)
        for block in range(blocks):
            value = gated[block].astype(F32)
            squares = squares + value * value
        scale = lax.rsqrt(jnp.sum(squares, axis=1, keepdims=True) / (blocks * width) + NORM_EPS)
        out[...] = (result[i * rows : (i + 1) * rows] * scale).astype(BF16)


def call(body, outs, scratch=(), vmem=16, flops=10**7, **kw):
    return pl.pallas_call(
        body,
        out_shape=outs,
        scratch_shapes=list(scratch),
        compiler_params=pltpu.CompilerParams(vmem_limit_bytes=vmem << 20),
        cost_estimate=pl.CostEstimate(flops=flops, bytes_accessed=1 << 21, transcendentals=1 << 17),
        **kw,
    )


def local(
    tokens, w_zx, w_bc, w_dt, dt_bias, a_rate, d_skip, conv_x, conv_bc, norm_gain, w_out, segments
):
    tok_rows, feat = tokens.shape
    width = w_zx.shape[2]
    heads = dt_bias.shape[0]
    head_w = width // heads
    state_w = w_bc.shape[1] // 2
    model = w_zx.shape[1]
    n_seq, n_tensor = lax.axis_size("seq"), lax.axis_size("tensor")
    seq_at = lax.axis_index("seq")
    rows = tok_rows // 2
    shape = lambda *s, kind=F32: jax.ShapeDtypeStruct(s, kind)

    spread = lambda v: jnp.repeat(v, head_w, axis=-1)
    expand = np.repeat(np.eye(heads, dtype=np.float32), head_w, axis=1)
    w_step = jnp.dot(w_dt, expand.astype(BF16))
    block = tokens.T
    core = seq_at % 2
    columns = model // 2
    own = (lax.dynamic_slice_in_dim(w_out, core * columns, columns, 1).astype(F32) * norm_gain[:, None]).astype(BF16)
    last = n_tensor // 2
    w_half = width // 2
    shift_rows = [(i, i + 1) for i in range(n_seq - 1)]


    def early_arrays(*earlier):
        seg_halo = lax.ppermute(after(segments[tok_rows - HALO :], *earlier), "seq", shift_rows)
        seg_all = jnp.concatenate([seg_halo, segments])[:, None]
        order = [2 * i if i < last else 2 * n_tensor - 1 - 2 * i for i in range(n_tensor)]
        moves = [
            (place * n_tensor + order[(i + last) % n_tensor], (place + 1) * n_tensor + order[i])
            for place in range(n_seq - 1)
            for i in range(n_tensor)
        ]
        halo_far = lax.ppermute(after(tokens[tok_rows - HALO :], *earlier), ("seq", "tensor"), moves)
        return (
            halo_far,
            (seg_all[: HALO + rows], seg_all[rows:]),
            (segments[None, :rows], segments[None, rows:]),
            (segments[None, :1], segments[None, tok_rows - 1 :]),
            (spread(dt_bias)[None], spread(a_rate)[None], spread(d_skip)[None]),
        )

    forth = back = block
    w_steps = []
    arrived, projs = [(0, block)], []
    for step in range(1, last + 1):
        if step > 1:
            ready = (projs[step - 2], small) if step == 3 else projs[step - 2]
            forth, back = after(forth, ready), after(back, ready)
        arrivals = (forth, back)
        if step < last:
            forth, back = ring_shift(forth, 1), ring_shift(back, -1)
        else:
            far = far_shift(forth, back)
        if step == 2:
            small = early_arrays(arrivals)
            w_forth, w_back = after((own, own), arrivals)
            w_steps.append((ring_shift(w_forth, 1), ring_shift(w_back, -1)))
        ahead = last if step == last else 0
        total = projs[-1:]
        fetched = len(arrived) + bool(ahead)
        outs = [shape(tok_rows, 4 * width)] + [shape(feat, 4 * width, kind=BF16)] * bool(ahead)
        results = call(
            functools.partial(project, [distance for distance, _ in arrived], ahead, not total),
            outs,
            [pltpu.VMEM((len(arrived), feat, 4 * width), BF16), pltpu.SemaphoreType.DMA((fetched, 4))],
            in_specs=[VMEM] * len(arrived) + [ANY] * 3 + [VMEM] * len(total),
            flops=10**9,
        )(*[part for _, part in arrived], w_zx, w_bc, w_step, *total)
        projs.append(results[0])
        arrived = [(-step, forth), (step, back)]
    halo_part = lax.ppermute(projs[-1][tok_rows - HALO :, width : 3 * width], "seq", shift_rows)
    w_forth, w_back = after(w_steps[-1], far, halo_part)
    w_steps.append((ring_shift(w_forth, 1), ring_shift(w_back, -1)))

    halo_far, (seg_ext_a, seg_ext_b), (seg_row_a, seg_row_b), (seg_first, seg_last), (bias, rate, skip) = small
    msg_rows = state_w + 8
    plane = shape(rows, width)
    state = shape(msg_rows, width)
    ext = pltpu.VMEM((HALO + rows, width), F32)
    *kept, message = call(
        functools.partial(front, heads, width, rows),
        [plane] * 10 + [state] * 2,
        [pltpu.VMEM((tok_rows, 4 * width), F32), pltpu.VMEM((msg_rows, width), F32), ext, ext],
        flops=10**8,
    )(*far, results[1], projs[-1], halo_part, halo_far, seg_ext_a, seg_ext_b, seg_row_b, seg_last,
      conv_x, conv_bc, bias, rate, skip)
    later, first = kept[:4], kept[4:]
    messages = lax.all_gather(message, "seq")
    gated = call(functools.partial(finish, heads, rows), shape(tok_rows, width, kind=BF16))(
        seg_first, messages, seg_ext_a, seg_row_a, skip, *first, *later
    )
    tok_own = tok_rows // n_tensor

    mine = lax.all_to_all(gated.reshape(n_tensor, tok_own, width), "tensor", 0, 0)
    for step in range(3, last):
        w_forth, w_back = after(w_steps[-1], messages)
        w_steps.append((ring_shift(w_forth, 1), ring_shift(w_back, -1)))
    w_far = far_shift(*after(w_steps[-1], mine))
    swap = [(i, i ^ 1) for i in range(n_seq)]
    other = lax.ppermute(mine, "seq", swap)
    pieces, distances = [own], [0]
    for i, pair in enumerate(w_steps):
        pieces += pair
        distances += [-i - 1, i + 1]
    total = call(functools.partial(product_early, distances), shape(2 * tok_own, columns), vmem=16 + len(pieces), flops=10**9)(
        mine, other, *pieces
    )
    half = shape(tok_own, columns, kind=BF16)
    out_own, out_other = call(
        functools.partial(product_last, last), [half, half], [pltpu.VMEM((width, columns), BF16)], flops=10**8
    )(mine, other, total, *w_far)
    arrived = lax.ppermute(out_other, "seq", swap)
    is_first = core == 0
    return jnp.concatenate([jnp.where(is_first, out_own, arrived), jnp.where(is_first, arrived, out_own)], 1)


def solution(mesh):
    in_specs = (
        P("seq", "tensor"),
        P(None, None, "tensor"),
        P(),
        P(None, "tensor"),
        P("tensor"),
        P("tensor"),
        P("tensor"),
        P(None, "tensor"),
        P(),
        P("tensor"),
        P("tensor", None),
        P("seq"),
    )
    out_specs = P(("seq", "tensor"), None)
    return jax.shard_map(local, mesh=mesh, in_specs=in_specs, out_specs=out_specs, check_vma=False)
```

```python
import functools

import jax
import jax.numpy as jnp
import numpy as np
from jax import lax
from jax.experimental import pallas as pl
from jax.experimental.pallas import tpu as pltpu
from jax.sharding import PartitionSpec as P

NORM_EPS = 1e-05
F32 = jnp.float32
BF16 = jnp.bfloat16
VMEM = pl.BlockSpec(memory_space=pltpu.VMEM)
ANY = pl.BlockSpec(memory_space=pl.ANY)
HALO = 8
W_FIRST = 3


def ring_place(index, n):
    return jnp.where(index % 2 == 0, index // 2, (2 * n - 1 - index) // 2)


def ring_index(place, n):
    return jnp.where(place < n // 2, 2 * place, 2 * n - 1 - 2 * place)


def ring_shift(block, step):
    n = lax.axis_size("tensor")
    order = [2 * i if i < n // 2 else 2 * n - 1 - 2 * i for i in range(n)]
    return lax.ppermute(block, "tensor", [(order[i], order[(i + step) % n]) for i in range(n)])


def after(values, *earlier):
    return lax.optimization_barrier((values, earlier))[0]


def far_shift(forth, back):
    cut = forth.shape[0] // 32 * 16
    parts = [jax.ShapeDtypeStruct((size, forth.shape[1]), forth.dtype) for size in (cut, forth.shape[0] - cut)]
    top, bottom = call(halves, parts)(forth, back)
    return ring_shift(top, 1), ring_shift(bottom, -1)


def halves(forth, back, top, bottom):
    size = top.shape[0]
    top[...] = forth[:size]
    bottom[...] = back[size:]


def silu(v):
    return v / (1.0 + jnp.exp(-v))


def dot(a, b, dims=((1,), (0,))):
    return lax.dot_general(a.astype(BF16), b.astype(BF16), (dims, ((), ())), preferred_element_type=F32)


def source_of(distance):
    n = lax.axis_size("tensor")
    return ring_index((ring_place(lax.axis_index("tensor"), n) + distance + n) % n, n)


def project(distances, ahead, first, *refs):
    count, fetched = len(distances), len(distances) + bool(ahead)
    blocks, (w_zx, w_bc, w_dt), refs = refs[:count], refs[count : count + 3], refs[count + 3 :]
    total, refs = (None, refs) if first else (refs[0], refs[1:])
    out, far_out, held, sems = refs if ahead else (refs[0], None, *refs[1:])
    feat, width = held.shape[1], w_bc.shape[1]
    sources = [w_zx.at[0], w_zx.at[1], w_bc, w_dt]
    copies = []
    for k, distance in enumerate([*distances, ahead][:fetched]):
        rows = pl.ds(pl.multiple_of(source_of(distance) * feat, 16), feat)
        for j, source in enumerate(sources):
            target = held.at[k] if k < count else far_out
            copies.append(
                pltpu.make_async_copy(source.at[rows], target.at[:, pl.ds(j * width, width)], sems.at[k, j])
            )
            copies[-1].start()
    result = 0.0 if first else total[...]
    for k in range(count):
        for j in range(len(sources)):
            copies[k * len(sources) + j].wait()
        result = result + dot(blocks[k][...], held[k], ((0,), (0,)))
    out[...] = result
    for copy in copies[count * len(sources) :]:
        copy.wait()


def project_far(top, bottom, weights, total, out):
    cut = top.shape[0]
    out[...] = (
        total[...] + dot(top[...], weights[:cut], ((0,), (0,))) + dot(bottom[...], weights[cut:], ((0,), (0,)))
    )


def conv(ext, seg_ext, taps, rows):
    size = taps.shape[0]
    seg_now = seg_ext[HALO : HALO + rows]
    total = taps[size - 1 : size] * ext[HALO : HALO + rows]
    for offset in range(1, size):
        same = seg_ext[HALO - offset : HALO - offset + rows] == seg_now
        total = total + taps[size - 1 - offset : size - offset] * jnp.where(
            same, ext[HALO - offset : HALO - offset + rows], 0.0
        )
    return silu(total)


def prefix_sum(values):
    rows = values.shape[0]
    lower = lax.broadcasted_iota(jnp.int32, (rows, rows), 0) >= lax.broadcasted_iota(jnp.int32, (rows, rows), 1)
    lower = jnp.where(lower, 1.0, 0.0).astype(BF16)
    total = jnp.zeros(values.shape, F32)
    rest = values
    parts = []
    for _ in range(3):
        part = rest.astype(BF16)
        parts.append(part)
        rest = rest - part.astype(F32)
    for part in reversed(parts):
        total = total + jnp.dot(lower, part, preferred_element_type=F32)
    return total


def block_front(ext_x, ext_bc, seg_ext, dt_raw, taps_x, taps_bc, bias, rate, rows, seg_enter, seg_leave):
    conv_x = conv(ext_x, seg_ext, taps_x, rows)
    conv_bc = conv(ext_bc, seg_ext, taps_bc, rows)
    seg = seg_ext[HALO : HALO + rows]
    shifted = dt_raw + bias
    step_size = jnp.maximum(shifted, 0.0) + jnp.log1p(jnp.exp(-jnp.abs(shifted)))
    cum = prefix_sum(-rate * step_size)
    scaled = conv_x * step_size
    last = cum[rows - 1 : rows]
    tail = jnp.where(seg == seg_leave, jnp.exp(last - cum), 0.0)
    state_w = conv_bc.shape[1] // 2
    state = dot(conv_bc, tail * scaled, ((0,), (0,)))[:state_w]
    enter = jnp.where(seg == seg_enter, jnp.exp(cum), 0.0)
    return conv_x, conv_bc, cum, scaled, state, enter, last


def block_inner(conv_bc, cum, scaled, seg_col, seg_row, heads):
    rows, width = scaled.shape
    state_w = conv_bc.shape[1] // 2
    head_w = width // heads
    scores = dot(conv_bc[:, state_w:], conv_bc[:, :state_w], ((1,), (1,)))
    later = lax.broadcasted_iota(jnp.int32, (rows, rows), 0) >= lax.broadcasted_iota(jnp.int32, (rows, rows), 1)
    visible = (seg_col == seg_row) & later
    cum_rows = cum.T
    lane = lax.broadcasted_iota(jnp.int32, (rows, width), 1)
    result = jnp.zeros((rows, width), F32)
    scaled = scaled.astype(BF16)
    for head in range(heads):
        at = head * head_w
        gap = jnp.where(visible, cum[:, at : at + 1] - cum_rows[at : at + 1, :], -jnp.inf)
        part = dot(jnp.exp(gap) * scores, scaled)
        result = jnp.where((lane >= at) & (lane < at + head_w), part, result)
    return result


def later_block(heads, width, rows, proj, seg_ext, seg_row, taps_x, taps_bc, bias, rate, skip,
                out, bc_out, enter_out, state_out, gate_out, ext_x, ext_bc):
    rounded = proj[rows - HALO :, : 3 * width].astype(BF16).astype(F32)
    gate_out[...] = silu(rounded[HALO:, :width])
    ext_x[...] = rounded[:, width : 2 * width]
    ext_bc[...] = rounded[:, 2 * width : 3 * width]
    seg_enter = seg_ext[HALO - 1 : HALO]
    seg_leave = seg_ext[HALO + rows - 1 : HALO + rows]
    conv_x, conv_bc, cum, scaled, state, enter, last = block_front(
        ext_x, ext_bc, seg_ext, proj[rows:, 3 * width :], taps_x, taps_bc[...], bias[...], rate[...], rows, seg_enter, seg_leave
    )
    out[...] = block_inner(conv_bc, cum, scaled, seg_ext[HALO:], seg_row[...], heads) + skip[...] * conv_x
    bc_out[...] = conv_bc
    enter_out[...] = enter
    keep = jnp.where(seg_enter == seg_leave, jnp.exp(last), 0.0)
    state_w = state.shape[0]
    state_out[:state_w] = state
    state_out[state_w : state_w + 1] = keep
    state_out[state_w + 1 : state_w + 2] = last
    state_out[state_w + 2 :] = jnp.zeros((state_out.shape[0] - state_w - 2, width), F32)


def first_front(width, rows, proj, halo, seg_ext, seg_last, state_b, taps_x, taps_bc, bias, rate,
                conv_out, bc_out, cum_out, scaled_out, enter_out, state_out, message, ext_x, ext_bc):
    ext_x[:HALO] = halo[:, :width].astype(F32)
    ext_bc[:HALO] = halo[:, width:].astype(F32)
    ext_x[HALO:] = proj[:rows, width : 2 * width].astype(BF16).astype(F32)
    ext_bc[HALO:] = proj[:rows, 2 * width : 3 * width].astype(BF16).astype(F32)
    seg_enter = seg_ext[HALO : HALO + 1]
    seg_leave = seg_ext[HALO + rows - 1 : HALO + rows]
    conv_x, conv_bc, cum, scaled, state, enter, last = block_front(
        ext_x, ext_bc, seg_ext, proj[:rows, 3 * width :], taps_x, taps_bc[...], bias[...], rate[...], rows, seg_enter, seg_leave
    )
    conv_out[...] = conv_x
    bc_out[...] = conv_bc
    cum_out[...] = cum
    scaled_out[...] = scaled
    enter_out[...] = enter
    keep = jnp.where(seg_enter == seg_leave, jnp.exp(last), 0.0)
    state_w = state.shape[0]
    state_out[:state_w] = state
    state_out[state_w : state_w + 1] = keep
    state_out[state_w + 1 :] = jnp.zeros((state_out.shape[0] - state_w - 1, width), F32)
    message[:state_w] = state_b[state_w : state_w + 1] * state + state_b[:state_w]
    message[state_w : state_w + 1] = last + state_b[state_w + 1 : state_w + 2]
    message[state_w + 1 : state_w + 2] = jnp.broadcast_to(seg_last[...].astype(F32), (1, width))
    message[state_w + 2 :] = jnp.zeros((message.shape[0] - state_w - 2, width), F32)


def finish(heads, rows, seg_first, messages, seg_ext_a, seg_row_a, skip, proj, conv_a, bc_a, cum_a, scaled_a, enter_a,
           state_a, out_b, gate_b, bc_b, enter_b, gated):
    state_w = bc_a.shape[1] // 2
    width = out_b.shape[1]
    entering = jnp.zeros((state_w, width), F32)
    decay = jnp.zeros((1, width), F32)
    first = seg_first[...].astype(F32)
    place = lax.axis_index("seq")
    for device in reversed(range(messages.shape[0] - 1)):
        earlier = device < place
        passes = earlier & (messages[device, state_w + 1 : state_w + 2] == first)
        passes = jnp.where(passes, jnp.exp(decay), 0.0)
        entering = entering + passes * messages[device, :state_w]
        decay = decay + jnp.where(earlier, messages[device, state_w : state_w + 1], 0.0)
    second = state_a[state_w : state_w + 1] * entering + state_a[:state_w]
    out_a = block_inner(bc_a[...], cum_a[...], scaled_a[...], seg_ext_a[HALO:], seg_row_a[...], heads)
    out_a = out_a + skip[...] * conv_a[...] + enter_a[...] * dot(bc_a[:, state_w:], entering)
    gated[:rows] = (out_a * silu(proj[:rows, :width].astype(BF16).astype(F32))).astype(BF16)
    gated[rows:] = ((out_b[...] + enter_b[...] * dot(bc_b[:, state_w:], second)) * gate_b[...]).astype(BF16)


def product(gated, distances, pieces):
    total = 0.0
    for distance, piece in zip(distances, pieces):
        source = source_of(distance)
        rows = jnp.concatenate([part[source] for part in gated], 0)
        total = total + jnp.dot(rows, piece[...], preferred_element_type=F32)
    return total


def product_early(distances, mine, other, *rest):
    rest[-1][...] = product((mine, other), distances, rest[:-1])


def product_last(distance, mine, other, total, top, bottom, mine_out, other_out, held):
    held[: top.shape[0]] = top[...]
    held[top.shape[0] :] = bottom[...]
    result = product((mine, other), [distance], [held]) + total[...]
    blocks, rows, width = mine.shape
    for i, (gated, out) in enumerate(((mine, mine_out), (other, other_out))):
        squares = jnp.zeros((rows, width), F32)
        for block in range(blocks):
            value = gated[block].astype(F32)
            squares = squares + value * value
        scale = lax.rsqrt(jnp.sum(squares, axis=1, keepdims=True) / (blocks * width) + NORM_EPS)
        out[...] = (result[i * rows : (i + 1) * rows] * scale).astype(BF16)


def call(body, outs, scratch=(), vmem=48, flops=10**7, **kw):
    return pl.pallas_call(
        body,
        out_shape=outs,
        scratch_shapes=list(scratch),
        compiler_params=pltpu.CompilerParams(vmem_limit_bytes=vmem << 20),
        cost_estimate=pl.CostEstimate(flops=flops, bytes_accessed=1 << 21, transcendentals=1 << 17),
        **kw,
    )


def local(
    tokens, w_zx, w_bc, w_dt, dt_bias, a_rate, d_skip, conv_x, conv_bc, norm_gain, w_out, segments
):
    tok_rows, feat = tokens.shape
    width = w_zx.shape[2]
    heads = dt_bias.shape[0]
    head_w = width // heads
    state_w = w_bc.shape[1] // 2
    model = w_zx.shape[1]
    n_seq, n_tensor = lax.axis_size("seq"), lax.axis_size("tensor")
    seq_at = lax.axis_index("seq")
    rows = tok_rows // 2
    shape = lambda *s, kind=F32: jax.ShapeDtypeStruct(s, kind)

    spread = lambda v: jnp.repeat(v, head_w, axis=-1)
    expand = np.repeat(np.eye(heads, dtype=np.float32), head_w, axis=1)
    w_step = jnp.dot(w_dt, expand.astype(BF16))
    block = tokens.T
    core = seq_at % 2
    columns = model // 2
    own = (lax.dynamic_slice_in_dim(w_out, core * columns, columns, 1).astype(F32) * norm_gain[:, None]).astype(BF16)
    last = n_tensor // 2
    w_half = width // 2
    shift_rows = [(i, i + 1) for i in range(n_seq - 1)]

    seg_halo = lax.ppermute(segments[tok_rows - HALO :], "seq", shift_rows)
    seg_all = jnp.concatenate([seg_halo, segments])[:, None]
    small = (
        (seg_all[: HALO + rows], seg_all[rows:]),
        (segments[None, :rows], segments[None, rows:]),
        (segments[None, :1], segments[None, tok_rows - 1 :]),
        (spread(dt_bias)[None], spread(a_rate)[None], spread(d_skip)[None]),
    )

    forth = back = block
    arrived, projs = [(0, block)], []
    for step in range(1, last + 1):
        if step == 3:
            forth, back = after(forth, projs[1], small), after(back, projs[1], small)
        elif step > 1:
            forth, back = after(forth, projs[step - 2]), after(back, projs[step - 2])
        arrivals = (forth, back)
        if step < last:
            forth, back = ring_shift(forth, 1), ring_shift(back, -1)
        else:
            far = far_shift(forth, back)
        if step == W_FIRST:
            w_forth, w_back = after((own, own), arrivals)
            w_forth, w_back = ring_shift(w_forth, 1), ring_shift(w_back, -1)
        ahead = last if step == last else 0
        total = projs[-1:]
        fetched = len(arrived) + bool(ahead)
        outs = [shape(tok_rows, 4 * width)] + [shape(feat, 4 * width, kind=BF16)] * bool(ahead)
        results = call(
            functools.partial(project, [distance for distance, _ in arrived], ahead, not total),
            outs,
            [pltpu.VMEM((len(arrived), feat, 4 * width), BF16), pltpu.SemaphoreType.DMA((fetched, 4))],
            in_specs=[VMEM] * len(arrived) + [ANY] * 3 + [VMEM] * len(total),
            flops=10**9,
        )(*[part for _, part in arrived], w_zx, w_bc, w_step, *total)
        projs.append(results[0])
        arrived = [(-step, forth), (step, back)]
    proj = call(project_far, shape(tok_rows, 4 * width), flops=10**9)(
        *far, results[1], projs[-1]
    )

    (seg_ext_a, seg_ext_b), (seg_row_a, seg_row_b), (seg_first, seg_last), (bias, rate, skip) = small
    halo = lax.ppermute(proj[tok_rows - HALO :, width : 3 * width].astype(BF16), "seq", shift_rows)

    msg_rows = state_w + 8
    plane = shape(rows, width)
    ext = pltpu.VMEM((HALO + rows, width), F32)
    out_b, bc_b, enter_b, state_b, gate_b = call(
        functools.partial(later_block, heads, width, rows),
        [plane, plane, plane, shape(msg_rows, width), plane],
        [ext, ext],
    )(proj, seg_ext_b, seg_row_b, conv_x, conv_bc, bias, rate, skip)
    cx_a, bc_a, cum_a, scaled_a, enter_a, state_a, message = call(
        functools.partial(first_front, width, rows),
        [plane] * 5 + [shape(msg_rows, width)] * 2,
        [ext, ext],
    )(proj, halo, seg_ext_a, seg_last, state_b, conv_x, conv_bc, bias, rate)
    messages = lax.all_gather(message, "seq")
    gated = call(functools.partial(finish, heads, rows), shape(tok_rows, width, kind=BF16))(
        seg_first, messages, seg_ext_a, seg_row_a, skip, proj, cx_a, bc_a, cum_a, scaled_a, enter_a, state_a,
        out_b, gate_b, bc_b, enter_b
    )
    tok_own = tok_rows // n_tensor

    w_steps = [(w_forth, w_back)]
    orders = [proj, messages]
    for step in range(2, last + 1):
        if step - 2 < len(orders):
            w_forth, w_back = after((w_forth, w_back), orders[step - 2])
        if step == 4:
            w_forth, w_back = after((w_forth, w_back), mine)
        if step == last:
            w_far = far_shift(w_forth, w_back)
            break
        w_forth, w_back = ring_shift(w_forth, 1), ring_shift(w_back, -1)
        w_steps.append((w_forth, w_back))
        if step == 2:
            blocks = after(gated, w_forth, w_back).reshape(n_tensor, tok_own, width)
            mine = lax.all_to_all(blocks, "tensor", 0, 0)
    swap = [(i, i ^ 1) for i in range(n_seq)]
    other = lax.ppermute(mine, "seq", swap)
    pieces, distances = [own], [0]
    for i, pair in enumerate(w_steps):
        pieces += pair
        distances += [-i - 1, i + 1]
    total = call(functools.partial(product_early, distances), shape(2 * tok_own, columns), flops=10**9)(
        mine, other, *pieces
    )
    half = shape(tok_own, columns, kind=BF16)
    out_own, out_other = call(
        functools.partial(product_last, last), [half, half], [pltpu.VMEM((width, columns), BF16)], flops=10**8
    )(mine, other, total, *w_far)
    arrived = lax.ppermute(out_other, "seq", swap)
    is_first = core == 0
    return jnp.concatenate([jnp.where(is_first, out_own, arrived), jnp.where(is_first, arrived, out_own)], 1)


def solution(mesh):
    in_specs = (
        P("seq", "tensor"),
        P(None, None, "tensor"),
        P(),
        P(None, "tensor"),
        P("tensor"),
        P("tensor"),
        P("tensor"),
        P(None, "tensor"),
        P(),
        P("tensor"),
        P("tensor", None),
        P("seq"),
    )
    out_specs = P(("seq", "tensor"), None)
    return jax.shard_map(local, mesh=mesh, in_specs=in_specs, out_specs=out_specs, check_vma=False)
```

```python
import functools

import jax
import jax.numpy as jnp
import numpy as np
from jax import lax
from jax.experimental import pallas as pl
from jax.experimental.pallas import tpu as pltpu
from jax.sharding import PartitionSpec as P

NORM_EPS = 1e-05
F32 = jnp.float32
BF16 = jnp.bfloat16
VMEM = pl.BlockSpec(memory_space=pltpu.VMEM)
ANY = pl.BlockSpec(memory_space=pl.ANY)
HALO = 8


def ring_place(index, n):
    return jnp.where(index % 2 == 0, index // 2, (2 * n - 1 - index) // 2)


def ring_index(place, n):
    return jnp.where(place < n // 2, 2 * place, 2 * n - 1 - 2 * place)


def ring_shift(block, step):
    n = lax.axis_size("tensor")
    order = [2 * i if i < n // 2 else 2 * n - 1 - 2 * i for i in range(n)]
    return lax.ppermute(block, "tensor", [(order[i], order[(i + step) % n]) for i in range(n)])


def after(values, *earlier):
    return lax.optimization_barrier((values, earlier))[0]


def far_shift(forth, back):
    cut = forth.shape[0] // 32 * 16
    parts = [jax.ShapeDtypeStruct((size, forth.shape[1]), forth.dtype) for size in (cut, forth.shape[0] - cut)]
    top, bottom = call(halves, parts)(forth, back)
    return ring_shift(top, 1), ring_shift(bottom, -1)


def halves(forth, back, top, bottom):
    size = top.shape[0]
    top[...] = forth[:size]
    bottom[...] = back[size:]


def silu(v):
    return v / (1.0 + jnp.exp(-v))


def dot(a, b, dims=((1,), (0,))):
    return lax.dot_general(a.astype(BF16), b.astype(BF16), (dims, ((), ())), preferred_element_type=F32)


def source_of(distance):
    n = lax.axis_size("tensor")
    return ring_index((ring_place(lax.axis_index("tensor"), n) + distance + n) % n, n)


def join(*refs):
    count = len(refs) // 3
    odd = lax.axis_index("seq") // 2 % 2
    for own, other, out in zip(refs[:count], refs[count : 2 * count], refs[2 * count :]):
        size = own.shape[0]
        out[pl.ds(pl.multiple_of(odd * size, size), size)] = own[...]
        out[pl.ds(pl.multiple_of((1 - odd) * size, size), size)] = other[...]


def project(distances, ahead, first, *refs):
    count, fetched = len(distances), len(distances) + bool(ahead)
    blocks, (w_zx, w_bc, w_dt), refs = refs[:count], refs[count : count + 3], refs[count + 3 :]
    total, refs = (None, refs) if first else (refs[0], refs[1:])
    out, far_out, held, sems = refs if ahead else (refs[0], None, *refs[1:])
    feat, width = held.shape[1], w_bc.shape[1]
    sources = [w_zx.at[0], w_zx.at[1], w_bc, w_dt]
    copies = []
    for k, distance in enumerate([*distances, ahead][:fetched]):
        rows = pl.ds(pl.multiple_of(source_of(distance) * feat, 16), feat)
        for j, source in enumerate(sources):
            target = held.at[k] if k < count else far_out
            copies.append(
                pltpu.make_async_copy(source.at[rows], target.at[:, pl.ds(j * width, width)], sems.at[k, j])
            )
            copies[-1].start()
    result = 0.0 if first else total[...]
    for k in range(count):
        for j in range(len(sources)):
            copies[k * len(sources) + j].wait()
        result = result + dot(blocks[k][...], held[k], ((0,), (0,)))
    out[...] = result
    for copy in copies[count * len(sources) :]:
        copy.wait()


def project_far(top, bottom, weights, total, out):
    cut = top.shape[0]
    out[...] = (
        total[...] + dot(top[...], weights[:cut], ((0,), (0,))) + dot(bottom[...], weights[cut:], ((0,), (0,)))
    )


def conv(ext, seg_ext, taps, rows):
    size = taps.shape[0]
    seg_now = seg_ext[HALO : HALO + rows]
    total = taps[size - 1 : size] * ext[HALO : HALO + rows]
    for offset in range(1, size):
        same = seg_ext[HALO - offset : HALO - offset + rows] == seg_now
        total = total + taps[size - 1 - offset : size - offset] * jnp.where(
            same, ext[HALO - offset : HALO - offset + rows], 0.0
        )
    return silu(total)


def prefix_sum(values):
    rows = values.shape[0]
    lower = lax.broadcasted_iota(jnp.int32, (rows, rows), 0) >= lax.broadcasted_iota(jnp.int32, (rows, rows), 1)
    lower = jnp.where(lower, 1.0, 0.0).astype(BF16)
    total = jnp.zeros(values.shape, F32)
    rest = values
    parts = []
    for _ in range(3):
        part = rest.astype(BF16)
        parts.append(part)
        rest = rest - part.astype(F32)
    for part in reversed(parts):
        total = total + jnp.dot(lower, part, preferred_element_type=F32)
    return total


def block_front(ext_x, ext_bc, seg_ext, dt_raw, taps_x, taps_bc, bias, rate, rows, seg_enter, seg_leave):
    conv_x = conv(ext_x, seg_ext, taps_x, rows)
    conv_bc = conv(ext_bc, seg_ext, taps_bc, rows)
    seg = seg_ext[HALO : HALO + rows]
    shifted = dt_raw + bias
    step_size = jnp.maximum(shifted, 0.0) + jnp.log1p(jnp.exp(-jnp.abs(shifted)))
    cum = prefix_sum(-rate * step_size)
    scaled = conv_x * step_size
    last = cum[rows - 1 : rows]
    tail = jnp.where(seg == seg_leave, jnp.exp(last - cum), 0.0)
    state_w = conv_bc.shape[1] // 2
    state = dot(conv_bc, tail * scaled, ((0,), (0,)))[:state_w]
    enter = jnp.where(seg == seg_enter, jnp.exp(cum), 0.0)
    return conv_x, conv_bc, cum, scaled, state, enter, last


def block_inner(conv_bc, cum, scaled, seg_col, seg_row, heads):
    rows, width = scaled.shape
    state_w = conv_bc.shape[1] // 2
    head_w = width // heads
    scores = dot(conv_bc[:, state_w:], conv_bc[:, :state_w], ((1,), (1,)))
    later = lax.broadcasted_iota(jnp.int32, (rows, rows), 0) >= lax.broadcasted_iota(jnp.int32, (rows, rows), 1)
    visible = (seg_col == seg_row) & later
    cum_rows = cum.T
    lane = lax.broadcasted_iota(jnp.int32, (rows, width), 1)
    result = jnp.zeros((rows, width), F32)
    scaled = scaled.astype(BF16)
    for head in range(heads):
        at = head * head_w
        gap = jnp.where(visible, cum[:, at : at + 1] - cum_rows[at : at + 1, :], -jnp.inf)
        part = dot(jnp.exp(gap) * scores, scaled)
        result = jnp.where((lane >= at) & (lane < at + head_w), part, result)
    return result


def later_block(heads, width, rows, proj, seg_ext, seg_row, taps_x, taps_bc, bias, rate, skip,
                out, bc_out, enter_out, state_out, gate_out, ext_x, ext_bc):
    rounded = proj[rows - HALO :, : 3 * width].astype(BF16).astype(F32)
    gate_out[...] = silu(rounded[HALO:, :width])
    ext_x[...] = rounded[:, width : 2 * width]
    ext_bc[...] = rounded[:, 2 * width : 3 * width]
    seg_enter = seg_ext[HALO - 1 : HALO]
    seg_leave = seg_ext[HALO + rows - 1 : HALO + rows]
    conv_x, conv_bc, cum, scaled, state, enter, last = block_front(
        ext_x, ext_bc, seg_ext, proj[rows:, 3 * width :], taps_x, taps_bc[...], bias[...], rate[...], rows, seg_enter, seg_leave
    )
    out[...] = block_inner(conv_bc, cum, scaled, seg_ext[HALO:], seg_row[...], heads) + skip[...] * conv_x
    bc_out[...] = conv_bc
    enter_out[...] = enter
    keep = jnp.where(seg_enter == seg_leave, jnp.exp(last), 0.0)
    state_w = state.shape[0]
    state_out[:state_w] = state
    state_out[state_w : state_w + 1] = keep
    state_out[state_w + 1 : state_w + 2] = last
    state_out[state_w + 2 :] = jnp.zeros((state_out.shape[0] - state_w - 2, width), F32)


def first_front(width, rows, proj, halo, seg_ext, seg_last, state_b, taps_x, taps_bc, bias, rate,
                conv_out, bc_out, cum_out, scaled_out, enter_out, state_out, message, ext_x, ext_bc):
    ext_x[:HALO] = halo[:, :width].astype(F32)
    ext_bc[:HALO] = halo[:, width:].astype(F32)
    ext_x[HALO:] = proj[:rows, width : 2 * width].astype(BF16).astype(F32)
    ext_bc[HALO:] = proj[:rows, 2 * width : 3 * width].astype(BF16).astype(F32)
    seg_enter = seg_ext[HALO : HALO + 1]
    seg_leave = seg_ext[HALO + rows - 1 : HALO + rows]
    conv_x, conv_bc, cum, scaled, state, enter, last = block_front(
        ext_x, ext_bc, seg_ext, proj[:rows, 3 * width :], taps_x, taps_bc[...], bias[...], rate[...], rows, seg_enter, seg_leave
    )
    conv_out[...] = conv_x
    bc_out[...] = conv_bc
    cum_out[...] = cum
    scaled_out[...] = scaled
    enter_out[...] = enter
    keep = jnp.where(seg_enter == seg_leave, jnp.exp(last), 0.0)
    state_w = state.shape[0]
    state_out[:state_w] = state
    state_out[state_w : state_w + 1] = keep
    state_out[state_w + 1 :] = jnp.zeros((state_out.shape[0] - state_w - 1, width), F32)
    message[:state_w] = state_b[state_w : state_w + 1] * state + state_b[:state_w]
    message[state_w : state_w + 1] = last + state_b[state_w + 1 : state_w + 2]
    message[state_w + 1 : state_w + 2] = jnp.broadcast_to(seg_last[...].astype(F32), (1, width))
    message[state_w + 2 :] = jnp.zeros((message.shape[0] - state_w - 2, width), F32)


def finish(heads, rows, seg_first, messages, seg_ext_a, seg_row_a, skip, proj, conv_a, bc_a, cum_a, scaled_a, enter_a,
           state_a, out_b, gate_b, bc_b, enter_b, gated):
    state_w = bc_a.shape[1] // 2
    width = out_b.shape[1]
    entering = jnp.zeros((state_w, width), F32)
    decay = jnp.zeros((1, width), F32)
    first = seg_first[...].astype(F32)
    place = lax.axis_index("seq")
    for device in reversed(range(messages.shape[0] - 1)):
        earlier = device < place
        passes = earlier & (messages[device, state_w + 1 : state_w + 2] == first)
        passes = jnp.where(passes, jnp.exp(decay), 0.0)
        entering = entering + passes * messages[device, :state_w]
        decay = decay + jnp.where(earlier, messages[device, state_w : state_w + 1], 0.0)
    second = state_a[state_w : state_w + 1] * entering + state_a[:state_w]
    out_a = block_inner(bc_a[...], cum_a[...], scaled_a[...], seg_ext_a[HALO:], seg_row_a[...], heads)
    out_a = out_a + skip[...] * conv_a[...] + enter_a[...] * dot(bc_a[:, state_w:], entering)
    gated[:rows] = (out_a * silu(proj[:rows, :width].astype(BF16).astype(F32))).astype(BF16)
    gated[rows:] = ((out_b[...] + enter_b[...] * dot(bc_b[:, state_w:], second)) * gate_b[...]).astype(BF16)


def product(gated, distances, pieces):
    total = 0.0
    for distance, piece in zip(distances, pieces):
        source = source_of(distance)
        rows = jnp.concatenate([part[source] for part in gated], 0)
        total = total + jnp.dot(rows, piece[...], preferred_element_type=F32)
    return total


def product_early(distances, mine, other, *rest):
    rest[-1][...] = product((mine, other), distances, rest[:-1])


def product_last(distance, mine, other, total, top, bottom, mine_out, other_out, held):
    held[: top.shape[0]] = top[...]
    held[top.shape[0] :] = bottom[...]
    result = product((mine, other), [distance], [held]) + total[...]
    blocks, rows, width = mine.shape
    for i, (gated, out) in enumerate(((mine, mine_out), (other, other_out))):
        squares = jnp.zeros((rows, width), F32)
        for block in range(blocks):
            value = gated[block].astype(F32)
            squares = squares + value * value
        scale = lax.rsqrt(jnp.sum(squares, axis=1, keepdims=True) / (blocks * width) + NORM_EPS)
        out[...] = (result[i * rows : (i + 1) * rows] * scale).astype(BF16)


def call(body, outs, scratch=(), vmem=48, flops=10**7, **kw):
    return pl.pallas_call(
        body,
        out_shape=outs,
        scratch_shapes=list(scratch),
        compiler_params=pltpu.CompilerParams(vmem_limit_bytes=vmem << 20),
        cost_estimate=pl.CostEstimate(flops=flops, bytes_accessed=1 << 21, transcendentals=1 << 17),
        **kw,
    )


def local(
    tokens, w_zx, w_bc, w_dt, dt_bias, a_rate, d_skip, conv_x, conv_bc, norm_gain, w_out, segments
):
    tok_rows, feat = tokens.shape
    width = w_zx.shape[2]
    heads = dt_bias.shape[0]
    head_w = width // heads
    state_w = w_bc.shape[1] // 2
    model = w_zx.shape[1]
    n_seq, n_tensor = lax.axis_size("seq"), lax.axis_size("tensor")
    seq_at = lax.axis_index("seq")
    rows = tok_rows // 2
    shape = lambda *s, kind=F32: jax.ShapeDtypeStruct(s, kind)

    spread = lambda v: jnp.repeat(v, head_w, axis=-1)
    expand = np.repeat(np.eye(heads, dtype=np.float32), head_w, axis=1)
    w_step = jnp.dot(w_dt, expand.astype(BF16))
    block = tokens.T
    core = seq_at % 2
    columns = model // 2
    own = (lax.dynamic_slice_in_dim(w_out, core * columns, columns, 1).astype(F32) * norm_gain[:, None]).astype(BF16)
    last = n_tensor // 2
    w_half = width // 2
    own_rows = lax.dynamic_slice_in_dim(own, seq_at // 2 % 2 * w_half, w_half, 0)
    other_y = [(i, i ^ 2) for i in range(n_seq)]
    shift_rows = [(i, i + 1) for i in range(n_seq - 1)]

    seg_halo = lax.ppermute(segments[tok_rows - HALO :], "seq", shift_rows)
    seg_all = jnp.concatenate([seg_halo, segments])[:, None]
    small = (
        (seg_all[: HALO + rows], seg_all[rows:]),
        (segments[None, :rows], segments[None, rows:]),
        (segments[None, :1], segments[None, tok_rows - 1 :]),
        (spread(dt_bias)[None], spread(a_rate)[None], spread(d_skip)[None]),
    )

    forth = back = block
    arrived, projs = [(0, block)], []
    for step in range(1, last + 1):
        if step == 3:
            forth, back = after(forth, projs[1], small), after(back, projs[1], small)
        elif step > 1:
            forth, back = after(forth, projs[step - 2]), after(back, projs[step - 2])
        arrivals = (forth, back)
        if step < last:
            forth, back = ring_shift(forth, 1), ring_shift(back, -1)
        else:
            far = far_shift(forth, back)
        if step == 2:
            w_near = after(own_rows, arrivals)
            w_near = ring_shift(w_near, 1), ring_shift(w_near, -1)
        if step == 3:
            w_other = [lax.ppermute(part, "seq", other_y) for part in after(w_near, arrivals)]
        ahead = last if step == last else 0
        total = projs[-1:]
        if step == last:
            total = [after(projs[-1], w_other)]
        fetched = len(arrived) + bool(ahead)
        outs = [shape(tok_rows, 4 * width)] + [shape(feat, 4 * width, kind=BF16)] * bool(ahead)
        results = call(
            functools.partial(project, [distance for distance, _ in arrived], ahead, not total),
            outs,
            [pltpu.VMEM((len(arrived), feat, 4 * width), BF16), pltpu.SemaphoreType.DMA((fetched, 4))],
            in_specs=[VMEM] * len(arrived) + [ANY] * 3 + [VMEM] * len(total),
            flops=10**9,
        )(*[part for _, part in arrived], w_zx, w_bc, w_step, *total)
        projs.append(results[0])
        arrived = [(-step, forth), (step, back)]
    whole = shape(width, columns, kind=BF16)
    w_forth, w_back = call(join, [whole, whole])(*after(w_near, projs[-1]), *w_other)
    proj = call(project_far, shape(tok_rows, 4 * width), flops=10**9)(
        *far, results[1], projs[-1]
    )

    (seg_ext_a, seg_ext_b), (seg_row_a, seg_row_b), (seg_first, seg_last), (bias, rate, skip) = small
    halo = lax.ppermute(proj[tok_rows - HALO :, width : 3 * width].astype(BF16), "seq", shift_rows)

    msg_rows = state_w + 8
    plane = shape(rows, width)
    ext = pltpu.VMEM((HALO + rows, width), F32)
    out_b, bc_b, enter_b, state_b, gate_b = call(
        functools.partial(later_block, heads, width, rows),
        [plane, plane, plane, shape(msg_rows, width), plane],
        [ext, ext],
    )(proj, seg_ext_b, seg_row_b, conv_x, conv_bc, bias, rate, skip)
    cx_a, bc_a, cum_a, scaled_a, enter_a, state_a, message = call(
        functools.partial(first_front, width, rows),
        [plane] * 5 + [shape(msg_rows, width)] * 2,
        [ext, ext],
    )(proj, halo, seg_ext_a, seg_last, state_b, conv_x, conv_bc, bias, rate)
    messages = lax.all_gather(message, "seq")
    gated = call(functools.partial(finish, heads, rows), shape(tok_rows, width, kind=BF16))(
        seg_first, messages, seg_ext_a, seg_row_a, skip, proj, cx_a, bc_a, cum_a, scaled_a, enter_a, state_a,
        out_b, gate_b, bc_b, enter_b
    )
    tok_own = tok_rows // n_tensor

    w_steps = [(w_forth, w_back)]
    orders = [proj, messages]
    for step in range(2, last + 1):
        if step - 2 < len(orders):
            w_forth, w_back = after((w_forth, w_back), orders[step - 2])
        if step == 4:
            w_forth, w_back = after((w_forth, w_back), mine)
        if step == last:
            w_far = far_shift(w_forth, w_back)
            break
        w_forth, w_back = ring_shift(w_forth, 1), ring_shift(w_back, -1)
        w_steps.append((w_forth, w_back))
        if step == 2:
            blocks = after(gated, w_forth, w_back).reshape(n_tensor, tok_own, width)
            mine = lax.all_to_all(blocks, "tensor", 0, 0)
    swap = [(i, i ^ 1) for i in range(n_seq)]
    other = lax.ppermute(mine, "seq", swap)
    pieces, distances = [own], [0]
    for i, pair in enumerate(w_steps):
        pieces += pair
        distances += [-i - 1, i + 1]
    total = call(functools.partial(product_early, distances), shape(2 * tok_own, columns), flops=10**9)(
        mine, other, *pieces
    )
    half = shape(tok_own, columns, kind=BF16)
    out_own, out_other = call(
        functools.partial(product_last, last), [half, half], [pltpu.VMEM((width, columns), BF16)], flops=10**8
    )(mine, other, total, *w_far)
    arrived = lax.ppermute(out_other, "seq", swap)
    is_first = core == 0
    return jnp.concatenate([jnp.where(is_first, out_own, arrived), jnp.where(is_first, arrived, out_own)], 1)


def solution(mesh):
    in_specs = (
        P("seq", "tensor"),
        P(None, None, "tensor"),
        P(),
        P(None, "tensor"),
        P("tensor"),
        P("tensor"),
        P("tensor"),
        P(None, "tensor"),
        P(),
        P("tensor"),
        P("tensor", None),
        P("seq"),
    )
    out_specs = P(("seq", "tensor"), None)
    return jax.shard_map(local, mesh=mesh, in_specs=in_specs, out_specs=out_specs, check_vma=False)
```

```python
import functools

import jax
import jax.numpy as jnp
import numpy as np
from jax import lax
from jax.experimental import pallas as pl
from jax.experimental.pallas import tpu as pltpu
from jax.sharding import PartitionSpec as P

NORM_EPS = 1e-05
F32 = jnp.float32
BF16 = jnp.bfloat16
VMEM = pl.BlockSpec(memory_space=pltpu.VMEM)
ANY = pl.BlockSpec(memory_space=pl.ANY)
HALO = 8
W_FIRST = 3


def ring_place(index, n):
    return jnp.where(index % 2 == 0, index // 2, (2 * n - 1 - index) // 2)


def ring_index(place, n):
    return jnp.where(place < n // 2, 2 * place, 2 * n - 1 - 2 * place)


def ring_shift(block, step):
    n = lax.axis_size("tensor")
    order = [2 * i if i < n // 2 else 2 * n - 1 - 2 * i for i in range(n)]
    return lax.ppermute(block, "tensor", [(order[i], order[(i + step) % n]) for i in range(n)])


def after(values, *earlier):
    return lax.optimization_barrier((values, earlier))[0]


def far_shift(forth, back):
    cut = forth.shape[0] // 32 * 16
    parts = [jax.ShapeDtypeStruct((size, forth.shape[1]), forth.dtype) for size in (cut, forth.shape[0] - cut)]
    top, bottom = call(halves, parts)(forth, back)
    return ring_shift(top, 1), ring_shift(bottom, -1)


def halves(forth, back, top, bottom):
    size = top.shape[0]
    top[...] = forth[:size]
    bottom[...] = back[size:]


def silu(v):
    return v / (1.0 + jnp.exp(-v))


def dot(a, b, dims=((1,), (0,))):
    return lax.dot_general(a.astype(BF16), b.astype(BF16), (dims, ((), ())), preferred_element_type=F32)


def source_of(distance):
    n = lax.axis_size("tensor")
    return ring_index((ring_place(lax.axis_index("tensor"), n) + distance + n) % n, n)


def project(distances, ahead, first, *refs):
    count, fetched = len(distances), len(distances) + bool(ahead)
    blocks, (w_zx, w_bc, w_dt), refs = refs[:count], refs[count : count + 3], refs[count + 3 :]
    total, refs = (None, refs) if first else (refs[0], refs[1:])
    out, far_out, held, sems = refs if ahead else (refs[0], None, *refs[1:])
    feat, width = held.shape[1], w_bc.shape[1]
    sources = [w_zx.at[0], w_zx.at[1], w_bc, w_dt]
    copies = []
    for k, distance in enumerate([*distances, ahead][:fetched]):
        rows = pl.ds(pl.multiple_of(source_of(distance) * feat, 16), feat)
        for j, source in enumerate(sources):
            target = held.at[k] if k < count else far_out
            copies.append(
                pltpu.make_async_copy(source.at[rows], target.at[:, pl.ds(j * width, width)], sems.at[k, j])
            )
            copies[-1].start()
    result = 0.0 if first else total[...]
    for k in range(count):
        for j in range(len(sources)):
            copies[k * len(sources) + j].wait()
        result = result + dot(blocks[k][...], held[k], ((0,), (0,)))
    out[...] = result
    for copy in copies[count * len(sources) :]:
        copy.wait()


def project_far(top, bottom, weights, total, out):
    cut = top.shape[0]
    out[...] = (
        total[...] + dot(top[...], weights[:cut], ((0,), (0,))) + dot(bottom[...], weights[cut:], ((0,), (0,)))
    )


def conv(ext, seg_ext, taps, rows):
    size = taps.shape[0]
    seg_now = seg_ext[HALO : HALO + rows]
    total = taps[size - 1 : size] * ext[HALO : HALO + rows]
    for offset in range(1, size):
        same = seg_ext[HALO - offset : HALO - offset + rows] == seg_now
        total = total + taps[size - 1 - offset : size - offset] * jnp.where(
            same, ext[HALO - offset : HALO - offset + rows], 0.0
        )
    return silu(total)


def prefix_sum(values):
    rows = values.shape[0]
    lower = lax.broadcasted_iota(jnp.int32, (rows, rows), 0) >= lax.broadcasted_iota(jnp.int32, (rows, rows), 1)
    lower = jnp.where(lower, 1.0, 0.0).astype(BF16)
    total = jnp.zeros(values.shape, F32)
    rest = values
    parts = []
    for _ in range(3):
        part = rest.astype(BF16)
        parts.append(part)
        rest = rest - part.astype(F32)
    for part in reversed(parts):
        total = total + jnp.dot(lower, part, preferred_element_type=F32)
    return total


def block_front(ext_x, ext_bc, seg_ext, dt_raw, taps_x, taps_bc, bias, rate, rows, seg_enter, seg_leave):
    conv_x = conv(ext_x, seg_ext, taps_x, rows)
    conv_bc = conv(ext_bc, seg_ext, taps_bc, rows)
    seg = seg_ext[HALO : HALO + rows]
    shifted = dt_raw + bias
    step_size = jnp.maximum(shifted, 0.0) + jnp.log1p(jnp.exp(-jnp.abs(shifted)))
    cum = prefix_sum(-rate * step_size)
    scaled = conv_x * step_size
    last = cum[rows - 1 : rows]
    tail = jnp.where(seg == seg_leave, jnp.exp(last - cum), 0.0)
    state_w = conv_bc.shape[1] // 2
    state = dot(conv_bc, tail * scaled, ((0,), (0,)))[:state_w]
    enter = jnp.where(seg == seg_enter, jnp.exp(cum), 0.0)
    return conv_x, conv_bc, cum, scaled, state, enter, last


def block_inner(conv_bc, cum, scaled, seg_col, seg_row, heads):
    rows, width = scaled.shape
    state_w = conv_bc.shape[1] // 2
    head_w = width // heads
    scores = dot(conv_bc[:, state_w:], conv_bc[:, :state_w], ((1,), (1,)))
    later = lax.broadcasted_iota(jnp.int32, (rows, rows), 0) >= lax.broadcasted_iota(jnp.int32, (rows, rows), 1)
    visible = (seg_col == seg_row) & later
    cum_rows = cum.T
    lane = lax.broadcasted_iota(jnp.int32, (rows, width), 1)
    result = jnp.zeros((rows, width), F32)
    scaled = scaled.astype(BF16)
    for head in range(heads):
        at = head * head_w
        gap = jnp.where(visible, cum[:, at : at + 1] - cum_rows[at : at + 1, :], -jnp.inf)
        part = dot(jnp.exp(gap) * scores, scaled)
        result = jnp.where((lane >= at) & (lane < at + head_w), part, result)
    return result


def later_block(heads, width, rows, proj, seg_ext, seg_row, taps_x, taps_bc, bias, rate, skip,
                out, bc_out, enter_out, state_out, gate_out, ext_x, ext_bc):
    rounded = proj[rows - HALO :, : 3 * width].astype(BF16).astype(F32)
    gate_out[...] = silu(rounded[HALO:, :width])
    ext_x[...] = rounded[:, width : 2 * width]
    ext_bc[...] = rounded[:, 2 * width : 3 * width]
    seg_enter = seg_ext[HALO - 1 : HALO]
    seg_leave = seg_ext[HALO + rows - 1 : HALO + rows]
    conv_x, conv_bc, cum, scaled, state, enter, last = block_front(
        ext_x, ext_bc, seg_ext, proj[rows:, 3 * width :], taps_x, taps_bc[...], bias[...], rate[...], rows, seg_enter, seg_leave
    )
    out[...] = block_inner(conv_bc, cum, scaled, seg_ext[HALO:], seg_row[...], heads) + skip[...] * conv_x
    bc_out[...] = conv_bc
    enter_out[...] = enter
    keep = jnp.where(seg_enter == seg_leave, jnp.exp(last), 0.0)
    state_w = state.shape[0]
    state_out[:state_w] = state
    state_out[state_w : state_w + 1] = keep
    state_out[state_w + 1 : state_w + 2] = last
    state_out[state_w + 2 :] = jnp.zeros((state_out.shape[0] - state_w - 2, width), F32)


def first_front(width, rows, proj, halo, seg_ext, seg_last, state_b, taps_x, taps_bc, bias, rate,
                conv_out, bc_out, cum_out, scaled_out, enter_out, state_out, message, ext_x, ext_bc):
    ext_x[:HALO] = halo[:, :width].astype(F32)
    ext_bc[:HALO] = halo[:, width:].astype(F32)
    ext_x[HALO:] = proj[:rows, width : 2 * width].astype(BF16).astype(F32)
    ext_bc[HALO:] = proj[:rows, 2 * width : 3 * width].astype(BF16).astype(F32)
    seg_enter = seg_ext[HALO : HALO + 1]
    seg_leave = seg_ext[HALO + rows - 1 : HALO + rows]
    conv_x, conv_bc, cum, scaled, state, enter, last = block_front(
        ext_x, ext_bc, seg_ext, proj[:rows, 3 * width :], taps_x, taps_bc[...], bias[...], rate[...], rows, seg_enter, seg_leave
    )
    conv_out[...] = conv_x
    bc_out[...] = conv_bc
    cum_out[...] = cum
    scaled_out[...] = scaled
    enter_out[...] = enter
    keep = jnp.where(seg_enter == seg_leave, jnp.exp(last), 0.0)
    state_w = state.shape[0]
    state_out[:state_w] = state
    state_out[state_w : state_w + 1] = keep
    state_out[state_w + 1 :] = jnp.zeros((state_out.shape[0] - state_w - 1, width), F32)
    message[:state_w] = state_b[state_w : state_w + 1] * state + state_b[:state_w]
    message[state_w : state_w + 1] = last + state_b[state_w + 1 : state_w + 2]
    message[state_w + 1 : state_w + 2] = jnp.broadcast_to(seg_last[...].astype(F32), (1, width))
    message[state_w + 2 :] = jnp.zeros((message.shape[0] - state_w - 2, width), F32)


def finish(heads, rows, seg_first, messages, seg_ext_a, seg_row_a, skip, proj, conv_a, bc_a, cum_a, scaled_a, enter_a,
           state_a, out_b, gate_b, bc_b, enter_b, gated):
    state_w = bc_a.shape[1] // 2
    width = out_b.shape[1]
    entering = jnp.zeros((state_w, width), F32)
    decay = jnp.zeros((1, width), F32)
    first = seg_first[...].astype(F32)
    place = lax.axis_index("seq")
    for device in reversed(range(messages.shape[0] - 1)):
        earlier = device < place
        passes = earlier & (messages[device, state_w + 1 : state_w + 2] == first)
        passes = jnp.where(passes, jnp.exp(decay), 0.0)
        entering = entering + passes * messages[device, :state_w]
        decay = decay + jnp.where(earlier, messages[device, state_w : state_w + 1], 0.0)
    second = state_a[state_w : state_w + 1] * entering + state_a[:state_w]
    out_a = block_inner(bc_a[...], cum_a[...], scaled_a[...], seg_ext_a[HALO:], seg_row_a[...], heads)
    out_a = out_a + skip[...] * conv_a[...] + enter_a[...] * dot(bc_a[:, state_w:], entering)
    gated[:rows] = (out_a * silu(proj[:rows, :width].astype(BF16).astype(F32))).astype(BF16)
    gated[rows:] = ((out_b[...] + enter_b[...] * dot(bc_b[:, state_w:], second)) * gate_b[...]).astype(BF16)


def product(gated, distances, pieces):
    total = 0.0
    for distance, piece in zip(distances, pieces):
        source = source_of(distance)
        rows = jnp.concatenate([part[source] for part in gated], 0)
        total = total + jnp.dot(rows, piece[...], preferred_element_type=F32)
    return total


def product_early(distances, mine, other, *rest):
    rest[-1][...] = product((mine, other), distances, rest[:-1])


def product_last(distance, mine, other, total, top, bottom, mine_out, other_out, held):
    held[: top.shape[0]] = top[...]
    held[top.shape[0] :] = bottom[...]
    result = product((mine, other), [distance], [held]) + total[...]
    blocks, rows, width = mine.shape
    for i, (gated, out) in enumerate(((mine, mine_out), (other, other_out))):
        squares = jnp.zeros((rows, width), F32)
        for block in range(blocks):
            value = gated[block].astype(F32)
            squares = squares + value * value
        scale = lax.rsqrt(jnp.sum(squares, axis=1, keepdims=True) / (blocks * width) + NORM_EPS)
        out[...] = (result[i * rows : (i + 1) * rows] * scale).astype(BF16)


def call(body, outs, scratch=(), vmem=48, flops=10**7, moved=1 << 21, **kw):
    return pl.pallas_call(
        body,
        out_shape=outs,
        scratch_shapes=list(scratch),
        compiler_params=pltpu.CompilerParams(vmem_limit_bytes=vmem << 20),
        cost_estimate=pl.CostEstimate(flops=flops, bytes_accessed=moved, transcendentals=0),
        **kw,
    )


def local(
    tokens, w_zx, w_bc, w_dt, dt_bias, a_rate, d_skip, conv_x, conv_bc, norm_gain, w_out, segments
):
    tok_rows, feat = tokens.shape
    width = w_zx.shape[2]
    heads = dt_bias.shape[0]
    head_w = width // heads
    state_w = w_bc.shape[1] // 2
    model = w_zx.shape[1]
    n_seq, n_tensor = lax.axis_size("seq"), lax.axis_size("tensor")
    seq_at = lax.axis_index("seq")
    rows = tok_rows // 2
    shape = lambda *s, kind=F32: jax.ShapeDtypeStruct(s, kind)

    spread = lambda v: jnp.repeat(v, head_w, axis=-1)
    expand = np.repeat(np.eye(heads, dtype=np.float32), head_w, axis=1)
    w_step = jnp.dot(w_dt, expand.astype(BF16))
    block = tokens.T
    core = seq_at % 2
    columns = model // 2
    own = (lax.dynamic_slice_in_dim(w_out, core * columns, columns, 1).astype(F32) * norm_gain[:, None]).astype(BF16)
    last = n_tensor // 2
    w_half = width // 2
    shift_rows = [(i, i + 1) for i in range(n_seq - 1)]

    seg_halo = lax.ppermute(segments[tok_rows - HALO :], "seq", shift_rows)
    seg_all = jnp.concatenate([seg_halo, segments])[:, None]
    small = (
        (seg_all[: HALO + rows], seg_all[rows:]),
        (segments[None, :rows], segments[None, rows:]),
        (segments[None, :1], segments[None, tok_rows - 1 :]),
        (spread(dt_bias)[None], spread(a_rate)[None], spread(d_skip)[None]),
    )

    forth = back = block
    arrived, projs = [(0, block)], []
    for step in range(1, last + 1):
        if step == 3:
            forth, back = after(forth, projs[1], small), after(back, projs[1], small)
        elif step > 1:
            forth, back = after(forth, projs[step - 2]), after(back, projs[step - 2])
        arrivals = (forth, back)
        if step < last:
            forth, back = ring_shift(forth, 1), ring_shift(back, -1)
        else:
            far = far_shift(forth, back)
        if step == W_FIRST:
            w_forth, w_back = after((own, own), arrivals)
            w_forth, w_back = ring_shift(w_forth, 1), ring_shift(w_back, -1)
        ahead = last if step == last else 0
        total = projs[-1:]
        fetched = len(arrived) + bool(ahead)
        outs = [shape(tok_rows, 4 * width)] + [shape(feat, 4 * width, kind=BF16)] * bool(ahead)
        results = call(
            functools.partial(project, [distance for distance, _ in arrived], ahead, not total),
            outs,
            [pltpu.VMEM((len(arrived), feat, 4 * width), BF16), pltpu.SemaphoreType.DMA((fetched, 4))],
            in_specs=[VMEM] * len(arrived) + [ANY] * 3 + [VMEM] * len(total),
            flops=10**9,
        )(*[part for _, part in arrived], w_zx, w_bc, w_step, *total)
        projs.append(results[0])
        arrived = [(-step, forth), (step, back)]
    proj = call(project_far, shape(tok_rows, 4 * width), flops=10**9)(
        *far, results[1], projs[-1]
    )

    (seg_ext_a, seg_ext_b), (seg_row_a, seg_row_b), (seg_first, seg_last), (bias, rate, skip) = small
    halo = lax.ppermute(proj[tok_rows - HALO :, width : 3 * width].astype(BF16), "seq", shift_rows)

    msg_rows = state_w + 8
    plane = shape(rows, width)
    ext = pltpu.VMEM((HALO + rows, width), F32)
    out_b, bc_b, enter_b, state_b, gate_b = call(
        functools.partial(later_block, heads, width, rows),
        [plane, plane, plane, shape(msg_rows, width), plane],
        [ext, ext],
    )(proj, seg_ext_b, seg_row_b, conv_x, conv_bc, bias, rate, skip)
    cx_a, bc_a, cum_a, scaled_a, enter_a, state_a, message = call(
        functools.partial(first_front, width, rows),
        [plane] * 5 + [shape(msg_rows, width)] * 2,
        [ext, ext],
    )(proj, halo, seg_ext_a, seg_last, state_b, conv_x, conv_bc, bias, rate)
    messages = lax.all_gather(message, "seq")
    gated = call(functools.partial(finish, heads, rows), shape(tok_rows, width, kind=BF16))(
        seg_first, messages, seg_ext_a, seg_row_a, skip, proj, cx_a, bc_a, cum_a, scaled_a, enter_a, state_a,
        out_b, gate_b, bc_b, enter_b
    )
    tok_own = tok_rows // n_tensor

    w_steps = [(w_forth, w_back)]
    orders = [proj, messages]
    for step in range(2, last + 1):
        if step - 2 < len(orders):
            w_forth, w_back = after((w_forth, w_back), orders[step - 2])
        if step == last:
            w_far = far_shift(w_forth, w_back)
            break
        w_forth, w_back = ring_shift(w_forth, 1), ring_shift(w_back, -1)
        w_steps.append((w_forth, w_back))
        if step == 2:
            blocks = after(gated, w_forth, w_back).reshape(n_tensor, tok_own, width)
            mine = lax.all_to_all(blocks, "tensor", 0, 0)
    swap = [(i, i ^ 1) for i in range(n_seq)]
    other = lax.ppermute(mine, "seq", swap)
    pieces, distances = [own], [0]
    for i, pair in enumerate(w_steps):
        pieces += pair
        distances += [-i - 1, i + 1]
    total = call(functools.partial(product_early, distances), shape(2 * tok_own, columns), flops=1, moved=1)(
        mine, other, *pieces
    )
    half = shape(tok_own, columns, kind=BF16)
    out_own, out_other = call(
        functools.partial(product_last, last), [half, half], [pltpu.VMEM((width, columns), BF16)], flops=10**8
    )(mine, other, total, *w_far)
    arrived = lax.ppermute(out_other, "seq", swap)
    is_first = core == 0
    return jnp.concatenate([jnp.where(is_first, out_own, arrived), jnp.where(is_first, arrived, out_own)], 1)


def solution(mesh):
    in_specs = (
        P("seq", "tensor"),
        P(None, None, "tensor"),
        P(),
        P(None, "tensor"),
        P("tensor"),
        P("tensor"),
        P("tensor"),
        P(None, "tensor"),
        P(),
        P("tensor"),
        P("tensor", None),
        P("seq"),
    )
    out_specs = P(("seq", "tensor"), None)
    return jax.shard_map(local, mesh=mesh, in_specs=in_specs, out_specs=out_specs, check_vma=False)
```

```python
import functools

import jax
import jax.numpy as jnp
import numpy as np
from jax import lax
from jax.experimental import pallas as pl
from jax.experimental.pallas import tpu as pltpu
from jax.sharding import PartitionSpec as P

NORM_EPS = 1e-05
F32 = jnp.float32
BF16 = jnp.bfloat16
VMEM = pl.BlockSpec(memory_space=pltpu.VMEM)
ANY = pl.BlockSpec(memory_space=pl.ANY)
HALO = 8
W_FIRST = 3


def ring_place(index, n):
    return jnp.where(index % 2 == 0, index // 2, (2 * n - 1 - index) // 2)


def ring_index(place, n):
    return jnp.where(place < n // 2, 2 * place, 2 * n - 1 - 2 * place)


def ring_shift(block, step):
    n = lax.axis_size("tensor")
    order = [2 * i if i < n // 2 else 2 * n - 1 - 2 * i for i in range(n)]
    return lax.ppermute(block, "tensor", [(order[i], order[(i + step) % n]) for i in range(n)])


def after(values, *earlier):
    return lax.optimization_barrier((values, earlier))[0]


def far_shift(forth, back):
    cut = forth.shape[0] // 32 * 16
    parts = [jax.ShapeDtypeStruct((size, forth.shape[1]), forth.dtype) for size in (cut, forth.shape[0] - cut)]
    top, bottom = call(halves, parts)(forth, back)
    return ring_shift(top, 1), ring_shift(bottom, -1)


def halves(forth, back, top, bottom):
    size = top.shape[0]
    top[...] = forth[:size]
    bottom[...] = back[size:]


def silu(v):
    return v / (1.0 + jnp.exp(-v))


def dot(a, b, dims=((1,), (0,))):
    return lax.dot_general(a.astype(BF16), b.astype(BF16), (dims, ((), ())), preferred_element_type=F32)


def source_of(distance):
    n = lax.axis_size("tensor")
    return ring_index((ring_place(lax.axis_index("tensor"), n) + distance + n) % n, n)


def near_start(side, whole, near):
    odd = lax.axis_index("seq") // 2 % 2
    return pl.multiple_of((odd if side == 0 else 1 - odd) * (whole - near), 16)


def take_near(*refs):
    for side, (block, out) in enumerate(zip(refs[:2], refs[2:])):
        near = out.shape[0]
        out[...] = block[pl.ds(near_start(side, block.shape[0], near), near)]


def pass_on(*refs):
    for side, (near, lacked, half) in enumerate(zip(refs[:2], refs[2:4], refs[4:])):
        odd = lax.axis_index("seq") // 2 % 2
        high = odd if side == 0 else 1 - odd
        for out in (lacked, half):
            first = pl.multiple_of(high * (near.shape[0] - out.shape[0]), 16)
            out[...] = near[pl.ds(first, out.shape[0])]


def project(distances, ahead, first, *refs):
    count, fetched = len(distances), len(distances) + bool(ahead)
    blocks, (w_zx, w_bc, w_dt), refs = refs[:count], refs[count : count + 3], refs[count + 3 :]
    total, refs = (None, refs) if first else (refs[0], refs[1:])
    out, far_out, held, sems = refs if ahead else (refs[0], None, *refs[1:])
    feat, width = held.shape[1], w_bc.shape[1]
    sources = [w_zx.at[0], w_zx.at[1], w_bc, w_dt]
    copies = []
    for k, distance in enumerate([*distances, ahead][:fetched]):
        rows = pl.ds(pl.multiple_of(source_of(distance) * feat, 16), feat)
        for j, source in enumerate(sources):
            target = held.at[k] if k < count else far_out
            copies.append(
                pltpu.make_async_copy(source.at[rows], target.at[:, pl.ds(j * width, width)], sems.at[k, j])
            )
            copies[-1].start()
    result = 0.0 if first else total[...]
    for k in range(count):
        for j in range(len(sources)):
            copies[k * len(sources) + j].wait()
        result = result + dot(blocks[k][...], held[k], ((0,), (0,)))
    out[...] = result
    for copy in copies[count * len(sources) :]:
        copy.wait()


def project_far(top, bottom, weights, total, out):
    cut = top.shape[0]
    out[...] = (
        total[...] + dot(top[...], weights[:cut], ((0,), (0,))) + dot(bottom[...], weights[cut:], ((0,), (0,)))
    )


def conv(ext, seg_ext, taps, rows):
    size = taps.shape[0]
    seg_now = seg_ext[HALO : HALO + rows]
    total = taps[size - 1 : size] * ext[HALO : HALO + rows]
    for offset in range(1, size):
        same = seg_ext[HALO - offset : HALO - offset + rows] == seg_now
        total = total + taps[size - 1 - offset : size - offset] * jnp.where(
            same, ext[HALO - offset : HALO - offset + rows], 0.0
        )
    return silu(total)


def prefix_sum(values):
    rows = values.shape[0]
    lower = lax.broadcasted_iota(jnp.int32, (rows, rows), 0) >= lax.broadcasted_iota(jnp.int32, (rows, rows), 1)
    lower = jnp.where(lower, 1.0, 0.0).astype(BF16)
    total = jnp.zeros(values.shape, F32)
    rest = values
    parts = []
    for _ in range(3):
        part = rest.astype(BF16)
        parts.append(part)
        rest = rest - part.astype(F32)
    for part in reversed(parts):
        total = total + jnp.dot(lower, part, preferred_element_type=F32)
    return total


def block_front(ext_x, ext_bc, seg_ext, dt_raw, taps_x, taps_bc, bias, rate, rows, seg_enter, seg_leave):
    conv_x = conv(ext_x, seg_ext, taps_x, rows)
    conv_bc = conv(ext_bc, seg_ext, taps_bc, rows)
    seg = seg_ext[HALO : HALO + rows]
    shifted = dt_raw + bias
    step_size = jnp.maximum(shifted, 0.0) + jnp.log1p(jnp.exp(-jnp.abs(shifted)))
    cum = prefix_sum(-rate * step_size)
    scaled = conv_x * step_size
    last = cum[rows - 1 : rows]
    tail = jnp.where(seg == seg_leave, jnp.exp(last - cum), 0.0)
    state_w = conv_bc.shape[1] // 2
    state = dot(conv_bc, tail * scaled, ((0,), (0,)))[:state_w]
    enter = jnp.where(seg == seg_enter, jnp.exp(cum), 0.0)
    return conv_x, conv_bc, cum, scaled, state, enter, last


def block_inner(conv_bc, cum, scaled, seg_col, seg_row, heads):
    rows, width = scaled.shape
    state_w = conv_bc.shape[1] // 2
    head_w = width // heads
    scores = dot(conv_bc[:, state_w:], conv_bc[:, :state_w], ((1,), (1,)))
    later = lax.broadcasted_iota(jnp.int32, (rows, rows), 0) >= lax.broadcasted_iota(jnp.int32, (rows, rows), 1)
    visible = (seg_col == seg_row) & later
    cum_rows = cum.T
    lane = lax.broadcasted_iota(jnp.int32, (rows, width), 1)
    result = jnp.zeros((rows, width), F32)
    scaled = scaled.astype(BF16)
    for head in range(heads):
        at = head * head_w
        gap = jnp.where(visible, cum[:, at : at + 1] - cum_rows[at : at + 1, :], -jnp.inf)
        part = dot(jnp.exp(gap) * scores, scaled)
        result = jnp.where((lane >= at) & (lane < at + head_w), part, result)
    return result


def later_block(heads, width, rows, proj, seg_ext, seg_row, taps_x, taps_bc, bias, rate, skip,
                out, bc_out, enter_out, state_out, gate_out, ext_x, ext_bc):
    rounded = proj[rows - HALO :, : 3 * width].astype(BF16).astype(F32)
    gate_out[...] = silu(rounded[HALO:, :width])
    ext_x[...] = rounded[:, width : 2 * width]
    ext_bc[...] = rounded[:, 2 * width : 3 * width]
    seg_enter = seg_ext[HALO - 1 : HALO]
    seg_leave = seg_ext[HALO + rows - 1 : HALO + rows]
    conv_x, conv_bc, cum, scaled, state, enter, last = block_front(
        ext_x, ext_bc, seg_ext, proj[rows:, 3 * width :], taps_x, taps_bc[...], bias[...], rate[...], rows, seg_enter, seg_leave
    )
    out[...] = block_inner(conv_bc, cum, scaled, seg_ext[HALO:], seg_row[...], heads) + skip[...] * conv_x
    bc_out[...] = conv_bc
    enter_out[...] = enter
    keep = jnp.where(seg_enter == seg_leave, jnp.exp(last), 0.0)
    state_w = state.shape[0]
    state_out[:state_w] = state
    state_out[state_w : state_w + 1] = keep
    state_out[state_w + 1 : state_w + 2] = last
    state_out[state_w + 2 :] = jnp.zeros((state_out.shape[0] - state_w - 2, width), F32)


def first_front(width, rows, proj, halo, seg_ext, seg_last, state_b, taps_x, taps_bc, bias, rate,
                conv_out, bc_out, cum_out, scaled_out, enter_out, state_out, message, ext_x, ext_bc):
    ext_x[:HALO] = halo[:, :width].astype(F32)
    ext_bc[:HALO] = halo[:, width:].astype(F32)
    ext_x[HALO:] = proj[:rows, width : 2 * width].astype(BF16).astype(F32)
    ext_bc[HALO:] = proj[:rows, 2 * width : 3 * width].astype(BF16).astype(F32)
    seg_enter = seg_ext[HALO : HALO + 1]
    seg_leave = seg_ext[HALO + rows - 1 : HALO + rows]
    conv_x, conv_bc, cum, scaled, state, enter, last = block_front(
        ext_x, ext_bc, seg_ext, proj[:rows, 3 * width :], taps_x, taps_bc[...], bias[...], rate[...], rows, seg_enter, seg_leave
    )
    conv_out[...] = conv_x
    bc_out[...] = conv_bc
    cum_out[...] = cum
    scaled_out[...] = scaled
    enter_out[...] = enter
    keep = jnp.where(seg_enter == seg_leave, jnp.exp(last), 0.0)
    state_w = state.shape[0]
    state_out[:state_w] = state
    state_out[state_w : state_w + 1] = keep
    state_out[state_w + 1 :] = jnp.zeros((state_out.shape[0] - state_w - 1, width), F32)
    message[:state_w] = state_b[state_w : state_w + 1] * state + state_b[:state_w]
    message[state_w : state_w + 1] = last + state_b[state_w + 1 : state_w + 2]
    message[state_w + 1 : state_w + 2] = jnp.broadcast_to(seg_last[...].astype(F32), (1, width))
    message[state_w + 2 :] = jnp.zeros((message.shape[0] - state_w - 2, width), F32)


def finish(heads, rows, seg_first, messages, seg_ext_a, seg_row_a, skip, proj, conv_a, bc_a, cum_a, scaled_a, enter_a,
           state_a, out_b, gate_b, bc_b, enter_b, gated):
    state_w = bc_a.shape[1] // 2
    width = out_b.shape[1]
    entering = jnp.zeros((state_w, width), F32)
    decay = jnp.zeros((1, width), F32)
    first = seg_first[...].astype(F32)
    place = lax.axis_index("seq")
    for device in reversed(range(messages.shape[0] - 1)):
        earlier = device < place
        passes = earlier & (messages[device, state_w + 1 : state_w + 2] == first)
        passes = jnp.where(passes, jnp.exp(decay), 0.0)
        entering = entering + passes * messages[device, :state_w]
        decay = decay + jnp.where(earlier, messages[device, state_w : state_w + 1], 0.0)
    second = state_a[state_w : state_w + 1] * entering + state_a[:state_w]
    out_a = block_inner(bc_a[...], cum_a[...], scaled_a[...], seg_ext_a[HALO:], seg_row_a[...], heads)
    out_a = out_a + skip[...] * conv_a[...] + enter_a[...] * dot(bc_a[:, state_w:], entering)
    gated[:rows] = (out_a * silu(proj[:rows, :width].astype(BF16).astype(F32))).astype(BF16)
    gated[rows:] = ((out_b[...] + enter_b[...] * dot(bc_b[:, state_w:], second)) * gate_b[...]).astype(BF16)


def product(gated, distances, pieces):
    total = 0.0
    for distance, piece in zip(distances, pieces):
        source = source_of(distance)
        rows = jnp.concatenate([part[source] for part in gated], 0)
        total = total + jnp.dot(rows, piece[...], preferred_element_type=F32)
    return total


def product_early(distances, mine, other, *rest):
    rest[-1][...] = product((mine, other), distances, rest[:-1])


def product_last(distance, mine, other, total, *refs):
    near, lacked, far, (mine_out, other_out, held) = refs[:2], refs[2:4], refs[4:6], refs[6:]
    whole = held.shape[1]
    for side in range(2):
        for block, part in ((side, near[side]), (2, far[side])):
            size = part.shape[0]
            held[block, pl.ds(near_start(side, whole, size), size)] = part[...]
        size = lacked[side].shape[0]
        held[side, pl.ds(near_start(1 - side, whole, size), size)] = lacked[side][...]
    result = product((mine, other), [1 - distance, distance - 1, distance], [held.at[k] for k in range(3)]) + total[...]
    blocks, rows, width = mine.shape
    for i, (gated, out) in enumerate(((mine, mine_out), (other, other_out))):
        squares = jnp.zeros((rows, width), F32)
        for block in range(blocks):
            value = gated[block].astype(F32)
            squares = squares + value * value
        scale = lax.rsqrt(jnp.sum(squares, axis=1, keepdims=True) / (blocks * width) + NORM_EPS)
        out[...] = (result[i * rows : (i + 1) * rows] * scale).astype(BF16)


def call(body, outs, scratch=(), vmem=48, flops=10**7, moved=1 << 21, **kw):
    return pl.pallas_call(
        body,
        out_shape=outs,
        scratch_shapes=list(scratch),
        compiler_params=pltpu.CompilerParams(vmem_limit_bytes=vmem << 20),
        cost_estimate=pl.CostEstimate(flops=flops, bytes_accessed=moved, transcendentals=0),
        **kw,
    )


def local(
    tokens, w_zx, w_bc, w_dt, dt_bias, a_rate, d_skip, conv_x, conv_bc, norm_gain, w_out, segments
):
    tok_rows, feat = tokens.shape
    width = w_zx.shape[2]
    heads = dt_bias.shape[0]
    head_w = width // heads
    state_w = w_bc.shape[1] // 2
    model = w_zx.shape[1]
    n_seq, n_tensor = lax.axis_size("seq"), lax.axis_size("tensor")
    seq_at = lax.axis_index("seq")
    rows = tok_rows // 2
    shape = lambda *s, kind=F32: jax.ShapeDtypeStruct(s, kind)

    spread = lambda v: jnp.repeat(v, head_w, axis=-1)
    expand = np.repeat(np.eye(heads, dtype=np.float32), head_w, axis=1)
    w_step = jnp.dot(w_dt, expand.astype(BF16))
    block = tokens.T
    core = seq_at % 2
    columns = model // 2
    own = (lax.dynamic_slice_in_dim(w_out, core * columns, columns, 1).astype(F32) * norm_gain[:, None]).astype(BF16)
    last = n_tensor // 2
    w_half = width // 2
    shift_rows = [(i, i + 1) for i in range(n_seq - 1)]

    seg_halo = lax.ppermute(segments[tok_rows - HALO :], "seq", shift_rows)
    seg_all = jnp.concatenate([seg_halo, segments])[:, None]
    small = (
        (seg_all[: HALO + rows], seg_all[rows:]),
        (segments[None, :rows], segments[None, rows:]),
        (segments[None, :1], segments[None, tok_rows - 1 :]),
        (spread(dt_bias)[None], spread(a_rate)[None], spread(d_skip)[None]),
    )

    forth = back = block
    arrived, projs = [(0, block)], []
    for step in range(1, last + 1):
        if step == 3:
            forth, back = after(forth, projs[1], small), after(back, projs[1], small)
        elif step > 1:
            forth, back = after(forth, projs[step - 2]), after(back, projs[step - 2])
        arrivals = (forth, back)
        if step < last:
            forth, back = ring_shift(forth, 1), ring_shift(back, -1)
        else:
            far = far_shift(forth, back)
        if step == W_FIRST:
            w_forth, w_back = after((own, own), arrivals)
            w_forth, w_back = ring_shift(w_forth, 1), ring_shift(w_back, -1)
        ahead = last if step == last else 0
        total = projs[-1:]
        fetched = len(arrived) + bool(ahead)
        outs = [shape(tok_rows, 4 * width)] + [shape(feat, 4 * width, kind=BF16)] * bool(ahead)
        results = call(
            functools.partial(project, [distance for distance, _ in arrived], ahead, not total),
            outs,
            [pltpu.VMEM((len(arrived), feat, 4 * width), BF16), pltpu.SemaphoreType.DMA((fetched, 4))],
            in_specs=[VMEM] * len(arrived) + [ANY] * 3 + [VMEM] * len(total),
            flops=10**9,
        )(*[part for _, part in arrived], w_zx, w_bc, w_step, *total)
        projs.append(results[0])
        arrived = [(-step, forth), (step, back)]
    proj = call(project_far, shape(tok_rows, 4 * width), flops=10**9)(
        *far, results[1], projs[-1]
    )

    (seg_ext_a, seg_ext_b), (seg_row_a, seg_row_b), (seg_first, seg_last), (bias, rate, skip) = small
    halo = lax.ppermute(proj[tok_rows - HALO :, width : 3 * width].astype(BF16), "seq", shift_rows)

    msg_rows = state_w + 8
    plane = shape(rows, width)
    ext = pltpu.VMEM((HALO + rows, width), F32)
    out_b, bc_b, enter_b, state_b, gate_b = call(
        functools.partial(later_block, heads, width, rows),
        [plane, plane, plane, shape(msg_rows, width), plane],
        [ext, ext],
    )(proj, seg_ext_b, seg_row_b, conv_x, conv_bc, bias, rate, skip)
    cx_a, bc_a, cum_a, scaled_a, enter_a, state_a, message = call(
        functools.partial(first_front, width, rows),
        [plane] * 5 + [shape(msg_rows, width)] * 2,
        [ext, ext],
    )(proj, halo, seg_ext_a, seg_last, state_b, conv_x, conv_bc, bias, rate)
    messages = lax.all_gather(message, "seq")
    gated = call(functools.partial(finish, heads, rows), shape(tok_rows, width, kind=BF16))(
        seg_first, messages, seg_ext_a, seg_row_a, skip, proj, cx_a, bc_a, cum_a, scaled_a, enter_a, state_a,
        out_b, gate_b, bc_b, enter_b
    )
    tok_own = tok_rows // n_tensor

    w_steps = [(w_forth, w_back)]
    for step in range(2, last - 1):
        w_forth, w_back = after((w_forth, w_back), proj)
        w_forth, w_back = ring_shift(w_forth, 1), ring_shift(w_back, -1)
        w_steps.append((w_forth, w_back))
    gated = after(gated, w_forth, w_back)
    near = width * 5 // 8
    parts = lambda size: [shape(size, columns, kind=BF16)] * 2
    w_forth, w_back = call(take_near, parts(near))(*after((w_forth, w_back), messages))
    w_near = ring_shift(w_forth, 1), ring_shift(w_back, -1)
    lacked_forth, lacked_back, *halves_on = call(
        pass_on, parts(width - near) + parts(width // 2)
    )(*w_near)
    w_far = ring_shift(halves_on[0], 1), ring_shift(halves_on[1], -1)
    other_y = [(i, i ^ 2) for i in range(n_seq)]
    w_lacked = [lax.ppermute(part, "seq", other_y) for part in (lacked_forth, lacked_back)]
    mine = lax.all_to_all(gated.reshape(n_tensor, tok_own, width), "tensor", 0, 0)
    swap = [(i, i ^ 1) for i in range(n_seq)]
    other = lax.ppermute(mine, "seq", swap)
    pieces, distances = [own], [0]
    for i, pair in enumerate(w_steps):
        pieces += pair
        distances += [-i - 1, i + 1]
    total = call(functools.partial(product_early, distances), shape(2 * tok_own, columns), flops=1, moved=1)(
        mine, other, *pieces
    )
    half = shape(tok_own, columns, kind=BF16)
    out_own, out_other = call(
        functools.partial(product_last, last), [half, half], [pltpu.VMEM((3, width, columns), BF16)], flops=10**8
    )(mine, other, total, *w_near, *w_lacked, *w_far)
    arrived = lax.ppermute(out_other, "seq", swap)
    is_first = core == 0
    return jnp.concatenate([jnp.where(is_first, out_own, arrived), jnp.where(is_first, arrived, out_own)], 1)


def solution(mesh):
    in_specs = (
        P("seq", "tensor"),
        P(None, None, "tensor"),
        P(),
        P(None, "tensor"),
        P("tensor"),
        P("tensor"),
        P("tensor"),
        P(None, "tensor"),
        P(),
        P("tensor"),
        P("tensor", None),
        P("seq"),
    )
    out_specs = P(("seq", "tensor"), None)
    return jax.shard_map(local, mesh=mesh, in_specs=in_specs, out_specs=out_specs, check_vma=False)
```

```python
import functools

import jax
import jax.numpy as jnp
import numpy as np
from jax import lax
from jax.experimental import pallas as pl
from jax.experimental.pallas import tpu as pltpu
from jax.sharding import PartitionSpec as P

NORM_EPS = 1e-05
F32 = jnp.float32
BF16 = jnp.bfloat16
VMEM = pl.BlockSpec(memory_space=pltpu.VMEM)
ANY = pl.BlockSpec(memory_space=pl.ANY)
HALO = 8


def ring_place(index, n):
    return jnp.where(index % 2 == 0, index // 2, (2 * n - 1 - index) // 2)


def ring_index(place, n):
    return jnp.where(place < n // 2, 2 * place, 2 * n - 1 - 2 * place)


def ring_shift(block, step):
    n = lax.axis_size("tensor")
    order = [2 * i if i < n // 2 else 2 * n - 1 - 2 * i for i in range(n)]
    return lax.ppermute(block, "tensor", [(order[i], order[(i + step) % n]) for i in range(n)])


def after(values, *earlier):
    return lax.optimization_barrier((values, earlier))[0]


def far_shift(forth, back):
    cut = forth.shape[0] // 32 * 16
    parts = [jax.ShapeDtypeStruct((size, forth.shape[1]), forth.dtype) for size in (cut, forth.shape[0] - cut)]
    top, bottom = call(halves, parts)(forth, back)
    return ring_shift(top, 1), ring_shift(bottom, -1)


def halves(forth, back, top, bottom):
    size = top.shape[0]
    top[...] = forth[:size]
    bottom[...] = back[size:]


def silu(v):
    return v / (1.0 + jnp.exp(-v))


def dot(a, b, dims=((1,), (0,))):
    return lax.dot_general(a.astype(BF16), b.astype(BF16), (dims, ((), ())), preferred_element_type=F32)


def source_of(distance):
    n = lax.axis_size("tensor")
    return ring_index((ring_place(lax.axis_index("tensor"), n) + distance + n) % n, n)


def project(distances, ahead, first, *refs):
    count, fetched = len(distances), len(distances) + bool(ahead)
    blocks, (w_zx, w_bc, w_dt), refs = refs[:count], refs[count : count + 3], refs[count + 3 :]
    total, refs = (None, refs) if first else (refs[0], refs[1:])
    out, far_out, held, sems = refs if ahead else (refs[0], None, *refs[1:])
    feat, width = held.shape[1], w_bc.shape[1]
    sources = [w_zx.at[0], w_zx.at[1], w_bc, w_dt]
    copies = []
    for k, distance in enumerate([*distances, ahead][:fetched]):
        rows = pl.ds(pl.multiple_of(source_of(distance) * feat, 16), feat)
        for j, source in enumerate(sources):
            target = held.at[k] if k < count else far_out
            copies.append(
                pltpu.make_async_copy(source.at[rows], target.at[:, pl.ds(j * width, width)], sems.at[k, j])
            )
            copies[-1].start()
    result = 0.0 if first else total[...]
    for k in range(count):
        for j in range(len(sources)):
            copies[k * len(sources) + j].wait()
        result = result + dot(blocks[k][...], held[k], ((0,), (0,)))
    out[...] = result
    for copy in copies[count * len(sources) :]:
        copy.wait()


def project_far(top, bottom, weights, total, out):
    cut = top.shape[0]
    out[...] = (
        total[...] + dot(top[...], weights[:cut], ((0,), (0,))) + dot(bottom[...], weights[cut:], ((0,), (0,)))
    )


def conv(ext, seg_ext, taps, rows):
    size = taps.shape[0]
    seg_now = seg_ext[HALO : HALO + rows]
    total = taps[size - 1 : size] * ext[HALO : HALO + rows]
    for offset in range(1, size):
        same = seg_ext[HALO - offset : HALO - offset + rows] == seg_now
        total = total + taps[size - 1 - offset : size - offset] * jnp.where(
            same, ext[HALO - offset : HALO - offset + rows], 0.0
        )
    return silu(total)


def prefix_sum(values):
    rows = values.shape[0]
    lower = lax.broadcasted_iota(jnp.int32, (rows, rows), 0) >= lax.broadcasted_iota(jnp.int32, (rows, rows), 1)
    lower = jnp.where(lower, 1.0, 0.0).astype(BF16)
    total = jnp.zeros(values.shape, F32)
    rest = values
    parts = []
    for _ in range(3):
        part = rest.astype(BF16)
        parts.append(part)
        rest = rest - part.astype(F32)
    for part in reversed(parts):
        total = total + jnp.dot(lower, part, preferred_element_type=F32)
    return total


def block_front(ext_x, ext_bc, seg_ext, dt_raw, taps_x, taps_bc, bias, rate, rows, seg_enter, seg_leave):
    conv_x = conv(ext_x, seg_ext, taps_x, rows)
    conv_bc = conv(ext_bc, seg_ext, taps_bc, rows)
    seg = seg_ext[HALO : HALO + rows]
    shifted = dt_raw + bias
    step_size = jnp.maximum(shifted, 0.0) + jnp.log1p(jnp.exp(-jnp.abs(shifted)))
    cum = prefix_sum(-rate * step_size)
    scaled = conv_x * step_size
    last = cum[rows - 1 : rows]
    tail = jnp.where(seg == seg_leave, jnp.exp(last - cum), 0.0)
    state_w = conv_bc.shape[1] // 2
    state = dot(conv_bc, tail * scaled, ((0,), (0,)))[:state_w]
    enter = jnp.where(seg == seg_enter, jnp.exp(cum), 0.0)
    return conv_x, conv_bc, cum, scaled, state, enter, last


def block_inner(conv_bc, cum, scaled, seg_col, seg_row, heads):
    rows, width = scaled.shape
    state_w = conv_bc.shape[1] // 2
    head_w = width // heads
    scores = dot(conv_bc[:, state_w:], conv_bc[:, :state_w], ((1,), (1,)))
    later = lax.broadcasted_iota(jnp.int32, (rows, rows), 0) >= lax.broadcasted_iota(jnp.int32, (rows, rows), 1)
    visible = (seg_col == seg_row) & later
    cum_rows = cum.T
    lane = lax.broadcasted_iota(jnp.int32, (rows, width), 1)
    result = jnp.zeros((rows, width), F32)
    scaled = scaled.astype(BF16)
    for head in range(heads):
        at = head * head_w
        gap = jnp.where(visible, cum[:, at : at + 1] - cum_rows[at : at + 1, :], -jnp.inf)
        part = dot(jnp.exp(gap) * scores, scaled)
        result = jnp.where((lane >= at) & (lane < at + head_w), part, result)
    return result


def later_block(heads, width, rows, proj, seg_ext, seg_row, taps_x, taps_bc, bias, rate, skip,
                out, bc_out, enter_out, state_out, gate_out, ext_x, ext_bc):
    rounded = proj[rows - HALO :, : 3 * width].astype(BF16).astype(F32)
    gate_out[...] = silu(rounded[HALO:, :width])
    ext_x[...] = rounded[:, width : 2 * width]
    ext_bc[...] = rounded[:, 2 * width : 3 * width]
    seg_enter = seg_ext[HALO - 1 : HALO]
    seg_leave = seg_ext[HALO + rows - 1 : HALO + rows]
    conv_x, conv_bc, cum, scaled, state, enter, last = block_front(
        ext_x, ext_bc, seg_ext, proj[rows:, 3 * width :], taps_x, taps_bc[...], bias[...], rate[...], rows, seg_enter, seg_leave
    )
    out[...] = block_inner(conv_bc, cum, scaled, seg_ext[HALO:], seg_row[...], heads) + skip[...] * conv_x
    bc_out[...] = conv_bc
    enter_out[...] = enter
    keep = jnp.where(seg_enter == seg_leave, jnp.exp(last), 0.0)
    state_w = state.shape[0]
    state_out[:state_w] = state
    state_out[state_w : state_w + 1] = keep
    state_out[state_w + 1 : state_w + 2] = last
    state_out[state_w + 2 :] = jnp.zeros((state_out.shape[0] - state_w - 2, width), F32)


def first_front(width, rows, proj, halo, seg_ext, seg_last, state_b, taps_x, taps_bc, bias, rate,
                conv_out, bc_out, cum_out, scaled_out, enter_out, state_out, message, ext_x, ext_bc):
    ext_x[:HALO] = halo[:, :width].astype(F32)
    ext_bc[:HALO] = halo[:, width:].astype(F32)
    ext_x[HALO:] = proj[:rows, width : 2 * width].astype(BF16).astype(F32)
    ext_bc[HALO:] = proj[:rows, 2 * width : 3 * width].astype(BF16).astype(F32)
    seg_enter = seg_ext[HALO : HALO + 1]
    seg_leave = seg_ext[HALO + rows - 1 : HALO + rows]
    conv_x, conv_bc, cum, scaled, state, enter, last = block_front(
        ext_x, ext_bc, seg_ext, proj[:rows, 3 * width :], taps_x, taps_bc[...], bias[...], rate[...], rows, seg_enter, seg_leave
    )
    conv_out[...] = conv_x
    bc_out[...] = conv_bc
    cum_out[...] = cum
    scaled_out[...] = scaled
    enter_out[...] = enter
    keep = jnp.where(seg_enter == seg_leave, jnp.exp(last), 0.0)
    state_w = state.shape[0]
    state_out[:state_w] = state
    state_out[state_w : state_w + 1] = keep
    state_out[state_w + 1 :] = jnp.zeros((state_out.shape[0] - state_w - 1, width), F32)
    message[:state_w] = state_b[state_w : state_w + 1] * state + state_b[:state_w]
    message[state_w : state_w + 1] = last + state_b[state_w + 1 : state_w + 2]
    message[state_w + 1 : state_w + 2] = jnp.broadcast_to(seg_last[...].astype(F32), (1, width))
    message[state_w + 2 :] = jnp.zeros((message.shape[0] - state_w - 2, width), F32)


def finish(heads, rows, seg_first, messages, seg_ext_a, seg_row_a, skip, proj, conv_a, bc_a, cum_a, scaled_a, enter_a,
           state_a, out_b, gate_b, bc_b, enter_b, gated):
    state_w = bc_a.shape[1] // 2
    width = out_b.shape[1]
    entering = jnp.zeros((state_w, width), F32)
    decay = jnp.zeros((1, width), F32)
    first = seg_first[...].astype(F32)
    place = lax.axis_index("seq")
    for device in reversed(range(messages.shape[0] - 1)):
        earlier = device < place
        passes = earlier & (messages[device, state_w + 1 : state_w + 2] == first)
        passes = jnp.where(passes, jnp.exp(decay), 0.0)
        entering = entering + passes * messages[device, :state_w]
        decay = decay + jnp.where(earlier, messages[device, state_w : state_w + 1], 0.0)
    second = state_a[state_w : state_w + 1] * entering + state_a[:state_w]
    out_a = block_inner(bc_a[...], cum_a[...], scaled_a[...], seg_ext_a[HALO:], seg_row_a[...], heads)
    out_a = out_a + skip[...] * conv_a[...] + enter_a[...] * dot(bc_a[:, state_w:], entering)
    gated[:rows] = (out_a * silu(proj[:rows, :width].astype(BF16).astype(F32))).astype(BF16)
    gated[rows:] = ((out_b[...] + enter_b[...] * dot(bc_b[:, state_w:], second)) * gate_b[...]).astype(BF16)


def product(gated, distances, pieces):
    total = 0.0
    for distance, piece in zip(distances, pieces):
        source = source_of(distance)
        rows = jnp.concatenate([part[source] for part in gated], 0)
        total = total + jnp.dot(rows, piece[...], preferred_element_type=F32)
    return total


def product_early(distances, mine, other, *rest):
    rest[-1][...] = product((mine, other), distances, rest[:-1])


def product_last(distance, mine, other, total, top, bottom, mine_out, other_out, held):
    held[: top.shape[0]] = top[...]
    held[top.shape[0] :] = bottom[...]
    result = product((mine, other), [distance], [held]) + total[...]
    blocks, rows, width = mine.shape
    for i, (gated, out) in enumerate(((mine, mine_out), (other, other_out))):
        squares = jnp.zeros((rows, width), F32)
        for block in range(blocks):
            value = gated[block].astype(F32)
            squares = squares + value * value
        scale = lax.rsqrt(jnp.sum(squares, axis=1, keepdims=True) / (blocks * width) + NORM_EPS)
        out[...] = (result[i * rows : (i + 1) * rows] * scale).astype(BF16)


def call(body, outs, scratch=(), vmem=48, flops=10**7, moved=1 << 21, **kw):
    return pl.pallas_call(
        body,
        out_shape=outs,
        scratch_shapes=list(scratch),
        compiler_params=pltpu.CompilerParams(vmem_limit_bytes=vmem << 20),
        cost_estimate=pl.CostEstimate(flops=flops, bytes_accessed=moved, transcendentals=0),
        **kw,
    )


def local(
    tokens, w_zx, w_bc, w_dt, dt_bias, a_rate, d_skip, conv_x, conv_bc, norm_gain, w_out, segments
):
    tok_rows, feat = tokens.shape
    width = w_zx.shape[2]
    heads = dt_bias.shape[0]
    head_w = width // heads
    state_w = w_bc.shape[1] // 2
    model = w_zx.shape[1]
    n_seq, n_tensor = lax.axis_size("seq"), lax.axis_size("tensor")
    seq_at = lax.axis_index("seq")
    rows = tok_rows // 2
    shape = lambda *s, kind=F32: jax.ShapeDtypeStruct(s, kind)

    spread = lambda v: jnp.repeat(v, head_w, axis=-1)
    expand = np.repeat(np.eye(heads, dtype=np.float32), head_w, axis=1)
    w_step = jnp.dot(w_dt, expand.astype(BF16))
    block = tokens.T
    core = seq_at % 2
    columns = model // 2
    own = (lax.dynamic_slice_in_dim(w_out, core * columns, columns, 1).astype(F32) * norm_gain[:, None]).astype(BF16)
    last = n_tensor // 2
    w_half = width // 2
    shift_rows = [(i, i + 1) for i in range(n_seq - 1)]

    seg_halo = lax.ppermute(segments[tok_rows - HALO :], "seq", shift_rows)
    seg_all = jnp.concatenate([seg_halo, segments])[:, None]
    small = (
        (seg_all[: HALO + rows], seg_all[rows:]),
        (segments[None, :rows], segments[None, rows:]),
        (segments[None, :1], segments[None, tok_rows - 1 :]),
        (spread(dt_bias)[None], spread(a_rate)[None], spread(d_skip)[None]),
    )

    forth = back = block
    arrived, projs = [(0, block)], []
    for step in range(1, last + 1):
        if step == 3:
            forth, back = after(forth, projs[1], small), after(back, projs[1], small)
        elif step > 1:
            forth, back = after(forth, projs[step - 2]), after(back, projs[step - 2])
        arrivals = (forth, back)
        if step < last:
            forth, back = ring_shift(forth, 1), ring_shift(back, -1)
        else:
            far = far_shift(forth, back)
        if step == 1:
            w_forth, w_back = ring_shift(own, 1), ring_shift(own, -1)
        ahead = last if step == last else 0
        total = projs[-1:]
        if step == 2:
            total = [after(projs[-1], w_forth, w_back)]
        fetched = len(arrived) + bool(ahead)
        outs = [shape(tok_rows, 4 * width)] + [shape(feat, 4 * width, kind=BF16)] * bool(ahead)
        results = call(
            functools.partial(project, [distance for distance, _ in arrived], ahead, not total),
            outs,
            [pltpu.VMEM((len(arrived), feat, 4 * width), BF16), pltpu.SemaphoreType.DMA((fetched, 4))],
            in_specs=[VMEM] * len(arrived) + [ANY] * 3 + [VMEM] * len(total),
            flops=10**9,
        )(*[part for _, part in arrived], w_zx, w_bc, w_step, *total)
        projs.append(results[0])
        arrived = [(-step, forth), (step, back)]
    proj = call(project_far, shape(tok_rows, 4 * width), flops=10**9)(
        *far, results[1], projs[-1]
    )

    (seg_ext_a, seg_ext_b), (seg_row_a, seg_row_b), (seg_first, seg_last), (bias, rate, skip) = small
    halo = lax.ppermute(proj[tok_rows - HALO :, width : 3 * width].astype(BF16), "seq", shift_rows)

    msg_rows = state_w + 8
    plane = shape(rows, width)
    ext = pltpu.VMEM((HALO + rows, width), F32)
    out_b, bc_b, enter_b, state_b, gate_b = call(
        functools.partial(later_block, heads, width, rows),
        [plane, plane, plane, shape(msg_rows, width), plane],
        [ext, ext],
    )(proj, seg_ext_b, seg_row_b, conv_x, conv_bc, bias, rate, skip)
    cx_a, bc_a, cum_a, scaled_a, enter_a, state_a, message = call(
        functools.partial(first_front, width, rows),
        [plane] * 5 + [shape(msg_rows, width)] * 2,
        [ext, ext],
    )(proj, halo, seg_ext_a, seg_last, state_b, conv_x, conv_bc, bias, rate)
    messages = lax.all_gather(message, "seq")
    gated = call(functools.partial(finish, heads, rows), shape(tok_rows, width, kind=BF16))(
        seg_first, messages, seg_ext_a, seg_row_a, skip, proj, cx_a, bc_a, cum_a, scaled_a, enter_a, state_a,
        out_b, gate_b, bc_b, enter_b
    )
    tok_own = tok_rows // n_tensor

    w_steps = [(w_forth, w_back)]
    orders = [proj, messages]
    for step in range(2, last + 1):
        if step - 2 < len(orders):
            w_forth, w_back = after((w_forth, w_back), orders[step - 2])
        if step == last:
            w_far = far_shift(w_forth, w_back)
            break
        w_forth, w_back = ring_shift(w_forth, 1), ring_shift(w_back, -1)
        w_steps.append((w_forth, w_back))
        if step == 2:
            blocks = after(gated, w_forth, w_back).reshape(n_tensor, tok_own, width)
            mine = lax.all_to_all(blocks, "tensor", 0, 0)
    swap = [(i, i ^ 1) for i in range(n_seq)]
    other = lax.ppermute(mine, "seq", swap)
    pieces, distances = [own], [0]
    for i, pair in enumerate(w_steps):
        pieces += pair
        distances += [-i - 1, i + 1]
    total = call(functools.partial(product_early, distances), shape(2 * tok_own, columns), flops=1, moved=1)(
        mine, other, *pieces
    )
    half = shape(tok_own, columns, kind=BF16)
    out_own, out_other = call(
        functools.partial(product_last, last), [half, half], [pltpu.VMEM((width, columns), BF16)], flops=10**8
    )(mine, other, total, *w_far)
    arrived = lax.ppermute(out_other, "seq", swap)
    is_first = core == 0
    return jnp.concatenate([jnp.where(is_first, out_own, arrived), jnp.where(is_first, arrived, out_own)], 1)


def solution(mesh):
    in_specs = (
        P("seq", "tensor"),
        P(None, None, "tensor"),
        P(),
        P(None, "tensor"),
        P("tensor"),
        P("tensor"),
        P("tensor"),
        P(None, "tensor"),
        P(),
        P("tensor"),
        P("tensor", None),
        P("seq"),
    )
    out_specs = P(("seq", "tensor"), None)
    return jax.shard_map(local, mesh=mesh, in_specs=in_specs, out_specs=out_specs, check_vma=False)
```

```python
import functools

import jax
import jax.numpy as jnp
import numpy as np
from jax import lax
from jax.experimental import pallas as pl
from jax.experimental.pallas import tpu as pltpu
from jax.sharding import PartitionSpec as P

NORM_EPS = 1e-05
F32 = jnp.float32
BF16 = jnp.bfloat16
VMEM = pl.BlockSpec(memory_space=pltpu.VMEM)
ANY = pl.BlockSpec(memory_space=pl.ANY)
HALO = 8
W_FIRST = 3


def ring_place(index, n):
    return jnp.where(index % 2 == 0, index // 2, (2 * n - 1 - index) // 2)


def ring_index(place, n):
    return jnp.where(place < n // 2, 2 * place, 2 * n - 1 - 2 * place)


def ring_shift(block, step):
    n = lax.axis_size("tensor")
    order = [2 * i if i < n // 2 else 2 * n - 1 - 2 * i for i in range(n)]
    return lax.ppermute(block, "tensor", [(order[i], order[(i + step) % n]) for i in range(n)])


def after(values, *earlier):
    return lax.optimization_barrier((values, earlier))[0]


def far_shift(forth, back):
    cut = forth.shape[0] // 32 * 16
    parts = [jax.ShapeDtypeStruct((size, forth.shape[1]), forth.dtype) for size in (cut, forth.shape[0] - cut)]
    top, bottom = call(halves, parts)(forth, back)
    return ring_shift(top, 1), ring_shift(bottom, -1)


def halves(forth, back, top, bottom):
    size = top.shape[0]
    top[...] = forth[:size]
    bottom[...] = back[size:]


def silu(v):
    return v / (1.0 + jnp.exp(-v))


def dot(a, b, dims=((1,), (0,))):
    return lax.dot_general(a.astype(BF16), b.astype(BF16), (dims, ((), ())), preferred_element_type=F32)


def source_of(distance):
    n = lax.axis_size("tensor")
    return ring_index((ring_place(lax.axis_index("tensor"), n) + distance + n) % n, n)


def project(distances, ahead, first, *refs):
    count, fetched = len(distances), len(distances) + bool(ahead)
    blocks, (w_zx, w_bc, w_dt), refs = refs[:count], refs[count : count + 3], refs[count + 3 :]
    total, refs = (None, refs) if first else (refs[0], refs[1:])
    out, far_out, held, sems = refs if ahead else (refs[0], None, *refs[1:])
    feat, width = held.shape[1], w_bc.shape[1]
    sources = [w_zx.at[0], w_zx.at[1], w_bc, w_dt]
    copies = []
    for k, distance in enumerate([*distances, ahead][:fetched]):
        rows = pl.ds(pl.multiple_of(source_of(distance) * feat, 16), feat)
        for j, source in enumerate(sources):
            target = held.at[k] if k < count else far_out
            copies.append(
                pltpu.make_async_copy(source.at[rows], target.at[:, pl.ds(j * width, width)], sems.at[k, j])
            )
            copies[-1].start()
    result = 0.0 if first else total[...]
    for k in range(count):
        for j in range(len(sources)):
            copies[k * len(sources) + j].wait()
        result = result + dot(blocks[k][...], held[k], ((0,), (0,)))
    out[...] = result
    for copy in copies[count * len(sources) :]:
        copy.wait()


def project_far(top, bottom, weights, total, out):
    cut = top.shape[0]
    out[...] = (
        total[...] + dot(top[...], weights[:cut], ((0,), (0,))) + dot(bottom[...], weights[cut:], ((0,), (0,)))
    )


def conv(ext, seg_ext, taps, rows):
    size = taps.shape[0]
    seg_now = seg_ext[HALO : HALO + rows]
    total = taps[size - 1 : size] * ext[HALO : HALO + rows]
    for offset in range(1, size):
        same = seg_ext[HALO - offset : HALO - offset + rows] == seg_now
        total = total + taps[size - 1 - offset : size - offset] * jnp.where(
            same, ext[HALO - offset : HALO - offset + rows], 0.0
        )
    return silu(total)


def prefix_sum(values):
    rows = values.shape[0]
    lower = lax.broadcasted_iota(jnp.int32, (rows, rows), 0) >= lax.broadcasted_iota(jnp.int32, (rows, rows), 1)
    lower = jnp.where(lower, 1.0, 0.0).astype(BF16)
    total = jnp.zeros(values.shape, F32)
    rest = values
    parts = []
    for _ in range(3):
        part = rest.astype(BF16)
        parts.append(part)
        rest = rest - part.astype(F32)
    for part in reversed(parts):
        total = total + jnp.dot(lower, part, preferred_element_type=F32)
    return total


def block_front(ext_x, ext_bc, seg_ext, dt_raw, taps_x, taps_bc, bias, rate, rows, seg_enter, seg_leave):
    conv_x = conv(ext_x, seg_ext, taps_x, rows)
    conv_bc = conv(ext_bc, seg_ext, taps_bc, rows)
    seg = seg_ext[HALO : HALO + rows]
    shifted = dt_raw + bias
    step_size = jnp.maximum(shifted, 0.0) + jnp.log1p(jnp.exp(-jnp.abs(shifted)))
    cum = prefix_sum(-rate * step_size)
    scaled = conv_x * step_size
    last = cum[rows - 1 : rows]
    tail = jnp.where(seg == seg_leave, jnp.exp(last - cum), 0.0)
    state_w = conv_bc.shape[1] // 2
    state = dot(conv_bc, tail * scaled, ((0,), (0,)))[:state_w]
    enter = jnp.where(seg == seg_enter, jnp.exp(cum), 0.0)
    return conv_x, conv_bc, cum, scaled, state, enter, last


def block_inner(conv_bc, cum, scaled, seg_col, seg_row, heads):
    rows, width = scaled.shape
    state_w = conv_bc.shape[1] // 2
    head_w = width // heads
    scores = dot(conv_bc[:, state_w:], conv_bc[:, :state_w], ((1,), (1,)))
    later = lax.broadcasted_iota(jnp.int32, (rows, rows), 0) >= lax.broadcasted_iota(jnp.int32, (rows, rows), 1)
    visible = (seg_col == seg_row) & later
    cum_rows = cum.T
    lane = lax.broadcasted_iota(jnp.int32, (rows, width), 1)
    result = jnp.zeros((rows, width), F32)
    scaled = scaled.astype(BF16)
    for head in range(heads):
        at = head * head_w
        gap = jnp.where(visible, cum[:, at : at + 1] - cum_rows[at : at + 1, :], -jnp.inf)
        part = dot(jnp.exp(gap) * scores, scaled)
        result = jnp.where((lane >= at) & (lane < at + head_w), part, result)
    return result


def later_front(width, rows, proj, seg_ext, taps_x, taps_bc, bias, rate,
                conv_out, bc_out, cum_out, scaled_out, enter_out, state_out, ext_x, ext_bc):
    rounded = proj[rows - HALO :, width : 3 * width].astype(BF16).astype(F32)
    ext_x[...] = rounded[:, :width]
    ext_bc[...] = rounded[:, width:]
    seg_enter = seg_ext[HALO - 1 : HALO]
    seg_leave = seg_ext[HALO + rows - 1 : HALO + rows]
    conv_x, conv_bc, cum, scaled, state, enter, last = block_front(
        ext_x, ext_bc, seg_ext, proj[rows:, 3 * width :], taps_x, taps_bc[...], bias[...], rate[...], rows, seg_enter, seg_leave
    )
    conv_out[...] = conv_x
    bc_out[...] = conv_bc
    cum_out[...] = cum
    scaled_out[...] = scaled
    enter_out[...] = enter
    keep = jnp.where(seg_enter == seg_leave, jnp.exp(last), 0.0)
    state_w = state.shape[0]
    state_out[:state_w] = state
    state_out[state_w : state_w + 1] = keep
    state_out[state_w + 1 : state_w + 2] = last
    state_out[state_w + 2 :] = jnp.zeros((state_out.shape[0] - state_w - 2, width), F32)


def first_front(width, rows, proj, halo, seg_ext, seg_last, state_b, taps_x, taps_bc, bias, rate,
                conv_out, bc_out, cum_out, scaled_out, enter_out, state_out, message, ext_x, ext_bc):
    ext_x[:HALO] = halo[:, :width].astype(F32)
    ext_bc[:HALO] = halo[:, width:].astype(F32)
    ext_x[HALO:] = proj[:rows, width : 2 * width].astype(BF16).astype(F32)
    ext_bc[HALO:] = proj[:rows, 2 * width : 3 * width].astype(BF16).astype(F32)
    seg_enter = seg_ext[HALO : HALO + 1]
    seg_leave = seg_ext[HALO + rows - 1 : HALO + rows]
    conv_x, conv_bc, cum, scaled, state, enter, last = block_front(
        ext_x, ext_bc, seg_ext, proj[:rows, 3 * width :], taps_x, taps_bc[...], bias[...], rate[...], rows, seg_enter, seg_leave
    )
    conv_out[...] = conv_x
    bc_out[...] = conv_bc
    cum_out[...] = cum
    scaled_out[...] = scaled
    enter_out[...] = enter
    keep = jnp.where(seg_enter == seg_leave, jnp.exp(last), 0.0)
    state_w = state.shape[0]
    state_out[:state_w] = state
    state_out[state_w : state_w + 1] = keep
    state_out[state_w + 1 :] = jnp.zeros((state_out.shape[0] - state_w - 1, width), F32)
    message[:state_w] = state_b[state_w : state_w + 1] * state + state_b[:state_w]
    message[state_w : state_w + 1] = last + state_b[state_w + 1 : state_w + 2]
    message[state_w + 1 : state_w + 2] = jnp.broadcast_to(seg_last[...].astype(F32), (1, width))
    message[state_w + 2 :] = jnp.zeros((message.shape[0] - state_w - 2, width), F32)


def finish(heads, rows, seg_first, messages, seg_ext_a, seg_row_a, seg_ext_b, seg_row_b, skip, proj,
           conv_a, bc_a, cum_a, scaled_a, enter_a, state_a, conv_b, bc_b, cum_b, scaled_b, enter_b, gated):
    state_w = bc_a.shape[1] // 2
    width = conv_a.shape[1]
    entering = jnp.zeros((state_w, width), F32)
    decay = jnp.zeros((1, width), F32)
    first = seg_first[...].astype(F32)
    place = lax.axis_index("seq")
    for device in reversed(range(messages.shape[0] - 1)):
        earlier = device < place
        passes = earlier & (messages[device, state_w + 1 : state_w + 2] == first)
        passes = jnp.where(passes, jnp.exp(decay), 0.0)
        entering = entering + passes * messages[device, :state_w]
        decay = decay + jnp.where(earlier, messages[device, state_w : state_w + 1], 0.0)
    second = state_a[state_w : state_w + 1] * entering + state_a[:state_w]
    blocks = (
        (0, seg_ext_a, seg_row_a, conv_a, bc_a, cum_a, scaled_a, enter_a, entering),
        (rows, seg_ext_b, seg_row_b, conv_b, bc_b, cum_b, scaled_b, enter_b, second),
    )
    for first, seg_ext, seg_row, conv_x, conv_bc, cum, scaled, enter, state in blocks:
        out = block_inner(conv_bc[...], cum[...], scaled[...], seg_ext[HALO:], seg_row[...], heads)
        out = out + skip[...] * conv_x[...] + enter[...] * dot(conv_bc[:, state_w:], state)
        gate = silu(proj[first : first + rows, :width].astype(BF16).astype(F32))
        gated[first : first + rows] = (out * gate).astype(BF16)


def lay_together(own, other, out):
    columns = own.shape[1]
    core = lax.axis_index("seq") % 2
    out[:, pl.ds(pl.multiple_of(core * columns, 128), columns)] = own[...]
    out[:, pl.ds(pl.multiple_of((1 - core) * columns, 128), columns)] = other[...]


def product(gated, distances, pieces):
    total = 0.0
    for distance, piece in zip(distances, pieces):
        source = source_of(distance)
        rows = jnp.concatenate([part[source] for part in gated], 0)
        total = total + jnp.dot(rows, piece[...], preferred_element_type=F32)
    return total


def product_early(distances, mine, other, *rest):
    rest[-1][...] = product((mine, other), distances, rest[:-1])


def product_last(distance, mine, other, total, top, bottom, mine_out, other_out, held):
    held[: top.shape[0]] = top[...]
    held[top.shape[0] :] = bottom[...]
    result = product((mine, other), [distance], [held]) + total[...]
    blocks, rows, width = mine.shape
    for i, (gated, out) in enumerate(((mine, mine_out), (other, other_out))):
        squares = jnp.zeros((rows, width), F32)
        for block in range(blocks):
            value = gated[block].astype(F32)
            squares = squares + value * value
        scale = lax.rsqrt(jnp.sum(squares, axis=1, keepdims=True) / (blocks * width) + NORM_EPS)
        out[...] = (result[i * rows : (i + 1) * rows] * scale).astype(BF16)


def call(body, outs, scratch=(), vmem=48, flops=10**7, moved=1 << 21, **kw):
    return pl.pallas_call(
        body,
        out_shape=outs,
        scratch_shapes=list(scratch),
        compiler_params=pltpu.CompilerParams(vmem_limit_bytes=vmem << 20),
        cost_estimate=pl.CostEstimate(flops=flops, bytes_accessed=moved, transcendentals=0),
        **kw,
    )


def local(
    tokens, w_zx, w_bc, w_dt, dt_bias, a_rate, d_skip, conv_x, conv_bc, norm_gain, w_out, segments
):
    tok_rows, feat = tokens.shape
    width = w_zx.shape[2]
    heads = dt_bias.shape[0]
    head_w = width // heads
    state_w = w_bc.shape[1] // 2
    model = w_zx.shape[1]
    n_seq, n_tensor = lax.axis_size("seq"), lax.axis_size("tensor")
    seq_at = lax.axis_index("seq")
    rows = tok_rows // 2
    shape = lambda *s, kind=F32: jax.ShapeDtypeStruct(s, kind)

    spread = lambda v: jnp.repeat(v, head_w, axis=-1)
    expand = np.repeat(np.eye(heads, dtype=np.float32), head_w, axis=1)
    w_step = jnp.dot(w_dt, expand.astype(BF16))
    block = tokens.T
    core = seq_at % 2
    columns = model // 2
    own = (lax.dynamic_slice_in_dim(w_out, core * columns, columns, 1).astype(F32) * norm_gain[:, None]).astype(BF16)
    last = n_tensor // 2
    w_half = width // 2
    shift_rows = [(i, i + 1) for i in range(n_seq - 1)]

    seg_halo = lax.ppermute(segments[tok_rows - HALO :], "seq", shift_rows)
    seg_all = jnp.concatenate([seg_halo, segments])[:, None]
    small = (
        (seg_all[: HALO + rows], seg_all[rows:]),
        (segments[None, :rows], segments[None, rows:]),
        (segments[None, :1], segments[None, tok_rows - 1 :]),
        (spread(dt_bias)[None], spread(a_rate)[None], spread(d_skip)[None]),
    )

    forth = back = block
    arrived, projs = [(0, block)], []
    for step in range(1, last + 1):
        if step == 3:
            forth, back = after(forth, projs[1], small), after(back, projs[1], small)
        elif step > 1:
            forth, back = after(forth, projs[step - 2]), after(back, projs[step - 2])
        arrivals = (forth, back)
        if step < last:
            forth, back = ring_shift(forth, 1), ring_shift(back, -1)
        else:
            far = far_shift(forth, back)
        if step == W_FIRST:
            w_forth, w_back = after((own, own), arrivals)
            w_forth, w_back = ring_shift(w_forth, 1), ring_shift(w_back, -1)
        ahead = last if step == last else 0
        total = projs[-1:]
        fetched = len(arrived) + bool(ahead)
        outs = [shape(tok_rows, 4 * width)] + [shape(feat, 4 * width, kind=BF16)] * bool(ahead)
        results = call(
            functools.partial(project, [distance for distance, _ in arrived], ahead, not total),
            outs,
            [pltpu.VMEM((len(arrived), feat, 4 * width), BF16), pltpu.SemaphoreType.DMA((fetched, 4))],
            in_specs=[VMEM] * len(arrived) + [ANY] * 3 + [VMEM] * len(total),
            flops=10**9,
        )(*[part for _, part in arrived], w_zx, w_bc, w_step, *total)
        projs.append(results[0])
        arrived = [(-step, forth), (step, back)]
    proj = call(project_far, shape(tok_rows, 4 * width), flops=10**9)(
        *far, results[1], projs[-1]
    )

    (seg_ext_a, seg_ext_b), (seg_row_a, seg_row_b), (seg_first, seg_last), (bias, rate, skip) = small
    halo = lax.ppermute(proj[tok_rows - HALO :, width : 3 * width].astype(BF16), "seq", shift_rows)

    msg_rows = state_w + 8
    plane = shape(rows, width)
    ext = pltpu.VMEM((HALO + rows, width), F32)
    *later, state_b = call(
        functools.partial(later_front, width, rows), [plane] * 5 + [shape(msg_rows, width)], [ext, ext]
    )(proj, seg_ext_b, conv_x, conv_bc, bias, rate)
    cx_a, bc_a, cum_a, scaled_a, enter_a, state_a, message = call(
        functools.partial(first_front, width, rows),
        [plane] * 5 + [shape(msg_rows, width)] * 2,
        [ext, ext],
    )(proj, halo, seg_ext_a, seg_last, state_b, conv_x, conv_bc, bias, rate)
    messages = lax.all_gather(message, "seq")
    gated = call(functools.partial(finish, heads, rows), shape(tok_rows, width, kind=BF16))(
        seg_first, messages, seg_ext_a, seg_row_a, seg_ext_b, seg_row_b, skip, proj,
        cx_a, bc_a, cum_a, scaled_a, enter_a, state_a, *later
    )
    tok_own = tok_rows // n_tensor

    w_steps = [(w_forth, w_back)]
    orders = [far, messages]
    for step in range(2, last + 1):
        if step - 2 < len(orders):
            w_forth, w_back = after((w_forth, w_back), orders[step - 2])
        if step == last:
            w_far = far_shift(w_forth, w_back)
            break
        w_forth, w_back = ring_shift(w_forth, 1), ring_shift(w_back, -1)
        w_steps.append((w_forth, w_back))
        if step == 2:
            blocks = after(gated, w_forth, w_back).reshape(n_tensor, tok_own, width)
            mine = lax.all_to_all(blocks, "tensor", 0, 0)
    swap = [(i, i ^ 1) for i in range(n_seq)]
    other = lax.ppermute(mine, "seq", swap)
    pieces, distances = [own], [0]
    for i, pair in enumerate(w_steps):
        pieces += pair
        distances += [-i - 1, i + 1]
    total = call(functools.partial(product_early, distances), shape(2 * tok_own, columns), flops=1, moved=1)(
        mine, other, *pieces
    )
    half = shape(tok_own, columns, kind=BF16)
    out_own, out_other = call(
        functools.partial(product_last, last), [half, half], [pltpu.VMEM((width, columns), BF16)], flops=10**8
    )(mine, other, total, *w_far)
    return call(lay_together, shape(tok_own, model, kind=BF16))(out_own, lax.ppermute(out_other, "seq", swap))


def solution(mesh):
    in_specs = (
        P("seq", "tensor"),
        P(None, None, "tensor"),
        P(),
        P(None, "tensor"),
        P("tensor"),
        P("tensor"),
        P("tensor"),
        P(None, "tensor"),
        P(),
        P("tensor"),
        P("tensor", None),
        P("seq"),
    )
    out_specs = P(("seq", "tensor"), None)
    return jax.shard_map(local, mesh=mesh, in_specs=in_specs, out_specs=out_specs, check_vma=False)
```

```python
import functools

import jax
import jax.numpy as jnp
import numpy as np
from jax import lax
from jax.experimental import pallas as pl
from jax.experimental.pallas import tpu as pltpu
from jax.sharding import PartitionSpec as P

NORM_EPS = 1e-05
F32 = jnp.float32
BF16 = jnp.bfloat16
VMEM = pl.BlockSpec(memory_space=pltpu.VMEM)
ANY = pl.BlockSpec(memory_space=pl.ANY)
HALO = 8
W_FIRST = 3


def ring_place(index, n):
    return jnp.where(index % 2 == 0, index // 2, (2 * n - 1 - index) // 2)


def ring_index(place, n):
    return jnp.where(place < n // 2, 2 * place, 2 * n - 1 - 2 * place)


def ring_shift(block, step):
    n = lax.axis_size("tensor")
    order = [2 * i if i < n // 2 else 2 * n - 1 - 2 * i for i in range(n)]
    return lax.ppermute(block, "tensor", [(order[i], order[(i + step) % n]) for i in range(n)])


def after(values, *earlier):
    return lax.optimization_barrier((values, earlier))[0]


def far_shift(forth, back):
    cut = forth.shape[0] // 32 * 16
    parts = [jax.ShapeDtypeStruct((size, forth.shape[1]), forth.dtype) for size in (cut, forth.shape[0] - cut)]
    top, bottom = call(halves, parts)(forth, back)
    return ring_shift(top, 1), ring_shift(bottom, -1)


def halves(forth, back, top, bottom):
    size = top.shape[0]
    top[...] = forth[:size]
    bottom[...] = back[size:]


def silu(v):
    return v / (1.0 + jnp.exp(-v))


def dot(a, b, dims=((1,), (0,))):
    return lax.dot_general(a.astype(BF16), b.astype(BF16), (dims, ((), ())), preferred_element_type=F32)


def source_of(distance):
    n = lax.axis_size("tensor")
    return ring_index((ring_place(lax.axis_index("tensor"), n) + distance + n) % n, n)


def project(distances, ahead, first, *refs):
    count, fetched = len(distances), len(distances) + bool(ahead)
    blocks, (w_zx, w_bc, w_dt), refs = refs[:count], refs[count : count + 3], refs[count + 3 :]
    total, refs = (None, refs) if first else (refs[0], refs[1:])
    out, far_out, held, sems = refs if ahead else (refs[0], None, *refs[1:])
    feat, width = held.shape[1], w_bc.shape[1]
    sources = [w_zx.at[0], w_zx.at[1], w_bc, w_dt]
    copies = []
    for k, distance in enumerate([*distances, ahead][:fetched]):
        rows = pl.ds(pl.multiple_of(source_of(distance) * feat, 16), feat)
        for j, source in enumerate(sources):
            target = held.at[k] if k < count else far_out
            copies.append(
                pltpu.make_async_copy(source.at[rows], target.at[:, pl.ds(j * width, width)], sems.at[k, j])
            )
            copies[-1].start()
    result = 0.0 if first else total[...]
    for k in range(count):
        for j in range(len(sources)):
            copies[k * len(sources) + j].wait()
        result = result + dot(blocks[k][...], held[k], ((0,), (0,)))
    out[...] = result
    for copy in copies[count * len(sources) :]:
        copy.wait()


def project_far(top, bottom, weights, total, out):
    cut = top.shape[0]
    out[...] = (
        total[...] + dot(top[...], weights[:cut], ((0,), (0,))) + dot(bottom[...], weights[cut:], ((0,), (0,)))
    )


def conv(ext, seg_ext, taps, rows):
    size = taps.shape[0]
    seg_now = seg_ext[HALO : HALO + rows]
    total = taps[size - 1 : size] * ext[HALO : HALO + rows]
    for offset in range(1, size):
        same = seg_ext[HALO - offset : HALO - offset + rows] == seg_now
        total = total + taps[size - 1 - offset : size - offset] * jnp.where(
            same, ext[HALO - offset : HALO - offset + rows], 0.0
        )
    return silu(total)


def prefix_sum(values):
    rows = values.shape[0]
    lower = lax.broadcasted_iota(jnp.int32, (rows, rows), 0) >= lax.broadcasted_iota(jnp.int32, (rows, rows), 1)
    lower = jnp.where(lower, 1.0, 0.0).astype(BF16)
    total = jnp.zeros(values.shape, F32)
    rest = values
    parts = []
    for _ in range(3):
        part = rest.astype(BF16)
        parts.append(part)
        rest = rest - part.astype(F32)
    for part in reversed(parts):
        total = total + jnp.dot(lower, part, preferred_element_type=F32)
    return total


def block_front(ext_x, ext_bc, seg_ext, dt_raw, taps_x, taps_bc, bias, rate, rows, seg_enter, seg_leave):
    conv_x = conv(ext_x, seg_ext, taps_x, rows)
    conv_bc = conv(ext_bc, seg_ext, taps_bc, rows)
    seg = seg_ext[HALO : HALO + rows]
    shifted = dt_raw + bias
    step_size = jnp.maximum(shifted, 0.0) + jnp.log1p(jnp.exp(-jnp.abs(shifted)))
    cum = prefix_sum(-rate * step_size)
    scaled = conv_x * step_size
    last = cum[rows - 1 : rows]
    tail = jnp.where(seg == seg_leave, jnp.exp(last - cum), 0.0)
    state_w = conv_bc.shape[1] // 2
    state = dot(conv_bc, tail * scaled, ((0,), (0,)))[:state_w]
    enter = jnp.where(seg == seg_enter, jnp.exp(cum), 0.0)
    return conv_x, conv_bc, cum, scaled, state, enter, last


def block_inner(conv_bc, cum, scaled, seg_col, seg_row, heads):
    rows, width = scaled.shape
    state_w = conv_bc.shape[1] // 2
    head_w = width // heads
    scores = dot(conv_bc[:, state_w:], conv_bc[:, :state_w], ((1,), (1,)))
    later = lax.broadcasted_iota(jnp.int32, (rows, rows), 0) >= lax.broadcasted_iota(jnp.int32, (rows, rows), 1)
    visible = (seg_col == seg_row) & later
    cum_rows = cum.T
    lane = lax.broadcasted_iota(jnp.int32, (rows, width), 1)
    result = jnp.zeros((rows, width), F32)
    scaled = scaled.astype(BF16)
    for head in range(heads):
        at = head * head_w
        gap = jnp.where(visible, cum[:, at : at + 1] - cum_rows[at : at + 1, :], -jnp.inf)
        part = dot(jnp.exp(gap) * scores, scaled)
        result = jnp.where((lane >= at) & (lane < at + head_w), part, result)
    return result


def later_front(width, rows, proj, seg_ext, taps_x, taps_bc, bias, rate,
                conv_out, bc_out, cum_out, scaled_out, enter_out, state_out, ext_x, ext_bc):
    rounded = proj[rows - HALO :, width : 3 * width].astype(BF16).astype(F32)
    ext_x[...] = rounded[:, :width]
    ext_bc[...] = rounded[:, width:]
    seg_enter = seg_ext[HALO - 1 : HALO]
    seg_leave = seg_ext[HALO + rows - 1 : HALO + rows]
    conv_x, conv_bc, cum, scaled, state, enter, last = block_front(
        ext_x, ext_bc, seg_ext, proj[rows:, 3 * width :], taps_x, taps_bc[...], bias[...], rate[...], rows, seg_enter, seg_leave
    )
    conv_out[...] = conv_x
    bc_out[...] = conv_bc
    cum_out[...] = cum
    scaled_out[...] = scaled
    enter_out[...] = enter
    keep = jnp.where(seg_enter == seg_leave, jnp.exp(last), 0.0)
    state_w = state.shape[0]
    state_out[:state_w] = state
    state_out[state_w : state_w + 1] = keep
    state_out[state_w + 1 : state_w + 2] = last
    state_out[state_w + 2 :] = jnp.zeros((state_out.shape[0] - state_w - 2, width), F32)


def first_front(width, rows, proj, halo, seg_ext, seg_last, state_b, taps_x, taps_bc, bias, rate,
                conv_out, bc_out, cum_out, scaled_out, enter_out, state_out, message, ext_x, ext_bc):
    ext_x[:HALO] = halo[:, :width].astype(F32)
    ext_bc[:HALO] = halo[:, width:].astype(F32)
    ext_x[HALO:] = proj[:rows, width : 2 * width].astype(BF16).astype(F32)
    ext_bc[HALO:] = proj[:rows, 2 * width : 3 * width].astype(BF16).astype(F32)
    seg_enter = seg_ext[HALO : HALO + 1]
    seg_leave = seg_ext[HALO + rows - 1 : HALO + rows]
    conv_x, conv_bc, cum, scaled, state, enter, last = block_front(
        ext_x, ext_bc, seg_ext, proj[:rows, 3 * width :], taps_x, taps_bc[...], bias[...], rate[...], rows, seg_enter, seg_leave
    )
    conv_out[...] = conv_x
    bc_out[...] = conv_bc
    cum_out[...] = cum
    scaled_out[...] = scaled
    enter_out[...] = enter
    keep = jnp.where(seg_enter == seg_leave, jnp.exp(last), 0.0)
    state_w = state.shape[0]
    state_out[:state_w] = state
    state_out[state_w : state_w + 1] = keep
    state_out[state_w + 1 :] = jnp.zeros((state_out.shape[0] - state_w - 1, width), F32)
    message[:state_w] = state_b[state_w : state_w + 1] * state + state_b[:state_w]
    message[state_w : state_w + 1] = last + state_b[state_w + 1 : state_w + 2]
    message[state_w + 1 : state_w + 2] = jnp.broadcast_to(seg_last[...].astype(F32), (1, width))
    message[state_w + 2 :] = jnp.zeros((message.shape[0] - state_w - 2, width), F32)


def finish(heads, rows, seg_first, messages, seg_ext_a, seg_row_a, seg_ext_b, seg_row_b, skip, proj,
           conv_a, bc_a, cum_a, scaled_a, enter_a, state_a, conv_b, bc_b, cum_b, scaled_b, enter_b, gated):
    state_w = bc_a.shape[1] // 2
    width = conv_a.shape[1]
    entering = jnp.zeros((state_w, width), F32)
    decay = jnp.zeros((1, width), F32)
    first = seg_first[...].astype(F32)
    place = lax.axis_index("seq")
    for device in reversed(range(messages.shape[0] - 1)):
        earlier = device < place
        passes = earlier & (messages[device, state_w + 1 : state_w + 2] == first)
        passes = jnp.where(passes, jnp.exp(decay), 0.0)
        entering = entering + passes * messages[device, :state_w]
        decay = decay + jnp.where(earlier, messages[device, state_w : state_w + 1], 0.0)
    second = state_a[state_w : state_w + 1] * entering + state_a[:state_w]
    blocks = (
        (0, seg_ext_a, seg_row_a, conv_a, bc_a, cum_a, scaled_a, enter_a, entering),
        (rows, seg_ext_b, seg_row_b, conv_b, bc_b, cum_b, scaled_b, enter_b, second),
    )
    for first, seg_ext, seg_row, conv_x, conv_bc, cum, scaled, enter, state in blocks:
        out = block_inner(conv_bc[...], cum[...], scaled[...], seg_ext[HALO:], seg_row[...], heads)
        out = out + skip[...] * conv_x[...] + enter[...] * dot(conv_bc[:, state_w:], state)
        gate = silu(proj[first : first + rows, :width].astype(BF16).astype(F32))
        gated[first : first + rows] = (out * gate).astype(BF16)


def lay_together(own, other, out):
    columns = own.shape[1]
    core = lax.axis_index("seq") % 2
    out[:, pl.ds(pl.multiple_of(core * columns, 128), columns)] = own[...]
    out[:, pl.ds(pl.multiple_of((1 - core) * columns, 128), columns)] = other[...]


def product(gated, distances, pieces):
    total = 0.0
    for distance, piece in zip(distances, pieces):
        source = source_of(distance)
        rows = jnp.concatenate([part[source] for part in gated], 0)
        total = total + jnp.dot(rows, piece[...], preferred_element_type=F32)
    return total


def product_early(distances, mine, other, *rest):
    rest[-1][...] = product((mine, other), distances, rest[:-1])


def product_last(distance, mine, other, total, top, bottom, mine_out, other_out, held):
    held[: top.shape[0]] = top[...]
    held[top.shape[0] :] = bottom[...]
    result = product((mine, other), [distance], [held]) + total[...]
    blocks, rows, width = mine.shape
    for i, (gated, out) in enumerate(((mine, mine_out), (other, other_out))):
        squares = jnp.zeros((rows, width), F32)
        for block in range(blocks):
            value = gated[block].astype(F32)
            squares = squares + value * value
        scale = lax.rsqrt(jnp.sum(squares, axis=1, keepdims=True) / (blocks * width) + NORM_EPS)
        out[...] = (result[i * rows : (i + 1) * rows] * scale).astype(BF16)


def call(body, outs, scratch=(), vmem=48, flops=10**7, moved=1 << 21, **kw):
    return pl.pallas_call(
        body,
        out_shape=outs,
        scratch_shapes=list(scratch),
        compiler_params=pltpu.CompilerParams(vmem_limit_bytes=vmem << 20),
        cost_estimate=pl.CostEstimate(flops=flops, bytes_accessed=moved, transcendentals=0),
        **kw,
    )


def local(
    tokens, w_zx, w_bc, w_dt, dt_bias, a_rate, d_skip, conv_x, conv_bc, norm_gain, w_out, segments
):
    tok_rows, feat = tokens.shape
    width = w_zx.shape[2]
    heads = dt_bias.shape[0]
    head_w = width // heads
    state_w = w_bc.shape[1] // 2
    model = w_zx.shape[1]
    n_seq, n_tensor = lax.axis_size("seq"), lax.axis_size("tensor")
    seq_at = lax.axis_index("seq")
    rows = tok_rows // 2
    shape = lambda *s, kind=F32: jax.ShapeDtypeStruct(s, kind)

    spread = lambda v: jnp.repeat(v, head_w, axis=-1)
    expand = np.repeat(np.eye(heads, dtype=np.float32), head_w, axis=1)
    w_step = jnp.dot(w_dt, expand.astype(BF16))
    block = tokens.T
    core = seq_at % 2
    columns = model // 2
    own = (lax.dynamic_slice_in_dim(w_out, core * columns, columns, 1).astype(F32) * norm_gain[:, None]).astype(BF16)
    last = n_tensor // 2
    w_half = width // 2
    shift_rows = [(i, i + 1) for i in range(n_seq - 1)]

    seg_halo = lax.ppermute(segments[tok_rows - HALO :], "seq", shift_rows)
    seg_all = jnp.concatenate([seg_halo, segments])[:, None]
    small = (
        (seg_all[: HALO + rows], seg_all[rows:]),
        (segments[None, :rows], segments[None, rows:]),
        (segments[None, :1], segments[None, tok_rows - 1 :]),
        (spread(dt_bias)[None], spread(a_rate)[None], spread(d_skip)[None]),
    )

    forth = back = block
    arrived, projs = [(0, block)], []
    for step in range(1, last + 1):
        if step == 3:
            forth, back = after(forth, projs[1], small), after(back, projs[1], small)
        elif step > 1:
            forth, back = after(forth, projs[step - 2]), after(back, projs[step - 2])
        arrivals = (forth, back)
        if step < last:
            forth, back = ring_shift(forth, 1), ring_shift(back, -1)
        else:
            far = far_shift(forth, back)
        if step == W_FIRST:
            w_forth, w_back = after((own, own), arrivals)
            w_forth, w_back = ring_shift(w_forth, 1), ring_shift(w_back, -1)
        ahead = last if step == last else 0
        total = projs[-1:]
        fetched = len(arrived) + bool(ahead)
        outs = [shape(tok_rows, 4 * width)] + [shape(feat, 4 * width, kind=BF16)] * bool(ahead)
        results = call(
            functools.partial(project, [distance for distance, _ in arrived], ahead, not total),
            outs,
            [pltpu.VMEM((len(arrived), feat, 4 * width), BF16), pltpu.SemaphoreType.DMA((fetched, 4))],
            in_specs=[VMEM] * len(arrived) + [ANY] * 3 + [VMEM] * len(total),
            flops=10**9,
        )(*[part for _, part in arrived], w_zx, w_bc, w_step, *total)
        projs.append(results[0])
        arrived = [(-step, forth), (step, back)]
    proj = call(project_far, shape(tok_rows, 4 * width), flops=10**9)(
        *far, results[1], projs[-1]
    )

    (seg_ext_a, seg_ext_b), (seg_row_a, seg_row_b), (seg_first, seg_last), (bias, rate, skip) = small
    halo = lax.ppermute(proj[tok_rows - HALO :, width : 3 * width].astype(BF16), "seq", shift_rows)

    msg_rows = state_w + 8
    plane = shape(rows, width)
    ext = pltpu.VMEM((HALO + rows, width), F32)
    *later, state_b = call(
        functools.partial(later_front, width, rows), [plane] * 5 + [shape(msg_rows, width)], [ext, ext]
    )(proj, seg_ext_b, conv_x, conv_bc, bias, rate)
    cx_a, bc_a, cum_a, scaled_a, enter_a, state_a, message = call(
        functools.partial(first_front, width, rows),
        [plane] * 5 + [shape(msg_rows, width)] * 2,
        [ext, ext],
    )(proj, halo, seg_ext_a, seg_last, state_b, conv_x, conv_bc, bias, rate)
    messages = lax.all_gather(message, "seq")
    gated = call(functools.partial(finish, heads, rows), shape(tok_rows, width, kind=BF16))(
        seg_first, messages, seg_ext_a, seg_row_a, seg_ext_b, seg_row_b, skip, proj,
        cx_a, bc_a, cum_a, scaled_a, enter_a, state_a, *later
    )
    tok_own = tok_rows // n_tensor

    w_steps = [(w_forth, w_back)]
    orders = [(far, projs[-1]), messages]
    for step in range(2, last + 1):
        if step - 2 < len(orders):
            w_forth, w_back = after((w_forth, w_back), orders[step - 2])
        if step == last:
            w_far = far_shift(w_forth, w_back)
            break
        w_forth, w_back = ring_shift(w_forth, 1), ring_shift(w_back, -1)
        w_steps.append((w_forth, w_back))
        if step == 2:
            blocks = after(gated, w_forth, w_back).reshape(n_tensor, tok_own, width)
            mine = lax.all_to_all(blocks, "tensor", 0, 0)
    swap = [(i, i ^ 1) for i in range(n_seq)]
    other = lax.ppermute(mine, "seq", swap)
    pieces, distances = [own], [0]
    for i, pair in enumerate(w_steps):
        pieces += pair
        distances += [-i - 1, i + 1]
    total = call(functools.partial(product_early, distances), shape(2 * tok_own, columns), flops=1, moved=1)(
        mine, other, *pieces
    )
    half = shape(tok_own, columns, kind=BF16)
    out_own, out_other = call(
        functools.partial(product_last, last), [half, half], [pltpu.VMEM((width, columns), BF16)], flops=10**8
    )(mine, other, total, *w_far)
    return call(lay_together, shape(tok_own, model, kind=BF16))(out_own, lax.ppermute(out_other, "seq", swap))


def solution(mesh):
    in_specs = (
        P("seq", "tensor"),
        P(None, None, "tensor"),
        P(),
        P(None, "tensor"),
        P("tensor"),
        P("tensor"),
        P("tensor"),
        P(None, "tensor"),
        P(),
        P("tensor"),
        P("tensor", None),
        P("seq"),
    )
    out_specs = P(("seq", "tensor"), None)
    return jax.shard_map(local, mesh=mesh, in_specs=in_specs, out_specs=out_specs, check_vma=False)
```

```python
import functools

import jax
import jax.numpy as jnp
import numpy as np
from jax import lax
from jax.experimental import pallas as pl
from jax.experimental.pallas import tpu as pltpu
from jax.sharding import PartitionSpec as P

NORM_EPS = 1e-05
F32 = jnp.float32
BF16 = jnp.bfloat16
VMEM = pl.BlockSpec(memory_space=pltpu.VMEM)
ANY = pl.BlockSpec(memory_space=pl.ANY)
HALO = 8
W_FIRST = 2


def ring_place(index, n):
    return jnp.where(index % 2 == 0, index // 2, (2 * n - 1 - index) // 2)


def ring_index(place, n):
    return jnp.where(place < n // 2, 2 * place, 2 * n - 1 - 2 * place)


def ring_shift(block, step):
    n = lax.axis_size("tensor")
    order = [2 * i if i < n // 2 else 2 * n - 1 - 2 * i for i in range(n)]
    return lax.ppermute(block, "tensor", [(order[i], order[(i + step) % n]) for i in range(n)])


def after(values, *earlier):
    return lax.optimization_barrier((values, earlier))[0]


def far_shift(forth, back):
    cut = forth.shape[0] // 32 * 16
    parts = [jax.ShapeDtypeStruct((size, forth.shape[1]), forth.dtype) for size in (cut, forth.shape[0] - cut)]
    top, bottom = call(halves, parts)(forth, back)
    return ring_shift(top, 1), ring_shift(bottom, -1)


def halves(forth, back, top, bottom):
    size = top.shape[0]
    top[...] = forth[:size]
    bottom[...] = back[size:]


def silu(v):
    return v / (1.0 + jnp.exp(-v))


def dot(a, b, dims=((1,), (0,))):
    return lax.dot_general(a.astype(BF16), b.astype(BF16), (dims, ((), ())), preferred_element_type=F32)


def source_of(distance):
    n = lax.axis_size("tensor")
    return ring_index((ring_place(lax.axis_index("tensor"), n) + distance + n) % n, n)


def project(distances, ahead, first, *refs):
    count, fetched = len(distances), len(distances) + bool(ahead)
    blocks, (w_zx, w_bc, w_dt), refs = refs[:count], refs[count : count + 3], refs[count + 3 :]
    total, refs = (None, refs) if first else (refs[0], refs[1:])
    out, far_out, held, sems = refs if ahead else (refs[0], None, *refs[1:])
    feat, width = held.shape[1], w_bc.shape[1]
    sources = [w_zx.at[0], w_zx.at[1], w_bc, w_dt]
    copies = []
    for k, distance in enumerate([*distances, ahead][:fetched]):
        rows = pl.ds(pl.multiple_of(source_of(distance) * feat, 16), feat)
        for j, source in enumerate(sources):
            target = held.at[k] if k < count else far_out
            copies.append(
                pltpu.make_async_copy(source.at[rows], target.at[:, pl.ds(j * width, width)], sems.at[k, j])
            )
            copies[-1].start()
    result = 0.0 if first else total[...]
    for k in range(count):
        for j in range(len(sources)):
            copies[k * len(sources) + j].wait()
        result = result + dot(blocks[k][...], held[k], ((0,), (0,)))
    out[...] = result
    for copy in copies[count * len(sources) :]:
        copy.wait()


def project_far(top, bottom, weights, total, out):
    cut = top.shape[0]
    out[...] = (
        total[...] + dot(top[...], weights[:cut], ((0,), (0,))) + dot(bottom[...], weights[cut:], ((0,), (0,)))
    )


def conv(ext, seg_ext, taps, rows):
    size = taps.shape[0]
    seg_now = seg_ext[HALO : HALO + rows]
    total = taps[size - 1 : size] * ext[HALO : HALO + rows]
    for offset in range(1, size):
        same = seg_ext[HALO - offset : HALO - offset + rows] == seg_now
        total = total + taps[size - 1 - offset : size - offset] * jnp.where(
            same, ext[HALO - offset : HALO - offset + rows], 0.0
        )
    return silu(total)


def prefix_sum(values):
    rows = values.shape[0]
    lower = lax.broadcasted_iota(jnp.int32, (rows, rows), 0) >= lax.broadcasted_iota(jnp.int32, (rows, rows), 1)
    lower = jnp.where(lower, 1.0, 0.0).astype(BF16)
    total = jnp.zeros(values.shape, F32)
    rest = values
    parts = []
    for _ in range(3):
        part = rest.astype(BF16)
        parts.append(part)
        rest = rest - part.astype(F32)
    for part in reversed(parts):
        total = total + jnp.dot(lower, part, preferred_element_type=F32)
    return total


def block_front(ext_x, ext_bc, seg_ext, dt_raw, taps_x, taps_bc, bias, rate, rows, seg_enter, seg_leave):
    conv_x = conv(ext_x, seg_ext, taps_x, rows)
    conv_bc = conv(ext_bc, seg_ext, taps_bc, rows)
    seg = seg_ext[HALO : HALO + rows]
    shifted = dt_raw + bias
    step_size = jnp.maximum(shifted, 0.0) + jnp.log1p(jnp.exp(-jnp.abs(shifted)))
    cum = prefix_sum(-rate * step_size)
    scaled = conv_x * step_size
    last = cum[rows - 1 : rows]
    tail = jnp.where(seg == seg_leave, jnp.exp(last - cum), 0.0)
    state_w = conv_bc.shape[1] // 2
    state = dot(conv_bc, tail * scaled, ((0,), (0,)))[:state_w]
    enter = jnp.where(seg == seg_enter, jnp.exp(cum), 0.0)
    return conv_x, conv_bc, cum, scaled, state, enter, last


def block_inner(conv_bc, cum, scaled, seg_col, seg_row, heads):
    rows, width = scaled.shape
    state_w = conv_bc.shape[1] // 2
    head_w = width // heads
    scores = dot(conv_bc[:, state_w:], conv_bc[:, :state_w], ((1,), (1,)))
    later = lax.broadcasted_iota(jnp.int32, (rows, rows), 0) >= lax.broadcasted_iota(jnp.int32, (rows, rows), 1)
    visible = (seg_col == seg_row) & later
    cum_rows = cum.T
    lane = lax.broadcasted_iota(jnp.int32, (rows, width), 1)
    result = jnp.zeros((rows, width), F32)
    scaled = scaled.astype(BF16)
    for head in range(heads):
        at = head * head_w
        gap = jnp.where(visible, cum[:, at : at + 1] - cum_rows[at : at + 1, :], -jnp.inf)
        part = dot(jnp.exp(gap) * scores, scaled)
        result = jnp.where((lane >= at) & (lane < at + head_w), part, result)
    return result


def later_block(heads, width, rows, proj, seg_ext, seg_row, taps_x, taps_bc, bias, rate, skip,
                out, bc_out, enter_out, state_out, gate_out, ext_x, ext_bc):
    rounded = proj[rows - HALO :, : 3 * width].astype(BF16).astype(F32)
    gate_out[...] = silu(rounded[HALO:, :width])
    ext_x[...] = rounded[:, width : 2 * width]
    ext_bc[...] = rounded[:, 2 * width : 3 * width]
    seg_enter = seg_ext[HALO - 1 : HALO]
    seg_leave = seg_ext[HALO + rows - 1 : HALO + rows]
    conv_x, conv_bc, cum, scaled, state, enter, last = block_front(
        ext_x, ext_bc, seg_ext, proj[rows:, 3 * width :], taps_x, taps_bc[...], bias[...], rate[...], rows, seg_enter, seg_leave
    )
    out[...] = block_inner(conv_bc, cum, scaled, seg_ext[HALO:], seg_row[...], heads) + skip[...] * conv_x
    bc_out[...] = conv_bc
    enter_out[...] = enter
    keep = jnp.where(seg_enter == seg_leave, jnp.exp(last), 0.0)
    state_w = state.shape[0]
    state_out[:state_w] = state
    state_out[state_w : state_w + 1] = keep
    state_out[state_w + 1 : state_w + 2] = last
    state_out[state_w + 2 :] = jnp.zeros((state_out.shape[0] - state_w - 2, width), F32)


def first_front(width, rows, proj, halo, seg_ext, seg_last, state_b, taps_x, taps_bc, bias, rate,
                conv_out, bc_out, cum_out, scaled_out, enter_out, state_out, message, ext_x, ext_bc):
    ext_x[:HALO] = halo[:, :width].astype(F32)
    ext_bc[:HALO] = halo[:, width:].astype(F32)
    ext_x[HALO:] = proj[:rows, width : 2 * width].astype(BF16).astype(F32)
    ext_bc[HALO:] = proj[:rows, 2 * width : 3 * width].astype(BF16).astype(F32)
    seg_enter = seg_ext[HALO : HALO + 1]
    seg_leave = seg_ext[HALO + rows - 1 : HALO + rows]
    conv_x, conv_bc, cum, scaled, state, enter, last = block_front(
        ext_x, ext_bc, seg_ext, proj[:rows, 3 * width :], taps_x, taps_bc[...], bias[...], rate[...], rows, seg_enter, seg_leave
    )
    conv_out[...] = conv_x
    bc_out[...] = conv_bc
    cum_out[...] = cum
    scaled_out[...] = scaled
    enter_out[...] = enter
    keep = jnp.where(seg_enter == seg_leave, jnp.exp(last), 0.0)
    state_w = state.shape[0]
    state_out[:state_w] = state
    state_out[state_w : state_w + 1] = keep
    state_out[state_w + 1 :] = jnp.zeros((state_out.shape[0] - state_w - 1, width), F32)
    message[:state_w] = state_b[state_w : state_w + 1] * state + state_b[:state_w]
    message[state_w : state_w + 1] = last + state_b[state_w + 1 : state_w + 2]
    message[state_w + 1 : state_w + 2] = jnp.broadcast_to(seg_last[...].astype(F32), (1, width))
    message[state_w + 2 :] = jnp.zeros((message.shape[0] - state_w - 2, width), F32)


def finish(heads, rows, seg_first, messages, seg_ext_a, seg_row_a, skip, proj, conv_a, bc_a, cum_a, scaled_a, enter_a,
           state_a, out_b, gate_b, bc_b, enter_b, gated):
    state_w = bc_a.shape[1] // 2
    width = out_b.shape[1]
    entering = jnp.zeros((state_w, width), F32)
    decay = jnp.zeros((1, width), F32)
    first = seg_first[...].astype(F32)
    place = lax.axis_index("seq")
    for device in reversed(range(messages.shape[0] - 1)):
        earlier = device < place
        passes = earlier & (messages[device, state_w + 1 : state_w + 2] == first)
        passes = jnp.where(passes, jnp.exp(decay), 0.0)
        entering = entering + passes * messages[device, :state_w]
        decay = decay + jnp.where(earlier, messages[device, state_w : state_w + 1], 0.0)
    second = state_a[state_w : state_w + 1] * entering + state_a[:state_w]
    out_a = block_inner(bc_a[...], cum_a[...], scaled_a[...], seg_ext_a[HALO:], seg_row_a[...], heads)
    out_a = out_a + skip[...] * conv_a[...] + enter_a[...] * dot(bc_a[:, state_w:], entering)
    gated[:rows] = (out_a * silu(proj[:rows, :width].astype(BF16).astype(F32))).astype(BF16)
    gated[rows:] = ((out_b[...] + enter_b[...] * dot(bc_b[:, state_w:], second)) * gate_b[...]).astype(BF16)


def product(gated, distances, pieces):
    total = 0.0
    for distance, piece in zip(distances, pieces):
        source = source_of(distance)
        rows = jnp.concatenate([part[source] for part in gated], 0)
        total = total + jnp.dot(rows, piece[...], preferred_element_type=F32)
    return total


def product_early(distances, mine, other, *rest):
    rest[-1][...] = product((mine, other), distances, rest[:-1])


def product_last(distance, mine, other, total, top, bottom, mine_out, other_out, held):
    held[: top.shape[0]] = top[...]
    held[top.shape[0] :] = bottom[...]
    result = product((mine, other), [distance], [held]) + total[...]
    blocks, rows, width = mine.shape
    for i, (gated, out) in enumerate(((mine, mine_out), (other, other_out))):
        squares = jnp.zeros((rows, width), F32)
        for block in range(blocks):
            value = gated[block].astype(F32)
            squares = squares + value * value
        scale = lax.rsqrt(jnp.sum(squares, axis=1, keepdims=True) / (blocks * width) + NORM_EPS)
        out[...] = (result[i * rows : (i + 1) * rows] * scale).astype(BF16)


def call(body, outs, scratch=(), vmem=48, flops=10**7, moved=1 << 21, **kw):
    return pl.pallas_call(
        body,
        out_shape=outs,
        scratch_shapes=list(scratch),
        compiler_params=pltpu.CompilerParams(vmem_limit_bytes=vmem << 20),
        cost_estimate=pl.CostEstimate(flops=flops, bytes_accessed=moved, transcendentals=0),
        **kw,
    )


def local(
    tokens, w_zx, w_bc, w_dt, dt_bias, a_rate, d_skip, conv_x, conv_bc, norm_gain, w_out, segments
):
    tok_rows, feat = tokens.shape
    width = w_zx.shape[2]
    heads = dt_bias.shape[0]
    head_w = width // heads
    state_w = w_bc.shape[1] // 2
    model = w_zx.shape[1]
    n_seq, n_tensor = lax.axis_size("seq"), lax.axis_size("tensor")
    seq_at = lax.axis_index("seq")
    rows = tok_rows // 2
    shape = lambda *s, kind=F32: jax.ShapeDtypeStruct(s, kind)

    spread = lambda v: jnp.repeat(v, head_w, axis=-1)
    expand = np.repeat(np.eye(heads, dtype=np.float32), head_w, axis=1)
    w_step = jnp.dot(w_dt, expand.astype(BF16))
    block = tokens.T
    core = seq_at % 2
    columns = model // 2
    own = (lax.dynamic_slice_in_dim(w_out, core * columns, columns, 1).astype(F32) * norm_gain[:, None]).astype(BF16)
    last = n_tensor // 2
    w_half = width // 2
    shift_rows = [(i, i + 1) for i in range(n_seq - 1)]

    seg_halo = lax.ppermute(segments[tok_rows - HALO :], "seq", shift_rows)
    seg_all = jnp.concatenate([seg_halo, segments])[:, None]
    small = (
        (seg_all[: HALO + rows], seg_all[rows:]),
        (segments[None, :rows], segments[None, rows:]),
        (segments[None, :1], segments[None, tok_rows - 1 :]),
        (spread(dt_bias)[None], spread(a_rate)[None], spread(d_skip)[None]),
    )

    forth = back = block
    arrived, projs = [(0, block)], []
    for step in range(1, last + 1):
        if step == 3:
            forth, back = after(forth, projs[1], small), after(back, projs[1], small)
        elif step > 1:
            forth, back = after(forth, projs[step - 2]), after(back, projs[step - 2])
        arrivals = (forth, back)
        if step < last:
            forth, back = ring_shift(forth, 1), ring_shift(back, -1)
        else:
            far = far_shift(forth, back)
        if step == W_FIRST:
            w_forth, w_back = after((own, own), arrivals)
            w_forth, w_back = ring_shift(w_forth, 1), ring_shift(w_back, -1)
        ahead = last if step == last else 0
        total = projs[-1:]
        if step == 3:
            total = [after(projs[-1], w_forth, w_back)]
        fetched = len(arrived) + bool(ahead)
        outs = [shape(tok_rows, 4 * width)] + [shape(feat, 4 * width, kind=BF16)] * bool(ahead)
        results = call(
            functools.partial(project, [distance for distance, _ in arrived], ahead, not total),
            outs,
            [pltpu.VMEM((len(arrived), feat, 4 * width), BF16), pltpu.SemaphoreType.DMA((fetched, 4))],
            in_specs=[VMEM] * len(arrived) + [ANY] * 3 + [VMEM] * len(total),
            flops=10**9,
        )(*[part for _, part in arrived], w_zx, w_bc, w_step, *total)
        projs.append(results[0])
        arrived = [(-step, forth), (step, back)]
    proj = call(project_far, shape(tok_rows, 4 * width), flops=10**9)(
        *far, results[1], projs[-1]
    )

    (seg_ext_a, seg_ext_b), (seg_row_a, seg_row_b), (seg_first, seg_last), (bias, rate, skip) = small
    halo = lax.ppermute(proj[tok_rows - HALO :, width : 3 * width].astype(BF16), "seq", shift_rows)

    msg_rows = state_w + 8
    plane = shape(rows, width)
    ext = pltpu.VMEM((HALO + rows, width), F32)
    out_b, bc_b, enter_b, state_b, gate_b = call(
        functools.partial(later_block, heads, width, rows),
        [plane, plane, plane, shape(msg_rows, width), plane],
        [ext, ext],
    )(proj, seg_ext_b, seg_row_b, conv_x, conv_bc, bias, rate, skip)
    cx_a, bc_a, cum_a, scaled_a, enter_a, state_a, message = call(
        functools.partial(first_front, width, rows),
        [plane] * 5 + [shape(msg_rows, width)] * 2,
        [ext, ext],
    )(proj, halo, seg_ext_a, seg_last, state_b, conv_x, conv_bc, bias, rate)
    messages = lax.all_gather(message, "seq")
    gated = call(functools.partial(finish, heads, rows), shape(tok_rows, width, kind=BF16))(
        seg_first, messages, seg_ext_a, seg_row_a, skip, proj, cx_a, bc_a, cum_a, scaled_a, enter_a, state_a,
        out_b, gate_b, bc_b, enter_b
    )
    tok_own = tok_rows // n_tensor

    w_steps = [(w_forth, w_back)]
    orders = [(far, projs[-1]), messages]
    for step in range(2, last + 1):
        if step - 2 < len(orders):
            w_forth, w_back = after((w_forth, w_back), orders[step - 2])
        if step == last:
            w_far = far_shift(w_forth, w_back)
            break
        w_forth, w_back = ring_shift(w_forth, 1), ring_shift(w_back, -1)
        w_steps.append((w_forth, w_back))
        if step == 2:
            blocks = after(gated, w_forth, w_back).reshape(n_tensor, tok_own, width)
            mine = lax.all_to_all(blocks, "tensor", 0, 0)
    swap = [(i, i ^ 1) for i in range(n_seq)]
    other = lax.ppermute(mine, "seq", swap)
    pieces, distances = [own], [0]
    for i, pair in enumerate(w_steps):
        pieces += pair
        distances += [-i - 1, i + 1]
    total = call(functools.partial(product_early, distances), shape(2 * tok_own, columns), flops=1, moved=1)(
        mine, other, *pieces
    )
    half = shape(tok_own, columns, kind=BF16)
    out_own, out_other = call(
        functools.partial(product_last, last), [half, half], [pltpu.VMEM((width, columns), BF16)], flops=10**8
    )(mine, other, total, *w_far)
    arrived = lax.ppermute(out_other, "seq", swap)
    is_first = core == 0
    return jnp.concatenate([jnp.where(is_first, out_own, arrived), jnp.where(is_first, arrived, out_own)], 1)


def solution(mesh):
    in_specs = (
        P("seq", "tensor"),
        P(None, None, "tensor"),
        P(),
        P(None, "tensor"),
        P("tensor"),
        P("tensor"),
        P("tensor"),
        P(None, "tensor"),
        P(),
        P("tensor"),
        P("tensor", None),
        P("seq"),
    )
    out_specs = P(("seq", "tensor"), None)
    return jax.shard_map(local, mesh=mesh, in_specs=in_specs, out_specs=out_specs, check_vma=False)
```

```python
import functools

import jax
import jax.numpy as jnp
import numpy as np
from jax import lax
from jax.experimental import pallas as pl
from jax.experimental.pallas import tpu as pltpu
from jax.sharding import PartitionSpec as P

NORM_EPS = 1e-05
F32 = jnp.float32
BF16 = jnp.bfloat16
VMEM = pl.BlockSpec(memory_space=pltpu.VMEM)
ANY = pl.BlockSpec(memory_space=pl.ANY)
HALO = 8
W_FIRST = 3


def ring_place(index, n):
    return jnp.where(index % 2 == 0, index // 2, (2 * n - 1 - index) // 2)


def ring_index(place, n):
    return jnp.where(place < n // 2, 2 * place, 2 * n - 1 - 2 * place)


def ring_shift(block, step):
    n = lax.axis_size("tensor")
    order = [2 * i if i < n // 2 else 2 * n - 1 - 2 * i for i in range(n)]
    return lax.ppermute(block, "tensor", [(order[i], order[(i + step) % n]) for i in range(n)])


def after(values, *earlier):
    return lax.optimization_barrier((values, earlier))[0]


def far_shift(forth, back):
    cut = forth.shape[0] // 32 * 16
    parts = [jax.ShapeDtypeStruct((size, forth.shape[1]), forth.dtype) for size in (cut, forth.shape[0] - cut)]
    top, bottom = call(halves, parts)(forth, back)
    return ring_shift(top, 1), ring_shift(bottom, -1)


def halves(forth, back, top, bottom):
    size = top.shape[0]
    top[...] = forth[:size]
    bottom[...] = back[size:]


def silu(v):
    return v / (1.0 + jnp.exp(-v))


def dot(a, b, dims=((1,), (0,))):
    return lax.dot_general(a.astype(BF16), b.astype(BF16), (dims, ((), ())), preferred_element_type=F32)


def source_of(distance):
    n = lax.axis_size("tensor")
    return ring_index((ring_place(lax.axis_index("tensor"), n) + distance + n) % n, n)


def project(distances, ahead, first, *refs):
    count, fetched = len(distances), len(distances) + bool(ahead)
    blocks, (w_zx, w_bc, w_dt), refs = refs[:count], refs[count : count + 3], refs[count + 3 :]
    total, refs = (None, refs) if first else (refs[0], refs[1:])
    out, far_out, held, sems = refs if ahead else (refs[0], None, *refs[1:])
    feat, width = held.shape[1], w_bc.shape[1]
    sources = [w_zx.at[0], w_zx.at[1], w_bc, w_dt]
    copies = []
    for k, distance in enumerate([*distances, ahead][:fetched]):
        rows = pl.ds(pl.multiple_of(source_of(distance) * feat, 16), feat)
        for j, source in enumerate(sources):
            target = held.at[k] if k < count else far_out
            copies.append(
                pltpu.make_async_copy(source.at[rows], target.at[:, pl.ds(j * width, width)], sems.at[k, j])
            )
            copies[-1].start()
    result = 0.0 if first else total[...]
    for k in range(count):
        for j in range(len(sources)):
            copies[k * len(sources) + j].wait()
        result = result + dot(blocks[k][...], held[k], ((0,), (0,)))
    out[...] = result
    for copy in copies[count * len(sources) :]:
        copy.wait()


def project_far(top, bottom, weights, total, out):
    cut = top.shape[0]
    out[...] = (
        total[...] + dot(top[...], weights[:cut], ((0,), (0,))) + dot(bottom[...], weights[cut:], ((0,), (0,)))
    )


def conv(ext, seg_ext, taps, rows):
    size = taps.shape[0]
    seg_now = seg_ext[HALO : HALO + rows]
    total = taps[size - 1 : size] * ext[HALO : HALO + rows]
    for offset in range(1, size):
        same = seg_ext[HALO - offset : HALO - offset + rows] == seg_now
        total = total + taps[size - 1 - offset : size - offset] * jnp.where(
            same, ext[HALO - offset : HALO - offset + rows], 0.0
        )
    return silu(total)


def prefix_sum(values):
    rows = values.shape[0]
    lower = lax.broadcasted_iota(jnp.int32, (rows, rows), 0) >= lax.broadcasted_iota(jnp.int32, (rows, rows), 1)
    lower = jnp.where(lower, 1.0, 0.0).astype(BF16)
    total = jnp.zeros(values.shape, F32)
    rest = values
    parts = []
    for _ in range(3):
        part = rest.astype(BF16)
        parts.append(part)
        rest = rest - part.astype(F32)
    for part in reversed(parts):
        total = total + jnp.dot(lower, part, preferred_element_type=F32)
    return total


def block_front(ext_x, ext_bc, seg_ext, dt_raw, taps_x, taps_bc, bias, rate, rows, seg_enter, seg_leave):
    conv_x = conv(ext_x, seg_ext, taps_x, rows)
    conv_bc = conv(ext_bc, seg_ext, taps_bc, rows)
    seg = seg_ext[HALO : HALO + rows]
    shifted = dt_raw + bias
    step_size = jnp.maximum(shifted, 0.0) + jnp.log1p(jnp.exp(-jnp.abs(shifted)))
    cum = prefix_sum(-rate * step_size)
    scaled = conv_x * step_size
    last = cum[rows - 1 : rows]
    tail = jnp.where(seg == seg_leave, jnp.exp(last - cum), 0.0)
    state_w = conv_bc.shape[1] // 2
    state = dot(conv_bc, tail * scaled, ((0,), (0,)))[:state_w]
    enter = jnp.where(seg == seg_enter, jnp.exp(cum), 0.0)
    return conv_x, conv_bc, cum, scaled, state, enter, last


def block_inner(conv_bc, cum, scaled, seg_col, seg_row, heads):
    rows, width = scaled.shape
    state_w = conv_bc.shape[1] // 2
    head_w = width // heads
    scores = dot(conv_bc[:, state_w:], conv_bc[:, :state_w], ((1,), (1,)))
    later = lax.broadcasted_iota(jnp.int32, (rows, rows), 0) >= lax.broadcasted_iota(jnp.int32, (rows, rows), 1)
    visible = (seg_col == seg_row) & later
    cum_rows = cum.T
    lane = lax.broadcasted_iota(jnp.int32, (rows, width), 1)
    result = jnp.zeros((rows, width), F32)
    scaled = scaled.astype(BF16)
    for head in range(heads):
        at = head * head_w
        gap = jnp.where(visible, cum[:, at : at + 1] - cum_rows[at : at + 1, :], -jnp.inf)
        part = dot(jnp.exp(gap) * scores, scaled)
        result = jnp.where((lane >= at) & (lane < at + head_w), part, result)
    return result


def later_block(heads, width, rows, proj, seg_ext, seg_row, taps_x, taps_bc, bias, rate, skip,
                out, bc_out, enter_out, state_out, gate_out, ext_x, ext_bc):
    rounded = proj[rows - HALO :, : 3 * width].astype(BF16).astype(F32)
    gate_out[...] = silu(rounded[HALO:, :width])
    ext_x[...] = rounded[:, width : 2 * width]
    ext_bc[...] = rounded[:, 2 * width : 3 * width]
    seg_enter = seg_ext[HALO - 1 : HALO]
    seg_leave = seg_ext[HALO + rows - 1 : HALO + rows]
    conv_x, conv_bc, cum, scaled, state, enter, last = block_front(
        ext_x, ext_bc, seg_ext, proj[rows:, 3 * width :], taps_x, taps_bc[...], bias[...], rate[...], rows, seg_enter, seg_leave
    )
    out[...] = block_inner(conv_bc, cum, scaled, seg_ext[HALO:], seg_row[...], heads) + skip[...] * conv_x
    bc_out[...] = conv_bc
    enter_out[...] = enter
    keep = jnp.where(seg_enter == seg_leave, jnp.exp(last), 0.0)
    state_w = state.shape[0]
    state_out[:state_w] = state
    state_out[state_w : state_w + 1] = keep
    state_out[state_w + 1 : state_w + 2] = last
    state_out[state_w + 2 :] = jnp.zeros((state_out.shape[0] - state_w - 2, width), F32)


def first_front(width, rows, proj, halo, seg_ext, seg_last, state_b, taps_x, taps_bc, bias, rate,
                conv_out, bc_out, cum_out, scaled_out, enter_out, state_out, message, ext_x, ext_bc):
    ext_x[:HALO] = halo[:, :width].astype(F32)
    ext_bc[:HALO] = halo[:, width:].astype(F32)
    ext_x[HALO:] = proj[:rows, width : 2 * width].astype(BF16).astype(F32)
    ext_bc[HALO:] = proj[:rows, 2 * width : 3 * width].astype(BF16).astype(F32)
    seg_enter = seg_ext[HALO : HALO + 1]
    seg_leave = seg_ext[HALO + rows - 1 : HALO + rows]
    conv_x, conv_bc, cum, scaled, state, enter, last = block_front(
        ext_x, ext_bc, seg_ext, proj[:rows, 3 * width :], taps_x, taps_bc[...], bias[...], rate[...], rows, seg_enter, seg_leave
    )
    conv_out[...] = conv_x
    bc_out[...] = conv_bc
    cum_out[...] = cum
    scaled_out[...] = scaled
    enter_out[...] = enter
    keep = jnp.where(seg_enter == seg_leave, jnp.exp(last), 0.0)
    state_w = state.shape[0]
    state_out[:state_w] = state
    state_out[state_w : state_w + 1] = keep
    state_out[state_w + 1 :] = jnp.zeros((state_out.shape[0] - state_w - 1, width), F32)
    message[:state_w] = state_b[state_w : state_w + 1] * state + state_b[:state_w]
    message[state_w : state_w + 1] = last + state_b[state_w + 1 : state_w + 2]
    message[state_w + 1 : state_w + 2] = jnp.broadcast_to(seg_last[...].astype(F32), (1, width))
    message[state_w + 2 :] = jnp.zeros((message.shape[0] - state_w - 2, width), F32)


def finish(heads, rows, seg_first, messages, seg_ext_a, seg_row_a, skip, proj, conv_a, bc_a, cum_a, scaled_a, enter_a,
           state_a, out_b, gate_b, bc_b, enter_b, gated):
    state_w = bc_a.shape[1] // 2
    width = out_b.shape[1]
    entering = jnp.zeros((state_w, width), F32)
    decay = jnp.zeros((1, width), F32)
    first = seg_first[...].astype(F32)
    place = lax.axis_index("seq")
    for device in reversed(range(messages.shape[0] - 1)):
        earlier = device < place
        passes = earlier & (messages[device, state_w + 1 : state_w + 2] == first)
        passes = jnp.where(passes, jnp.exp(decay), 0.0)
        entering = entering + passes * messages[device, :state_w]
        decay = decay + jnp.where(earlier, messages[device, state_w : state_w + 1], 0.0)
    second = state_a[state_w : state_w + 1] * entering + state_a[:state_w]
    out_a = block_inner(bc_a[...], cum_a[...], scaled_a[...], seg_ext_a[HALO:], seg_row_a[...], heads)
    out_a = out_a + skip[...] * conv_a[...] + enter_a[...] * dot(bc_a[:, state_w:], entering)
    gated[:rows] = (out_a * silu(proj[:rows, :width].astype(BF16).astype(F32))).astype(BF16)
    gated[rows:] = ((out_b[...] + enter_b[...] * dot(bc_b[:, state_w:], second)) * gate_b[...]).astype(BF16)


def product(gated, distances, pieces):
    total = 0.0
    for distance, piece in zip(distances, pieces):
        source = source_of(distance)
        rows = jnp.concatenate([part[source] for part in gated], 0)
        total = total + jnp.dot(rows, piece[...], preferred_element_type=F32)
    return total


def product_early(distances, mine, other, *rest):
    rest[-1][...] = product((mine, other), distances, rest[:-1])


def last_rows(distance, gated, total, top, bottom, held):
    held[: top.shape[0]] = top[...]
    held[top.shape[0] :] = bottom[...]
    blocks, rows, width = gated.shape
    squares = jnp.zeros((rows, width), F32)
    for block in range(blocks):
        value = gated[block].astype(F32)
        squares = squares + value * value
    scale = lax.rsqrt(jnp.sum(squares, axis=1, keepdims=True) / (blocks * width) + NORM_EPS)
    return ((product((gated,), [distance], [held]) + total) * scale).astype(BF16)


def last_other(distance, other, total, top, bottom, out, held):
    rows = other.shape[1]
    out[...] = last_rows(distance, other, total[rows:], top, bottom, held)


def last_mine(distance, mine, total, top, bottom, out, held):
    rows, columns = mine.shape[1], held.shape[1]
    start = pl.multiple_of(lax.axis_index("seq") % 2 * columns, 128)
    out[:, pl.ds(start, columns)] = last_rows(distance, mine, total[:rows], top, bottom, held)


def put_other(whole, arrived, out, sem):
    del whole
    columns = arrived.shape[1]
    start = pl.multiple_of((1 - lax.axis_index("seq") % 2) * columns, 128)
    copy = pltpu.make_async_copy(arrived, out.at[:, pl.ds(start, columns)], sem)
    copy.start()
    copy.wait()


def call(body, outs, scratch=(), vmem=48, flops=10**7, moved=1 << 21, **kw):
    return pl.pallas_call(
        body,
        out_shape=outs,
        scratch_shapes=list(scratch),
        compiler_params=pltpu.CompilerParams(vmem_limit_bytes=vmem << 20),
        cost_estimate=pl.CostEstimate(flops=flops, bytes_accessed=moved, transcendentals=0),
        **kw,
    )


def local(
    tokens, w_zx, w_bc, w_dt, dt_bias, a_rate, d_skip, conv_x, conv_bc, norm_gain, w_out, segments
):
    tok_rows, feat = tokens.shape
    width = w_zx.shape[2]
    heads = dt_bias.shape[0]
    head_w = width // heads
    state_w = w_bc.shape[1] // 2
    model = w_zx.shape[1]
    n_seq, n_tensor = lax.axis_size("seq"), lax.axis_size("tensor")
    seq_at = lax.axis_index("seq")
    rows = tok_rows // 2
    shape = lambda *s, kind=F32: jax.ShapeDtypeStruct(s, kind)

    spread = lambda v: jnp.repeat(v, head_w, axis=-1)
    expand = np.repeat(np.eye(heads, dtype=np.float32), head_w, axis=1)
    w_step = jnp.dot(w_dt, expand.astype(BF16))
    block = tokens.T
    core = seq_at % 2
    columns = model // 2
    own = (lax.dynamic_slice_in_dim(w_out, core * columns, columns, 1).astype(F32) * norm_gain[:, None]).astype(BF16)
    last = n_tensor // 2
    w_half = width // 2
    shift_rows = [(i, i + 1) for i in range(n_seq - 1)]

    seg_halo = lax.ppermute(segments[tok_rows - HALO :], "seq", shift_rows)
    seg_all = jnp.concatenate([seg_halo, segments])[:, None]
    small = (
        (seg_all[: HALO + rows], seg_all[rows:]),
        (segments[None, :rows], segments[None, rows:]),
        (segments[None, :1], segments[None, tok_rows - 1 :]),
        (spread(dt_bias)[None], spread(a_rate)[None], spread(d_skip)[None]),
    )

    forth = back = block
    arrived, projs = [(0, block)], []
    for step in range(1, last + 1):
        if step == 3:
            forth, back = after(forth, projs[1], small), after(back, projs[1], small)
        elif step > 1:
            forth, back = after(forth, projs[step - 2]), after(back, projs[step - 2])
        arrivals = (forth, back)
        if step < last:
            forth, back = ring_shift(forth, 1), ring_shift(back, -1)
        else:
            far = far_shift(forth, back)
        if step == W_FIRST:
            w_forth, w_back = after((own, own), arrivals)
            w_forth, w_back = ring_shift(w_forth, 1), ring_shift(w_back, -1)
        ahead = last if step == last else 0
        total = projs[-1:]
        fetched = len(arrived) + bool(ahead)
        outs = [shape(tok_rows, 4 * width)] + [shape(feat, 4 * width, kind=BF16)] * bool(ahead)
        results = call(
            functools.partial(project, [distance for distance, _ in arrived], ahead, not total),
            outs,
            [pltpu.VMEM((len(arrived), feat, 4 * width), BF16), pltpu.SemaphoreType.DMA((fetched, 4))],
            in_specs=[VMEM] * len(arrived) + [ANY] * 3 + [VMEM] * len(total),
            flops=10**9,
        )(*[part for _, part in arrived], w_zx, w_bc, w_step, *total)
        projs.append(results[0])
        arrived = [(-step, forth), (step, back)]
    proj = call(project_far, shape(tok_rows, 4 * width), flops=10**9)(
        *far, results[1], projs[-1]
    )

    (seg_ext_a, seg_ext_b), (seg_row_a, seg_row_b), (seg_first, seg_last), (bias, rate, skip) = small
    halo = lax.ppermute(proj[tok_rows - HALO :, width : 3 * width].astype(BF16), "seq", shift_rows)

    msg_rows = state_w + 8
    plane = shape(rows, width)
    ext = pltpu.VMEM((HALO + rows, width), F32)
    out_b, bc_b, enter_b, state_b, gate_b = call(
        functools.partial(later_block, heads, width, rows),
        [plane, plane, plane, shape(msg_rows, width), plane],
        [ext, ext],
    )(proj, seg_ext_b, seg_row_b, conv_x, conv_bc, bias, rate, skip)
    cx_a, bc_a, cum_a, scaled_a, enter_a, state_a, message = call(
        functools.partial(first_front, width, rows),
        [plane] * 5 + [shape(msg_rows, width)] * 2,
        [ext, ext],
    )(proj, halo, seg_ext_a, seg_last, state_b, conv_x, conv_bc, bias, rate)
    messages = lax.all_gather(message, "seq")
    gated = call(functools.partial(finish, heads, rows), shape(tok_rows, width, kind=BF16))(
        seg_first, messages, seg_ext_a, seg_row_a, skip, proj, cx_a, bc_a, cum_a, scaled_a, enter_a, state_a,
        out_b, gate_b, bc_b, enter_b
    )
    tok_own = tok_rows // n_tensor

    w_steps = [(w_forth, w_back)]
    orders = [(far, projs[-1]), messages]
    for step in range(2, last + 1):
        if step - 2 < len(orders):
            w_forth, w_back = after((w_forth, w_back), orders[step - 2])
        if step == last:
            w_far = far_shift(w_forth, w_back)
            break
        w_forth, w_back = ring_shift(w_forth, 1), ring_shift(w_back, -1)
        w_steps.append((w_forth, w_back))
        if step == 2:
            blocks = after(gated, w_forth, w_back).reshape(n_tensor, tok_own, width)
            mine = lax.all_to_all(blocks, "tensor", 0, 0)
    swap = [(i, i ^ 1) for i in range(n_seq)]
    other = lax.ppermute(mine, "seq", swap)
    pieces, distances = [own], [0]
    for i, pair in enumerate(w_steps):
        pieces += pair
        distances += [-i - 1, i + 1]
    total = call(functools.partial(product_early, distances), shape(2 * tok_own, columns), flops=1, moved=1)(
        mine, other, *pieces
    )
    half = shape(tok_own, columns, kind=BF16)
    held = [pltpu.VMEM((width, columns), BF16)]
    out_other = call(functools.partial(last_other, last), half, held)(other, total, *w_far)
    arrived = lax.ppermute(out_other, "seq", swap)
    whole = call(functools.partial(last_mine, last), shape(tok_own, model, kind=BF16), held)(mine, total, *w_far)
    return call(
        put_other,
        shape(tok_own, model, kind=BF16),
        [pltpu.SemaphoreType.DMA],
        in_specs=[ANY, VMEM],
        out_specs=ANY,
        input_output_aliases={0: 0},
    )(whole, arrived)


def solution(mesh):
    in_specs = (
        P("seq", "tensor"),
        P(None, None, "tensor"),
        P(),
        P(None, "tensor"),
        P("tensor"),
        P("tensor"),
        P("tensor"),
        P(None, "tensor"),
        P(),
        P("tensor"),
        P("tensor", None),
        P("seq"),
    )
    out_specs = P(("seq", "tensor"), None)
    return jax.shard_map(local, mesh=mesh, in_specs=in_specs, out_specs=out_specs, check_vma=False)
```

```python
import functools

import jax
import jax.numpy as jnp
import numpy as np
from jax import lax
from jax.experimental import pallas as pl
from jax.experimental.pallas import tpu as pltpu
from jax.sharding import PartitionSpec as P

NORM_EPS = 1e-05
F32 = jnp.float32
BF16 = jnp.bfloat16
VMEM = pl.BlockSpec(memory_space=pltpu.VMEM)
ANY = pl.BlockSpec(memory_space=pl.ANY)
HALO = 8


def ring_place(index, n):
    return jnp.where(index % 2 == 0, index // 2, (2 * n - 1 - index) // 2)


def ring_index(place, n):
    return jnp.where(place < n // 2, 2 * place, 2 * n - 1 - 2 * place)


def ring_shift(block, step):
    n = lax.axis_size("tensor")
    order = [2 * i if i < n // 2 else 2 * n - 1 - 2 * i for i in range(n)]
    return lax.ppermute(block, "tensor", [(order[i], order[(i + step) % n]) for i in range(n)])


def after(values, *earlier):
    return lax.optimization_barrier((values, earlier))[0]


def far_shift(forth, back):
    cut = forth.shape[0] // 32 * 16
    parts = [jax.ShapeDtypeStruct((size, forth.shape[1]), forth.dtype) for size in (cut, forth.shape[0] - cut)]
    top, bottom = call(halves, parts)(forth, back)
    return ring_shift(top, 1), ring_shift(bottom, -1)


def halves(forth, back, top, bottom):
    size = top.shape[0]
    top[...] = forth[:size]
    bottom[...] = back[size:]


def silu(v):
    return v / (1.0 + jnp.exp(-v))


def dot(a, b, dims=((1,), (0,))):
    return lax.dot_general(a.astype(BF16), b.astype(BF16), (dims, ((), ())), preferred_element_type=F32)


def source_of(distance):
    n = lax.axis_size("tensor")
    return ring_index((ring_place(lax.axis_index("tensor"), n) + distance + n) % n, n)


def near_start(side, whole, size):
    odd = lax.axis_index("seq") // 2 % 2
    return pl.multiple_of((odd if side == 0 else 1 - odd) * (whole - size), 16)


def lacked_rows(*refs):
    for side, (near, out) in enumerate(zip(refs[:2], refs[2:])):
        out[...] = near[pl.ds(near_start(side, near.shape[0], out.shape[0]), out.shape[0])]


def join(*refs):
    for side, (near, lacked, out) in enumerate(zip(refs[:2], refs[2:4], refs[4:])):
        for part, place in ((near, side), (lacked, 1 - side)):
            size = part.shape[0]
            out[pl.ds(near_start(place, out.shape[0], size), size)] = part[...]


def project(distances, ahead, first, *refs):
    count, fetched = len(distances), len(distances) + bool(ahead)
    blocks, (w_zx, w_bc, w_dt), refs = refs[:count], refs[count : count + 3], refs[count + 3 :]
    total, refs = (None, refs) if first else (refs[0], refs[1:])
    out, far_out, held, sems = refs if ahead else (refs[0], None, *refs[1:])
    feat, width = held.shape[1], w_bc.shape[1]
    sources = [w_zx.at[0], w_zx.at[1], w_bc, w_dt]
    copies = []
    for k, distance in enumerate([*distances, ahead][:fetched]):
        rows = pl.ds(pl.multiple_of(source_of(distance) * feat, 16), feat)
        for j, source in enumerate(sources):
            target = held.at[k] if k < count else far_out
            copies.append(
                pltpu.make_async_copy(source.at[rows], target.at[:, pl.ds(j * width, width)], sems.at[k, j])
            )
            copies[-1].start()
    result = 0.0 if first else total[...]
    for k in range(count):
        for j in range(len(sources)):
            copies[k * len(sources) + j].wait()
        result = result + dot(blocks[k][...], held[k], ((0,), (0,)))
    out[...] = result
    for copy in copies[count * len(sources) :]:
        copy.wait()


def project_far(top, bottom, weights, total, out):
    cut = top.shape[0]
    out[...] = (
        total[...] + dot(top[...], weights[:cut], ((0,), (0,))) + dot(bottom[...], weights[cut:], ((0,), (0,)))
    )


def conv(ext, seg_ext, taps, rows):
    size = taps.shape[0]
    seg_now = seg_ext[HALO : HALO + rows]
    total = taps[size - 1 : size] * ext[HALO : HALO + rows]
    for offset in range(1, size):
        same = seg_ext[HALO - offset : HALO - offset + rows] == seg_now
        total = total + taps[size - 1 - offset : size - offset] * jnp.where(
            same, ext[HALO - offset : HALO - offset + rows], 0.0
        )
    return silu(total)


def prefix_sum(values):
    rows = values.shape[0]
    lower = lax.broadcasted_iota(jnp.int32, (rows, rows), 0) >= lax.broadcasted_iota(jnp.int32, (rows, rows), 1)
    lower = jnp.where(lower, 1.0, 0.0).astype(BF16)
    total = jnp.zeros(values.shape, F32)
    rest = values
    parts = []
    for _ in range(3):
        part = rest.astype(BF16)
        parts.append(part)
        rest = rest - part.astype(F32)
    for part in reversed(parts):
        total = total + jnp.dot(lower, part, preferred_element_type=F32)
    return total


def block_front(ext_x, ext_bc, seg_ext, dt_raw, taps_x, taps_bc, bias, rate, rows, seg_enter, seg_leave):
    conv_x = conv(ext_x, seg_ext, taps_x, rows)
    conv_bc = conv(ext_bc, seg_ext, taps_bc, rows)
    seg = seg_ext[HALO : HALO + rows]
    shifted = dt_raw + bias
    step_size = jnp.maximum(shifted, 0.0) + jnp.log1p(jnp.exp(-jnp.abs(shifted)))
    cum = prefix_sum(-rate * step_size)
    scaled = conv_x * step_size
    last = cum[rows - 1 : rows]
    tail = jnp.where(seg == seg_leave, jnp.exp(last - cum), 0.0)
    state_w = conv_bc.shape[1] // 2
    state = dot(conv_bc, tail * scaled, ((0,), (0,)))[:state_w]
    enter = jnp.where(seg == seg_enter, jnp.exp(cum), 0.0)
    return conv_x, conv_bc, cum, scaled, state, enter, last


def block_inner(conv_bc, cum, scaled, seg_col, seg_row, heads):
    rows, width = scaled.shape
    state_w = conv_bc.shape[1] // 2
    head_w = width // heads
    scores = dot(conv_bc[:, state_w:], conv_bc[:, :state_w], ((1,), (1,)))
    later = lax.broadcasted_iota(jnp.int32, (rows, rows), 0) >= lax.broadcasted_iota(jnp.int32, (rows, rows), 1)
    visible = (seg_col == seg_row) & later
    cum_rows = cum.T
    lane = lax.broadcasted_iota(jnp.int32, (rows, width), 1)
    result = jnp.zeros((rows, width), F32)
    scaled = scaled.astype(BF16)
    for head in range(heads):
        at = head * head_w
        gap = jnp.where(visible, cum[:, at : at + 1] - cum_rows[at : at + 1, :], -jnp.inf)
        part = dot(jnp.exp(gap) * scores, scaled)
        result = jnp.where((lane >= at) & (lane < at + head_w), part, result)
    return result


def later_block(heads, width, rows, proj, seg_ext, seg_row, taps_x, taps_bc, bias, rate, skip,
                out, bc_out, enter_out, state_out, gate_out, ext_x, ext_bc):
    rounded = proj[rows - HALO :, : 3 * width].astype(BF16).astype(F32)
    gate_out[...] = silu(rounded[HALO:, :width])
    ext_x[...] = rounded[:, width : 2 * width]
    ext_bc[...] = rounded[:, 2 * width : 3 * width]
    seg_enter = seg_ext[HALO - 1 : HALO]
    seg_leave = seg_ext[HALO + rows - 1 : HALO + rows]
    conv_x, conv_bc, cum, scaled, state, enter, last = block_front(
        ext_x, ext_bc, seg_ext, proj[rows:, 3 * width :], taps_x, taps_bc[...], bias[...], rate[...], rows, seg_enter, seg_leave
    )
    out[...] = block_inner(conv_bc, cum, scaled, seg_ext[HALO:], seg_row[...], heads) + skip[...] * conv_x
    bc_out[...] = conv_bc
    enter_out[...] = enter
    keep = jnp.where(seg_enter == seg_leave, jnp.exp(last), 0.0)
    state_w = state.shape[0]
    state_out[:state_w] = state
    state_out[state_w : state_w + 1] = keep
    state_out[state_w + 1 : state_w + 2] = last
    state_out[state_w + 2 :] = jnp.zeros((state_out.shape[0] - state_w - 2, width), F32)


def first_front(width, rows, proj, halo, seg_ext, seg_last, state_b, taps_x, taps_bc, bias, rate,
                conv_out, bc_out, cum_out, scaled_out, enter_out, state_out, message, ext_x, ext_bc):
    ext_x[:HALO] = halo[:, :width].astype(F32)
    ext_bc[:HALO] = halo[:, width:].astype(F32)
    ext_x[HALO:] = proj[:rows, width : 2 * width].astype(BF16).astype(F32)
    ext_bc[HALO:] = proj[:rows, 2 * width : 3 * width].astype(BF16).astype(F32)
    seg_enter = seg_ext[HALO : HALO + 1]
    seg_leave = seg_ext[HALO + rows - 1 : HALO + rows]
    conv_x, conv_bc, cum, scaled, state, enter, last = block_front(
        ext_x, ext_bc, seg_ext, proj[:rows, 3 * width :], taps_x, taps_bc[...], bias[...], rate[...], rows, seg_enter, seg_leave
    )
    conv_out[...] = conv_x
    bc_out[...] = conv_bc
    cum_out[...] = cum
    scaled_out[...] = scaled
    enter_out[...] = enter
    keep = jnp.where(seg_enter == seg_leave, jnp.exp(last), 0.0)
    state_w = state.shape[0]
    state_out[:state_w] = state
    state_out[state_w : state_w + 1] = keep
    state_out[state_w + 1 :] = jnp.zeros((state_out.shape[0] - state_w - 1, width), F32)
    message[:state_w] = state_b[state_w : state_w + 1] * state + state_b[:state_w]
    message[state_w : state_w + 1] = last + state_b[state_w + 1 : state_w + 2]
    message[state_w + 1 : state_w + 2] = jnp.broadcast_to(seg_last[...].astype(F32), (1, width))
    message[state_w + 2 :] = jnp.zeros((message.shape[0] - state_w - 2, width), F32)


def finish(heads, rows, seg_first, messages, seg_ext_a, seg_row_a, skip, proj, conv_a, bc_a, cum_a, scaled_a, enter_a,
           state_a, out_b, gate_b, bc_b, enter_b, gated):
    state_w = bc_a.shape[1] // 2
    width = out_b.shape[1]
    entering = jnp.zeros((state_w, width), F32)
    decay = jnp.zeros((1, width), F32)
    first = seg_first[...].astype(F32)
    place = lax.axis_index("seq")
    for device in reversed(range(messages.shape[0] - 1)):
        earlier = device < place
        passes = earlier & (messages[device, state_w + 1 : state_w + 2] == first)
        passes = jnp.where(passes, jnp.exp(decay), 0.0)
        entering = entering + passes * messages[device, :state_w]
        decay = decay + jnp.where(earlier, messages[device, state_w : state_w + 1], 0.0)
    second = state_a[state_w : state_w + 1] * entering + state_a[:state_w]
    out_a = block_inner(bc_a[...], cum_a[...], scaled_a[...], seg_ext_a[HALO:], seg_row_a[...], heads)
    out_a = out_a + skip[...] * conv_a[...] + enter_a[...] * dot(bc_a[:, state_w:], entering)
    gated[:rows] = (out_a * silu(proj[:rows, :width].astype(BF16).astype(F32))).astype(BF16)
    gated[rows:] = ((out_b[...] + enter_b[...] * dot(bc_b[:, state_w:], second)) * gate_b[...]).astype(BF16)


def product(gated, distances, pieces):
    total = 0.0
    for distance, piece in zip(distances, pieces):
        source = source_of(distance)
        rows = jnp.concatenate([part[source] for part in gated], 0)
        total = total + jnp.dot(rows, piece[...], preferred_element_type=F32)
    return total


def product_early(distances, mine, other, *rest):
    rest[-1][...] = product((mine, other), distances, rest[:-1])


def last_rows(distance, gated, total, top, bottom, held):
    held[: top.shape[0]] = top[...]
    held[top.shape[0] :] = bottom[...]
    blocks, rows, width = gated.shape
    squares = jnp.zeros((rows, width), F32)
    for block in range(blocks):
        value = gated[block].astype(F32)
        squares = squares + value * value
    scale = lax.rsqrt(jnp.sum(squares, axis=1, keepdims=True) / (blocks * width) + NORM_EPS)
    return ((product((gated,), [distance], [held]) + total) * scale).astype(BF16)


def last_other(distance, other, total, top, bottom, out, held):
    rows = other.shape[1]
    out[...] = last_rows(distance, other, total[rows:], top, bottom, held)


def last_mine(distance, mine, total, top, bottom, out, held):
    rows, columns = mine.shape[1], held.shape[1]
    start = pl.multiple_of(lax.axis_index("seq") % 2 * columns, 128)
    out[:, pl.ds(start, columns)] = last_rows(distance, mine, total[:rows], top, bottom, held)


def put_other(whole, arrived, out, sem):
    del whole
    columns = arrived.shape[1]
    start = pl.multiple_of((1 - lax.axis_index("seq") % 2) * columns, 128)
    copy = pltpu.make_async_copy(arrived, out.at[:, pl.ds(start, columns)], sem)
    copy.start()
    copy.wait()


def call(body, outs, scratch=(), vmem=48, flops=10**7, moved=1 << 21, **kw):
    return pl.pallas_call(
        body,
        out_shape=outs,
        scratch_shapes=list(scratch),
        compiler_params=pltpu.CompilerParams(vmem_limit_bytes=vmem << 20),
        cost_estimate=pl.CostEstimate(flops=flops, bytes_accessed=moved, transcendentals=0),
        **kw,
    )


def local(
    tokens, w_zx, w_bc, w_dt, dt_bias, a_rate, d_skip, conv_x, conv_bc, norm_gain, w_out, segments
):
    tok_rows, feat = tokens.shape
    width = w_zx.shape[2]
    heads = dt_bias.shape[0]
    head_w = width // heads
    state_w = w_bc.shape[1] // 2
    model = w_zx.shape[1]
    n_seq, n_tensor = lax.axis_size("seq"), lax.axis_size("tensor")
    seq_at = lax.axis_index("seq")
    rows = tok_rows // 2
    shape = lambda *s, kind=F32: jax.ShapeDtypeStruct(s, kind)

    spread = lambda v: jnp.repeat(v, head_w, axis=-1)
    expand = np.repeat(np.eye(heads, dtype=np.float32), head_w, axis=1)
    w_step = jnp.dot(w_dt, expand.astype(BF16))
    block = tokens.T
    core = seq_at % 2
    columns = model // 2
    own = (lax.dynamic_slice_in_dim(w_out, core * columns, columns, 1).astype(F32) * norm_gain[:, None]).astype(BF16)
    last = n_tensor // 2
    w_half = width // 2
    near = width * 5 // 8
    odd = seq_at // 2 % 2
    own_near = [lax.dynamic_slice_in_dim(own, place * (width - near), near, 0) for place in (odd, 1 - odd)]
    other_y = [(i, i ^ 2) for i in range(n_seq)]
    parts = lambda size: [shape(size, columns, kind=BF16)] * 2
    shift_rows = [(i, i + 1) for i in range(n_seq - 1)]

    seg_halo = lax.ppermute(segments[tok_rows - HALO :], "seq", shift_rows)
    seg_all = jnp.concatenate([seg_halo, segments])[:, None]
    small = (
        (seg_all[: HALO + rows], seg_all[rows:]),
        (segments[None, :rows], segments[None, rows:]),
        (segments[None, :1], segments[None, tok_rows - 1 :]),
        (spread(dt_bias)[None], spread(a_rate)[None], spread(d_skip)[None]),
    )

    forth = back = block
    arrived, projs = [(0, block)], []
    for step in range(1, last + 1):
        if step == 3:
            forth, back = after(forth, projs[1], small), after(back, projs[1], small)
        elif step > 1:
            forth, back = after(forth, projs[step - 2]), after(back, projs[step - 2])
        if step == 4:
            w_lacked, forth, back = after((w_lacked, forth, back))
        arrivals = (forth, back)
        if step < last:
            forth, back = ring_shift(forth, 1), ring_shift(back, -1)
        else:
            far = far_shift(forth, back)
        if step == 2:
            pair = after(own_near, arrivals)
            w_near = ring_shift(pair[0], 1), ring_shift(pair[1], -1)
        if step == 3:
            lacked = call(lacked_rows, parts(width - near))(*after(w_near, arrivals))
            w_lacked = [lax.ppermute(part, "seq", other_y) for part in lacked]
        ahead = last if step == last else 0
        total = projs[-1:]
        fetched = len(arrived) + bool(ahead)
        outs = [shape(tok_rows, 4 * width)] + [shape(feat, 4 * width, kind=BF16)] * bool(ahead)
        results = call(
            functools.partial(project, [distance for distance, _ in arrived], ahead, not total),
            outs,
            [pltpu.VMEM((len(arrived), feat, 4 * width), BF16), pltpu.SemaphoreType.DMA((fetched, 4))],
            in_specs=[VMEM] * len(arrived) + [ANY] * 3 + [VMEM] * len(total),
            flops=10**9,
        )(*[part for _, part in arrived], w_zx, w_bc, w_step, *total)
        projs.append(results[0])
        arrived = [(-step, forth), (step, back)]
    w_forth, w_back = call(join, parts(width))(*w_near, *w_lacked)
    proj = call(project_far, shape(tok_rows, 4 * width), flops=10**9)(
        *far, results[1], projs[-1]
    )

    (seg_ext_a, seg_ext_b), (seg_row_a, seg_row_b), (seg_first, seg_last), (bias, rate, skip) = small
    halo = lax.ppermute(proj[tok_rows - HALO :, width : 3 * width].astype(BF16), "seq", shift_rows)

    msg_rows = state_w + 8
    plane = shape(rows, width)
    ext = pltpu.VMEM((HALO + rows, width), F32)
    out_b, bc_b, enter_b, state_b, gate_b = call(
        functools.partial(later_block, heads, width, rows),
        [plane, plane, plane, shape(msg_rows, width), plane],
        [ext, ext],
    )(proj, seg_ext_b, seg_row_b, conv_x, conv_bc, bias, rate, skip)
    cx_a, bc_a, cum_a, scaled_a, enter_a, state_a, message = call(
        functools.partial(first_front, width, rows),
        [plane] * 5 + [shape(msg_rows, width)] * 2,
        [ext, ext],
    )(proj, halo, seg_ext_a, seg_last, state_b, conv_x, conv_bc, bias, rate)
    messages = lax.all_gather(message, "seq")
    gated = call(functools.partial(finish, heads, rows), shape(tok_rows, width, kind=BF16))(
        seg_first, messages, seg_ext_a, seg_row_a, skip, proj, cx_a, bc_a, cum_a, scaled_a, enter_a, state_a,
        out_b, gate_b, bc_b, enter_b
    )
    tok_own = tok_rows // n_tensor

    w_steps = [(w_forth, w_back)]
    orders = [(far, projs[-1]), messages]
    for step in range(2, last + 1):
        if step - 2 < len(orders):
            w_forth, w_back = after((w_forth, w_back), orders[step - 2])
        if step == last:
            w_far = far_shift(w_forth, w_back)
            break
        w_forth, w_back = ring_shift(w_forth, 1), ring_shift(w_back, -1)
        w_steps.append((w_forth, w_back))
        if step == 2:
            blocks = after(gated, w_forth, w_back).reshape(n_tensor, tok_own, width)
            mine = lax.all_to_all(blocks, "tensor", 0, 0)
    swap = [(i, i ^ 1) for i in range(n_seq)]
    other = lax.ppermute(mine, "seq", swap)
    pieces, distances = [own], [0]
    for i, pair in enumerate(w_steps):
        pieces += pair
        distances += [-i - 1, i + 1]
    total = call(functools.partial(product_early, distances), shape(2 * tok_own, columns), flops=1, moved=1)(
        mine, other, *pieces
    )
    half = shape(tok_own, columns, kind=BF16)
    held = [pltpu.VMEM((width, columns), BF16)]
    out_other = call(functools.partial(last_other, last), half, held)(other, total, *w_far)
    arrived = lax.ppermute(out_other, "seq", swap)
    whole = call(functools.partial(last_mine, last), shape(tok_own, model, kind=BF16), held)(mine, total, *w_far)
    return call(
        put_other,
        shape(tok_own, model, kind=BF16),
        [pltpu.SemaphoreType.DMA],
        in_specs=[ANY, VMEM],
        out_specs=ANY,
        input_output_aliases={0: 0},
    )(whole, arrived)


def solution(mesh):
    in_specs = (
        P("seq", "tensor"),
        P(None, None, "tensor"),
        P(),
        P(None, "tensor"),
        P("tensor"),
        P("tensor"),
        P("tensor"),
        P(None, "tensor"),
        P(),
        P("tensor"),
        P("tensor", None),
        P("seq"),
    )
    out_specs = P(("seq", "tensor"), None)
    return jax.shard_map(local, mesh=mesh, in_specs=in_specs, out_specs=out_specs, check_vma=False)
```

```python
import functools

import jax
import jax.numpy as jnp
import numpy as np
from jax import lax
from jax.experimental import pallas as pl
from jax.experimental.pallas import tpu as pltpu
from jax.sharding import PartitionSpec as P

NORM_EPS = 1e-05
F32 = jnp.float32
BF16 = jnp.bfloat16
VMEM = pl.BlockSpec(memory_space=pltpu.VMEM)
ANY = pl.BlockSpec(memory_space=pl.ANY)
HALO = 8
W_FIRST = 3


def ring_place(index, n):
    return jnp.where(index % 2 == 0, index // 2, (2 * n - 1 - index) // 2)


def ring_index(place, n):
    return jnp.where(place < n // 2, 2 * place, 2 * n - 1 - 2 * place)


def ring_shift(block, step):
    n = lax.axis_size("tensor")
    order = [2 * i if i < n // 2 else 2 * n - 1 - 2 * i for i in range(n)]
    return lax.ppermute(block, "tensor", [(order[i], order[(i + step) % n]) for i in range(n)])


def after(values, *earlier):
    return lax.optimization_barrier((values, earlier))[0]


def far_shift(forth, back):
    cut = forth.shape[0] // 32 * 16
    parts = [jax.ShapeDtypeStruct((size, forth.shape[1]), forth.dtype) for size in (cut, forth.shape[0] - cut)]
    top, bottom = call(halves, parts)(forth, back)
    return ring_shift(top, 1), ring_shift(bottom, -1)


def halves(forth, back, top, bottom):
    size = top.shape[0]
    top[...] = forth[:size]
    bottom[...] = back[size:]


def silu(v):
    return v / (1.0 + jnp.exp(-v))


def dot(a, b, dims=((1,), (0,))):
    return lax.dot_general(a.astype(BF16), b.astype(BF16), (dims, ((), ())), preferred_element_type=F32)


def source_of(distance):
    n = lax.axis_size("tensor")
    return ring_index((ring_place(lax.axis_index("tensor"), n) + distance + n) % n, n)


def project(distances, ahead, first, *refs):
    count, fetched = len(distances), len(distances) + bool(ahead)
    blocks, (w_zx, w_bc, w_dt), refs = refs[:count], refs[count : count + 3], refs[count + 3 :]
    total, refs = (None, refs) if first else (refs[0], refs[1:])
    out, far_out, held, sems = refs if ahead else (refs[0], None, *refs[1:])
    feat, width = held.shape[1], w_bc.shape[1]
    sources = [w_zx.at[0], w_zx.at[1], w_bc, w_dt]
    copies = []
    for k, distance in enumerate([*distances, ahead][:fetched]):
        rows = pl.ds(pl.multiple_of(source_of(distance) * feat, 16), feat)
        for j, source in enumerate(sources):
            target = held.at[k] if k < count else far_out
            copies.append(
                pltpu.make_async_copy(source.at[rows], target.at[:, pl.ds(j * width, width)], sems.at[k, j])
            )
            copies[-1].start()
    result = 0.0 if first else total[...]
    for k in range(count):
        for j in range(len(sources)):
            copies[k * len(sources) + j].wait()
        result = result + dot(blocks[k][...], held[k], ((0,), (0,)))
    out[...] = result
    for copy in copies[count * len(sources) :]:
        copy.wait()


def project_far(top, bottom, weights, total, out):
    cut = top.shape[0]
    out[...] = (
        total[...] + dot(top[...], weights[:cut], ((0,), (0,))) + dot(bottom[...], weights[cut:], ((0,), (0,)))
    )


def conv(ext, seg_ext, taps, rows):
    size = taps.shape[0]
    seg_now = seg_ext[HALO : HALO + rows]
    total = taps[size - 1 : size] * ext[HALO : HALO + rows]
    for offset in range(1, size):
        same = seg_ext[HALO - offset : HALO - offset + rows] == seg_now
        total = total + taps[size - 1 - offset : size - offset] * jnp.where(
            same, ext[HALO - offset : HALO - offset + rows], 0.0
        )
    return silu(total)


def prefix_sum(values):
    rows = values.shape[0]
    lower = lax.broadcasted_iota(jnp.int32, (rows, rows), 0) >= lax.broadcasted_iota(jnp.int32, (rows, rows), 1)
    lower = jnp.where(lower, 1.0, 0.0).astype(BF16)
    total = jnp.zeros(values.shape, F32)
    rest = values
    parts = []
    for _ in range(3):
        part = rest.astype(BF16)
        parts.append(part)
        rest = rest - part.astype(F32)
    for part in reversed(parts):
        total = total + jnp.dot(lower, part, preferred_element_type=F32)
    return total


def block_front(ext_x, ext_bc, seg_ext, dt_raw, taps_x, taps_bc, bias, rate, rows, seg_enter, seg_leave):
    conv_x = conv(ext_x, seg_ext, taps_x, rows)
    conv_bc = conv(ext_bc, seg_ext, taps_bc, rows)
    seg = seg_ext[HALO : HALO + rows]
    shifted = dt_raw + bias
    step_size = jnp.maximum(shifted, 0.0) + jnp.log1p(jnp.exp(-jnp.abs(shifted)))
    cum = prefix_sum(-rate * step_size)
    scaled = conv_x * step_size
    last = cum[rows - 1 : rows]
    tail = jnp.where(seg == seg_leave, jnp.exp(last - cum), 0.0)
    state_w = conv_bc.shape[1] // 2
    state = dot(conv_bc, tail * scaled, ((0,), (0,)))[:state_w]
    enter = jnp.where(seg == seg_enter, jnp.exp(cum), 0.0)
    return conv_x, conv_bc, cum, scaled, state, enter, last


def block_inner(conv_bc, cum, scaled, seg_col, seg_row, heads):
    rows, width = scaled.shape
    state_w = conv_bc.shape[1] // 2
    head_w = width // heads
    scores = dot(conv_bc[:, state_w:], conv_bc[:, :state_w], ((1,), (1,)))
    later = lax.broadcasted_iota(jnp.int32, (rows, rows), 0) >= lax.broadcasted_iota(jnp.int32, (rows, rows), 1)
    visible = (seg_col == seg_row) & later
    cum_rows = cum.T
    lane = lax.broadcasted_iota(jnp.int32, (rows, width), 1)
    result = jnp.zeros((rows, width), F32)
    scaled = scaled.astype(BF16)
    for head in range(heads):
        at = head * head_w
        gap = jnp.where(visible, cum[:, at : at + 1] - cum_rows[at : at + 1, :], -jnp.inf)
        part = dot(jnp.exp(gap) * scores, scaled)
        result = jnp.where((lane >= at) & (lane < at + head_w), part, result)
    return result


def later_block(heads, width, rows, proj, seg_ext, seg_row, taps_x, taps_bc, bias, rate, skip,
                out, bc_out, enter_out, state_out, gate_out, ext_x, ext_bc):
    rounded = proj[rows - HALO :, : 3 * width].astype(BF16).astype(F32)
    gate_out[...] = silu(rounded[HALO:, :width])
    ext_x[...] = rounded[:, width : 2 * width]
    ext_bc[...] = rounded[:, 2 * width : 3 * width]
    seg_enter = seg_ext[HALO - 1 : HALO]
    seg_leave = seg_ext[HALO + rows - 1 : HALO + rows]
    conv_x, conv_bc, cum, scaled, state, enter, last = block_front(
        ext_x, ext_bc, seg_ext, proj[rows:, 3 * width :], taps_x, taps_bc[...], bias[...], rate[...], rows, seg_enter, seg_leave
    )
    out[...] = block_inner(conv_bc, cum, scaled, seg_ext[HALO:], seg_row[...], heads) + skip[...] * conv_x
    bc_out[...] = conv_bc
    enter_out[...] = enter
    keep = jnp.where(seg_enter == seg_leave, jnp.exp(last), 0.0)
    state_w = state.shape[0]
    state_out[:state_w] = state
    state_out[state_w : state_w + 1] = keep
    state_out[state_w + 1 : state_w + 2] = last
    state_out[state_w + 2 :] = jnp.zeros((state_out.shape[0] - state_w - 2, width), F32)


def first_front(width, rows, proj, halo, seg_ext, seg_last, state_b, taps_x, taps_bc, bias, rate,
                conv_out, bc_out, cum_out, scaled_out, enter_out, state_out, message, ext_x, ext_bc):
    ext_x[:HALO] = halo[:, :width].astype(F32)
    ext_bc[:HALO] = halo[:, width:].astype(F32)
    ext_x[HALO:] = proj[:rows, width : 2 * width].astype(BF16).astype(F32)
    ext_bc[HALO:] = proj[:rows, 2 * width : 3 * width].astype(BF16).astype(F32)
    seg_enter = seg_ext[HALO : HALO + 1]
    seg_leave = seg_ext[HALO + rows - 1 : HALO + rows]
    conv_x, conv_bc, cum, scaled, state, enter, last = block_front(
        ext_x, ext_bc, seg_ext, proj[:rows, 3 * width :], taps_x, taps_bc[...], bias[...], rate[...], rows, seg_enter, seg_leave
    )
    conv_out[...] = conv_x
    bc_out[...] = conv_bc
    cum_out[...] = cum
    scaled_out[...] = scaled
    enter_out[...] = enter
    keep = jnp.where(seg_enter == seg_leave, jnp.exp(last), 0.0)
    state_w = state.shape[0]
    state_out[:state_w] = state
    state_out[state_w : state_w + 1] = keep
    state_out[state_w + 1 :] = jnp.zeros((state_out.shape[0] - state_w - 1, width), F32)
    message[:state_w] = state_b[state_w : state_w + 1] * state + state_b[:state_w]
    message[state_w : state_w + 1] = last + state_b[state_w + 1 : state_w + 2]
    message[state_w + 1 : state_w + 2] = jnp.broadcast_to(seg_last[...].astype(F32), (1, width))
    message[state_w + 2 :] = jnp.zeros((message.shape[0] - state_w - 2, width), F32)


def finish(heads, rows, count, seg_first, *refs):
    messages, refs = refs[:count], refs[count:]
    finish_with(heads, rows, seg_first, messages, *refs)


def message_from(messages, device):
    if len(messages) == 1:
        return messages[0][device]
    place = lax.axis_index("seq")
    core = place % 2 == device % 2
    plane = place // 2 == device // 2
    own, other_core, other_plane, other_both = (m[...] for m in messages)
    return jnp.where(plane, jnp.where(core, own, other_core), jnp.where(core, other_plane, other_both))


def finish_with(heads, rows, seg_first, messages, seg_ext_a, seg_row_a, skip, proj, conv_a, bc_a, cum_a, scaled_a, enter_a,
           state_a, out_b, gate_b, bc_b, enter_b, gated):
    state_w = bc_a.shape[1] // 2
    width = out_b.shape[1]
    entering = jnp.zeros((state_w, width), F32)
    decay = jnp.zeros((1, width), F32)
    first = seg_first[...].astype(F32)
    place = lax.axis_index("seq")
    for device in reversed(range(lax.axis_size("seq") - 1)):
        earlier = device < place
        message = message_from(messages, device)
        passes = earlier & (message[state_w + 1 : state_w + 2] == first)
        passes = jnp.where(passes, jnp.exp(decay), 0.0)
        entering = entering + passes * message[:state_w]
        decay = decay + jnp.where(earlier, message[state_w : state_w + 1], 0.0)
    second = state_a[state_w : state_w + 1] * entering + state_a[:state_w]
    out_a = block_inner(bc_a[...], cum_a[...], scaled_a[...], seg_ext_a[HALO:], seg_row_a[...], heads)
    out_a = out_a + skip[...] * conv_a[...] + enter_a[...] * dot(bc_a[:, state_w:], entering)
    gated[:rows] = (out_a * silu(proj[:rows, :width].astype(BF16).astype(F32))).astype(BF16)
    gated[rows:] = ((out_b[...] + enter_b[...] * dot(bc_b[:, state_w:], second)) * gate_b[...]).astype(BF16)


def product(gated, distances, pieces):
    total = 0.0
    for distance, piece in zip(distances, pieces):
        source = source_of(distance)
        rows = jnp.concatenate([part[source] for part in gated], 0)
        total = total + jnp.dot(rows, piece[...], preferred_element_type=F32)
    return total


def product_early(distances, mine, other, *rest):
    rest[-1][...] = product((mine, other), distances, rest[:-1])


def last_rows(distance, gated, total, top, bottom, held):
    held[: top.shape[0]] = top[...]
    held[top.shape[0] :] = bottom[...]
    blocks, rows, width = gated.shape
    squares = jnp.zeros((rows, width), F32)
    for block in range(blocks):
        value = gated[block].astype(F32)
        squares = squares + value * value
    scale = lax.rsqrt(jnp.sum(squares, axis=1, keepdims=True) / (blocks * width) + NORM_EPS)
    return ((product((gated,), [distance], [held]) + total) * scale).astype(BF16)


def last_other(distance, other, total, top, bottom, out, held):
    rows = other.shape[1]
    out[...] = last_rows(distance, other, total[rows:], top, bottom, held)


def last_mine(distance, mine, total, top, bottom, out, held):
    rows, columns = mine.shape[1], held.shape[1]
    start = pl.multiple_of(lax.axis_index("seq") % 2 * columns, 128)
    out[:, pl.ds(start, columns)] = last_rows(distance, mine, total[:rows], top, bottom, held)


def put_other(whole, arrived, out, sem):
    del whole
    columns = arrived.shape[1]
    start = pl.multiple_of((1 - lax.axis_index("seq") % 2) * columns, 128)
    copy = pltpu.make_async_copy(arrived, out.at[:, pl.ds(start, columns)], sem)
    copy.start()
    copy.wait()


def call(body, outs, scratch=(), vmem=48, flops=10**7, moved=1 << 21, **kw):
    return pl.pallas_call(
        body,
        out_shape=outs,
        scratch_shapes=list(scratch),
        compiler_params=pltpu.CompilerParams(vmem_limit_bytes=vmem << 20),
        cost_estimate=pl.CostEstimate(flops=flops, bytes_accessed=moved, transcendentals=0),
        **kw,
    )


def local(
    tokens, w_zx, w_bc, w_dt, dt_bias, a_rate, d_skip, conv_x, conv_bc, norm_gain, w_out, segments
):
    tok_rows, feat = tokens.shape
    width = w_zx.shape[2]
    heads = dt_bias.shape[0]
    head_w = width // heads
    state_w = w_bc.shape[1] // 2
    model = w_zx.shape[1]
    n_seq, n_tensor = lax.axis_size("seq"), lax.axis_size("tensor")
    seq_at = lax.axis_index("seq")
    rows = tok_rows // 2
    shape = lambda *s, kind=F32: jax.ShapeDtypeStruct(s, kind)

    spread = lambda v: jnp.repeat(v, head_w, axis=-1)
    expand = np.repeat(np.eye(heads, dtype=np.float32), head_w, axis=1)
    w_step = jnp.dot(w_dt, expand.astype(BF16))
    block = tokens.T
    core = seq_at % 2
    columns = model // 2
    own = (lax.dynamic_slice_in_dim(w_out, core * columns, columns, 1).astype(F32) * norm_gain[:, None]).astype(BF16)
    last = n_tensor // 2
    w_half = width // 2
    shift_rows = [(i, i + 1) for i in range(n_seq - 1)]

    seg_halo = lax.ppermute(segments[tok_rows - HALO :], "seq", shift_rows)
    seg_all = jnp.concatenate([seg_halo, segments])[:, None]
    small = (
        (seg_all[: HALO + rows], seg_all[rows:]),
        (segments[None, :rows], segments[None, rows:]),
        (segments[None, :1], segments[None, tok_rows - 1 :]),
        (spread(dt_bias)[None], spread(a_rate)[None], spread(d_skip)[None]),
    )

    forth = back = block
    arrived, projs = [(0, block)], []
    for step in range(1, last + 1):
        if step == 3:
            forth, back = after(forth, projs[1], small), after(back, projs[1], small)
        elif step > 1:
            forth, back = after(forth, projs[step - 2]), after(back, projs[step - 2])
        arrivals = (forth, back)
        if step < last:
            forth, back = ring_shift(forth, 1), ring_shift(back, -1)
        else:
            far = far_shift(forth, back)
        if step == W_FIRST:
            w_forth, w_back = after((own, own), arrivals)
            w_forth, w_back = ring_shift(w_forth, 1), ring_shift(w_back, -1)
        ahead = last if step == last else 0
        total = projs[-1:]
        fetched = len(arrived) + bool(ahead)
        outs = [shape(tok_rows, 4 * width)] + [shape(feat, 4 * width, kind=BF16)] * bool(ahead)
        results = call(
            functools.partial(project, [distance for distance, _ in arrived], ahead, not total),
            outs,
            [pltpu.VMEM((len(arrived), feat, 4 * width), BF16), pltpu.SemaphoreType.DMA((fetched, 4))],
            in_specs=[VMEM] * len(arrived) + [ANY] * 3 + [VMEM] * len(total),
            flops=10**9,
        )(*[part for _, part in arrived], w_zx, w_bc, w_step, *total)
        projs.append(results[0])
        arrived = [(-step, forth), (step, back)]
    proj = call(project_far, shape(tok_rows, 4 * width), flops=10**9)(
        *far, results[1], projs[-1]
    )

    (seg_ext_a, seg_ext_b), (seg_row_a, seg_row_b), (seg_first, seg_last), (bias, rate, skip) = small
    halo = lax.ppermute(proj[tok_rows - HALO :, width : 3 * width].astype(BF16), "seq", shift_rows)

    msg_rows = state_w + 8
    plane = shape(rows, width)
    ext = pltpu.VMEM((HALO + rows, width), F32)
    out_b, bc_b, enter_b, state_b, gate_b = call(
        functools.partial(later_block, heads, width, rows),
        [plane, plane, plane, shape(msg_rows, width), plane],
        [ext, ext],
    )(proj, seg_ext_b, seg_row_b, conv_x, conv_bc, bias, rate, skip)
    cx_a, bc_a, cum_a, scaled_a, enter_a, state_a, message = call(
        functools.partial(first_front, width, rows),
        [plane] * 5 + [shape(msg_rows, width)] * 2,
        [ext, ext],
    )(proj, halo, seg_ext_a, seg_last, state_b, conv_x, conv_bc, bias, rate)
    if n_seq == 4:
        other_core = lax.ppermute(message, "seq", [(i, i ^ 1) for i in range(n_seq)])
        other_plane = lax.ppermute(message, "seq", [(i, i ^ 2) for i in range(n_seq)])
        other_both = lax.ppermute(other_core, "seq", [(i, i ^ 2) for i in range(n_seq)])
        messages = (message, other_core, other_plane, other_both)
    else:
        messages = (lax.all_gather(message, "seq"),)
    gated = call(functools.partial(finish, heads, rows, len(messages)), shape(tok_rows, width, kind=BF16))(
        seg_first, *messages, seg_ext_a, seg_row_a, skip, proj, cx_a, bc_a, cum_a, scaled_a, enter_a, state_a,
        out_b, gate_b, bc_b, enter_b
    )
    tok_own = tok_rows // n_tensor

    w_steps = [(w_forth, w_back)]
    orders = [(far, projs[-1]), messages]
    for step in range(2, last + 1):
        if step - 2 < len(orders):
            w_forth, w_back = after((w_forth, w_back), orders[step - 2])
        if step == last:
            w_far = far_shift(w_forth, w_back)
            break
        w_forth, w_back = ring_shift(w_forth, 1), ring_shift(w_back, -1)
        w_steps.append((w_forth, w_back))
        if step == 2:
            blocks = after(gated, w_forth, w_back).reshape(n_tensor, tok_own, width)
            mine = lax.all_to_all(blocks, "tensor", 0, 0)
    swap = [(i, i ^ 1) for i in range(n_seq)]
    other = lax.ppermute(mine, "seq", swap)
    pieces, distances = [own], [0]
    for i, pair in enumerate(w_steps):
        pieces += pair
        distances += [-i - 1, i + 1]
    total = call(functools.partial(product_early, distances), shape(2 * tok_own, columns), flops=1, moved=1)(
        mine, other, *pieces
    )
    half = shape(tok_own, columns, kind=BF16)
    held = [pltpu.VMEM((width, columns), BF16)]
    out_other = call(functools.partial(last_other, last), half, held)(other, total, *w_far)
    arrived = lax.ppermute(out_other, "seq", swap)
    whole = call(functools.partial(last_mine, last), shape(tok_own, model, kind=BF16), held)(mine, total, *w_far)
    return call(
        put_other,
        shape(tok_own, model, kind=BF16),
        [pltpu.SemaphoreType.DMA],
        in_specs=[ANY, VMEM],
        out_specs=ANY,
        input_output_aliases={0: 0},
    )(whole, arrived)


def solution(mesh):
    in_specs = (
        P("seq", "tensor"),
        P(None, None, "tensor"),
        P(),
        P(None, "tensor"),
        P("tensor"),
        P("tensor"),
        P("tensor"),
        P(None, "tensor"),
        P(),
        P("tensor"),
        P("tensor", None),
        P("seq"),
    )
    out_specs = P(("seq", "tensor"), None)
    return jax.shard_map(local, mesh=mesh, in_specs=in_specs, out_specs=out_specs, check_vma=False)
```

```python
import functools

import jax
import jax.numpy as jnp
import numpy as np
from jax import lax
from jax.experimental import pallas as pl
from jax.experimental.pallas import tpu as pltpu
from jax.sharding import PartitionSpec as P

NORM_EPS = 1e-05
F32 = jnp.float32
BF16 = jnp.bfloat16
VMEM = pl.BlockSpec(memory_space=pltpu.VMEM)
ANY = pl.BlockSpec(memory_space=pl.ANY)
HALO = 8
W_FIRST = 3


def ring_place(index, n):
    return jnp.where(index % 2 == 0, index // 2, (2 * n - 1 - index) // 2)


def ring_index(place, n):
    return jnp.where(place < n // 2, 2 * place, 2 * n - 1 - 2 * place)


def ring_shift(block, step):
    n = lax.axis_size("tensor")
    order = [2 * i if i < n // 2 else 2 * n - 1 - 2 * i for i in range(n)]
    return lax.ppermute(block, "tensor", [(order[i], order[(i + step) % n]) for i in range(n)])


def after(values, *earlier):
    return lax.optimization_barrier((values, earlier))[0]


def far_shift(forth, back):
    cut = forth.shape[0] // 32 * 16
    parts = [jax.ShapeDtypeStruct((size, forth.shape[1]), forth.dtype) for size in (cut, forth.shape[0] - cut)]
    top, bottom = call(halves, parts)(forth, back)
    return ring_shift(top, 1), ring_shift(bottom, -1)


def halves(forth, back, top, bottom):
    size = top.shape[0]
    top[...] = forth[:size]
    bottom[...] = back[size:]


def silu(v):
    return v / (1.0 + jnp.exp(-v))


def dot(a, b, dims=((1,), (0,))):
    return lax.dot_general(a.astype(BF16), b.astype(BF16), (dims, ((), ())), preferred_element_type=F32)


def source_of(distance):
    n = lax.axis_size("tensor")
    return ring_index((ring_place(lax.axis_index("tensor"), n) + distance + n) % n, n)


def project(distances, ahead, first, *refs):
    count, fetched = len(distances), len(distances) + bool(ahead)
    blocks, (w_zx, w_bc, w_dt), refs = refs[:count], refs[count : count + 3], refs[count + 3 :]
    total, refs = (None, refs) if first else (refs[0], refs[1:])
    out, far_out, held, sems = refs if ahead else (refs[0], None, *refs[1:])
    feat, width = held.shape[1], w_bc.shape[1]
    sources = [w_zx.at[0], w_zx.at[1], w_bc, w_dt]
    copies = []
    for k, distance in enumerate([*distances, ahead][:fetched]):
        rows = pl.ds(pl.multiple_of(source_of(distance) * feat, 16), feat)
        for j, source in enumerate(sources):
            target = held.at[k] if k < count else far_out
            copies.append(
                pltpu.make_async_copy(source.at[rows], target.at[:, pl.ds(j * width, width)], sems.at[k, j])
            )
            copies[-1].start()
    result = 0.0 if first else total[...]
    for k in range(count):
        for j in range(len(sources)):
            copies[k * len(sources) + j].wait()
        result = result + dot(blocks[k][...], held[k], ((0,), (0,)))
    out[...] = result
    for copy in copies[count * len(sources) :]:
        copy.wait()


def project_far(top, bottom, weights, total, out):
    cut = top.shape[0]
    out[...] = (
        total[...] + dot(top[...], weights[:cut], ((0,), (0,))) + dot(bottom[...], weights[cut:], ((0,), (0,)))
    )


def conv(ext, seg_ext, taps, rows):
    size = taps.shape[0]
    seg_now = seg_ext[HALO : HALO + rows]
    total = taps[size - 1 : size] * ext[HALO : HALO + rows]
    for offset in range(1, size):
        same = seg_ext[HALO - offset : HALO - offset + rows] == seg_now
        total = total + taps[size - 1 - offset : size - offset] * jnp.where(
            same, ext[HALO - offset : HALO - offset + rows], 0.0
        )
    return silu(total)


def prefix_sum(values):
    rows = values.shape[0]
    lower = lax.broadcasted_iota(jnp.int32, (rows, rows), 0) >= lax.broadcasted_iota(jnp.int32, (rows, rows), 1)
    lower = jnp.where(lower, 1.0, 0.0).astype(BF16)
    total = jnp.zeros(values.shape, F32)
    rest = values
    parts = []
    for _ in range(3):
        part = rest.astype(BF16)
        parts.append(part)
        rest = rest - part.astype(F32)
    for part in reversed(parts):
        total = total + jnp.dot(lower, part, preferred_element_type=F32)
    return total


def block_front(ext_x, ext_bc, seg_ext, dt_raw, taps_x, taps_bc, bias, rate, rows, seg_enter, seg_leave):
    conv_x = conv(ext_x, seg_ext, taps_x, rows)
    conv_bc = conv(ext_bc, seg_ext, taps_bc, rows)
    seg = seg_ext[HALO : HALO + rows]
    shifted = dt_raw + bias
    step_size = jnp.maximum(shifted, 0.0) + jnp.log1p(jnp.exp(-jnp.abs(shifted)))
    cum = prefix_sum(-rate * step_size)
    scaled = conv_x * step_size
    last = cum[rows - 1 : rows]
    tail = jnp.where(seg == seg_leave, jnp.exp(last - cum), 0.0)
    state_w = conv_bc.shape[1] // 2
    state = dot(conv_bc, tail * scaled, ((0,), (0,)))[:state_w]
    enter = jnp.where(seg == seg_enter, jnp.exp(cum), 0.0)
    return conv_x, conv_bc, cum, scaled, state, enter, last


def block_inner(conv_bc, cum, scaled, seg_col, seg_row, heads):
    rows, width = scaled.shape
    state_w = conv_bc.shape[1] // 2
    head_w = width // heads
    scores = dot(conv_bc[:, state_w:], conv_bc[:, :state_w], ((1,), (1,)))
    later = lax.broadcasted_iota(jnp.int32, (rows, rows), 0) >= lax.broadcasted_iota(jnp.int32, (rows, rows), 1)
    visible = (seg_col == seg_row) & later
    cum_rows = cum.T
    lane = lax.broadcasted_iota(jnp.int32, (rows, width), 1)
    result = jnp.zeros((rows, width), F32)
    scaled = scaled.astype(BF16)
    for head in range(heads):
        at = head * head_w
        gap = jnp.where(visible, cum[:, at : at + 1] - cum_rows[at : at + 1, :], -jnp.inf)
        part = dot(jnp.exp(gap) * scores, scaled)
        result = jnp.where((lane >= at) & (lane < at + head_w), part, result)
    return result


def later_block(heads, width, rows, proj, seg_ext, seg_row, taps_x, taps_bc, bias, rate, skip,
                out, bc_out, enter_out, state_out, gate_out, ext_x, ext_bc):
    rounded = proj[rows - HALO :, : 3 * width].astype(BF16).astype(F32)
    gate_out[...] = silu(rounded[HALO:, :width])
    ext_x[...] = rounded[:, width : 2 * width]
    ext_bc[...] = rounded[:, 2 * width : 3 * width]
    seg_enter = seg_ext[HALO - 1 : HALO]
    seg_leave = seg_ext[HALO + rows - 1 : HALO + rows]
    conv_x, conv_bc, cum, scaled, state, enter, last = block_front(
        ext_x, ext_bc, seg_ext, proj[rows:, 3 * width :], taps_x, taps_bc[...], bias[...], rate[...], rows, seg_enter, seg_leave
    )
    out[...] = block_inner(conv_bc, cum, scaled, seg_ext[HALO:], seg_row[...], heads) + skip[...] * conv_x
    bc_out[...] = conv_bc
    enter_out[...] = enter
    keep = jnp.where(seg_enter == seg_leave, jnp.exp(last), 0.0)
    state_w = state.shape[0]
    state_out[:state_w] = state
    state_out[state_w : state_w + 1] = keep
    state_out[state_w + 1 : state_w + 2] = last
    state_out[state_w + 2 :] = jnp.zeros((state_out.shape[0] - state_w - 2, width), F32)


def first_front(width, rows, proj, halo, seg_ext, seg_last, state_b, taps_x, taps_bc, bias, rate,
                conv_out, bc_out, cum_out, scaled_out, enter_out, state_out, message, ext_x, ext_bc):
    ext_x[:HALO] = halo[:, :width].astype(F32)
    ext_bc[:HALO] = halo[:, width:].astype(F32)
    ext_x[HALO:] = proj[:rows, width : 2 * width].astype(BF16).astype(F32)
    ext_bc[HALO:] = proj[:rows, 2 * width : 3 * width].astype(BF16).astype(F32)
    seg_enter = seg_ext[HALO : HALO + 1]
    seg_leave = seg_ext[HALO + rows - 1 : HALO + rows]
    conv_x, conv_bc, cum, scaled, state, enter, last = block_front(
        ext_x, ext_bc, seg_ext, proj[:rows, 3 * width :], taps_x, taps_bc[...], bias[...], rate[...], rows, seg_enter, seg_leave
    )
    conv_out[...] = conv_x
    bc_out[...] = conv_bc
    cum_out[...] = cum
    scaled_out[...] = scaled
    enter_out[...] = enter
    keep = jnp.where(seg_enter == seg_leave, jnp.exp(last), 0.0)
    state_w = state.shape[0]
    state_out[:state_w] = state
    state_out[state_w : state_w + 1] = keep
    state_out[state_w + 1 :] = jnp.zeros((state_out.shape[0] - state_w - 1, width), F32)
    message[:state_w] = state_b[state_w : state_w + 1] * state + state_b[:state_w]
    message[state_w : state_w + 1] = last + state_b[state_w + 1 : state_w + 2]
    message[state_w + 1 : state_w + 2] = jnp.broadcast_to(seg_last[...].astype(F32), (1, width))
    message[state_w + 2 :] = jnp.zeros((message.shape[0] - state_w - 2, width), F32)


def finish(heads, rows, count, seg_first, *refs):
    messages, refs = refs[:count], refs[count:]
    finish_with(heads, rows, seg_first, messages, *refs)


def message_from(messages, device):
    if len(messages) == 1:
        return messages[0][device]
    place = lax.axis_index("seq")
    core = place % 2 == device % 2
    plane = place // 2 == device // 2
    own, other_core, other_plane, other_both = (m[...] for m in messages)
    return jnp.where(plane, jnp.where(core, own, other_core), jnp.where(core, other_plane, other_both))


def finish_with(heads, rows, seg_first, messages, seg_ext_a, seg_row_a, skip, proj, conv_a, bc_a, cum_a, scaled_a, enter_a,
           state_a, out_b, gate_b, bc_b, enter_b, gated):
    state_w = bc_a.shape[1] // 2
    width = out_b.shape[1]
    entering = jnp.zeros((state_w, width), F32)
    decay = jnp.zeros((1, width), F32)
    first = seg_first[...].astype(F32)
    place = lax.axis_index("seq")
    for device in reversed(range(lax.axis_size("seq") - 1)):
        earlier = device < place
        message = message_from(messages, device)
        passes = earlier & (message[state_w + 1 : state_w + 2] == first)
        passes = jnp.where(passes, jnp.exp(decay), 0.0)
        entering = entering + passes * message[:state_w]
        decay = decay + jnp.where(earlier, message[state_w : state_w + 1], 0.0)
    second = state_a[state_w : state_w + 1] * entering + state_a[:state_w]
    out_a = block_inner(bc_a[...], cum_a[...], scaled_a[...], seg_ext_a[HALO:], seg_row_a[...], heads)
    out_a = out_a + skip[...] * conv_a[...] + enter_a[...] * dot(bc_a[:, state_w:], entering)
    gated[:rows] = (out_a * silu(proj[:rows, :width].astype(BF16).astype(F32))).astype(BF16)
    gated[rows:] = ((out_b[...] + enter_b[...] * dot(bc_b[:, state_w:], second)) * gate_b[...]).astype(BF16)


def product(gated, distances, pieces):
    total = 0.0
    for distance, piece in zip(distances, pieces):
        source = source_of(distance)
        rows = jnp.concatenate([part[source] for part in gated], 0)
        total = total + jnp.dot(rows, piece[...], preferred_element_type=F32)
    return total


def product_early(distances, mine, other, *rest):
    rest[-1][...] = product((mine, other), distances, rest[:-1])


def last_rows(distance, gated, total, top, bottom, held):
    held[: top.shape[0]] = top[...]
    held[top.shape[0] :] = bottom[...]
    blocks, rows, width = gated.shape
    squares = jnp.zeros((rows, width), F32)
    for block in range(blocks):
        value = gated[block].astype(F32)
        squares = squares + value * value
    scale = lax.rsqrt(jnp.sum(squares, axis=1, keepdims=True) / (blocks * width) + NORM_EPS)
    return ((product((gated,), [distance], [held]) + total) * scale).astype(BF16)


def last_other(distance, other, total, top, bottom, out, held):
    rows = other.shape[1]
    out[...] = last_rows(distance, other, total[rows:], top, bottom, held)


def last_mine(distance, mine, total, top, bottom, out, held):
    rows, columns = mine.shape[1], held.shape[1]
    start = pl.multiple_of(lax.axis_index("seq") % 2 * columns, 128)
    out[:, pl.ds(start, columns)] = last_rows(distance, mine, total[:rows], top, bottom, held)


def put_other(whole, arrived, out, sem):
    del whole
    columns = arrived.shape[1]
    start = pl.multiple_of((1 - lax.axis_index("seq") % 2) * columns, 128)
    copy = pltpu.make_async_copy(arrived, out.at[:, pl.ds(start, columns)], sem)
    copy.start()
    copy.wait()


def call(body, outs, scratch=(), vmem=48, flops=10**7, moved=1 << 21, **kw):
    return pl.pallas_call(
        body,
        out_shape=outs,
        scratch_shapes=list(scratch),
        compiler_params=pltpu.CompilerParams(vmem_limit_bytes=vmem << 20),
        cost_estimate=pl.CostEstimate(flops=flops, bytes_accessed=moved, transcendentals=0),
        **kw,
    )


def local(
    tokens, w_zx, w_bc, w_dt, dt_bias, a_rate, d_skip, conv_x, conv_bc, norm_gain, w_out, segments
):
    tok_rows, feat = tokens.shape
    width = w_zx.shape[2]
    heads = dt_bias.shape[0]
    head_w = width // heads
    state_w = w_bc.shape[1] // 2
    model = w_zx.shape[1]
    n_seq, n_tensor = lax.axis_size("seq"), lax.axis_size("tensor")
    seq_at = lax.axis_index("seq")
    rows = tok_rows // 2
    shape = lambda *s, kind=F32: jax.ShapeDtypeStruct(s, kind)

    spread = lambda v: jnp.repeat(v, head_w, axis=-1)
    expand = np.repeat(np.eye(heads, dtype=np.float32), head_w, axis=1)
    w_step = jnp.dot(w_dt, expand.astype(BF16))
    block = tokens.T
    core = seq_at % 2
    columns = model // 2
    own = (lax.dynamic_slice_in_dim(w_out, core * columns, columns, 1).astype(F32) * norm_gain[:, None]).astype(BF16)
    last = n_tensor // 2
    w_half = width // 2
    shift_rows = [(i, i + 1) for i in range(n_seq - 1)]

    seg_halo = lax.ppermute(segments[tok_rows - HALO :], "seq", shift_rows)
    seg_all = jnp.concatenate([seg_halo, segments])[:, None]
    small = (
        (seg_all[: HALO + rows], seg_all[rows:]),
        (segments[None, :rows], segments[None, rows:]),
        (segments[None, :1], segments[None, tok_rows - 1 :]),
        (spread(dt_bias)[None], spread(a_rate)[None], spread(d_skip)[None]),
    )

    forth = back = block
    arrived, projs = [(0, block)], []
    for step in range(1, last + 1):
        if step == 3:
            forth, back = after(forth, projs[1], small), after(back, projs[1], small)
        elif step > 1:
            forth, back = after(forth, projs[step - 2]), after(back, projs[step - 2])
        arrivals = (forth, back)
        if step < last:
            forth, back = ring_shift(forth, 1), ring_shift(back, -1)
        else:
            far = far_shift(forth, back)
        if step == W_FIRST:
            w_forth, w_back = after((own, own), arrivals)
            w_forth, w_back = ring_shift(w_forth, 1), ring_shift(w_back, -1)
        ahead = last if step == last else 0
        total = projs[-1:]
        fetched = len(arrived) + bool(ahead)
        outs = [shape(tok_rows, 4 * width)] + [shape(feat, 4 * width, kind=BF16)] * bool(ahead)
        results = call(
            functools.partial(project, [distance for distance, _ in arrived], ahead, not total),
            outs,
            [pltpu.VMEM((len(arrived), feat, 4 * width), BF16), pltpu.SemaphoreType.DMA((fetched, 4))],
            in_specs=[VMEM] * len(arrived) + [ANY] * 3 + [VMEM] * len(total),
            flops=10**9,
        )(*[part for _, part in arrived], w_zx, w_bc, w_step, *total)
        projs.append(results[0])
        arrived = [(-step, forth), (step, back)]
    proj = call(project_far, shape(tok_rows, 4 * width), flops=10**9)(
        *far, results[1], projs[-1]
    )

    (seg_ext_a, seg_ext_b), (seg_row_a, seg_row_b), (seg_first, seg_last), (bias, rate, skip) = small
    halo = lax.ppermute(proj[tok_rows - HALO :, width : 3 * width].astype(BF16), "seq", shift_rows)

    msg_rows = state_w + 8
    plane = shape(rows, width)
    ext = pltpu.VMEM((HALO + rows, width), F32)
    out_b, bc_b, enter_b, state_b, gate_b = call(
        functools.partial(later_block, heads, width, rows),
        [plane, plane, plane, shape(msg_rows, width), plane],
        [ext, ext],
    )(proj, seg_ext_b, seg_row_b, conv_x, conv_bc, bias, rate, skip)
    cx_a, bc_a, cum_a, scaled_a, enter_a, state_a, message = call(
        functools.partial(first_front, width, rows),
        [plane] * 5 + [shape(msg_rows, width)] * 2,
        [ext, ext],
    )(proj, halo, seg_ext_a, seg_last, state_b, conv_x, conv_bc, bias, rate)
    if n_seq == 4:
        other_core = lax.ppermute(message, "seq", [(i, i ^ 1) for i in range(n_seq)])
        other_plane = lax.ppermute(message, "seq", [(i, i ^ 2) for i in range(n_seq)])
        other_both = lax.ppermute(other_core, "seq", [(i, i ^ 2) for i in range(n_seq)])
        messages = (message, other_core, other_plane, other_both)
        enough = other_plane
    else:
        messages = (lax.all_gather(message, "seq"),)
        enough = messages
    gated = call(functools.partial(finish, heads, rows, len(messages)), shape(tok_rows, width, kind=BF16))(
        seg_first, *messages, seg_ext_a, seg_row_a, skip, proj, cx_a, bc_a, cum_a, scaled_a, enter_a, state_a,
        out_b, gate_b, bc_b, enter_b
    )
    tok_own = tok_rows // n_tensor

    w_steps = [(w_forth, w_back)]
    orders = [(far, projs[-1]), enough]
    for step in range(2, last + 1):
        if step - 2 < len(orders):
            w_forth, w_back = after((w_forth, w_back), orders[step - 2])
        if step == last:
            w_far = far_shift(w_forth, w_back)
            break
        w_forth, w_back = ring_shift(w_forth, 1), ring_shift(w_back, -1)
        w_steps.append((w_forth, w_back))
        if step == 2:
            blocks = after(gated, w_forth, w_back).reshape(n_tensor, tok_own, width)
            mine = lax.all_to_all(blocks, "tensor", 0, 0)
    swap = [(i, i ^ 1) for i in range(n_seq)]
    other = lax.ppermute(mine, "seq", swap)
    pieces, distances = [own], [0]
    for i, pair in enumerate(w_steps):
        pieces += pair
        distances += [-i - 1, i + 1]
    total = call(functools.partial(product_early, distances), shape(2 * tok_own, columns), flops=1, moved=1)(
        mine, other, *pieces
    )
    half = shape(tok_own, columns, kind=BF16)
    held = [pltpu.VMEM((width, columns), BF16)]
    out_other = call(functools.partial(last_other, last), half, held)(other, total, *w_far)
    arrived = lax.ppermute(out_other, "seq", swap)
    whole = call(functools.partial(last_mine, last), shape(tok_own, model, kind=BF16), held)(mine, total, *w_far)
    return call(
        put_other,
        shape(tok_own, model, kind=BF16),
        [pltpu.SemaphoreType.DMA],
        in_specs=[ANY, VMEM],
        out_specs=ANY,
        input_output_aliases={0: 0},
    )(whole, arrived)


def solution(mesh):
    in_specs = (
        P("seq", "tensor"),
        P(None, None, "tensor"),
        P(),
        P(None, "tensor"),
        P("tensor"),
        P("tensor"),
        P("tensor"),
        P(None, "tensor"),
        P(),
        P("tensor"),
        P("tensor", None),
        P("seq"),
    )
    out_specs = P(("seq", "tensor"), None)
    return jax.shard_map(local, mesh=mesh, in_specs=in_specs, out_specs=out_specs, check_vma=False)
```

```python
import functools

import jax
import jax.numpy as jnp
import numpy as np
from jax import lax
from jax.experimental import pallas as pl
from jax.experimental.pallas import tpu as pltpu
from jax.sharding import PartitionSpec as P

NORM_EPS = 1e-05
F32 = jnp.float32
BF16 = jnp.bfloat16
VMEM = pl.BlockSpec(memory_space=pltpu.VMEM)
ANY = pl.BlockSpec(memory_space=pl.ANY)
HALO = 8
W_FIRST = 3


def ring_place(index, n):
    return jnp.where(index % 2 == 0, index // 2, (2 * n - 1 - index) // 2)


def ring_index(place, n):
    return jnp.where(place < n // 2, 2 * place, 2 * n - 1 - 2 * place)


def ring_shift(block, step):
    n = lax.axis_size("tensor")
    order = [2 * i if i < n // 2 else 2 * n - 1 - 2 * i for i in range(n)]
    return lax.ppermute(block, "tensor", [(order[i], order[(i + step) % n]) for i in range(n)])


def after(values, *earlier):
    return lax.optimization_barrier((values, earlier))[0]


def far_shift(forth, back):
    cut = forth.shape[0] // 32 * 16
    parts = [jax.ShapeDtypeStruct((size, forth.shape[1]), forth.dtype) for size in (cut, forth.shape[0] - cut)]
    top, bottom = call(halves, parts)(forth, back)
    return ring_shift(top, 1), ring_shift(bottom, -1)


def halves(forth, back, top, bottom):
    size = top.shape[0]
    top[...] = forth[:size]
    bottom[...] = back[size:]


def silu(v):
    return v / (1.0 + jnp.exp(-v))


def dot(a, b, dims=((1,), (0,))):
    return lax.dot_general(a.astype(BF16), b.astype(BF16), (dims, ((), ())), preferred_element_type=F32)


def source_of(distance):
    n = lax.axis_size("tensor")
    return ring_index((ring_place(lax.axis_index("tensor"), n) + distance + n) % n, n)


def project(distances, ahead, first, *refs):
    count, fetched = len(distances), len(distances) + bool(ahead)
    blocks, (w_zx, w_bc, w_dt), refs = refs[:count], refs[count : count + 3], refs[count + 3 :]
    total, refs = (None, refs) if first else (refs[0], refs[1:])
    out, far_out, held, sems = refs if ahead else (refs[0], None, *refs[1:])
    feat, width = held.shape[1], w_bc.shape[1]
    sources = [w_zx.at[0], w_zx.at[1], w_bc, w_dt]
    copies = []
    for k, distance in enumerate([*distances, ahead][:fetched]):
        rows = pl.ds(pl.multiple_of(source_of(distance) * feat, 16), feat)
        for j, source in enumerate(sources):
            target = held.at[k] if k < count else far_out
            copies.append(
                pltpu.make_async_copy(source.at[rows], target.at[:, pl.ds(j * width, width)], sems.at[k, j])
            )
            copies[-1].start()
    result = 0.0 if first else total[...]
    for k in range(count):
        for j in range(len(sources)):
            copies[k * len(sources) + j].wait()
        result = result + dot(blocks[k][...], held[k], ((0,), (0,)))
    out[...] = result
    for copy in copies[count * len(sources) :]:
        copy.wait()


def project_far(top, bottom, weights, total, out):
    cut = top.shape[0]
    out[...] = (
        total[...] + dot(top[...], weights[:cut], ((0,), (0,))) + dot(bottom[...], weights[cut:], ((0,), (0,)))
    )


def conv(ext, seg_ext, taps, rows):
    size = taps.shape[0]
    seg_now = seg_ext[HALO : HALO + rows]
    total = taps[size - 1 : size] * ext[HALO : HALO + rows]
    for offset in range(1, size):
        same = seg_ext[HALO - offset : HALO - offset + rows] == seg_now
        total = total + taps[size - 1 - offset : size - offset] * jnp.where(
            same, ext[HALO - offset : HALO - offset + rows], 0.0
        )
    return silu(total)


def prefix_sum(values):
    rows = values.shape[0]
    lower = lax.broadcasted_iota(jnp.int32, (rows, rows), 0) >= lax.broadcasted_iota(jnp.int32, (rows, rows), 1)
    lower = jnp.where(lower, 1.0, 0.0).astype(BF16)
    total = jnp.zeros(values.shape, F32)
    rest = values
    parts = []
    for _ in range(3):
        part = rest.astype(BF16)
        parts.append(part)
        rest = rest - part.astype(F32)
    for part in reversed(parts):
        total = total + jnp.dot(lower, part, preferred_element_type=F32)
    return total


def block_front(ext_x, ext_bc, seg_ext, dt_raw, taps_x, taps_bc, bias, rate, rows, seg_enter, seg_leave):
    conv_x = conv(ext_x, seg_ext, taps_x, rows)
    conv_bc = conv(ext_bc, seg_ext, taps_bc, rows)
    seg = seg_ext[HALO : HALO + rows]
    shifted = dt_raw + bias
    step_size = jnp.maximum(shifted, 0.0) + jnp.log1p(jnp.exp(-jnp.abs(shifted)))
    cum = prefix_sum(-rate * step_size)
    scaled = conv_x * step_size
    last = cum[rows - 1 : rows]
    tail = jnp.where(seg == seg_leave, jnp.exp(last - cum), 0.0)
    state_w = conv_bc.shape[1] // 2
    state = dot(conv_bc, tail * scaled, ((0,), (0,)))[:state_w]
    enter = jnp.where(seg == seg_enter, jnp.exp(cum), 0.0)
    return conv_x, conv_bc, cum, scaled, state, enter, last


def block_inner(conv_bc, cum, scaled, seg_col, seg_row, heads):
    rows, width = scaled.shape
    state_w = conv_bc.shape[1] // 2
    head_w = width // heads
    scores = dot(conv_bc[:, state_w:], conv_bc[:, :state_w], ((1,), (1,)))
    later = lax.broadcasted_iota(jnp.int32, (rows, rows), 0) >= lax.broadcasted_iota(jnp.int32, (rows, rows), 1)
    visible = (seg_col == seg_row) & later
    cum_rows = cum.T
    lane = lax.broadcasted_iota(jnp.int32, (rows, width), 1)
    result = jnp.zeros((rows, width), F32)
    scaled = scaled.astype(BF16)
    for head in range(heads):
        at = head * head_w
        gap = jnp.where(visible, cum[:, at : at + 1] - cum_rows[at : at + 1, :], -jnp.inf)
        part = dot(jnp.exp(gap) * scores, scaled)
        result = jnp.where((lane >= at) & (lane < at + head_w), part, result)
    return result


def later_block(heads, width, rows, proj, seg_ext, seg_row, taps_x, taps_bc, bias, rate, skip,
                out, bc_out, enter_out, state_out, gate_out, ext_x, ext_bc):
    rounded = proj[rows - HALO :, : 3 * width].astype(BF16).astype(F32)
    gate_out[...] = silu(rounded[HALO:, :width])
    ext_x[...] = rounded[:, width : 2 * width]
    ext_bc[...] = rounded[:, 2 * width : 3 * width]
    seg_enter = seg_ext[HALO - 1 : HALO]
    seg_leave = seg_ext[HALO + rows - 1 : HALO + rows]
    conv_x, conv_bc, cum, scaled, state, enter, last = block_front(
        ext_x, ext_bc, seg_ext, proj[rows:, 3 * width :], taps_x, taps_bc[...], bias[...], rate[...], rows, seg_enter, seg_leave
    )
    out[...] = block_inner(conv_bc, cum, scaled, seg_ext[HALO:], seg_row[...], heads) + skip[...] * conv_x
    bc_out[...] = conv_bc
    enter_out[...] = enter
    keep = jnp.where(seg_enter == seg_leave, jnp.exp(last), 0.0)
    state_w = state.shape[0]
    state_out[:state_w] = state
    state_out[state_w : state_w + 1] = keep
    state_out[state_w + 1 : state_w + 2] = last
    state_out[state_w + 2 :] = jnp.zeros((state_out.shape[0] - state_w - 2, width), F32)


def first_front(width, rows, proj, halo, seg_ext, seg_last, state_b, taps_x, taps_bc, bias, rate,
                conv_out, bc_out, cum_out, scaled_out, enter_out, state_out, message, ext_x, ext_bc):
    ext_x[:HALO] = halo[:, :width].astype(F32)
    ext_bc[:HALO] = halo[:, width:].astype(F32)
    ext_x[HALO:] = proj[:rows, width : 2 * width].astype(BF16).astype(F32)
    ext_bc[HALO:] = proj[:rows, 2 * width : 3 * width].astype(BF16).astype(F32)
    seg_enter = seg_ext[HALO : HALO + 1]
    seg_leave = seg_ext[HALO + rows - 1 : HALO + rows]
    conv_x, conv_bc, cum, scaled, state, enter, last = block_front(
        ext_x, ext_bc, seg_ext, proj[:rows, 3 * width :], taps_x, taps_bc[...], bias[...], rate[...], rows, seg_enter, seg_leave
    )
    conv_out[...] = conv_x
    bc_out[...] = conv_bc
    cum_out[...] = cum
    scaled_out[...] = scaled
    enter_out[...] = enter
    keep = jnp.where(seg_enter == seg_leave, jnp.exp(last), 0.0)
    state_w = state.shape[0]
    state_out[:state_w] = state
    state_out[state_w : state_w + 1] = keep
    state_out[state_w + 1 :] = jnp.zeros((state_out.shape[0] - state_w - 1, width), F32)
    message[:state_w] = state_b[state_w : state_w + 1] * state + state_b[:state_w]
    message[state_w : state_w + 1] = last + state_b[state_w + 1 : state_w + 2]
    message[state_w + 1 : state_w + 2] = jnp.broadcast_to(seg_last[...].astype(F32), (1, width))
    message[state_w + 2 :] = jnp.zeros((message.shape[0] - state_w - 2, width), F32)


def finish(heads, rows, count, seg_first, *refs):
    messages, refs = refs[:count], refs[count:]
    finish_with(heads, rows, seg_first, messages, *refs)


def stack(first, second, out):
    out[0] = first[...]
    out[1] = second[...]


def message_from(messages, device):
    if len(messages) == 1:
        return messages[0][device]
    place = lax.axis_index("seq")
    core = place % 2 == device % 2
    plane = place // 2 == device // 2
    own, other_core, other_plane = messages
    here = jnp.where(core, own[...], other_core[...])
    return jnp.where(plane, here, jnp.where(core, other_plane[0], other_plane[1]))


def finish_with(heads, rows, seg_first, messages, seg_ext_a, seg_row_a, skip, proj, conv_a, bc_a, cum_a, scaled_a, enter_a,
           state_a, out_b, gate_b, bc_b, enter_b, gated):
    state_w = bc_a.shape[1] // 2
    width = out_b.shape[1]
    entering = jnp.zeros((state_w, width), F32)
    decay = jnp.zeros((1, width), F32)
    first = seg_first[...].astype(F32)
    place = lax.axis_index("seq")
    for device in reversed(range(lax.axis_size("seq") - 1)):
        earlier = device < place
        message = message_from(messages, device)
        passes = earlier & (message[state_w + 1 : state_w + 2] == first)
        passes = jnp.where(passes, jnp.exp(decay), 0.0)
        entering = entering + passes * message[:state_w]
        decay = decay + jnp.where(earlier, message[state_w : state_w + 1], 0.0)
    second = state_a[state_w : state_w + 1] * entering + state_a[:state_w]
    out_a = block_inner(bc_a[...], cum_a[...], scaled_a[...], seg_ext_a[HALO:], seg_row_a[...], heads)
    out_a = out_a + skip[...] * conv_a[...] + enter_a[...] * dot(bc_a[:, state_w:], entering)
    gated[:rows] = (out_a * silu(proj[:rows, :width].astype(BF16).astype(F32))).astype(BF16)
    gated[rows:] = ((out_b[...] + enter_b[...] * dot(bc_b[:, state_w:], second)) * gate_b[...]).astype(BF16)


def product(gated, distances, pieces):
    total = 0.0
    for distance, piece in zip(distances, pieces):
        source = source_of(distance)
        rows = jnp.concatenate([part[source] for part in gated], 0)
        total = total + jnp.dot(rows, piece[...], preferred_element_type=F32)
    return total


def product_early(distances, mine, other, *rest):
    rest[-1][...] = product((mine, other), distances, rest[:-1])


def last_rows(distance, gated, total, top, bottom, held):
    held[: top.shape[0]] = top[...]
    held[top.shape[0] :] = bottom[...]
    blocks, rows, width = gated.shape
    squares = jnp.zeros((rows, width), F32)
    for block in range(blocks):
        value = gated[block].astype(F32)
        squares = squares + value * value
    scale = lax.rsqrt(jnp.sum(squares, axis=1, keepdims=True) / (blocks * width) + NORM_EPS)
    return ((product((gated,), [distance], [held]) + total) * scale).astype(BF16)


def last_other(distance, other, total, top, bottom, out, held):
    rows = other.shape[1]
    out[...] = last_rows(distance, other, total[rows:], top, bottom, held)


def last_mine(distance, mine, total, top, bottom, out, held):
    rows, columns = mine.shape[1], held.shape[1]
    start = pl.multiple_of(lax.axis_index("seq") % 2 * columns, 128)
    out[:, pl.ds(start, columns)] = last_rows(distance, mine, total[:rows], top, bottom, held)


def put_other(whole, arrived, out, sem):
    del whole
    columns = arrived.shape[1]
    start = pl.multiple_of((1 - lax.axis_index("seq") % 2) * columns, 128)
    copy = pltpu.make_async_copy(arrived, out.at[:, pl.ds(start, columns)], sem)
    copy.start()
    copy.wait()


def call(body, outs, scratch=(), vmem=48, flops=10**7, moved=1 << 21, **kw):
    return pl.pallas_call(
        body,
        out_shape=outs,
        scratch_shapes=list(scratch),
        compiler_params=pltpu.CompilerParams(vmem_limit_bytes=vmem << 20),
        cost_estimate=pl.CostEstimate(flops=flops, bytes_accessed=moved, transcendentals=0),
        **kw,
    )


def local(
    tokens, w_zx, w_bc, w_dt, dt_bias, a_rate, d_skip, conv_x, conv_bc, norm_gain, w_out, segments
):
    tok_rows, feat = tokens.shape
    width = w_zx.shape[2]
    heads = dt_bias.shape[0]
    head_w = width // heads
    state_w = w_bc.shape[1] // 2
    model = w_zx.shape[1]
    n_seq, n_tensor = lax.axis_size("seq"), lax.axis_size("tensor")
    seq_at = lax.axis_index("seq")
    rows = tok_rows // 2
    shape = lambda *s, kind=F32: jax.ShapeDtypeStruct(s, kind)

    spread = lambda v: jnp.repeat(v, head_w, axis=-1)
    expand = np.repeat(np.eye(heads, dtype=np.float32), head_w, axis=1)
    w_step = jnp.dot(w_dt, expand.astype(BF16))
    block = tokens.T
    core = seq_at % 2
    columns = model // 2
    own = (lax.dynamic_slice_in_dim(w_out, core * columns, columns, 1).astype(F32) * norm_gain[:, None]).astype(BF16)
    last = n_tensor // 2
    w_half = width // 2
    shift_rows = [(i, i + 1) for i in range(n_seq - 1)]

    seg_halo = lax.ppermute(segments[tok_rows - HALO :], "seq", shift_rows)
    seg_all = jnp.concatenate([seg_halo, segments])[:, None]
    small = (
        (seg_all[: HALO + rows], seg_all[rows:]),
        (segments[None, :rows], segments[None, rows:]),
        (segments[None, :1], segments[None, tok_rows - 1 :]),
        (spread(dt_bias)[None], spread(a_rate)[None], spread(d_skip)[None]),
    )

    forth = back = block
    arrived, projs = [(0, block)], []
    for step in range(1, last + 1):
        if step == 3:
            forth, back = after(forth, projs[1], small), after(back, projs[1], small)
        elif step > 1:
            forth, back = after(forth, projs[step - 2]), after(back, projs[step - 2])
        arrivals = (forth, back)
        if step < last:
            forth, back = ring_shift(forth, 1), ring_shift(back, -1)
        else:
            far = far_shift(forth, back)
        if step == W_FIRST:
            w_forth, w_back = after((own, own), arrivals)
            w_forth, w_back = ring_shift(w_forth, 1), ring_shift(w_back, -1)
        ahead = last if step == last else 0
        total = projs[-1:]
        fetched = len(arrived) + bool(ahead)
        outs = [shape(tok_rows, 4 * width)] + [shape(feat, 4 * width, kind=BF16)] * bool(ahead)
        results = call(
            functools.partial(project, [distance for distance, _ in arrived], ahead, not total),
            outs,
            [pltpu.VMEM((len(arrived), feat, 4 * width), BF16), pltpu.SemaphoreType.DMA((fetched, 4))],
            in_specs=[VMEM] * len(arrived) + [ANY] * 3 + [VMEM] * len(total),
            flops=10**9,
        )(*[part for _, part in arrived], w_zx, w_bc, w_step, *total)
        projs.append(results[0])
        arrived = [(-step, forth), (step, back)]
    proj = call(project_far, shape(tok_rows, 4 * width), flops=10**9)(
        *far, results[1], projs[-1]
    )

    (seg_ext_a, seg_ext_b), (seg_row_a, seg_row_b), (seg_first, seg_last), (bias, rate, skip) = small
    halo = lax.ppermute(proj[tok_rows - HALO :, width : 3 * width].astype(BF16), "seq", shift_rows)

    msg_rows = state_w + 8
    plane = shape(rows, width)
    ext = pltpu.VMEM((HALO + rows, width), F32)
    out_b, bc_b, enter_b, state_b, gate_b = call(
        functools.partial(later_block, heads, width, rows),
        [plane, plane, plane, shape(msg_rows, width), plane],
        [ext, ext],
    )(proj, seg_ext_b, seg_row_b, conv_x, conv_bc, bias, rate, skip)
    cx_a, bc_a, cum_a, scaled_a, enter_a, state_a, message = call(
        functools.partial(first_front, width, rows),
        [plane] * 5 + [shape(msg_rows, width)] * 2,
        [ext, ext],
    )(proj, halo, seg_ext_a, seg_last, state_b, conv_x, conv_bc, bias, rate)
    if n_seq == 4:
        other_core = lax.ppermute(message, "seq", [(i, i ^ 1) for i in range(n_seq)])
        chip = call(stack, shape(2, msg_rows, width))(message, other_core)
        messages = (message, other_core, lax.ppermute(chip, "seq", [(i, i ^ 2) for i in range(n_seq)]))
    else:
        messages = (lax.all_gather(message, "seq"),)
    gated = call(functools.partial(finish, heads, rows, len(messages)), shape(tok_rows, width, kind=BF16))(
        seg_first, *messages, seg_ext_a, seg_row_a, skip, proj, cx_a, bc_a, cum_a, scaled_a, enter_a, state_a,
        out_b, gate_b, bc_b, enter_b
    )
    tok_own = tok_rows // n_tensor

    w_steps = [(w_forth, w_back)]
    orders = [(far, projs[-1]), messages]
    for step in range(2, last + 1):
        if step - 2 < len(orders):
            w_forth, w_back = after((w_forth, w_back), orders[step - 2])
        if step == last:
            w_far = far_shift(w_forth, w_back)
            break
        w_forth, w_back = ring_shift(w_forth, 1), ring_shift(w_back, -1)
        w_steps.append((w_forth, w_back))
        if step == 2:
            blocks = after(gated, w_forth, w_back).reshape(n_tensor, tok_own, width)
            mine = lax.all_to_all(blocks, "tensor", 0, 0)
    swap = [(i, i ^ 1) for i in range(n_seq)]
    other = lax.ppermute(mine, "seq", swap)
    pieces, distances = [own], [0]
    for i, pair in enumerate(w_steps):
        pieces += pair
        distances += [-i - 1, i + 1]
    total = call(functools.partial(product_early, distances), shape(2 * tok_own, columns), flops=1, moved=1)(
        mine, other, *pieces
    )
    half = shape(tok_own, columns, kind=BF16)
    held = [pltpu.VMEM((width, columns), BF16)]
    out_other = call(functools.partial(last_other, last), half, held)(other, total, *w_far)
    arrived = lax.ppermute(out_other, "seq", swap)
    whole = call(functools.partial(last_mine, last), shape(tok_own, model, kind=BF16), held)(mine, total, *w_far)
    return call(
        put_other,
        shape(tok_own, model, kind=BF16),
        [pltpu.SemaphoreType.DMA],
        in_specs=[ANY, VMEM],
        out_specs=ANY,
        input_output_aliases={0: 0},
    )(whole, arrived)


def solution(mesh):
    in_specs = (
        P("seq", "tensor"),
        P(None, None, "tensor"),
        P(),
        P(None, "tensor"),
        P("tensor"),
        P("tensor"),
        P("tensor"),
        P(None, "tensor"),
        P(),
        P("tensor"),
        P("tensor", None),
        P("seq"),
    )
    out_specs = P(("seq", "tensor"), None)
    return jax.shard_map(local, mesh=mesh, in_specs=in_specs, out_specs=out_specs, check_vma=False)
```

```python
import functools

import jax
import jax.numpy as jnp
import numpy as np
from jax import lax
from jax.experimental import pallas as pl
from jax.experimental.pallas import tpu as pltpu
from jax.sharding import PartitionSpec as P

NORM_EPS = 1e-05
F32 = jnp.float32
BF16 = jnp.bfloat16
VMEM = pl.BlockSpec(memory_space=pltpu.VMEM)
ANY = pl.BlockSpec(memory_space=pl.ANY)
HALO = 8
W_FIRST = 3


def ring_place(index, n):
    return jnp.where(index % 2 == 0, index // 2, (2 * n - 1 - index) // 2)


def ring_index(place, n):
    return jnp.where(place < n // 2, 2 * place, 2 * n - 1 - 2 * place)


def ring_shift(block, step):
    n = lax.axis_size("tensor")
    order = [2 * i if i < n // 2 else 2 * n - 1 - 2 * i for i in range(n)]
    return lax.ppermute(block, "tensor", [(order[i], order[(i + step) % n]) for i in range(n)])


def after(values, *earlier):
    return lax.optimization_barrier((values, earlier))[0]


def far_shift(forth, back):
    cut = forth.shape[0] // 32 * 16
    parts = [jax.ShapeDtypeStruct((size, forth.shape[1]), forth.dtype) for size in (cut, forth.shape[0] - cut)]
    top, bottom = call(halves, parts)(forth, back)
    return ring_shift(top, 1), ring_shift(bottom, -1)


def halves(forth, back, top, bottom):
    size = top.shape[0]
    top[...] = forth[:size]
    bottom[...] = back[size:]


def silu(v):
    return v / (1.0 + jnp.exp(-v))


def dot(a, b, dims=((1,), (0,))):
    return lax.dot_general(a.astype(BF16), b.astype(BF16), (dims, ((), ())), preferred_element_type=F32)


def source_of(distance):
    n = lax.axis_size("tensor")
    return ring_index((ring_place(lax.axis_index("tensor"), n) + distance + n) % n, n)


def project(distances, ahead, first, *refs):
    count, fetched = len(distances), len(distances) + bool(ahead)
    blocks, (w_zx, w_bc, w_dt), refs = refs[:count], refs[count : count + 3], refs[count + 3 :]
    total, refs = (None, refs) if first else (refs[0], refs[1:])
    out, far_out, held, sems = refs if ahead else (refs[0], None, *refs[1:])
    feat, width = held.shape[1], w_bc.shape[1]
    sources = [w_zx.at[0], w_zx.at[1], w_bc, w_dt]
    copies = []
    for k, distance in enumerate([*distances, ahead][:fetched]):
        rows = pl.ds(pl.multiple_of(source_of(distance) * feat, 16), feat)
        for j, source in enumerate(sources):
            target = held.at[k] if k < count else far_out
            copies.append(
                pltpu.make_async_copy(source.at[rows], target.at[:, pl.ds(j * width, width)], sems.at[k, j])
            )
            copies[-1].start()
    result = 0.0 if first else total[...]
    for k in range(count):
        for j in range(len(sources)):
            copies[k * len(sources) + j].wait()
        result = result + dot(blocks[k][...], held[k], ((0,), (0,)))
    out[...] = result
    for copy in copies[count * len(sources) :]:
        copy.wait()


def project_far(top, bottom, weights, total, out):
    cut = top.shape[0]
    out[...] = (
        total[...] + dot(top[...], weights[:cut], ((0,), (0,))) + dot(bottom[...], weights[cut:], ((0,), (0,)))
    )


def conv(ext, seg_ext, taps, rows):
    size = taps.shape[0]
    seg_now = seg_ext[HALO : HALO + rows]
    total = taps[size - 1 : size] * ext[HALO : HALO + rows]
    for offset in range(1, size):
        same = seg_ext[HALO - offset : HALO - offset + rows] == seg_now
        total = total + taps[size - 1 - offset : size - offset] * jnp.where(
            same, ext[HALO - offset : HALO - offset + rows], 0.0
        )
    return silu(total)


def prefix_sum(values):
    rows = values.shape[0]
    lower = lax.broadcasted_iota(jnp.int32, (rows, rows), 0) >= lax.broadcasted_iota(jnp.int32, (rows, rows), 1)
    lower = jnp.where(lower, 1.0, 0.0).astype(BF16)
    total = jnp.zeros(values.shape, F32)
    rest = values
    parts = []
    for _ in range(3):
        part = rest.astype(BF16)
        parts.append(part)
        rest = rest - part.astype(F32)
    for part in reversed(parts):
        total = total + jnp.dot(lower, part, preferred_element_type=F32)
    return total


def block_front(ext_x, ext_bc, seg_ext, dt_raw, taps_x, taps_bc, bias, rate, rows, seg_enter, seg_leave):
    conv_x = conv(ext_x, seg_ext, taps_x, rows)
    conv_bc = conv(ext_bc, seg_ext, taps_bc, rows)
    seg = seg_ext[HALO : HALO + rows]
    shifted = dt_raw + bias
    step_size = jnp.maximum(shifted, 0.0) + jnp.log1p(jnp.exp(-jnp.abs(shifted)))
    cum = prefix_sum(-rate * step_size)
    scaled = conv_x * step_size
    last = cum[rows - 1 : rows]
    tail = jnp.where(seg == seg_leave, jnp.exp(last - cum), 0.0)
    state_w = conv_bc.shape[1] // 2
    state = dot(conv_bc, tail * scaled, ((0,), (0,)))[:state_w]
    enter = jnp.where(seg == seg_enter, jnp.exp(cum), 0.0)
    return conv_x, conv_bc, cum, scaled, state, enter, last


def block_inner(conv_bc, cum, scaled, seg_col, seg_row, heads):
    rows, width = scaled.shape
    state_w = conv_bc.shape[1] // 2
    head_w = width // heads
    scores = dot(conv_bc[:, state_w:], conv_bc[:, :state_w], ((1,), (1,)))
    later = lax.broadcasted_iota(jnp.int32, (rows, rows), 0) >= lax.broadcasted_iota(jnp.int32, (rows, rows), 1)
    visible = (seg_col == seg_row) & later
    cum_rows = cum.T
    lane = lax.broadcasted_iota(jnp.int32, (rows, width), 1)
    result = jnp.zeros((rows, width), F32)
    scaled = scaled.astype(BF16)
    for head in range(heads):
        at = head * head_w
        gap = jnp.where(visible, cum[:, at : at + 1] - cum_rows[at : at + 1, :], -jnp.inf)
        part = dot(jnp.exp(gap) * scores, scaled)
        result = jnp.where((lane >= at) & (lane < at + head_w), part, result)
    return result


def later_block(heads, width, rows, proj, seg_ext, seg_row, taps_x, taps_bc, bias, rate, skip,
                out, bc_out, enter_out, state_out, gate_out, ext_x, ext_bc):
    rounded = proj[rows - HALO :, : 3 * width].astype(BF16).astype(F32)
    gate_out[...] = silu(rounded[HALO:, :width])
    ext_x[...] = rounded[:, width : 2 * width]
    ext_bc[...] = rounded[:, 2 * width : 3 * width]
    seg_enter = seg_ext[HALO - 1 : HALO]
    seg_leave = seg_ext[HALO + rows - 1 : HALO + rows]
    conv_x, conv_bc, cum, scaled, state, enter, last = block_front(
        ext_x, ext_bc, seg_ext, proj[rows:, 3 * width :], taps_x, taps_bc[...], bias[...], rate[...], rows, seg_enter, seg_leave
    )
    out[...] = block_inner(conv_bc, cum, scaled, seg_ext[HALO:], seg_row[...], heads) + skip[...] * conv_x
    bc_out[...] = conv_bc
    enter_out[...] = enter
    keep = jnp.where(seg_enter == seg_leave, jnp.exp(last), 0.0)
    state_w = state.shape[0]
    state_out[:state_w] = state
    state_out[state_w : state_w + 1] = keep
    state_out[state_w + 1 : state_w + 2] = last
    state_out[state_w + 2 :] = jnp.zeros((state_out.shape[0] - state_w - 2, width), F32)


def first_front(width, rows, proj, halo, seg_ext, seg_last, state_b, taps_x, taps_bc, bias, rate,
                conv_out, bc_out, cum_out, scaled_out, enter_out, state_out, message, ext_x, ext_bc):
    ext_x[:HALO] = halo[:, :width].astype(F32)
    ext_bc[:HALO] = halo[:, width:].astype(F32)
    ext_x[HALO:] = proj[:rows, width : 2 * width].astype(BF16).astype(F32)
    ext_bc[HALO:] = proj[:rows, 2 * width : 3 * width].astype(BF16).astype(F32)
    seg_enter = seg_ext[HALO : HALO + 1]
    seg_leave = seg_ext[HALO + rows - 1 : HALO + rows]
    conv_x, conv_bc, cum, scaled, state, enter, last = block_front(
        ext_x, ext_bc, seg_ext, proj[:rows, 3 * width :], taps_x, taps_bc[...], bias[...], rate[...], rows, seg_enter, seg_leave
    )
    conv_out[...] = conv_x
    bc_out[...] = conv_bc
    cum_out[...] = cum
    scaled_out[...] = scaled
    enter_out[...] = enter
    keep = jnp.where(seg_enter == seg_leave, jnp.exp(last), 0.0)
    state_w = state.shape[0]
    state_out[:state_w] = state
    state_out[state_w : state_w + 1] = keep
    state_out[state_w + 1 :] = jnp.zeros((state_out.shape[0] - state_w - 1, width), F32)
    message[:state_w] = state_b[state_w : state_w + 1] * state + state_b[:state_w]
    message[state_w : state_w + 1] = last + state_b[state_w + 1 : state_w + 2]
    message[state_w + 1 : state_w + 2] = jnp.broadcast_to(seg_last[...].astype(F32), (1, width))
    message[state_w + 2 :] = jnp.zeros((message.shape[0] - state_w - 2, width), F32)


def finish(heads, rows, count, seg_first, *refs):
    messages, refs = refs[:count], refs[count:]
    finish_with(heads, rows, seg_first, messages, *refs)


def message_from(messages, device):
    if len(messages) == 1:
        return messages[0][device]
    place = lax.axis_index("seq")
    core = place % 2 == device % 2
    plane = place // 2 == device // 2
    own, other_core, other_plane, other_both = (m[...] for m in messages)
    return jnp.where(plane, jnp.where(core, own, other_core), jnp.where(core, other_plane, other_both))


def finish_with(heads, rows, seg_first, messages, seg_ext_a, seg_row_a, skip, proj, conv_a, bc_a, cum_a, scaled_a, enter_a,
           state_a, out_b, gate_b, bc_b, enter_b, gated):
    state_w = bc_a.shape[1] // 2
    width = out_b.shape[1]
    entering = jnp.zeros((state_w, width), F32)
    decay = jnp.zeros((1, width), F32)
    first = seg_first[...].astype(F32)
    place = lax.axis_index("seq")
    for device in reversed(range(lax.axis_size("seq") - 1)):
        earlier = device < place
        message = message_from(messages, device)
        passes = earlier & (message[state_w + 1 : state_w + 2] == first)
        passes = jnp.where(passes, jnp.exp(decay), 0.0)
        entering = entering + passes * message[:state_w]
        decay = decay + jnp.where(earlier, message[state_w : state_w + 1], 0.0)
    second = state_a[state_w : state_w + 1] * entering + state_a[:state_w]
    out_a = block_inner(bc_a[...], cum_a[...], scaled_a[...], seg_ext_a[HALO:], seg_row_a[...], heads)
    out_a = out_a + skip[...] * conv_a[...] + enter_a[...] * dot(bc_a[:, state_w:], entering)
    gated[:rows] = (out_a * silu(proj[:rows, :width].astype(BF16).astype(F32))).astype(BF16)
    gated[rows:] = ((out_b[...] + enter_b[...] * dot(bc_b[:, state_w:], second)) * gate_b[...]).astype(BF16)


def product(gated, distances, pieces):
    total = 0.0
    for distance, piece in zip(distances, pieces):
        source = source_of(distance)
        rows = jnp.concatenate([part[source] for part in gated], 0)
        total = total + jnp.dot(rows, piece[...], preferred_element_type=F32)
    return total


def product_early(distances, mine, other, *rest):
    rest[-1][...] = product((mine, other), distances, rest[:-1])


def last_rows(distance, gated, total, top, bottom, held):
    held[: top.shape[0]] = top[...]
    held[top.shape[0] :] = bottom[...]
    blocks, rows, width = gated.shape
    squares = jnp.zeros((rows, width), F32)
    for block in range(blocks):
        value = gated[block].astype(F32)
        squares = squares + value * value
    scale = lax.rsqrt(jnp.sum(squares, axis=1, keepdims=True) / (blocks * width) + NORM_EPS)
    return ((product((gated,), [distance], [held]) + total) * scale).astype(BF16)


def last_other(distance, other, total, top, bottom, out, held):
    rows = other.shape[1]
    out[...] = last_rows(distance, other, total[rows:], top, bottom, held)


def last_mine(distance, mine, total, top, bottom, out, held):
    rows, columns = mine.shape[1], held.shape[1]
    start = pl.multiple_of(lax.axis_index("seq") % 2 * columns, 128)
    out[:, pl.ds(start, columns)] = last_rows(distance, mine, total[:rows], top, bottom, held)


def put_other(whole, arrived, out, sem):
    del whole
    columns = arrived.shape[1]
    start = pl.multiple_of((1 - lax.axis_index("seq") % 2) * columns, 128)
    copy = pltpu.make_async_copy(arrived, out.at[:, pl.ds(start, columns)], sem)
    copy.start()
    copy.wait()


def call(body, outs, scratch=(), vmem=40, flops=10**7, moved=1 << 21, **kw):
    return pl.pallas_call(
        body,
        out_shape=outs,
        scratch_shapes=list(scratch),
        compiler_params=pltpu.CompilerParams(vmem_limit_bytes=vmem << 20),
        cost_estimate=pl.CostEstimate(flops=flops, bytes_accessed=moved, transcendentals=0),
        **kw,
    )


def local(
    tokens, w_zx, w_bc, w_dt, dt_bias, a_rate, d_skip, conv_x, conv_bc, norm_gain, w_out, segments
):
    tok_rows, feat = tokens.shape
    width = w_zx.shape[2]
    heads = dt_bias.shape[0]
    head_w = width // heads
    state_w = w_bc.shape[1] // 2
    model = w_zx.shape[1]
    n_seq, n_tensor = lax.axis_size("seq"), lax.axis_size("tensor")
    seq_at = lax.axis_index("seq")
    rows = tok_rows // 2
    shape = lambda *s, kind=F32: jax.ShapeDtypeStruct(s, kind)

    spread = lambda v: jnp.repeat(v, head_w, axis=-1)
    expand = np.repeat(np.eye(heads, dtype=np.float32), head_w, axis=1)
    w_step = jnp.dot(w_dt, expand.astype(BF16))
    block = tokens.T
    core = seq_at % 2
    columns = model // 2
    own = (lax.dynamic_slice_in_dim(w_out, core * columns, columns, 1).astype(F32) * norm_gain[:, None]).astype(BF16)
    last = n_tensor // 2
    w_half = width // 2
    shift_rows = [(i, i + 1) for i in range(n_seq - 1)]

    seg_halo = lax.ppermute(segments[tok_rows - HALO :], "seq", shift_rows)
    seg_all = jnp.concatenate([seg_halo, segments])[:, None]
    small = (
        (seg_all[: HALO + rows], seg_all[rows:]),
        (segments[None, :rows], segments[None, rows:]),
        (segments[None, :1], segments[None, tok_rows - 1 :]),
        (spread(dt_bias)[None], spread(a_rate)[None], spread(d_skip)[None]),
    )

    forth = back = block
    arrived, projs = [(0, block)], []
    for step in range(1, last + 1):
        if step == 3:
            forth, back = after(forth, projs[1], small), after(back, projs[1], small)
        elif step > 1:
            forth, back = after(forth, projs[step - 2]), after(back, projs[step - 2])
        arrivals = (forth, back)
        if step < last:
            forth, back = ring_shift(forth, 1), ring_shift(back, -1)
        else:
            far = far_shift(forth, back)
        if step == W_FIRST:
            w_forth, w_back = after((own, own), arrivals)
            w_forth, w_back = ring_shift(w_forth, 1), ring_shift(w_back, -1)
        ahead = last if step == last else 0
        total = projs[-1:]
        fetched = len(arrived) + bool(ahead)
        outs = [shape(tok_rows, 4 * width)] + [shape(feat, 4 * width, kind=BF16)] * bool(ahead)
        results = call(
            functools.partial(project, [distance for distance, _ in arrived], ahead, not total),
            outs,
            [pltpu.VMEM((len(arrived), feat, 4 * width), BF16), pltpu.SemaphoreType.DMA((fetched, 4))],
            in_specs=[VMEM] * len(arrived) + [ANY] * 3 + [VMEM] * len(total),
            flops=10**9,
        )(*[part for _, part in arrived], w_zx, w_bc, w_step, *total)
        projs.append(results[0])
        arrived = [(-step, forth), (step, back)]
    proj = call(project_far, shape(tok_rows, 4 * width), flops=10**9)(
        *far, results[1], projs[-1]
    )

    (seg_ext_a, seg_ext_b), (seg_row_a, seg_row_b), (seg_first, seg_last), (bias, rate, skip) = small
    halo = lax.ppermute(proj[tok_rows - HALO :, width : 3 * width].astype(BF16), "seq", shift_rows)

    msg_rows = state_w + 8
    plane = shape(rows, width)
    ext = pltpu.VMEM((HALO + rows, width), F32)
    out_b, bc_b, enter_b, state_b, gate_b = call(
        functools.partial(later_block, heads, width, rows),
        [plane, plane, plane, shape(msg_rows, width), plane],
        [ext, ext],
    )(proj, seg_ext_b, seg_row_b, conv_x, conv_bc, bias, rate, skip)
    cx_a, bc_a, cum_a, scaled_a, enter_a, state_a, message = call(
        functools.partial(first_front, width, rows),
        [plane] * 5 + [shape(msg_rows, width)] * 2,
        [ext, ext],
    )(proj, halo, seg_ext_a, seg_last, state_b, conv_x, conv_bc, bias, rate)
    if n_seq == 4:
        other_core = lax.ppermute(message, "seq", [(i, i ^ 1) for i in range(n_seq)])
        other_plane = lax.ppermute(message, "seq", [(i, i ^ 2) for i in range(n_seq)])
        other_both = lax.ppermute(other_core, "seq", [(i, i ^ 2) for i in range(n_seq)])
        messages = (message, other_core, other_plane, other_both)
    else:
        messages = (lax.all_gather(message, "seq"),)
    gated = call(functools.partial(finish, heads, rows, len(messages)), shape(tok_rows, width, kind=BF16))(
        seg_first, *messages, seg_ext_a, seg_row_a, skip, proj, cx_a, bc_a, cum_a, scaled_a, enter_a, state_a,
        out_b, gate_b, bc_b, enter_b
    )
    tok_own = tok_rows // n_tensor

    w_steps = [(w_forth, w_back)]
    orders = [(far, projs[-1]), messages]
    for step in range(2, last + 1):
        if step - 2 < len(orders):
            w_forth, w_back = after((w_forth, w_back), orders[step - 2])
        if step == last:
            w_far = far_shift(w_forth, w_back)
            break
        w_forth, w_back = ring_shift(w_forth, 1), ring_shift(w_back, -1)
        w_steps.append((w_forth, w_back))
        if step == 2:
            blocks = after(gated, w_forth, w_back).reshape(n_tensor, tok_own, width)
            mine = lax.all_to_all(blocks, "tensor", 0, 0)
    swap = [(i, i ^ 1) for i in range(n_seq)]
    other = lax.ppermute(mine, "seq", swap)
    pieces, distances = [own], [0]
    for i, pair in enumerate(w_steps):
        pieces += pair
        distances += [-i - 1, i + 1]
    total = call(functools.partial(product_early, distances), shape(2 * tok_own, columns), flops=1, moved=1)(
        mine, other, *pieces
    )
    half = shape(tok_own, columns, kind=BF16)
    held = [pltpu.VMEM((width, columns), BF16)]
    out_other = call(functools.partial(last_other, last), half, held)(other, total, *w_far)
    arrived = lax.ppermute(out_other, "seq", swap)
    whole = call(functools.partial(last_mine, last), shape(tok_own, model, kind=BF16), held)(mine, total, *w_far)
    return call(
        put_other,
        shape(tok_own, model, kind=BF16),
        [pltpu.SemaphoreType.DMA],
        in_specs=[ANY, VMEM],
        out_specs=ANY,
        input_output_aliases={0: 0},
    )(whole, arrived)


def solution(mesh):
    in_specs = (
        P("seq", "tensor"),
        P(None, None, "tensor"),
        P(),
        P(None, "tensor"),
        P("tensor"),
        P("tensor"),
        P("tensor"),
        P(None, "tensor"),
        P(),
        P("tensor"),
        P("tensor", None),
        P("seq"),
    )
    out_specs = P(("seq", "tensor"), None)
    return jax.shard_map(local, mesh=mesh, in_specs=in_specs, out_specs=out_specs, check_vma=False)
```

```python
import functools

import jax
import jax.numpy as jnp
import numpy as np
from jax import lax
from jax.experimental import pallas as pl
from jax.experimental.pallas import tpu as pltpu
from jax.sharding import PartitionSpec as P

NORM_EPS = 1e-05
F32 = jnp.float32
BF16 = jnp.bfloat16
VMEM = pl.BlockSpec(memory_space=pltpu.VMEM)
ANY = pl.BlockSpec(memory_space=pl.ANY)
HALO = 8
W_FIRST = 3


def ring_place(index, n):
    return jnp.where(index % 2 == 0, index // 2, (2 * n - 1 - index) // 2)


def ring_index(place, n):
    return jnp.where(place < n // 2, 2 * place, 2 * n - 1 - 2 * place)


def ring_shift(block, step):
    n = lax.axis_size("tensor")
    order = [2 * i if i < n // 2 else 2 * n - 1 - 2 * i for i in range(n)]
    return lax.ppermute(block, "tensor", [(order[i], order[(i + step) % n]) for i in range(n)])


def after(values, *earlier):
    return lax.optimization_barrier((values, earlier))[0]


def far_shift(forth, back):
    cut = forth.shape[0] // 32 * 16
    parts = [jax.ShapeDtypeStruct((size, forth.shape[1]), forth.dtype) for size in (cut, forth.shape[0] - cut)]
    top, bottom = call(halves, parts)(forth, back)
    return ring_shift(top, 1), ring_shift(bottom, -1)


def halves(forth, back, top, bottom):
    size = top.shape[0]
    top[...] = forth[:size]
    bottom[...] = back[size:]


def silu(v):
    return v / (1.0 + jnp.exp(-v))


def dot(a, b, dims=((1,), (0,))):
    return lax.dot_general(a.astype(BF16), b.astype(BF16), (dims, ((), ())), preferred_element_type=F32)


def source_of(distance):
    n = lax.axis_size("tensor")
    return ring_index((ring_place(lax.axis_index("tensor"), n) + distance + n) % n, n)


def project(distances, ahead, first, *refs):
    count, fetched = len(distances), len(distances) + bool(ahead)
    blocks, (w_zx, w_bc, w_dt), refs = refs[:count], refs[count : count + 3], refs[count + 3 :]
    total, refs = (None, refs) if first else (refs[0], refs[1:])
    out, far_out, held, sems = refs if ahead else (refs[0], None, *refs[1:])
    feat, width = held.shape[1], w_bc.shape[1]
    sources = [w_zx.at[0], w_zx.at[1], w_bc, w_dt]
    copies = []
    for k, distance in enumerate([*distances, ahead][:fetched]):
        rows = pl.ds(pl.multiple_of(source_of(distance) * feat, 16), feat)
        for j, source in enumerate(sources):
            target = held.at[k] if k < count else far_out
            copies.append(
                pltpu.make_async_copy(source.at[rows], target.at[:, pl.ds(j * width, width)], sems.at[k, j])
            )
            copies[-1].start()
    result = 0.0 if first else total[...]
    for k in range(count):
        for j in range(len(sources)):
            copies[k * len(sources) + j].wait()
        result = result + dot(blocks[k][...], held[k], ((0,), (0,)))
    out[...] = result
    for copy in copies[count * len(sources) :]:
        copy.wait()


def project_far(top, bottom, weights, total, out):
    cut = top.shape[0]
    out[...] = (
        total[...] + dot(top[...], weights[:cut], ((0,), (0,))) + dot(bottom[...], weights[cut:], ((0,), (0,)))
    )


def conv(ext, seg_ext, taps, rows):
    size = taps.shape[0]
    seg_now = seg_ext[HALO : HALO + rows]
    total = taps[size - 1 : size] * ext[HALO : HALO + rows]
    for offset in range(1, size):
        same = seg_ext[HALO - offset : HALO - offset + rows] == seg_now
        total = total + taps[size - 1 - offset : size - offset] * jnp.where(
            same, ext[HALO - offset : HALO - offset + rows], 0.0
        )
    return silu(total)


def prefix_sum(values):
    rows = values.shape[0]
    lower = lax.broadcasted_iota(jnp.int32, (rows, rows), 0) >= lax.broadcasted_iota(jnp.int32, (rows, rows), 1)
    lower = jnp.where(lower, 1.0, 0.0).astype(BF16)
    total = jnp.zeros(values.shape, F32)
    rest = values
    parts = []
    for _ in range(3):
        part = rest.astype(BF16)
        parts.append(part)
        rest = rest - part.astype(F32)
    for part in reversed(parts):
        total = total + jnp.dot(lower, part, preferred_element_type=F32)
    return total


def block_front(ext_x, ext_bc, seg_ext, dt_raw, taps_x, taps_bc, bias, rate, rows, seg_enter, seg_leave):
    conv_x = conv(ext_x, seg_ext, taps_x, rows)
    conv_bc = conv(ext_bc, seg_ext, taps_bc, rows)
    seg = seg_ext[HALO : HALO + rows]
    shifted = dt_raw + bias
    step_size = jnp.maximum(shifted, 0.0) + jnp.log1p(jnp.exp(-jnp.abs(shifted)))
    cum = prefix_sum(-rate * step_size)
    scaled = conv_x * step_size
    last = cum[rows - 1 : rows]
    tail = jnp.where(seg == seg_leave, jnp.exp(last - cum), 0.0)
    state_w = conv_bc.shape[1] // 2
    state = dot(conv_bc, tail * scaled, ((0,), (0,)))[:state_w]
    enter = jnp.where(seg == seg_enter, jnp.exp(cum), 0.0)
    return conv_x, conv_bc, cum, scaled, state, enter, last


def block_inner(conv_bc, cum, scaled, seg_col, seg_row, heads):
    rows, width = scaled.shape
    state_w = conv_bc.shape[1] // 2
    head_w = width // heads
    scores = dot(conv_bc[:, state_w:], conv_bc[:, :state_w], ((1,), (1,)))
    later = lax.broadcasted_iota(jnp.int32, (rows, rows), 0) >= lax.broadcasted_iota(jnp.int32, (rows, rows), 1)
    visible = (seg_col == seg_row) & later
    cum_rows = cum.T
    lane = lax.broadcasted_iota(jnp.int32, (rows, width), 1)
    result = jnp.zeros((rows, width), F32)
    scaled = scaled.astype(BF16)
    for head in range(heads):
        at = head * head_w
        gap = jnp.where(visible, cum[:, at : at + 1] - cum_rows[at : at + 1, :], -jnp.inf)
        part = dot(jnp.exp(gap) * scores, scaled)
        result = jnp.where((lane >= at) & (lane < at + head_w), part, result)
    return result


def later_block(heads, width, rows, proj, seg_ext, seg_row, taps_x, taps_bc, bias, rate, skip,
                out, bc_out, enter_out, state_out, gate_out, ext_x, ext_bc):
    rounded = proj[rows - HALO :, : 3 * width].astype(BF16).astype(F32)
    gate_out[...] = silu(rounded[HALO:, :width])
    ext_x[...] = rounded[:, width : 2 * width]
    ext_bc[...] = rounded[:, 2 * width : 3 * width]
    seg_enter = seg_ext[HALO - 1 : HALO]
    seg_leave = seg_ext[HALO + rows - 1 : HALO + rows]
    conv_x, conv_bc, cum, scaled, state, enter, last = block_front(
        ext_x, ext_bc, seg_ext, proj[rows:, 3 * width :], taps_x, taps_bc[...], bias[...], rate[...], rows, seg_enter, seg_leave
    )
    out[...] = block_inner(conv_bc, cum, scaled, seg_ext[HALO:], seg_row[...], heads) + skip[...] * conv_x
    bc_out[...] = conv_bc
    enter_out[...] = enter
    keep = jnp.where(seg_enter == seg_leave, jnp.exp(last), 0.0)
    state_w = state.shape[0]
    state_out[:state_w] = state
    state_out[state_w : state_w + 1] = keep
    state_out[state_w + 1 : state_w + 2] = last
    state_out[state_w + 2 :] = jnp.zeros((state_out.shape[0] - state_w - 2, width), F32)


def first_front(width, rows, proj, halo, seg_ext, seg_last, state_b, taps_x, taps_bc, bias, rate,
                conv_out, bc_out, cum_out, scaled_out, enter_out, state_out, message, ext_x, ext_bc):
    ext_x[:HALO] = halo[:, :width].astype(F32)
    ext_bc[:HALO] = halo[:, width:].astype(F32)
    ext_x[HALO:] = proj[:rows, width : 2 * width].astype(BF16).astype(F32)
    ext_bc[HALO:] = proj[:rows, 2 * width : 3 * width].astype(BF16).astype(F32)
    seg_enter = seg_ext[HALO : HALO + 1]
    seg_leave = seg_ext[HALO + rows - 1 : HALO + rows]
    conv_x, conv_bc, cum, scaled, state, enter, last = block_front(
        ext_x, ext_bc, seg_ext, proj[:rows, 3 * width :], taps_x, taps_bc[...], bias[...], rate[...], rows, seg_enter, seg_leave
    )
    conv_out[...] = conv_x
    bc_out[...] = conv_bc
    cum_out[...] = cum
    scaled_out[...] = scaled
    enter_out[...] = enter
    keep = jnp.where(seg_enter == seg_leave, jnp.exp(last), 0.0)
    state_w = state.shape[0]
    state_out[:state_w] = state
    state_out[state_w : state_w + 1] = keep
    state_out[state_w + 1 :] = jnp.zeros((state_out.shape[0] - state_w - 1, width), F32)
    message[:state_w] = (state_b[state_w : state_w + 1] * state + state_b[:state_w]).astype(BF16)
    rest = last + state_b[state_w + 1 : state_w + 2]
    row = lax.broadcasted_iota(jnp.int32, (message.shape[0] - state_w, width), 0)
    head = jnp.where(row == 3, seg_last[...].astype(F32), 0.0)
    for k in range(3):
        part = rest.astype(BF16).astype(F32)
        head = jnp.where(row == k, part, head)
        rest = rest - part
    message[state_w:] = head.astype(BF16)


def finish(heads, rows, count, seg_first, *refs):
    messages, refs = refs[:count], refs[count:]
    finish_with(heads, rows, seg_first, messages, *refs)


def message_from(messages, device):
    if len(messages) == 1:
        return messages[0][device].astype(F32)
    place = lax.axis_index("seq")
    core = place % 2 == device % 2
    plane = place // 2 == device // 2
    own, other_core, other_plane, other_both = (m[...].astype(F32) for m in messages)
    return jnp.where(plane, jnp.where(core, own, other_core), jnp.where(core, other_plane, other_both))


def finish_with(heads, rows, seg_first, messages, seg_ext_a, seg_row_a, skip, proj, conv_a, bc_a, cum_a, scaled_a, enter_a,
           state_a, out_b, gate_b, bc_b, enter_b, gated):
    state_w = bc_a.shape[1] // 2
    width = out_b.shape[1]
    entering = jnp.zeros((state_w, width), F32)
    decay = jnp.zeros((1, width), F32)
    first = seg_first[...].astype(F32)
    place = lax.axis_index("seq")
    for device in reversed(range(lax.axis_size("seq") - 1)):
        earlier = device < place
        message = message_from(messages, device)
        total = sum(message[state_w + k : state_w + k + 1] for k in (2, 1, 0))
        passes = earlier & (message[state_w + 3 : state_w + 4] == first)
        passes = jnp.where(passes, jnp.exp(decay), 0.0)
        entering = entering + passes * message[:state_w]
        decay = decay + jnp.where(earlier, total, 0.0)
    second = state_a[state_w : state_w + 1] * entering + state_a[:state_w]
    out_a = block_inner(bc_a[...], cum_a[...], scaled_a[...], seg_ext_a[HALO:], seg_row_a[...], heads)
    out_a = out_a + skip[...] * conv_a[...] + enter_a[...] * dot(bc_a[:, state_w:], entering)
    gated[:rows] = (out_a * silu(proj[:rows, :width].astype(BF16).astype(F32))).astype(BF16)
    gated[rows:] = ((out_b[...] + enter_b[...] * dot(bc_b[:, state_w:], second)) * gate_b[...]).astype(BF16)


def product(gated, distances, pieces):
    total = 0.0
    for distance, piece in zip(distances, pieces):
        source = source_of(distance)
        rows = jnp.concatenate([part[source] for part in gated], 0)
        total = total + jnp.dot(rows, piece[...], preferred_element_type=F32)
    return total


def product_early(distances, mine, other, *rest):
    rest[-1][...] = product((mine, other), distances, rest[:-1])


def last_rows(distance, gated, total, top, bottom, held):
    held[: top.shape[0]] = top[...]
    held[top.shape[0] :] = bottom[...]
    blocks, rows, width = gated.shape
    squares = jnp.zeros((rows, width), F32)
    for block in range(blocks):
        value = gated[block].astype(F32)
        squares = squares + value * value
    scale = lax.rsqrt(jnp.sum(squares, axis=1, keepdims=True) / (blocks * width) + NORM_EPS)
    return ((product((gated,), [distance], [held]) + total) * scale).astype(BF16)


def last_other(distance, other, total, top, bottom, out, held):
    rows = other.shape[1]
    out[...] = last_rows(distance, other, total[rows:], top, bottom, held)


def last_mine(distance, mine, total, top, bottom, out, held):
    rows, columns = mine.shape[1], held.shape[1]
    start = pl.multiple_of(lax.axis_index("seq") % 2 * columns, 128)
    out[:, pl.ds(start, columns)] = last_rows(distance, mine, total[:rows], top, bottom, held)


def put_other(whole, arrived, out, sem):
    del whole
    columns = arrived.shape[1]
    start = pl.multiple_of((1 - lax.axis_index("seq") % 2) * columns, 128)
    copy = pltpu.make_async_copy(arrived, out.at[:, pl.ds(start, columns)], sem)
    copy.start()
    copy.wait()


def call(body, outs, scratch=(), vmem=48, flops=10**7, moved=1 << 21, **kw):
    return pl.pallas_call(
        body,
        out_shape=outs,
        scratch_shapes=list(scratch),
        compiler_params=pltpu.CompilerParams(vmem_limit_bytes=vmem << 20),
        cost_estimate=pl.CostEstimate(flops=flops, bytes_accessed=moved, transcendentals=0),
        **kw,
    )


def local(
    tokens, w_zx, w_bc, w_dt, dt_bias, a_rate, d_skip, conv_x, conv_bc, norm_gain, w_out, segments
):
    tok_rows, feat = tokens.shape
    width = w_zx.shape[2]
    heads = dt_bias.shape[0]
    head_w = width // heads
    state_w = w_bc.shape[1] // 2
    model = w_zx.shape[1]
    n_seq, n_tensor = lax.axis_size("seq"), lax.axis_size("tensor")
    seq_at = lax.axis_index("seq")
    rows = tok_rows // 2
    shape = lambda *s, kind=F32: jax.ShapeDtypeStruct(s, kind)

    spread = lambda v: jnp.repeat(v, head_w, axis=-1)
    expand = np.repeat(np.eye(heads, dtype=np.float32), head_w, axis=1)
    w_step = jnp.dot(w_dt, expand.astype(BF16))
    block = tokens.T
    core = seq_at % 2
    columns = model // 2
    own = (lax.dynamic_slice_in_dim(w_out, core * columns, columns, 1).astype(F32) * norm_gain[:, None]).astype(BF16)
    last = n_tensor // 2
    w_half = width // 2
    shift_rows = [(i, i + 1) for i in range(n_seq - 1)]

    seg_halo = lax.ppermute(segments[tok_rows - HALO :], "seq", shift_rows)
    seg_all = jnp.concatenate([seg_halo, segments])[:, None]
    small = (
        (seg_all[: HALO + rows], seg_all[rows:]),
        (segments[None, :rows], segments[None, rows:]),
        (segments[None, :1], segments[None, tok_rows - 1 :]),
        (spread(dt_bias)[None], spread(a_rate)[None], spread(d_skip)[None]),
    )

    forth = back = block
    arrived, projs = [(0, block)], []
    for step in range(1, last + 1):
        if step == 3:
            forth, back = after(forth, projs[1], small), after(back, projs[1], small)
        elif step > 1:
            forth, back = after(forth, projs[step - 2]), after(back, projs[step - 2])
        arrivals = (forth, back)
        if step < last:
            forth, back = ring_shift(forth, 1), ring_shift(back, -1)
        else:
            far = far_shift(forth, back)
        if step == W_FIRST:
            w_forth, w_back = after((own, own), arrivals)
            w_forth, w_back = ring_shift(w_forth, 1), ring_shift(w_back, -1)
        ahead = last if step == last else 0
        total = projs[-1:]
        fetched = len(arrived) + bool(ahead)
        outs = [shape(tok_rows, 4 * width)] + [shape(feat, 4 * width, kind=BF16)] * bool(ahead)
        results = call(
            functools.partial(project, [distance for distance, _ in arrived], ahead, not total),
            outs,
            [pltpu.VMEM((len(arrived), feat, 4 * width), BF16), pltpu.SemaphoreType.DMA((fetched, 4))],
            in_specs=[VMEM] * len(arrived) + [ANY] * 3 + [VMEM] * len(total),
            flops=10**9,
        )(*[part for _, part in arrived], w_zx, w_bc, w_step, *total)
        projs.append(results[0])
        arrived = [(-step, forth), (step, back)]
    proj = call(project_far, shape(tok_rows, 4 * width), flops=10**9)(
        *far, results[1], projs[-1]
    )

    (seg_ext_a, seg_ext_b), (seg_row_a, seg_row_b), (seg_first, seg_last), (bias, rate, skip) = small
    halo = lax.ppermute(proj[tok_rows - HALO :, width : 3 * width].astype(BF16), "seq", shift_rows)

    msg_rows = state_w + 8
    plane = shape(rows, width)
    ext = pltpu.VMEM((HALO + rows, width), F32)
    out_b, bc_b, enter_b, state_b, gate_b = call(
        functools.partial(later_block, heads, width, rows),
        [plane, plane, plane, shape(msg_rows, width), plane],
        [ext, ext],
    )(proj, seg_ext_b, seg_row_b, conv_x, conv_bc, bias, rate, skip)
    cx_a, bc_a, cum_a, scaled_a, enter_a, state_a, message = call(
        functools.partial(first_front, width, rows),
        [plane] * 5 + [shape(msg_rows, width), shape(state_w + 16, width, kind=BF16)],
        [ext, ext],
    )(proj, halo, seg_ext_a, seg_last, state_b, conv_x, conv_bc, bias, rate)
    if n_seq == 4:
        other_core = lax.ppermute(message, "seq", [(i, i ^ 1) for i in range(n_seq)])
        other_plane = lax.ppermute(message, "seq", [(i, i ^ 2) for i in range(n_seq)])
        other_both = lax.ppermute(other_core, "seq", [(i, i ^ 2) for i in range(n_seq)])
        messages = (message, other_core, other_plane, other_both)
    else:
        messages = (lax.all_gather(message, "seq"),)
    gated = call(functools.partial(finish, heads, rows, len(messages)), shape(tok_rows, width, kind=BF16))(
        seg_first, *messages, seg_ext_a, seg_row_a, skip, proj, cx_a, bc_a, cum_a, scaled_a, enter_a, state_a,
        out_b, gate_b, bc_b, enter_b
    )
    tok_own = tok_rows // n_tensor

    w_steps = [(w_forth, w_back)]
    orders = [(far, projs[-1]), messages]
    for step in range(2, last + 1):
        if step - 2 < len(orders):
            w_forth, w_back = after((w_forth, w_back), orders[step - 2])
        if step == last:
            w_far = far_shift(w_forth, w_back)
            break
        w_forth, w_back = ring_shift(w_forth, 1), ring_shift(w_back, -1)
        w_steps.append((w_forth, w_back))
        if step == 2:
            blocks = after(gated, w_forth, w_back).reshape(n_tensor, tok_own, width)
            mine = lax.all_to_all(blocks, "tensor", 0, 0)
    swap = [(i, i ^ 1) for i in range(n_seq)]
    other = lax.ppermute(mine, "seq", swap)
    pieces, distances = [own], [0]
    for i, pair in enumerate(w_steps):
        pieces += pair
        distances += [-i - 1, i + 1]
    total = call(functools.partial(product_early, distances), shape(2 * tok_own, columns), flops=1, moved=1)(
        mine, other, *pieces
    )
    half = shape(tok_own, columns, kind=BF16)
    held = [pltpu.VMEM((width, columns), BF16)]
    out_other = call(functools.partial(last_other, last), half, held)(other, total, *w_far)
    arrived = lax.ppermute(out_other, "seq", swap)
    whole = call(functools.partial(last_mine, last), shape(tok_own, model, kind=BF16), held)(mine, total, *w_far)
    return call(
        put_other,
        shape(tok_own, model, kind=BF16),
        [pltpu.SemaphoreType.DMA],
        in_specs=[ANY, VMEM],
        out_specs=ANY,
        input_output_aliases={0: 0},
    )(whole, arrived)


def solution(mesh):
    in_specs = (
        P("seq", "tensor"),
        P(None, None, "tensor"),
        P(),
        P(None, "tensor"),
        P("tensor"),
        P("tensor"),
        P("tensor"),
        P(None, "tensor"),
        P(),
        P("tensor"),
        P("tensor", None),
        P("seq"),
    )
    out_specs = P(("seq", "tensor"), None)
    return jax.shard_map(local, mesh=mesh, in_specs=in_specs, out_specs=out_specs, check_vma=False)
```

```python
import functools

import jax
import jax.numpy as jnp
import numpy as np
from jax import lax
from jax.experimental import pallas as pl
from jax.experimental.pallas import tpu as pltpu
from jax.sharding import PartitionSpec as P

NORM_EPS = 1e-05
F32 = jnp.float32
BF16 = jnp.bfloat16
VMEM = pl.BlockSpec(memory_space=pltpu.VMEM)
ANY = pl.BlockSpec(memory_space=pl.ANY)
HALO = 8
W_FIRST = 3


def ring_place(index, n):
    return jnp.where(index % 2 == 0, index // 2, (2 * n - 1 - index) // 2)


def ring_index(place, n):
    return jnp.where(place < n // 2, 2 * place, 2 * n - 1 - 2 * place)


def ring_shift(block, step):
    n = lax.axis_size("tensor")
    order = [2 * i if i < n // 2 else 2 * n - 1 - 2 * i for i in range(n)]
    return lax.ppermute(block, "tensor", [(order[i], order[(i + step) % n]) for i in range(n)])


def after(values, *earlier):
    return lax.optimization_barrier((values, earlier))[0]


def far_shift(forth, back):
    cut = forth.shape[0] // 32 * 16
    parts = [jax.ShapeDtypeStruct((size, forth.shape[1]), forth.dtype) for size in (cut, forth.shape[0] - cut)]
    top, bottom = call(halves, parts)(forth, back)
    return ring_shift(top, 1), ring_shift(bottom, -1)


def halves(forth, back, top, bottom):
    size = top.shape[0]
    top[...] = forth[:size]
    bottom[...] = back[size:]


def silu(v):
    return v / (1.0 + jnp.exp(-v))


def dot(a, b, dims=((1,), (0,))):
    return lax.dot_general(a.astype(BF16), b.astype(BF16), (dims, ((), ())), preferred_element_type=F32)


def source_of(distance):
    n = lax.axis_size("tensor")
    return ring_index((ring_place(lax.axis_index("tensor"), n) + distance + n) % n, n)


def project(distances, ahead, first, *refs):
    count, fetched = len(distances), len(distances) + bool(ahead)
    blocks, (w_zx, w_bc, w_dt), refs = refs[:count], refs[count : count + 3], refs[count + 3 :]
    total, refs = (None, refs) if first else (refs[0], refs[1:])
    out, far_out, held, sems = refs if ahead else (refs[0], None, *refs[1:])
    feat, width = held.shape[1], w_bc.shape[1]
    sources = [w_zx.at[0], w_zx.at[1], w_bc, w_dt]
    copies = []
    for k, distance in enumerate([*distances, ahead][:fetched]):
        rows = pl.ds(pl.multiple_of(source_of(distance) * feat, 16), feat)
        for j, source in enumerate(sources):
            target = held.at[k] if k < count else far_out
            copies.append(
                pltpu.make_async_copy(source.at[rows], target.at[:, pl.ds(j * width, width)], sems.at[k, j])
            )
            copies[-1].start()
    result = 0.0 if first else total[...]
    for k in range(count):
        for j in range(len(sources)):
            copies[k * len(sources) + j].wait()
        result = result + dot(blocks[k][...], held[k], ((0,), (0,)))
    out[...] = result
    for copy in copies[count * len(sources) :]:
        copy.wait()


def project_far(top, bottom, weights, total, out):
    cut = top.shape[0]
    out[...] = (
        total[...] + dot(top[...], weights[:cut], ((0,), (0,))) + dot(bottom[...], weights[cut:], ((0,), (0,)))
    )


def conv(ext, seg_ext, taps, rows):
    size = taps.shape[0]
    seg_now = seg_ext[HALO : HALO + rows]
    total = taps[size - 1 : size] * ext[HALO : HALO + rows]
    for offset in range(1, size):
        same = seg_ext[HALO - offset : HALO - offset + rows] == seg_now
        total = total + taps[size - 1 - offset : size - offset] * jnp.where(
            same, ext[HALO - offset : HALO - offset + rows], 0.0
        )
    return silu(total)


def prefix_sum(values):
    rows = values.shape[0]
    lower = lax.broadcasted_iota(jnp.int32, (rows, rows), 0) >= lax.broadcasted_iota(jnp.int32, (rows, rows), 1)
    lower = jnp.where(lower, 1.0, 0.0).astype(BF16)
    total = jnp.zeros(values.shape, F32)
    rest = values
    parts = []
    for _ in range(3):
        part = rest.astype(BF16)
        parts.append(part)
        rest = rest - part.astype(F32)
    for part in reversed(parts):
        total = total + jnp.dot(lower, part, preferred_element_type=F32)
    return total


def block_front(ext_x, ext_bc, seg_ext, dt_raw, taps_x, taps_bc, bias, rate, rows, seg_enter, seg_leave):
    conv_x = conv(ext_x, seg_ext, taps_x, rows)
    conv_bc = conv(ext_bc, seg_ext, taps_bc, rows)
    seg = seg_ext[HALO : HALO + rows]
    shifted = dt_raw + bias
    step_size = jnp.maximum(shifted, 0.0) + jnp.log1p(jnp.exp(-jnp.abs(shifted)))
    cum = prefix_sum(-rate * step_size)
    scaled = conv_x * step_size
    last = cum[rows - 1 : rows]
    tail = jnp.where(seg == seg_leave, jnp.exp(last - cum), 0.0)
    state_w = conv_bc.shape[1] // 2
    state = dot(conv_bc, tail * scaled, ((0,), (0,)))[:state_w]
    enter = jnp.where(seg == seg_enter, jnp.exp(cum), 0.0)
    return conv_x, conv_bc, cum, scaled, state, enter, last


def block_inner(conv_bc, cum, scaled, seg_col, seg_row, heads):
    rows, width = scaled.shape
    state_w = conv_bc.shape[1] // 2
    head_w = width // heads
    scores = dot(conv_bc[:, state_w:], conv_bc[:, :state_w], ((1,), (1,)))
    later = lax.broadcasted_iota(jnp.int32, (rows, rows), 0) >= lax.broadcasted_iota(jnp.int32, (rows, rows), 1)
    visible = (seg_col == seg_row) & later
    cum_rows = cum.T
    lane = lax.broadcasted_iota(jnp.int32, (rows, width), 1)
    result = jnp.zeros((rows, width), F32)
    scaled = scaled.astype(BF16)
    for head in range(heads):
        at = head * head_w
        gap = jnp.where(visible, cum[:, at : at + 1] - cum_rows[at : at + 1, :], -jnp.inf)
        part = dot(jnp.exp(gap) * scores, scaled)
        result = jnp.where((lane >= at) & (lane < at + head_w), part, result)
    return result


def later_block(heads, width, rows, proj, seg_ext, seg_row, taps_x, taps_bc, bias, rate, skip,
                out, bc_out, enter_out, state_out, gate_out, ext_x, ext_bc):
    rounded = proj[rows - HALO :, : 3 * width].astype(BF16).astype(F32)
    gate_out[...] = silu(rounded[HALO:, :width])
    ext_x[...] = rounded[:, width : 2 * width]
    ext_bc[...] = rounded[:, 2 * width : 3 * width]
    seg_enter = seg_ext[HALO - 1 : HALO]
    seg_leave = seg_ext[HALO + rows - 1 : HALO + rows]
    conv_x, conv_bc, cum, scaled, state, enter, last = block_front(
        ext_x, ext_bc, seg_ext, proj[rows:, 3 * width :], taps_x, taps_bc[...], bias[...], rate[...], rows, seg_enter, seg_leave
    )
    out[...] = block_inner(conv_bc, cum, scaled, seg_ext[HALO:], seg_row[...], heads) + skip[...] * conv_x
    bc_out[...] = conv_bc
    enter_out[...] = enter
    keep = jnp.where(seg_enter == seg_leave, jnp.exp(last), 0.0)
    state_w = state.shape[0]
    state_out[:state_w] = state
    state_out[state_w : state_w + 1] = keep
    state_out[state_w + 1 : state_w + 2] = last
    state_out[state_w + 2 :] = jnp.zeros((state_out.shape[0] - state_w - 2, width), F32)


def first_front(width, rows, proj, halo, seg_ext, seg_last, state_b, taps_x, taps_bc, bias, rate,
                conv_out, bc_out, cum_out, scaled_out, enter_out, state_out, message, ext_x, ext_bc):
    ext_x[:HALO] = halo[:, :width].astype(F32)
    ext_bc[:HALO] = halo[:, width:].astype(F32)
    ext_x[HALO:] = proj[:rows, width : 2 * width].astype(BF16).astype(F32)
    ext_bc[HALO:] = proj[:rows, 2 * width : 3 * width].astype(BF16).astype(F32)
    seg_enter = seg_ext[HALO : HALO + 1]
    seg_leave = seg_ext[HALO + rows - 1 : HALO + rows]
    conv_x, conv_bc, cum, scaled, state, enter, last = block_front(
        ext_x, ext_bc, seg_ext, proj[:rows, 3 * width :], taps_x, taps_bc[...], bias[...], rate[...], rows, seg_enter, seg_leave
    )
    conv_out[...] = conv_x
    bc_out[...] = conv_bc
    cum_out[...] = cum
    scaled_out[...] = scaled
    enter_out[...] = enter
    keep = jnp.where(seg_enter == seg_leave, jnp.exp(last), 0.0)
    state_w = state.shape[0]
    state_out[:state_w] = state
    state_out[state_w : state_w + 1] = keep
    state_out[state_w + 1 :] = jnp.zeros((state_out.shape[0] - state_w - 1, width), F32)
    message[:state_w] = (state_b[state_w : state_w + 1] * state + state_b[:state_w]).astype(BF16)
    rest = last + state_b[state_w + 1 : state_w + 2]
    row = lax.broadcasted_iota(jnp.int32, (message.shape[0] - state_w, width), 0)
    head = jnp.where(row == 3, seg_last[...].astype(F32), 0.0)
    for k in range(3):
        part = rest.astype(BF16).astype(F32)
        head = jnp.where(row == k, part, head)
        rest = rest - part
    message[state_w:] = head.astype(BF16)


def finish(heads, rows, count, seg_first, *refs):
    messages, refs = refs[:count], refs[count:]
    finish_with(heads, rows, seg_first, messages, *refs)


def stack(first, second, out):
    out[0] = first[...]
    out[1] = second[...]


def message_from(messages, device):
    if len(messages) == 1:
        return messages[0][device].astype(F32)
    place = lax.axis_index("seq")
    core = place % 2 == device % 2
    plane = place // 2 == device // 2
    own, other_core, other_plane = (m[...].astype(F32) for m in messages)
    here = jnp.where(core, own, other_core)
    return jnp.where(plane, here, jnp.where(core, other_plane[0], other_plane[1]))


def finish_with(heads, rows, seg_first, messages, seg_ext_a, seg_row_a, skip, proj, conv_a, bc_a, cum_a, scaled_a, enter_a,
           state_a, out_b, gate_b, bc_b, enter_b, gated):
    state_w = bc_a.shape[1] // 2
    width = out_b.shape[1]
    entering = jnp.zeros((state_w, width), F32)
    decay = jnp.zeros((1, width), F32)
    first = seg_first[...].astype(F32)
    place = lax.axis_index("seq")
    for device in reversed(range(lax.axis_size("seq") - 1)):
        earlier = device < place
        message = message_from(messages, device)
        total = sum(message[state_w + k : state_w + k + 1] for k in (2, 1, 0))
        passes = earlier & (message[state_w + 3 : state_w + 4] == first)
        passes = jnp.where(passes, jnp.exp(decay), 0.0)
        entering = entering + passes * message[:state_w]
        decay = decay + jnp.where(earlier, total, 0.0)
    second = state_a[state_w : state_w + 1] * entering + state_a[:state_w]
    out_a = block_inner(bc_a[...], cum_a[...], scaled_a[...], seg_ext_a[HALO:], seg_row_a[...], heads)
    out_a = out_a + skip[...] * conv_a[...] + enter_a[...] * dot(bc_a[:, state_w:], entering)
    gated[:rows] = (out_a * silu(proj[:rows, :width].astype(BF16).astype(F32))).astype(BF16)
    gated[rows:] = ((out_b[...] + enter_b[...] * dot(bc_b[:, state_w:], second)) * gate_b[...]).astype(BF16)


def product(gated, distances, pieces):
    total = 0.0
    for distance, piece in zip(distances, pieces):
        source = source_of(distance)
        rows = jnp.concatenate([part[source] for part in gated], 0)
        total = total + jnp.dot(rows, piece[...], preferred_element_type=F32)
    return total


def product_early(distances, mine, other, *rest):
    rest[-1][...] = product((mine, other), distances, rest[:-1])


def last_rows(distance, gated, total, top, bottom, held):
    held[: top.shape[0]] = top[...]
    held[top.shape[0] :] = bottom[...]
    blocks, rows, width = gated.shape
    squares = jnp.zeros((rows, width), F32)
    for block in range(blocks):
        value = gated[block].astype(F32)
        squares = squares + value * value
    scale = lax.rsqrt(jnp.sum(squares, axis=1, keepdims=True) / (blocks * width) + NORM_EPS)
    return ((product((gated,), [distance], [held]) + total) * scale).astype(BF16)


def last_other(distance, other, total, top, bottom, out, held):
    rows = other.shape[1]
    out[...] = last_rows(distance, other, total[rows:], top, bottom, held)


def last_mine(distance, mine, total, top, bottom, out, held):
    rows, columns = mine.shape[1], held.shape[1]
    start = pl.multiple_of(lax.axis_index("seq") % 2 * columns, 128)
    out[:, pl.ds(start, columns)] = last_rows(distance, mine, total[:rows], top, bottom, held)


def put_other(whole, arrived, out, sem):
    del whole
    columns = arrived.shape[1]
    start = pl.multiple_of((1 - lax.axis_index("seq") % 2) * columns, 128)
    copy = pltpu.make_async_copy(arrived, out.at[:, pl.ds(start, columns)], sem)
    copy.start()
    copy.wait()


def call(body, outs, scratch=(), vmem=48, flops=10**7, moved=1 << 21, **kw):
    return pl.pallas_call(
        body,
        out_shape=outs,
        scratch_shapes=list(scratch),
        compiler_params=pltpu.CompilerParams(vmem_limit_bytes=vmem << 20),
        cost_estimate=pl.CostEstimate(flops=flops, bytes_accessed=moved, transcendentals=0),
        **kw,
    )


def local(
    tokens, w_zx, w_bc, w_dt, dt_bias, a_rate, d_skip, conv_x, conv_bc, norm_gain, w_out, segments
):
    tok_rows, feat = tokens.shape
    width = w_zx.shape[2]
    heads = dt_bias.shape[0]
    head_w = width // heads
    state_w = w_bc.shape[1] // 2
    model = w_zx.shape[1]
    n_seq, n_tensor = lax.axis_size("seq"), lax.axis_size("tensor")
    seq_at = lax.axis_index("seq")
    rows = tok_rows // 2
    shape = lambda *s, kind=F32: jax.ShapeDtypeStruct(s, kind)

    spread = lambda v: jnp.repeat(v, head_w, axis=-1)
    expand = np.repeat(np.eye(heads, dtype=np.float32), head_w, axis=1)
    w_step = jnp.dot(w_dt, expand.astype(BF16))
    block = tokens.T
    core = seq_at % 2
    columns = model // 2
    own = (lax.dynamic_slice_in_dim(w_out, core * columns, columns, 1).astype(F32) * norm_gain[:, None]).astype(BF16)
    last = n_tensor // 2
    w_half = width // 2
    shift_rows = [(i, i + 1) for i in range(n_seq - 1)]

    seg_halo = lax.ppermute(segments[tok_rows - HALO :], "seq", shift_rows)
    seg_all = jnp.concatenate([seg_halo, segments])[:, None]
    small = (
        (seg_all[: HALO + rows], seg_all[rows:]),
        (segments[None, :rows], segments[None, rows:]),
        (segments[None, :1], segments[None, tok_rows - 1 :]),
        (spread(dt_bias)[None], spread(a_rate)[None], spread(d_skip)[None]),
    )

    forth = back = block
    arrived, projs = [(0, block)], []
    for step in range(1, last + 1):
        if step == 3:
            forth, back = after(forth, projs[1], small), after(back, projs[1], small)
        elif step > 1:
            forth, back = after(forth, projs[step - 2]), after(back, projs[step - 2])
        arrivals = (forth, back)
        if step < last:
            forth, back = ring_shift(forth, 1), ring_shift(back, -1)
        else:
            far = far_shift(forth, back)
        if step == W_FIRST:
            w_forth, w_back = after((own, own), arrivals)
            w_forth, w_back = ring_shift(w_forth, 1), ring_shift(w_back, -1)
        ahead = last if step == last else 0
        total = projs[-1:]
        fetched = len(arrived) + bool(ahead)
        outs = [shape(tok_rows, 4 * width)] + [shape(feat, 4 * width, kind=BF16)] * bool(ahead)
        results = call(
            functools.partial(project, [distance for distance, _ in arrived], ahead, not total),
            outs,
            [pltpu.VMEM((len(arrived), feat, 4 * width), BF16), pltpu.SemaphoreType.DMA((fetched, 4))],
            in_specs=[VMEM] * len(arrived) + [ANY] * 3 + [VMEM] * len(total),
            flops=10**9,
        )(*[part for _, part in arrived], w_zx, w_bc, w_step, *total)
        projs.append(results[0])
        arrived = [(-step, forth), (step, back)]
    proj = call(project_far, shape(tok_rows, 4 * width), flops=10**9)(
        *far, results[1], projs[-1]
    )

    (seg_ext_a, seg_ext_b), (seg_row_a, seg_row_b), (seg_first, seg_last), (bias, rate, skip) = small
    halo = lax.ppermute(proj[tok_rows - HALO :, width : 3 * width].astype(BF16), "seq", shift_rows)

    msg_rows = state_w + 8
    plane = shape(rows, width)
    ext = pltpu.VMEM((HALO + rows, width), F32)
    out_b, bc_b, enter_b, state_b, gate_b = call(
        functools.partial(later_block, heads, width, rows),
        [plane, plane, plane, shape(msg_rows, width), plane],
        [ext, ext],
    )(proj, seg_ext_b, seg_row_b, conv_x, conv_bc, bias, rate, skip)
    cx_a, bc_a, cum_a, scaled_a, enter_a, state_a, message = call(
        functools.partial(first_front, width, rows),
        [plane] * 5 + [shape(msg_rows, width), shape(state_w + 16, width, kind=BF16)],
        [ext, ext],
    )(proj, halo, seg_ext_a, seg_last, state_b, conv_x, conv_bc, bias, rate)
    if n_seq == 4:
        other_core = lax.ppermute(message, "seq", [(i, i ^ 1) for i in range(n_seq)])
        chip = call(stack, shape(2, *message.shape, kind=BF16))(message, other_core)
        messages = (message, other_core, lax.ppermute(chip, "seq", [(i, i ^ 2) for i in range(n_seq)]))
    else:
        messages = (lax.all_gather(message, "seq"),)
    gated = call(functools.partial(finish, heads, rows, len(messages)), shape(tok_rows, width, kind=BF16))(
        seg_first, *messages, seg_ext_a, seg_row_a, skip, proj, cx_a, bc_a, cum_a, scaled_a, enter_a, state_a,
        out_b, gate_b, bc_b, enter_b
    )
    tok_own = tok_rows // n_tensor

    w_steps = [(w_forth, w_back)]
    orders = [(far, projs[-1]), messages]
    for step in range(2, last + 1):
        if step - 2 < len(orders):
            w_forth, w_back = after((w_forth, w_back), orders[step - 2])
        if step == last:
            w_far = far_shift(w_forth, w_back)
            break
        w_forth, w_back = ring_shift(w_forth, 1), ring_shift(w_back, -1)
        w_steps.append((w_forth, w_back))
        if step == 2:
            blocks = after(gated, w_forth, w_back).reshape(n_tensor, tok_own, width)
            mine = lax.all_to_all(blocks, "tensor", 0, 0)
    swap = [(i, i ^ 1) for i in range(n_seq)]
    other = lax.ppermute(mine, "seq", swap)
    pieces, distances = [own], [0]
    for i, pair in enumerate(w_steps):
        pieces += pair
        distances += [-i - 1, i + 1]
    total = call(functools.partial(product_early, distances), shape(2 * tok_own, columns), flops=1, moved=1)(
        mine, other, *pieces
    )
    half = shape(tok_own, columns, kind=BF16)
    held = [pltpu.VMEM((width, columns), BF16)]
    out_other = call(functools.partial(last_other, last), half, held)(other, total, *w_far)
    arrived = lax.ppermute(out_other, "seq", swap)
    whole = call(functools.partial(last_mine, last), shape(tok_own, model, kind=BF16), held)(mine, total, *w_far)
    return call(
        put_other,
        shape(tok_own, model, kind=BF16),
        [pltpu.SemaphoreType.DMA],
        in_specs=[ANY, VMEM],
        out_specs=ANY,
        input_output_aliases={0: 0},
    )(whole, arrived)


def solution(mesh):
    in_specs = (
        P("seq", "tensor"),
        P(None, None, "tensor"),
        P(),
        P(None, "tensor"),
        P("tensor"),
        P("tensor"),
        P("tensor"),
        P(None, "tensor"),
        P(),
        P("tensor"),
        P("tensor", None),
        P("seq"),
    )
    out_specs = P(("seq", "tensor"), None)
    return jax.shard_map(local, mesh=mesh, in_specs=in_specs, out_specs=out_specs, check_vma=False)
```
